32 devices in a mesh: section: 2 (over core), inner: 4 (over y, x), outer: 4 (over z).
Axes of the slice: x: 2, y: 2, z: 4, core: 2. Of those that a mesh axis runs over, the one named last changes fastest.
Arguments:
- hidden_in: bfloat16 [128, 128, 768], P(('inner', 'outer')), may hold values from -6 to 6
- caption_len: int32 [128], P(('inner', 'outer')), may hold values from 1 to 28, as said below
- region_len: int32 [128], P(('inner', 'outer')), may hold values from 10 to 100, as said below
- cotangent: bfloat16 [128, 128, 768], P(('inner', 'outer')), may hold values from -6 to 6
- w_qkv: bfloat16 [2, 768, 2304], P('section'), may hold values from -0.21875 to 0.21875
- b_qv: float32 [2, 2, 768], P('section'), may hold values from -3 to 3
- w_out: bfloat16 [2, 768, 768], P('section'), may hold values from -1.75 to 1.75
- b_out: float32 [2, 768], P('section'), may hold values from -3 to 3
- ln_gain: float32 [2, 2, 768], P('section'), may hold values from 0.5 to 1.5
- ln_bias: float32 [2, 2, 768], P('section'), may hold values from -2 to 2
- w_up: bfloat16 [2, 768, 3072], P('section'), may hold values from -0.21875 to 0.21875
- b_up: float32 [2, 3072], P('section'), may hold values from -3 to 3
- w_down: bfloat16 [2, 3072, 768], P('section'), may hold values from -0.109375 to 0.109375
- b_down: float32 [2, 768], P('section'), may hold values from -3 to 3
Outputs:
- activations: bfloat16 [2, 128, 128, 768], P('section', ('inner', 'outer'))
- input_grads: float32 [2, 128, 128, 768], P('section', ('inner', 'outer'))
- grad_w_qkv: float32 [2, 768, 2304], P('section', 'inner')
- grad_b_qv: float32 [2, 2, 768], P('section', None, 'inner')
- grad_w_out: float32 [2, 768, 768], P('section', 'inner')
- grad_b_out: float32 [2, 768], P('section', 'inner')
- grad_ln_gain: float32 [2, 2, 768], P('section', None, 'inner')
- grad_ln_bias: float32 [2, 2, 768], P('section', None, 'inner')
- grad_w_up: float32 [2, 768, 3072], P('section', 'inner')
- grad_b_up: float32 [2, 3072], P('section', 'inner')
- grad_w_down: float32 [2, 3072, 768], P('section', 'inner')
- grad_b_down: float32 [2, 768], P('section', 'inner')
The draws below stay inside these ranges and needn't reach their ends.
Inputs may be any that keep to these rules, and one draw needn't show every extreme that they name: `caption_len`: some sequence has 28 caption tokens. `region_len`: some sequence has 100 regions.
All inputs are finite; a program needn't handle non-finite values.
Results may differ from the reference program's by a relative error of at most 0.018.
Values may be sent and summed in bfloat16 or wider, within the bound.
No kernel may reach another device: no remote copies, remote signals or barrier semaphores. Data moves between devices by JAX's collectives and lax.ppermute only.
A program may use at most 192 MiB of HBM per device.

```python
import math
import jax
import jax.numpy as jnp
from jax import lax

D = 768
HEADS = 12
FF = 3072
CAP = 28
REG = 100
LENGTH = 128
SEQS = 128


def draw_caption_len(key, part):
    key = jax.random.fold_in(key, 11)
    values = jax.random.randint(jax.random.fold_in(key, 1), (SEQS,), 1, CAP + 1)
    chosen = jax.random.randint(jax.random.fold_in(key, 2), (), 0, SEQS)
    return values.at[chosen].set(CAP).astype(jnp.int32)


def draw_region_len(key, part):
    key = jax.random.fold_in(key, 23)
    values = jax.random.randint(jax.random.fold_in(key, 1), (SEQS,), min(10, REG), REG + 1)
    chosen = jax.random.randint(jax.random.fold_in(key, 2), (), 0, SEQS)
    return values.at[chosen].set(REG).astype(jnp.int32)


def shard_levels(stream_key, shape, split, smallest, high):
    level, own = 1.0, jax.random.fold_in(stream_key, 6)
    for position, shards_of in split:
        heights = jnp.exp(jax.random.uniform(jax.random.fold_in(own, position), (shards_of,), jnp.float32, smallest / len(split), high / len(split)))
        level = level * jnp.repeat(heights, shape[position] // shards_of).reshape([-1 if axis == position else 1 for axis in range(len(shape))])
    return level


def centred(key, extent, scale, bound, pieces=(), kind=jnp.bfloat16):
    entries = scale * jax.random.normal(key, extent, jnp.float32)
    if pieces:
        entries = entries * shard_levels(key, extent, pieces, -0.22, 0.18)
    return jnp.clip(entries, -bound, bound).astype(kind)


def setup_inputs(seed: int = 0) -> dict:
    key_of = jax.random.split(jax.random.key(seed), 15)
    hidden_in = centred(key_of[0], (SEQS, LENGTH, D), 1.0, 6.0, ((0, 16),))
    caption_len = draw_caption_len(jax.random.fold_in(key_of[14], 71), 0)
    region_len = draw_region_len(jax.random.fold_in(key_of[14], 71), 0)
    cotangent = centred(key_of[3], (SEQS, LENGTH, D), 1.0, 6.0, ((0, 16),))
    w_qkv = centred(key_of[4], (2, D, 3 * D), D ** -0.5, 0.21875, ((0, 2),))
    b_qv = centred(key_of[5], (2, 2, D), 0.5, 3.0, ((0, 2),), jnp.float32)
    w_out = centred(key_of[6], (2, D, D), (D // 64) ** -0.5, 1.75, ((0, 2),))
    b_out = centred(key_of[7], (2, D), 0.5, 3.0, ((0, 2),), jnp.float32)
    ln_gain = jnp.clip(1.0 + 0.1 * jax.random.normal(key_of[8], (2, 2, D), jnp.float32), 0.5, 1.5)
    ln_bias = centred(key_of[9], (2, 2, D), 0.3, 2.0, ((0, 2),), jnp.float32)
    w_up = centred(key_of[10], (2, D, FF), D ** -0.5, 0.21875, ((0, 2),))
    b_up = centred(key_of[11], (2, FF), 0.5, 3.0, ((0, 2),), jnp.float32)
    w_down = centred(key_of[12], (2, FF, D), FF ** -0.5, 0.109375, ((0, 2),))
    b_down = centred(key_of[13], (2, D), 0.5, 3.0, ((0, 2),), jnp.float32)
    return dict(hidden_in=hidden_in, caption_len=caption_len, region_len=region_len, cotangent=cotangent, w_qkv=w_qkv, b_qv=b_qv, w_out=w_out, b_out=b_out, ln_gain=ln_gain, ln_bias=ln_bias, w_up=w_up, b_up=b_up, w_down=w_down, b_down=b_down)


@jax.custom_vjp
def low(v):
    return lax.optimization_barrier(v.astype(jnp.bfloat16)).astype(jnp.float32)

@jax.custom_vjp
def low_back(v):
    return v

def low_keep(v):
    return (low(v), None)

def low_pass(kept, grad):
    return (grad,)

def back_keep(v):
    return (v, None)

def back_low(kept, grad):
    return (low(grad),)
low.defvjp(low_keep, low_pass)
low_back.defvjp(back_keep, back_low)
layer_eps = 1e-12

def matmul(left, right):
    return jnp.dot(left, right, precision=lax.Precision.HIGHEST, preferred_element_type=jnp.float32)

def normalize(summed, gain, offset):
    centre = lax.optimization_barrier(jnp.mean(summed, axis=-1, keepdims=True))
    shifted = summed - centre
    spread = lax.optimization_barrier(jnp.mean(shifted * shifted, axis=-1, keepdims=True))
    return shifted * lax.rsqrt(spread + layer_eps) * gain + offset

def layer(layer_in, params, key_valid):
    w_qkv, b_qv, w_out, b_out, gains, offsets, w_up, b_up, w_down, b_down = params
    seq_count, length, width = layer_in.shape
    head_size = width // HEADS
    in_rows = layer_in.reshape(seq_count * length, width)
    bias_row = jnp.concatenate([b_qv[0], jnp.zeros_like(b_qv[0]), b_qv[1]])
    projected = low(low_back(matmul(in_rows, w_qkv) + bias_row)).reshape(seq_count, length, 3, HEADS, head_size)
    queries = projected[:, :, 0]
    keys_all = projected[:, :, 1]
    values = projected[:, :, 2]
    products = jnp.einsum('sqhe,skhe->shqk', queries, keys_all, precision=lax.Precision.HIGHEST)
    scores = jnp.where(key_valid[:, None, None, :], low_back(products * head_size ** (-0.5)), -1e+30)
    probs = low(jax.nn.softmax(scores, axis=-1))
    context = jnp.einsum('shqk,skhe->sqhe', probs, values, precision=lax.Precision.HIGHEST)
    context = low(low_back(context.reshape(seq_count * length, width)))
    attended = low_back(matmul(context, w_out) + b_out)
    normed = normalize(in_rows + attended, gains[0], offsets[0])
    pre_act = low_back(matmul(low(normed), w_up) + b_up)
    act_low = low(jax.nn.gelu(pre_act, approximate=False))
    branch = low_back(matmul(act_low, w_down) + b_down)
    result = normalize(normed + branch, gains[1], offsets[1])
    return result.reshape(seq_count, length, width)

def reference(hidden_in, caption_len, region_len, cotangent, w_qkv, b_qv, w_out, b_out, ln_gain, ln_bias, w_up, b_up, w_down, b_down):
    stacked = tuple((item.astype(jnp.float32) for item in (w_qkv, b_qv, w_out, b_out, ln_gain, ln_bias, w_up, b_up, w_down, b_down)))
    layer_one = tuple((item[0] for item in stacked))
    layer_two = tuple((item[1] for item in stacked))
    group = math.gcd(SEQS, 32)
    groups = SEQS // group
    positions = jnp.arange(LENGTH, dtype=jnp.int32)

    def forward(first_in, probe, params_one, params_two, key_valid):
        out_one = layer(first_in, params_one, key_valid)
        second_in = low_back(low(out_one) + probe)
        out_two = layer(second_in, params_two, key_valid)
        return (out_one, out_two)

    def visit(carried, items):
        block_in, block_cap, block_reg, block_cot = items
        key_valid = (positions[None, :] < block_cap[:, None]) | (positions[None, :] >= CAP) & (positions[None, :] < CAP + block_reg[:, None])
        first_in = block_in.astype(jnp.float32)
        probe = jnp.zeros_like(first_in)
        (out_one, out_two), backward = jax.vjp(lambda first_arg, probe_arg, params_one, params_two: forward(first_arg, probe_arg, params_one, params_two, key_valid), first_in, probe, layer_one, layer_two)
        grad_last = block_cot.astype(jnp.float32) * key_valid[:, :, None].astype(jnp.float32)
        grad_first, grad_probe, grad_one, grad_two = backward((jnp.zeros_like(out_one), grad_last))
        carried = jax.tree.map(lambda summed, latest: summed + latest, carried, (grad_one, grad_two))
        return (carried, (out_one.astype(jnp.bfloat16), out_two.astype(jnp.bfloat16), grad_first, grad_probe))
    zeros_init = jax.tree.map(jnp.zeros_like, (layer_one, layer_two))
    items = (hidden_in.reshape(groups, group, LENGTH, D), caption_len.reshape(groups, group), region_len.reshape(groups, group), cotangent.reshape(groups, group, LENGTH, D))
    (grad_one, grad_two), (act_one, act_two, grad_in_one, grad_in_two) = lax.scan(visit, zeros_init, items)
    activations = jnp.stack([act_one.reshape(SEQS, LENGTH, D), act_two.reshape(SEQS, LENGTH, D)])
    input_grads = jnp.stack([grad_in_one.reshape(SEQS, LENGTH, D), grad_in_two.reshape(SEQS, LENGTH, D)])
    weight_grads = tuple((jnp.stack([former, latter]) for former, latter in zip(grad_one, grad_two)))
    return (activations, input_grads, weight_grads[0], weight_grads[1], weight_grads[2], weight_grads[3], weight_grads[4], weight_grads[5], weight_grads[6], weight_grads[7], weight_grads[8], weight_grads[9])
```

```python
import functools

import jax
import jax.numpy as jnp
from jax import lax
from jax.experimental import pallas as pl
from jax.experimental.pallas import tpu as pltpu
from jax.sharding import PartitionSpec as P

HEADS = 12
CAP = 28
EPS = 1e-12
VMEM = 56 * 1024 * 1024
F32 = jnp.float32
BF16 = jnp.bfloat16


def dot(left, right):
    return jnp.dot(left, right, preferred_element_type=F32)


def dot_t(left, right):
    return lax.dot_general(left, right, (((1,), (1,)), ((), ())), preferred_element_type=F32)


def t_dot(left, right):
    return lax.dot_general(left, right, (((0,), (0,)), ((), ())), preferred_element_type=F32)


def column_sum(values):
    return jnp.sum(values, axis=0, keepdims=True)


def either(flag, body):
    pl.when(flag)(lambda: body(0))
    pl.when(jnp.logical_not(flag))(lambda: body(1))


def standardize(summed):
    centre = jnp.mean(summed, axis=-1, keepdims=True)
    shifted = summed - centre
    spread = jnp.mean(shifted * shifted, axis=-1, keepdims=True)
    scale = lax.rsqrt(spread + EPS)
    return shifted * scale, scale


def norm_back(grad, hat, scale, gain):
    scaled = grad * gain
    return scale * (
        scaled
        - jnp.mean(scaled, axis=-1, keepdims=True)
        - hat * jnp.mean(scaled * hat, axis=-1, keepdims=True)
    )


def lane_halves():
    lane = lax.broadcasted_iota(jnp.int32, (1, 128), 1)
    lower = jnp.where(lane < 64, 1.0, 0.0)
    return lower.astype(BF16), (1.0 - lower).astype(BF16)


def two_heads(block, halves):
    return jnp.concatenate([block * halves[0], block * halves[1]], axis=0)


def call(kernel, grid, in_specs, out_specs, out_shape, scratch, name, flops, nbytes):
    return pl.pallas_call(
        kernel,
        grid_spec=pltpu.PrefetchScalarGridSpec(
            num_scalar_prefetch=1,
            grid=grid,
            in_specs=in_specs,
            out_specs=out_specs,
            scratch_shapes=scratch,
        ),
        out_shape=out_shape,
        compiler_params=pltpu.CompilerParams(vmem_limit_bytes=VMEM),
        cost_estimate=pl.CostEstimate(flops=flops, bytes_accessed=nbytes, transcendentals=0),
        name=name,
    )


def whole(shape):
    return pl.BlockSpec(shape, lambda *_: (0,) * len(shape))


def sds(shape, dtype):
    return jax.ShapeDtypeStruct(shape, dtype)


def attend_kernel(layer, seqs, sec, x, q_a, k_a, v_a, q_b, k_b, v_b, bq, bv, mask, q_o, k_o, v_o, p_o, c_o):
    halves = lane_halves()

    def body(pick):
        wq, wk, wv = ((q_a, k_a, v_a), (q_b, k_b, v_b))[pick]
        rows = x[...]
        q_o[...] = (dot(rows, wq[...]) + bq[...]).astype(BF16)
        k_o[...] = dot(rows, wk[...]).astype(BF16)
        v_o[...] = (dot(rows, wv[...]) + bv[...]).astype(BF16)

    either(sec[0] == layer, body)
    for pair in range(q_o.shape[1] // 128):
        lanes = slice(pair * 128, pair * 128 + 128)
        for seq in range(seqs):
            rows = slice(seq * 128, seq * 128 + 128)
            scores = dot_t(q_o[rows, lanes], two_heads(k_o[rows, lanes], halves)) * 0.125
            scores = jnp.where(mask[seq : seq + 1, :] > 0.5, scores, -1e30)
            probs = []
            for part in (scores[:, :128], scores[:, 128:]):
                e = jnp.exp(part - jnp.max(part, axis=-1, keepdims=True))
                probs.append(e / jnp.sum(e, axis=-1, keepdims=True))
            probs = jnp.concatenate(probs, axis=1)
            p_o[seq, pair] = probs
            c_o[rows, lanes] = dot(
                probs.astype(BF16), two_heads(v_o[rows, lanes], halves)
            ).astype(BF16)


def attend_forward(layer, sec, x, w_own, w_other, bias_q, bias_v, mask):
    rows, width = x.shape
    seqs = mask.shape[0]
    wide = 256
    steps = width // wide
    own = lambda part: pl.BlockSpec(
        (width, wide), lambda j, s: (0, part * steps + jnp.where(s[0] == layer, j, 0))
    )
    other = lambda part: pl.BlockSpec(
        (width, wide), lambda j, s: (0, part * steps + jnp.where(s[0] == layer, 0, j))
    )
    column = pl.BlockSpec((rows, wide), lambda j, s: (0, j))
    bias = pl.BlockSpec((1, wide), lambda j, s: (0, j))
    return call(
        functools.partial(attend_kernel, layer, seqs),
        (steps,),
        [whole((rows, width)), own(0), own(1), own(2), other(0), other(1), other(2), bias, bias, whole(mask.shape)],
        [column, column, column, pl.BlockSpec((seqs, wide // 128, 128, 256), lambda j, s: (0, j, 0, 0)), column],
        [sds((rows, width), BF16)] * 3 + [sds((seqs, HEADS // 2, 128, 256), F32), sds((rows, width), BF16)],
        [],
        "attend_forward",
        2 * rows * width * width * 4,
        20 << 20,
    )(sec, x, w_own, w_own, w_own, w_other, w_other, w_other, bias_q, bias_v, mask)


def erf(value):
    value = jnp.clip(value, -4.0, 4.0)
    square = value * value
    top = -2.72614225801306e-10
    for item in (
        2.77068142495902e-08,
        -2.10102402082508e-06,
        -5.69250639462346e-05,
        -7.34990630326855e-04,
        -2.95459980854025e-03,
        -1.60960333262415e-02,
    ):
        top = top * square + item
    low = -1.45660718464996e-05
    for item in (
        -2.13374055278905e-04,
        -1.68282697438203e-03,
        -7.37332916720468e-03,
        -1.42647390514189e-02,
    ):
        low = low * square + item
    return value * top / low


def up_kernel(layer, sec, x, ctx, wo_a, wo_b, b_out, gain, offset, wu_a, wu_b, b_up, hat_o, scale_o, low_o, act_o, slope_o):
    step = pl.program_id(0)

    def first(pick):
        summed = x[...].astype(F32) + dot(ctx[...], (wo_a, wo_b)[pick][...]) + b_out[...]
        hat, scale = standardize(summed)
        hat_o[...] = hat
        scale_o[...] = scale
        low_o[...] = (hat * gain[...] + offset[...]).astype(BF16)

    def body(pick):
        pl.when(step == 0)(lambda: first(pick))
        pre = dot(low_o[...], (wu_a, wu_b)[pick][...]) + b_up[...]
        share = 0.5 + 0.5 * erf(pre * 0.7071067811865476)
        act_o[...] = (pre * share).astype(BF16)
        slope_o[...] = share + pre * (0.3989422804014327 * jnp.exp(-0.5 * pre * pre))

    either(sec[0] == layer, body)


def up_forward(layer, sec, x, ctx, wo, wo_other, b_out, gain, offset, wu, wu_other, b_up):
    rows, width = x.shape
    hidden = wu.shape[1]
    wide = 768
    steps = hidden // wide
    row = whole((1, width))
    flat = whole((rows, width))
    column = pl.BlockSpec((rows, wide), lambda j, s: (0, j))
    return call(
        functools.partial(up_kernel, layer),
        (steps,),
        [
            flat,
            flat,
            whole((width, width)),
            whole((width, width)),
            row,
            row,
            row,
            pl.BlockSpec((width, wide), lambda j, s: (0, jnp.where(s[0] == layer, j, 0))),
            pl.BlockSpec((width, wide), lambda j, s: (0, jnp.where(s[0] == layer, 0, j))),
            pl.BlockSpec((1, wide), lambda j, s: (0, j)),
        ],
        [flat, whole((rows, 1)), flat, column, column],
        [sds((rows, width), F32), sds((rows, 1), F32), sds((rows, width), BF16), sds((rows, hidden), BF16), sds((rows, hidden), F32)],
        [],
        "up_forward",
        2 * rows * width * (width + hidden),
        20 << 20,
    )(sec, x, ctx, wo, wo_other, b_out, gain, offset, wu, wu_other, b_up)


def down_kernel(layer, sec, act, wd_a, wd_b, hat_one, gain_one, offset_one, b_down, gain, offset, y_o, hat_o, scale_o, total):
    step = pl.program_id(0)

    @pl.when(step == 0)
    def _():
        total[...] = hat_one[...] * gain_one[...] + offset_one[...] + b_down[...]

    def body(pick):
        total[...] += dot(act[...], (wd_a, wd_b)[pick][...])

    either(sec[0] == layer, body)

    @pl.when(step == pl.num_programs(0) - 1)
    def _():
        hat, scale = standardize(total[...])
        hat_o[...] = hat
        scale_o[...] = scale
        y_o[...] = (hat * gain[...] + offset[...]).astype(BF16)


def down_forward(layer, sec, act, wd, wd_other, hat_one, gain_one, offset_one, b_down, gain, offset):
    rows, hidden = act.shape
    width = wd.shape[1]
    wide = 768
    row = whole((1, width))
    flat = whole((rows, width))
    return call(
        functools.partial(down_kernel, layer),
        (hidden // wide,),
        [
            pl.BlockSpec((rows, wide), lambda j, s: (0, j)),
            pl.BlockSpec((wide, width), lambda j, s: (jnp.where(s[0] == layer, j, 0), 0)),
            pl.BlockSpec((wide, width), lambda j, s: (jnp.where(s[0] == layer, 0, j), 0)),
            flat,
            row,
            row,
            row,
            row,
            row,
        ],
        [flat, flat, whole((rows, 1))],
        [sds((rows, width), BF16), sds((rows, width), F32), sds((rows, 1), F32)],
        [pltpu.VMEM((rows, width), F32)],
        "down_forward",
        2 * rows * width * hidden,
        14 << 20,
    )(sec, act, wd, wd_other, hat_one, gain_one, offset_one, b_down, gain, offset)


def down_grad_kernel(sec, gy, hat, scale, gain, act, second_o, branch_o, gain_o, offset_o, bias_o, send_o, keep_o):
    step = pl.program_id(0)
    half = pl.num_programs(0) // 2

    @pl.when(step == 0)
    def _():
        grad = gy[...].astype(F32)
        offset_o[...] = column_sum(grad)
        gain_o[...] = column_sum(grad * hat[...])
        second = norm_back(grad, hat[...], scale[...], gain[...])
        second_o[...] = second
        low = second.astype(BF16)
        branch_o[...] = low
        bias_o[...] = column_sum(low.astype(F32))

    block = t_dot(act[...], branch_o[...]).astype(BF16)

    @pl.when(step < half)
    def _():
        send_o[0] = block

    @pl.when(step >= half)
    def _():
        keep_o[0] = block


def down_grad(sec, gy, hat, scale, gain, act, shards):
    rows, width = gy.shape
    hidden = act.shape[1]
    tall = hidden // shards // 2
    row = whole((1, width))
    flat = whole((rows, width))
    return call(
        down_grad_kernel,
        (2 * shards,),
        [
            flat,
            flat,
            whole((rows, 1)),
            row,
            pl.BlockSpec(
                (rows, tall),
                lambda j, s: (0, 2 * (j % shards) + jnp.where(j < shards, 1 - s[0], s[0])),
            ),
        ],
        [
            flat,
            flat,
            row,
            row,
            row,
            pl.BlockSpec((1, tall, width), lambda j, s: (jnp.minimum(j, shards - 1), 0, 0)),
            pl.BlockSpec((1, tall, width), lambda j, s: (jnp.maximum(j - shards, 0), 0, 0)),
        ],
        [sds((rows, width), F32), sds((rows, width), BF16)]
        + [sds((1, width), F32)] * 3
        + [sds((shards, tall, width), BF16)] * 2,
        [],
        "down_grad",
        2 * rows * width * hidden,
        14 << 20,
    )(sec, gy, hat, scale, gain, act)


def up_grad_kernel(
    layer, sec, branch, second, wd_a, wd_b, slope, low, wu_a, wu_b, hat, scale, gain,
    first_o, attend_o, gain_o, offset_o, b_out_o, b_up_o, send_o, keep_o, total, pre,
):
    step = pl.program_id(0)
    half = pl.num_programs(0) // 2

    @pl.when(step == 0)
    def _():
        total[...] = second[...]

    def body(pick):
        grad = (dot_t(branch[...], (wd_a, wd_b)[pick][...]) * slope[...]).astype(BF16)
        pre[...] = grad
        total[...] += dot_t(grad, (wu_a, wu_b)[pick][...])

    either(sec[0] == layer, body)
    b_up_o[...] = column_sum(pre[...].astype(F32))
    block = t_dot(low[...], pre[...]).astype(BF16)

    @pl.when(step < half)
    def _():
        send_o[...] = block

    @pl.when(step >= half)
    def _():
        keep_o[...] = block

    @pl.when(step == pl.num_programs(0) - 1)
    def _():
        grad = total[...]
        offset_o[...] = column_sum(grad)
        gain_o[...] = column_sum(grad * hat[...])
        first = norm_back(grad, hat[...], scale[...], gain[...])
        first_o[...] = first
        attend = first.astype(BF16)
        attend_o[...] = attend
        b_out_o[...] = column_sum(attend.astype(F32))


def up_grad(layer, sec, branch, second, wd, wd_other, slope, low, wu, wu_other, hat, scale, gain):
    rows, width = branch.shape
    hidden = slope.shape[1]
    wide = 768
    steps = hidden // wide
    half = steps // 2
    row = whole((1, width))
    flat = whole((rows, width))
    at = lambda j, s: (j + half * (1 - s[0])) % steps
    mine = lambda j, s: jnp.where(s[0] == layer, at(j, s), 0)
    theirs = lambda j, s: jnp.where(s[0] == layer, 0, at(j, s))
    return call(
        functools.partial(up_grad_kernel, layer),
        (steps,),
        [
            flat,
            flat,
            pl.BlockSpec((wide, width), lambda j, s: (mine(j, s), 0)),
            pl.BlockSpec((wide, width), lambda j, s: (theirs(j, s), 0)),
            pl.BlockSpec((rows, wide), lambda j, s: (0, at(j, s))),
            flat,
            pl.BlockSpec((width, wide), lambda j, s: (0, mine(j, s))),
            pl.BlockSpec((width, wide), lambda j, s: (0, theirs(j, s))),
            flat,
            whole((rows, 1)),
            row,
        ],
        [
            flat,
            flat,
            row,
            row,
            row,
            pl.BlockSpec((1, wide), lambda j, s: (0, at(j, s))),
            pl.BlockSpec((width, wide), lambda j, s: (0, jnp.minimum(j, half - 1))),
            pl.BlockSpec((width, wide), lambda j, s: (0, jnp.maximum(j - half, 0))),
        ],
        [sds((rows, width), F32), sds((rows, width), BF16)]
        + [sds((1, width), F32)] * 3
        + [sds((1, hidden), F32)]
        + [sds((width, hidden // 2), BF16)] * 2,
        [pltpu.VMEM((rows, width), F32), pltpu.VMEM((rows, wide), BF16)],
        "up_grad",
        6 * rows * width * hidden,
        30 << 20,
    )(sec, branch, second, wd, wd_other, slope, low, wu, wu_other, hat, scale, gain)


def attend_grad_kernel(
    layer, seqs, sec, attend, attend_part, ctx, first, x, q, k, v, probs, wo_a, wo_b,
    q_a, k_a, v_a, q_b, k_b, v_b, bq_o, bv_o, gx_o, low_o, send_o, keep_o, total, gc, gq, gk, gv,
):
    step = pl.program_id(0)
    halves = lane_halves()
    wide = q.shape[1]

    @pl.when(step == 0)
    def _():
        total[...] = first[...]

    def before(pick):
        gc[...] = dot_t(attend[...], (wo_a, wo_b)[pick][...]).astype(BF16)

    either(sec[0] == layer, before)
    lower = lax.broadcasted_iota(jnp.int32, (128, 128), 1) < 64
    for pair in range(wide // 128):
        lanes = slice(pair * 128, pair * 128 + 128)
        for seq in range(seqs):
            rows = slice(seq * 128, seq * 128 + 128)
            grad = gc[rows, lanes]
            p = probs[seq, pair]
            gv_full = t_dot(p.astype(BF16), grad)
            gv[rows, lanes] = jnp.where(lower, gv_full[:128], gv_full[128:]).astype(BF16)
            gp = dot_t(grad, two_heads(v[rows, lanes], halves))
            parts = []
            for side in (slice(0, 128), slice(128, 256)):
                g, pp = gp[:, side], p[:, side]
                parts.append(pp * (g - jnp.sum(g * pp, axis=-1, keepdims=True)))
            gs = jnp.concatenate(parts, axis=1).astype(BF16)
            gq[rows, lanes] = (dot(gs, two_heads(k[rows, lanes], halves)) * 0.125).astype(BF16)
            gk_full = t_dot(gs, q[rows, lanes]) * 0.125
            gk[rows, lanes] = jnp.where(lower, gk_full[:128], gk_full[128:]).astype(BF16)

    bq_o[...] = column_sum(gq[...].astype(F32))
    bv_o[...] = column_sum(gv[...].astype(F32))

    def after(pick):
        wq, wk, wv = ((q_a, k_a, v_a), (q_b, k_b, v_b))[pick]
        total[...] += dot_t(gq[...], wq[...]) + dot_t(gk[...], wk[...]) + dot_t(gv[...], wv[...])

    either(sec[0] == layer, after)

    def store(out):
        rows = x[...]
        out[:, 0:wide] = t_dot(rows, gq[...]).astype(BF16)
        out[:, wide : 2 * wide] = t_dot(rows, gk[...]).astype(BF16)
        out[:, 2 * wide : 3 * wide] = t_dot(rows, gv[...]).astype(BF16)
        out[:, 3 * wide :] = t_dot(ctx[...], attend_part[...]).astype(BF16)

    pl.when(step == 0)(lambda: store(send_o))

    @pl.when(step == 1)
    def _():
        store(keep_o)
        gx_o[...] = total[...]
        low_o[...] = total[...].astype(BF16)


def attend_grad(layer, sec, attend, ctx, first, x, q, k, v, probs, wo, wo_other, w, w_other):
    rows, width = x.shape
    seqs = probs.shape[0]
    wide = width // 2
    row = pl.BlockSpec((1, wide), lambda j, s: (0, at(j, s)))
    flat = whole((rows, width))
    at = lambda j, s: jnp.where(j == 0, 1 - s[0], s[0])
    mine = lambda j, s: jnp.where(s[0] == layer, at(j, s), 0)
    theirs = lambda j, s: jnp.where(s[0] == layer, 0, at(j, s))
    column = pl.BlockSpec((rows, wide), lambda j, s: (0, at(j, s)))
    own = lambda part: pl.BlockSpec((width, wide), lambda j, s: (0, 2 * part + mine(j, s)))
    other = lambda part: pl.BlockSpec((width, wide), lambda j, s: (0, 2 * part + theirs(j, s)))
    return call(
        functools.partial(attend_grad_kernel, layer, seqs),
        (2,),
        [
            flat,
            column,
            flat,
            flat,
            flat,
            column,
            column,
            column,
            pl.BlockSpec((seqs, wide // 128, 128, 256), lambda j, s: (0, at(j, s), 0, 0)),
            pl.BlockSpec((wide, width), lambda j, s: (mine(j, s), 0)),
            pl.BlockSpec((wide, width), lambda j, s: (theirs(j, s), 0)),
            own(0),
            own(1),
            own(2),
            other(0),
            other(1),
            other(2),
        ],
        [row, row, flat, flat, whole((width, 4 * wide)), whole((width, 4 * wide))],
        [sds((1, width), F32)] * 2
        + [sds((rows, width), F32), sds((rows, width), BF16)]
        + [sds((width, 4 * wide), BF16)] * 2,
        [pltpu.VMEM((rows, width), F32)] + [pltpu.VMEM((rows, wide), BF16)] * 4,
        "attend_grad",
        2 * rows * width * width * 10,
        30 << 20,
    )(sec, attend, attend, ctx, first, x, q, k, v, probs, wo, wo_other, w, w, w, w_other, w_other, w_other)


def layer_forward(layer, sec, x, mask, big, other, small):
    w_qkv, w_out, w_up, w_down = big
    o_qkv, o_out, o_up, o_down = other
    b_q, b_v, b_out, gain_one, gain_two, offset_one, offset_two, b_up, b_down = small
    q, k, v, probs, ctx = attend_forward(layer, sec, x, w_qkv, o_qkv, b_q, b_v, mask)
    hat_one, scale_one, low, act, slope = up_forward(
        layer, sec, x, ctx, w_out, o_out, b_out, gain_one, offset_one, w_up, o_up, b_up
    )
    y, hat_two, scale_two = down_forward(
        layer, sec, act, w_down, o_down, hat_one, gain_one, offset_one, b_down, gain_two, offset_two
    )
    return y, (x, q, k, v, probs, ctx, hat_one, scale_one, low, act, slope, hat_two, scale_two)


def layer_backward(layer, sec, gy, cache, big, other, small, shards):
    w_qkv, w_out, w_up, w_down = big
    o_qkv, o_out, o_up, o_down = other
    b_q, b_v, b_out, gain_one, gain_two, offset_one, offset_two, b_up, b_down = small
    x, q, k, v, probs, ctx, hat_one, scale_one, low, act, slope, hat_two, scale_two = cache
    second, branch, g_gain_two, g_offset_two, g_b_down, d_send, d_keep = down_grad(
        sec, gy, hat_two, scale_two, gain_two, act, shards
    )
    first, attend, g_gain_one, g_offset_one, g_b_out, g_b_up, u_send, u_keep = up_grad(
        layer, sec, branch, second, w_down, o_down, slope, low, w_up, o_up, hat_one, scale_one, gain_one
    )
    g_bq, g_bv, gx, gx_low, a_send, a_keep = attend_grad(
        layer, sec, attend, ctx, first, x, q, k, v, probs, w_out, o_out, w_qkv, o_qkv
    )
    little = (g_bq, g_bv, g_b_out, g_gain_one, g_gain_two, g_offset_one, g_offset_two, g_b_up, g_b_down)
    return gx, gx_low, little, ((d_send, d_keep), (u_send, u_keep), (a_send, a_keep))


def exchange(array, axis, bit):
    length = lax.axis_size(axis)
    return lax.ppermute(array, axis, [(i, i ^ bit) for i in range(length)])


def plus(left, right):
    return (left.astype(F32) + right.astype(F32)).astype(BF16)


def pick(array, index, axis):
    return lax.dynamic_index_in_dim(array, index, axis, keepdims=False)


def inner_sum(part):
    shards, rows, columns = part.shape
    if shards != 4:
        return lax.psum_scatter(part, "inner", scatter_dimension=0, tiled=False)
    place = lax.axis_index("inner")
    low_bit, high_bit = place % 2, place // 2
    top = part[:, : rows // 2].reshape(2, 2, rows // 2, columns)
    bottom = part[:, rows // 2 :].reshape(2, 2, rows // 2, columns)
    top_got = exchange(pick(top, 1 - low_bit, 1), "inner", 1)
    bottom_got = exchange(pick(bottom, 1 - high_bit, 0), "inner", 2)
    top = plus(pick(top, low_bit, 1), top_got)
    bottom = plus(pick(bottom, high_bit, 0), bottom_got)
    top_got = exchange(pick(top, 1 - high_bit, 0), "inner", 2)
    bottom_got = exchange(pick(bottom, 1 - low_bit, 0), "inner", 1)
    top = plus(pick(top, high_bit, 0), top_got)
    bottom = plus(pick(bottom, low_bit, 0), bottom_got)
    return jnp.concatenate([top, bottom], axis=0)


def outer_sum(part):
    length = lax.axis_size("outer")
    if length != 4:
        return lax.psum(part, "outer")
    place = lax.axis_index("outer")
    part = plus(part, lax.ppermute(part, "outer", [(0, 1), (3, 2)]))
    part = plus(part, lax.ppermute(part, "outer", [(1, 2), (2, 1)]))
    last = lax.ppermute(part, "outer", [(1, 0), (2, 3)])
    return jnp.where((place == 0) | (place == 3), last, part)


def total_sum(send, keep, shards):
    got = exchange(send, "section", 1)
    part = plus(keep, got)
    part = part.reshape(shards, part.size // shards // part.shape[-1], part.shape[-1])
    return outer_sum(inner_sum(part))


def local(
    hidden_in, caption_len, region_len, cotangent, w_qkv, b_qv, w_out, b_out, ln_gain, ln_bias, w_up, b_up, w_down, b_down
):
    section = lax.axis_index("section")
    shards = lax.axis_size("inner")
    sec = section.astype(jnp.int32)[None]
    seqs_local, length, width = hidden_in.shape
    seqs = seqs_local // 2
    rows = seqs * length
    positions = jnp.arange(length, dtype=jnp.int32)[None, :]
    mine = lambda array: lax.dynamic_slice_in_dim(array, section * seqs, seqs, 0)
    caption, region = mine(caption_len)[:, None], mine(region_len)[:, None]
    valid = (positions < caption) | (positions >= CAP) & (positions < CAP + region)
    mask = jnp.concatenate([valid, valid], axis=1).astype(F32)
    x = mine(hidden_in).reshape(rows, width)
    gy = jnp.where(valid[:, :, None], mine(cotangent), jnp.zeros((), BF16)).reshape(rows, width)

    little = jnp.concatenate(
        [b_qv[0, 0], b_qv[0, 1], b_out[0], ln_gain[0, 0], ln_gain[0, 1], ln_bias[0, 0], ln_bias[0, 1], b_up[0], b_down[0]]
    )
    little_other = exchange(little, "section", 1)
    big = (w_qkv[0], w_out[0], w_up[0], w_down[0])
    other = tuple(exchange(item, "section", 1) for item in big)

    def split(flat):
        flat = flat[None]
        cuts = [0, 1, 2, 3, 4, 5, 6, 7, 11, 12]
        return tuple(flat[:, a * width : b * width] for a, b in zip(cuts[:-1], cuts[1:]))

    smalls = [split(jnp.where(section == layer, little, little_other)) for layer in (0, 1)]
    y_one, cache_one = layer_forward(0, sec, x, mask, big, other, smalls[0])
    y_two, cache_two = layer_forward(1, sec, y_one, mask, big, other, smalls[1])
    gx_two, gx_two_low, little_two, chunks_two = layer_backward(
        1, sec, gy, cache_two, big, other, smalls[1], shards
    )
    gx_one, gx_one_low, little_one, chunks_one = layer_backward(
        0, sec, gx_two_low, cache_one, big, other, smalls[0], shards
    )

    def gather(for_zero, for_one):
        kept = jnp.where(section == 0, for_zero, for_one)
        got = exchange(jnp.where(section == 0, for_one, for_zero), "section", 1)
        return jnp.where(section == 0, kept, got), jnp.where(section == 0, got, kept)

    activations = jnp.concatenate(gather(y_one, y_two), axis=0).reshape(seqs_local, length, width)
    input_grads = jnp.concatenate(
        gather(gx_one, gx_two_low.astype(F32)), axis=0
    ).reshape(seqs_local, length, width)
    sums_two = [total_sum(send, keep, shards) for send, keep in chunks_two]
    sums_one = [total_sum(send, keep, shards) for send, keep in chunks_one]
    down, up, attend = [gather(one, two) for one, two in zip(sums_one, sums_two)]
    g_w_down = jnp.concatenate(down, axis=0).astype(F32)
    g_w_up = jnp.concatenate(up, axis=1).astype(F32)
    part = width // 2
    g_w_qkv = jnp.concatenate(
        [side[:, i * part : (i + 1) * part] for i in range(3) for side in attend], axis=1
    ).astype(F32)
    g_w_out = jnp.concatenate([side[:, 3 * part :] for side in attend], axis=1).astype(F32)

    stacked = jnp.stack([jnp.concatenate([item[0] for item in little_one]), jnp.concatenate([item[0] for item in little_two])])
    stacked = lax.psum(stacked, ("section", "inner", "outer"))
    summed = pick(stacked, section, 0)
    place = lax.axis_index("inner")

    def shard(first, count):
        span = count * width // shards
        return lax.dynamic_slice_in_dim(summed[first * width : (first + count) * width], place * span, span, 0)

    return (
        activations[None],
        input_grads[None],
        g_w_qkv[None],
        jnp.stack([shard(0, 1), shard(1, 1)])[None],
        g_w_out[None],
        shard(2, 1)[None],
        jnp.stack([shard(3, 1), shard(4, 1)])[None],
        jnp.stack([shard(5, 1), shard(6, 1)])[None],
        g_w_up[None],
        shard(7, 4)[None],
        g_w_down[None],
        shard(11, 1)[None],
    )


def solution(mesh):
    rows = ("inner", "outer")
    return jax.shard_map(
        local,
        mesh=mesh,
        in_specs=(
            P(rows, None, None),
            P(rows),
            P(rows),
            P(rows, None, None),
            P("section", None, None),
            P("section", None, None),
            P("section", None, None),
            P("section", None),
            P("section", None, None),
            P("section", None, None),
            P("section", None, None),
            P("section", None),
            P("section", None, None),
            P("section", None),
        ),
        out_specs=(
            P("section", rows, None, None),
            P("section", rows, None, None),
            P("section", "inner", None),
            P("section", None, "inner"),
            P("section", "inner", None),
            P("section", "inner"),
            P("section", None, "inner"),
            P("section", None, "inner"),
            P("section", "inner", None),
            P("section", "inner"),
            P("section", "inner", None),
            P("section", "inner"),
        ),
        check_vma=False,
    )
```

```python
import functools

import jax
import jax.numpy as jnp
from jax import lax
from jax.experimental import pallas as pl
from jax.experimental.pallas import tpu as pltpu
from jax.sharding import PartitionSpec as P

HEADS = 12
CAP = 28
EPS = 1e-12
SCALE = 0.125
VMEM = 30 * 1024 * 1024
F32 = jnp.float32
BF16 = jnp.bfloat16
B_Q, B_V, B_OUT, GAIN_ONE, GAIN_TWO, OFFSET_ONE, OFFSET_TWO, B_DOWN, B_UP = range(9)


def dot(left, right):
    return jnp.dot(left, right, preferred_element_type=F32)


def dot_t(left, right):
    return lax.dot_general(left, right, (((1,), (1,)), ((), ())), preferred_element_type=F32)


def t_dot(left, right):
    return lax.dot_general(left, right, (((0,), (0,)), ((), ())), preferred_element_type=F32)


def column_sum(values):
    return jnp.sum(values, axis=0, keepdims=True)


def standardize(summed):
    centre = jnp.mean(summed, axis=-1, keepdims=True)
    shifted = summed - centre
    spread = jnp.mean(shifted * shifted, axis=-1, keepdims=True)
    scale = lax.rsqrt(spread + EPS)
    return shifted * scale, scale


def norm_back(grad, hat, scale, gain):
    scaled = grad * gain
    return scale * (
        scaled
        - jnp.mean(scaled, axis=-1, keepdims=True)
        - hat * jnp.mean(scaled * hat, axis=-1, keepdims=True)
    )


def gauss_share(value):
    bell = jnp.exp2(value * value * -0.7213475204444817)
    part = 1.0 / (1.0 + 0.2316418882 * jnp.abs(value))
    tail = 0.5307027145
    for item in (-0.7265760135, 0.7107068705, -0.142248368, 0.127414796):
        tail = tail * part + item
    tail = tail * part * bell
    return jnp.where(value < 0.0, tail, 1.0 - tail), bell


def lane_halves():
    lane = lax.broadcasted_iota(jnp.int32, (1, 128), 1)
    lower = jnp.where(lane < 64, 1.0, 0.0)
    return lower.astype(BF16), (1.0 - lower).astype(BF16)


def two_heads(block, halves):
    return jnp.concatenate([block * halves[0], block * halves[1]], axis=0)


def sds(shape, dtype):
    return jax.ShapeDtypeStruct(shape, dtype)


class Mover:
    def __init__(self, sems):
        self.sems, self.used, self.outs = sems, 0, []

    def copy(self, source, target):
        self.used += 1
        return pltpu.make_async_copy(source, target, self.sems.at[self.used - 1])

    def load(self, source, target):
        self.last = self.copy(source, target)
        self.last.start()

    def choose(self, first, one, two, target):
        copy = self.copy(one, target)
        other = pltpu.make_async_copy(two, target, self.sems.at[self.used - 1])
        pl.when(first)(copy.start)
        pl.when(jnp.logical_not(first))(other.start)
        return copy

    def store(self, source, target):
        copy = self.copy(source, target)
        copy.start()
        self.outs.append(copy)

    def finish(self):
        for copy in self.outs:
            copy.wait()


class Operand:
    def __init__(self, ref, buffer, far):
        self.ref, self.buffer, self.far = ref, buffer, far

    def fetch(self, move, *index):
        if self.far:
            move.load(*(ref.at[index] if index else ref for ref in (self.ref, self.buffer)))
            return [move.last]
        return []

    def flush(self, move, *index):
        if self.far:
            move.store(*(ref.at[index] if index else ref for ref in (self.buffer, self.ref)))


NEAR, FAR, RAW = "near", "far", "raw"


def ready(waits):
    for item in waits:
        item.wait()


def call(kernel, ids, ins, outs, scratch, name, flops, nbytes):
    space = lambda kind: pl.BlockSpec(memory_space=pltpu.VMEM if kind == NEAR else pltpu.HBM)
    kinds = [kind for _, kind in ins] + [kind for _, kind in outs]
    shapes = [array for array, _ in ins] + [shape for shape, _ in outs]
    buffers = [pltpu.VMEM(shape.shape, shape.dtype) for shape, kind in zip(shapes, kinds) if kind == FAR]

    def body(ids_ref, *refs):
        count = len(kinds)
        spare = list(refs[count : count + len(buffers)])
        operands = []
        for ref, kind in zip(refs[:count], kinds):
            buffer = spare.pop(0) if kind == FAR else ref
            operands.append(Operand(ref, buffer, kind == FAR))
        kernel(ids_ref, *operands, *refs[count + len(buffers) :])

    return pl.pallas_call(
        body,
        in_specs=[pl.BlockSpec(memory_space=pltpu.SMEM)] + [space(kind) for _, kind in ins],
        out_specs=[space(kind) for _, kind in outs],
        out_shape=[shape for shape, _ in outs],
        scratch_shapes=buffers + [pltpu.VMEM(*item) for item in scratch] + [pltpu.SemaphoreType.DMA((64,))],
        compiler_params=pltpu.CompilerParams(vmem_limit_bytes=VMEM),
        cost_estimate=pl.CostEstimate(flops=flops, bytes_accessed=nbytes, transcendentals=0),
        name=name,
    )(ids, *(array for array, _ in ins))


def attend_phase(q, k, v, probs, ctx, mask, pairs):
    seqs = mask.shape[1]
    halves = lane_halves()
    feature = lax.broadcasted_iota(jnp.int32, (128, 128), 0)
    first_half = jnp.where(feature < 64, 1.0, 0.0).astype(BF16)
    second_half = jnp.where(feature < 64, 0.0, 1.0).astype(BF16)

    @pl.loop(*pairs)
    def _(pair):
        lanes = pl.ds(pl.multiple_of(pair * 128, 128), 128)
        for seq in range(seqs):
            rows = slice(seq * 128, seq * 128 + 128)
            seen = jnp.broadcast_to(mask[:, seq : seq + 1], (256, 128)) > 0.5
            scores = dot_t(two_heads(k[rows, lanes], halves), q[rows, lanes] * SCALE)
            scores = jnp.where(seen, scores, -1e30)
            parts = []
            for part in (scores[:128], scores[128:]):
                e = jnp.exp(part - jnp.max(part, axis=0, keepdims=True))
                parts.append(e * (1.0 / jnp.sum(e, axis=0, keepdims=True)))
            parts = jnp.concatenate(parts, axis=0)
            probs[seq, pair] = parts
            turned = v[rows, lanes].T
            turned = jnp.concatenate([turned * first_half, turned * second_half], axis=1)
            ctx[lanes, rows] = dot(turned, parts.astype(BF16)).astype(BF16)


def attend_kernel(layer, sec, x, w_a, w_b, small, mask, q, k, v, probs, ctx, w, sems):
    move = Mover(sems)
    mine = sec[0] == layer
    rows, width = x.buffer.shape
    waits = x.fetch(move) + small.fetch(move) + mask.fetch(move)
    parts = [
        move.choose(mine, w_a.ref.at[:, pl.ds(i * width, width)], w_b.ref.at[:, pl.ds(i * width, width)], w.at[i])
        for i in (1, 0, 2)
    ]
    ready(waits)
    x, small = x.buffer, small.buffer
    parts[0].wait()
    k.buffer[...] = dot(x[...], w[1]).astype(BF16)
    k.flush(move)
    parts[1].wait()
    q.buffer[...] = (dot(x[...], w[0]) + small[B_Q : B_Q + 1]).astype(BF16)
    q.flush(move)
    parts[2].wait()
    v.buffer[...] = (dot(x[...], w[2]) + small[B_V : B_V + 1]).astype(BF16)
    v.flush(move)
    half = width // 128 // 2
    for i in range(2):
        attend_phase(
            q.buffer, k.buffer, v.buffer, probs.buffer, ctx.buffer, mask.buffer, (i * half, i * half + half)
        )
        probs.flush(move, slice(None), pl.ds(i * half, half))
    ctx.flush(move)
    move.finish()


def attend_forward(layer, sec, x, x_kind, w_own, w_other, small, mask):
    rows, width = x.shape
    seqs = mask.shape[1]
    pairs = width // 128
    wide = sds((rows, width), BF16)
    return call(
        functools.partial(attend_kernel, layer),
        sec,
        [(x, x_kind), (w_own, RAW), (w_other, RAW), (small, FAR), (mask, FAR)],
        [(wide, FAR)] * 3 + [(sds((seqs, pairs, 256, 128), F32), FAR), (sds((width, rows), BF16), NEAR)],
        [((3, width, width), BF16)],
        "attend_forward",
        2 * rows * width * width * 4,
        12 << 20,
    )


def up_kernel(layer, sec, x, ctx, wo_a, wo_b, wu_a, wu_b, small, hat, scale, turned, act, slope, wo, wu, low, sems):
    move = Mover(sems)
    mine = sec[0] == layer
    blocks, _, wide = wu.shape
    waits = ctx.fetch(move) + [move.choose(mine, wo_a.ref, wo_b.ref, wo)] + small.fetch(move) + x.fetch(move)
    span = lambda i: pl.ds(i * wide, wide)
    parts = [move.choose(mine, wu_a.ref.at[:, span(i)], wu_b.ref.at[:, span(i)], wu.at[i]) for i in range(blocks)]
    ready(waits)
    small = small.buffer
    summed = x.buffer[...].astype(F32) + t_dot(ctx.buffer[...], wo[...]) + small[B_OUT : B_OUT + 1]
    unit, root = standardize(summed)
    hat.buffer[...] = unit
    hat.flush(move)
    scale.buffer[...] = jnp.broadcast_to(root, scale.buffer.shape)
    scale.flush(move)
    low[...] = (unit * small[GAIN_ONE : GAIN_ONE + 1] + small[OFFSET_ONE : OFFSET_ONE + 1]).astype(BF16)
    turned.buffer[...] = low[...].T
    turned.flush(move)
    for i in range(blocks):
        parts[i].wait()
        pre = dot(low[...], wu[i]) + small[B_UP + i : B_UP + i + 1]
        share, bell = gauss_share(pre)
        act.buffer[i] = (pre * share).astype(BF16)
        slope.buffer[i] = share + pre * 0.3989422804014327 * bell
        act.flush(move, i)
        slope.flush(move, i)
    move.finish()


def up_forward(layer, sec, x, x_kind, ctx, wo, wo_other, wu, wu_other, small):
    rows, width = x.shape
    blocks = wu.shape[1] // width
    wide = (rows, width)
    return call(
        functools.partial(up_kernel, layer),
        sec,
        [(x, x_kind), (ctx, NEAR), (wo, RAW), (wo_other, RAW), (wu, RAW), (wu_other, RAW), (small, FAR)],
        [
            (sds(wide, F32), NEAR),
            (sds((rows, 128), F32), FAR),
            (sds((width, rows), BF16), FAR),
            (sds((blocks,) + wide, BF16), NEAR),
            (sds((blocks,) + wide, F32), FAR),
        ],
        [((width, width), BF16), ((blocks, width, width), BF16), (wide, BF16)],
        "up_forward",
        2 * rows * width * width * (blocks + 1),
        20 << 20,
    )


def down_kernel(layer, sec, act, wd_a, wd_b, hat, small, y, two, scale, wd, total, sems):
    move = Mover(sems)
    mine = sec[0] == layer
    blocks, wide, _ = wd.shape
    parts = []
    for i in range(blocks):
        span = pl.ds(i * wide, wide)
        parts.append(act.fetch(move, i) + [move.choose(mine, wd_a.ref.at[span], wd_b.ref.at[span], wd.at[i])])
        if i == 0:
            waits = small.fetch(move) + hat.fetch(move)
    for i in range(blocks):
        ready(parts[i])
        product = dot(act.buffer[i], wd[i])
        total[...] = product if i == 0 else total[...] + product
    ready(waits)
    small = small.buffer
    normed = hat.buffer[...] * small[GAIN_ONE : GAIN_ONE + 1] + small[OFFSET_ONE : OFFSET_ONE + 1]
    unit, root = standardize(total[...] + normed + small[B_DOWN : B_DOWN + 1])
    y.buffer[...] = (unit * small[GAIN_TWO : GAIN_TWO + 1] + small[OFFSET_TWO : OFFSET_TWO + 1]).astype(BF16)
    y.flush(move)
    two.buffer[...] = unit
    two.flush(move)
    scale.buffer[...] = jnp.broadcast_to(root, scale.buffer.shape)
    scale.flush(move)
    move.finish()


def down_forward(layer, sec, act, wd, wd_other, hat, small, y_kind, two_kind):
    blocks, rows, width = act.shape
    wide = (rows, width)
    return call(
        functools.partial(down_kernel, layer),
        sec,
        [(act, NEAR), (wd, RAW), (wd_other, RAW), (hat, NEAR), (small, FAR)],
        [(sds(wide, BF16), y_kind), (sds(wide, F32), two_kind), (sds((rows, 128), F32), two_kind)],
        [((blocks, width, width), BF16), (wide, F32)],
        "down_forward",
        2 * rows * width * width * blocks,
        12 << 20,
    )


def down_grad_kernel(sec, gy, hat, scale, small, act, second, branch, sums, send, keep, turned, sems):
    move = Mover(sems)
    blocks = act.buffer.shape[0]
    tall = send.buffer.shape[1]
    waits = gy.fetch(move) + small.fetch(move) + scale.fetch(move) + hat.fetch(move)
    parts = [act.fetch(move, i) for i in range(blocks)]
    ready(waits)
    grad = gy.buffer[...].astype(F32)
    sums.buffer[0:1] = column_sum(grad * hat.buffer[...])
    sums.buffer[1:2] = column_sum(grad)
    unit = norm_back(grad, hat.buffer[...], scale.buffer[:, 0:1], small.buffer[GAIN_TWO : GAIN_TWO + 1])
    second.buffer[...] = unit
    second.flush(move)
    low = unit.astype(BF16)
    branch.buffer[...] = low
    branch.flush(move)
    sums.buffer[2:3] = column_sum(low.astype(F32))
    sums.buffer[3:] = jnp.zeros_like(sums.buffer[3:])
    sums.flush(move)
    turned[...] = branch.buffer[...].T
    for half, out in ((1 - sec[0], send), (sec[0], keep)):
        left = pl.ds(pl.multiple_of(half * tall, tall), tall)
        for i in range(blocks):
            if out is send:
                ready(parts[i])
            out.buffer[i] = dot(turned[left, :], act.buffer[i]).astype(BF16)
            out.flush(move, i)
    move.finish()


def down_grad(sec, gy, gy_kind, hat, scale, small, act, kind):
    rows, width = gy.shape
    blocks = act.shape[0]
    wide = (rows, width)
    part = sds((blocks, width // 2, width), BF16)
    return call(
        down_grad_kernel,
        sec,
        [(gy, gy_kind), (hat, kind), (scale, kind), (small, FAR), (act, kind)],
        [(sds(wide, F32), NEAR), (sds(wide, BF16), NEAR), (sds((8, width), F32), NEAR), (part, FAR), (part, FAR)],
        [((width, rows), BF16)],
        "down_grad",
        2 * rows * width * width * blocks,
        14 << 20,
    )


def up_grad_kernel(
    layer, sec, branch, second, wd_a, wd_b, slope, low, wu_a, wu_b, hat, scale, small,
    first, attend, sums, send, keep, wd, wu, pre, send_buffer, keep_buffer, sems,
):
    move = Mover(sems)
    mine = sec[0] == layer
    blocks, wide, _ = wd.shape
    half = blocks // 2
    at = [lax.rem(i + half * (1 - sec[0]), blocks) for i in range(blocks)]
    span = [pl.ds(pl.multiple_of(place * wide, wide), wide) for place in at]
    parts = []
    early = branch.fetch(move)
    for i in range(blocks):
        parts.append(
            [move.choose(mine, wd_a.ref.at[span[i]], wd_b.ref.at[span[i]], wd.at[i])]
            + slope.fetch(move, at[i])
            + [move.choose(mine, wu_a.ref.at[:, span[i]], wu_b.ref.at[:, span[i]], wu.at[i])]
        )
        if i == 0:
            early += low.fetch(move)
    late = second.fetch(move) + hat.fetch(move) + scale.fetch(move) + small.fetch(move)
    ready(early)
    branch, low, total = branch.buffer, low.buffer, first.buffer
    for i in range(blocks):
        ready(parts[i])
        pre[...] = (dot_t(branch[...], wd[i]) * slope.buffer[at[i]]).astype(BF16)
        sums.buffer[pl.ds(3 + at[i], 1)] = column_sum(pre[...].astype(F32))
        out, out_h, place = (send_buffer, send, i) if i < half else (keep_buffer, keep, i - half)
        out[place] = dot(low[...], pre[...]).astype(BF16)
        move.store(out.at[place], out_h.ref.at[:, pl.ds(place * wide, wide)])
        if i == 0:
            ready(late)
            total[...] = second.buffer[...] + dot_t(pre[...], wu[i])
        else:
            total[...] += dot_t(pre[...], wu[i])
    grad = total[...]
    sums.buffer[0:1] = column_sum(grad * hat.buffer[...])
    sums.buffer[1:2] = column_sum(grad)
    unit = norm_back(grad, hat.buffer[...], scale.buffer[:, 0:1], small.buffer[GAIN_ONE : GAIN_ONE + 1])
    attend.buffer[...] = unit.astype(BF16)
    attend.flush(move)
    total[...] = unit
    first.flush(move)
    sums.buffer[2:3] = column_sum(attend.buffer[...].astype(F32))
    sums.buffer[3 + blocks :] = jnp.zeros_like(sums.buffer[3 + blocks :])
    sums.flush(move)
    move.finish()


def up_grad(layer, sec, branch, second, wd, wd_other, slope, low, wu, wu_other, hat, scale, small):
    blocks, rows, width = slope.shape
    wide = (rows, width)
    part = sds((width, blocks * width // 2), BF16)
    square = ((blocks, width, width), BF16)
    return call(
        functools.partial(up_grad_kernel, layer),
        sec,
        [
            (branch, NEAR),
            (second, NEAR),
            (wd, RAW),
            (wd_other, RAW),
            (slope, FAR),
            (low, FAR),
            (wu, RAW),
            (wu_other, RAW),
            (hat, FAR),
            (scale, FAR),
            (small, FAR),
        ],
        [(sds(wide, F32), NEAR), (sds(wide, BF16), NEAR), (sds((8, width), F32), NEAR), (part, RAW), (part, RAW)],
        [square, square, (wide, BF16)] + [((blocks // 2, width, width), BF16)] * 2,
        "up_grad",
        6 * rows * width * width * blocks,
        30 << 20,
    )


def attend_grad_kernel(
    layer, shards, sec, attend, ctx, first, x, q, k, v, probs, wo_a, wo_b, w_a, w_b, down, up,
    gx, gx_low, send, keep, turned, wo, w, gc, grads, sems,
):
    move = Mover(sems)
    mine = sec[0] == layer
    rows_all, width = x.buffer.shape
    seqs = probs.buffer.shape[0]
    wide = width // 2
    tall = width // shards
    pairs = wide // 128
    waits = attend.fetch(move) + [move.choose(mine, wo_a.ref, wo_b.ref, wo)]
    near = probs.fetch(move) + v.fetch(move) + k.fetch(move) + q.fetch(move)
    later = x.fetch(move) + ctx.fetch(move) + down.fetch(move) + up.fetch(move)
    last = [
        move.choose(mine, w_a.ref.at[:, pl.ds(i * width, width)], w_b.ref.at[:, pl.ds(i * width, width)], w.at[i])
        for i in range(3)
    ] + first.fetch(move)
    ready(waits)
    attend, q, k, v, probs = (item.buffer for item in (attend, q, k, v, probs))
    gc[...] = dot_t(attend[...], wo[...]).astype(BF16)
    ready(near)
    halves = lane_halves()
    lower = lax.broadcasted_iota(jnp.int32, (128, 128), 1) < 64

    def attention(first_pair):
        @pl.loop(0, pairs)
        def _(index):
            pair = first_pair + index
            lanes = pl.ds(pl.multiple_of(pair * 128, 128), 128)
            for seq in range(seqs):
                rows = slice(seq * 128, seq * 128 + 128)
                grad = gc[rows, lanes]
                p = probs[seq, pair]
                full = dot(p.astype(BF16), grad)
                grads[2, rows, lanes] = jnp.where(lower, full[:128], full[128:]).astype(BF16)
                gp = dot_t(two_heads(v[rows, lanes], halves), grad)
                parts = []
                for side in (slice(0, 128), slice(128, 256)):
                    g, pp = gp[side], p[side]
                    parts.append(pp * (g - jnp.sum(g * pp, axis=0, keepdims=True)))
                gs = jnp.concatenate(parts, axis=0).astype(BF16)
                grads[0, rows, lanes] = t_dot(gs, two_heads(k[rows, lanes] * SCALE, halves)).astype(BF16)
                full = dot(gs, q[rows, lanes] * SCALE)
                grads[1, rows, lanes] = jnp.where(lower, full[:128], full[128:]).astype(BF16)

    def products(half, out):
        lanes = pl.ds(pl.multiple_of(half * wide, wide), wide)
        for part in range(4):
            if part < 3:
                block = dot(turned[...], grads[part, :, lanes]).astype(BF16)
            else:
                block = dot(ctx.buffer[...], attend[:, lanes]).astype(BF16)
            for shard in range(shards):
                out.buffer[shard, :tall, part * wide : part * wide + wide] = block[shard * tall : shard * tall + tall]

    attention((1 - sec[0]) * pairs)
    ready(later)
    turned[...] = x.buffer[...].T
    products(1 - sec[0], send)
    attention(sec[0] * pairs)
    products(sec[0], keep)
    b_v = column_sum(grads[2].astype(F32))
    b_q = column_sum(grads[0].astype(F32))
    little = jnp.concatenate([down.buffer[0:3], b_v, down.buffer[4:8], up.buffer[0:7], b_q], axis=0).astype(BF16)
    little = jnp.concatenate([little, jnp.zeros_like(little)], axis=1)
    for shard in range(shards):
        send.buffer[shard, tall:] = little
        keep.buffer[shard, tall:] = little
    send.flush(move)
    keep.flush(move)
    ready(last)
    total = first.buffer[...] + dot_t(grads[0], w[0]) + dot_t(grads[1], w[1]) + dot_t(grads[2], w[2])
    gx.buffer[...] = total
    gx.flush(move)
    gx_low.buffer[...] = total.astype(BF16)
    gx_low.flush(move)
    move.finish()


def attend_grad(layer, sec, attend, ctx, first, x, q, k, v, probs, wo, wo_other, w, w_other, down, up, shards, low_kind):
    rows, width = x.shape
    wide = (rows, width)
    part = sds((shards, width // shards + 16, 2 * width), BF16)
    return call(
        functools.partial(attend_grad_kernel, layer, shards),
        sec,
        [(attend, NEAR), (ctx, FAR), (first, NEAR)]
        + [(item, FAR) for item in (x, q, k, v, probs)]
        + [(wo, RAW), (wo_other, RAW), (w, RAW), (w_other, RAW), (down, NEAR), (up, NEAR)],
        [(sds(wide, F32), FAR), (sds(wide, BF16), low_kind), (part, FAR), (part, FAR)],
        [((width, rows), BF16), ((width, width), BF16), ((3, width, width), BF16), (wide, BF16), ((3,) + wide, BF16)],
        "attend_grad",
        2 * rows * width * width * 10,
        30 << 20,
    )


def layer_forward(layer, sec, x, mask, big, other, small):
    w_qkv, w_out, w_up, w_down = big
    o_qkv, o_out, o_up, o_down = other
    x_kind = FAR if layer == 0 else NEAR
    q, k, v, probs, ctx = attend_forward(layer, sec, x, x_kind, w_qkv, o_qkv, small, mask)
    hat_one, scale_one, low, act, slope = up_forward(layer, sec, x, x_kind, ctx, w_out, o_out, w_up, o_up, small)
    kinds = (NEAR, FAR) if layer == 0 else (FAR, NEAR)
    y, hat_two, scale_two = down_forward(layer, sec, act, w_down, o_down, hat_one, small, *kinds)
    return y, (x, q, k, v, probs, ctx, hat_one, scale_one, low, act, slope, hat_two, scale_two)


def layer_backward(line, layer, sec, gy, cache, big, other, small, shards):
    w_qkv, w_out, w_up, w_down = big
    o_qkv, o_out, o_up, o_down = other
    x, q, k, v, probs, ctx, hat_one, scale_one, low, act, slope, hat_two, scale_two = cache
    kinds = (NEAR, FAR) if layer == 0 else (FAR, NEAR)
    second, branch, down, d_send, d_keep = line.advance(
        lambda: down_grad(sec, gy, kinds[0], hat_two, scale_two, small, act, kinds[1])
    )
    line.add(d_send, d_keep)
    first, attend, up, u_send, u_keep = line.advance(
        lambda: up_grad(
            layer, sec, branch, second, w_down, o_down, slope, low, w_up, o_up, hat_one, scale_one, small
        )
    )
    line.add(*(item.reshape(shards, item.shape[0] // shards, item.shape[1]) for item in (u_send, u_keep)))
    gx, gx_low, a_send, a_keep = line.advance(
        lambda: attend_grad(
            layer, sec, attend, ctx, first, x, q, k, v, probs, w_out, o_out, w_qkv, o_qkv, down, up, shards,
            FAR if layer == 0 else NEAR,
        )
    )
    line.add(a_send, a_keep)
    return gx, gx_low


def exchange(array, axis, bit):
    length = lax.axis_size(axis)
    return lax.ppermute(array, axis, [(i, i ^ bit) for i in range(length)])


def pick(array, index, axis):
    return lax.dynamic_index_in_dim(array, index, axis, keepdims=False)


def split_at(rows):
    return (rows // 2 + 15) // 16 * 16


def join_section(ids, ins, outs):
    kept, got = ins
    top_send, top_keep, bottom_send, bottom_keep = outs
    low_bit, high_bit = ids[1], ids[2]
    cut = top_send.shape[1]
    for i in range(2):
        for out, shard in ((top_send, 2 * i + 1 - low_bit), (top_keep, 2 * i + low_bit)):
            out[i] = kept[shard, :cut] + got[shard, :cut]
        for out, shard in ((bottom_send, 2 * (1 - high_bit) + i), (bottom_keep, 2 * high_bit + i)):
            out[i] = kept[shard, cut:] + got[shard, cut:]


def join_first(ids, ins, outs):
    top, top_got, bottom, bottom_got = ins
    top_send, top_keep, bottom_send, bottom_keep = outs
    low_bit, high_bit = ids[1], ids[2]
    top_send[...] = top[1 - high_bit] + top_got[1 - high_bit]
    top_keep[...] = top[high_bit] + top_got[high_bit]
    bottom_send[...] = bottom[1 - low_bit] + bottom_got[1 - low_bit]
    bottom_keep[...] = bottom[low_bit] + bottom_got[low_bit]


def join_second(ids, ins, outs):
    top, top_got, bottom, bottom_got = ins
    cut = top.shape[0]
    outs[0][:cut] = top[...] + top_got[...]
    outs[0][cut:] = bottom[...] + bottom_got[...]


def join_add(ids, ins, outs):
    outs[0][...] = ins[0][...] + ins[1][...]


def join_last(ids, ins, outs):
    @pl.when(ids[3] == 1)
    def _():
        outs[0][...] = ins[1][...]

    @pl.when(ids[3] == 0)
    def _():
        outs[0][...] = ins[0][...]


def join(ids, jobs):
    counts = [(len(ins), len(shapes)) for _, ins, shapes in jobs]
    n_in = sum(a for a, _ in counts)

    def kernel(ids_ref, *refs):
        at_in, at_out = 0, n_in
        for (function, _, _), (a, b) in zip(jobs, counts):
            function(ids_ref, refs[at_in : at_in + a], refs[at_out : at_out + b])
            at_in, at_out = at_in + a, at_out + b

    flat = [array for _, ins, _ in jobs for array in ins]
    shapes = [sds(shape, BF16) for _, _, shapes in jobs for shape in shapes]
    vmem = pl.BlockSpec(memory_space=pltpu.VMEM)
    outs = pl.pallas_call(
        kernel,
        in_specs=[pl.BlockSpec(memory_space=pltpu.SMEM)] + [vmem] * n_in,
        out_specs=[vmem] * len(shapes),
        out_shape=shapes,
        compiler_params=pltpu.CompilerParams(vmem_limit_bytes=VMEM),
        name="join_sums",
    )(ids, *flat)
    result = []
    for _, b in counts:
        result.append(outs[:b])
        outs = outs[b:]
    return result


def move_section(parts):
    send, keep = parts
    shards = lax.axis_size("inner")
    if shards != 4:
        got = lax.psum_scatter(send.astype(BF16), "inner", scatter_dimension=0, tiled=False)
        own = lax.psum_scatter(keep.astype(BF16), "inner", scatter_dimension=0, tiled=False)
        got = exchange(got, "section", 1)
        return [own, got], join_add, [own.shape]
    got = exchange(send, "section", 1)
    _, rows, columns = keep.shape
    cut = split_at(rows)
    return [keep, got], join_section, [(2, cut, columns)] * 2 + [(2, rows - cut, columns)] * 2


def move_first(parts):
    top_send, top, bottom_send, bottom = parts
    top_got = exchange(top_send, "inner", 1)
    bottom_got = exchange(bottom_send, "inner", 2)
    return [top, top_got, bottom, bottom_got], join_first, [top.shape[1:]] * 2 + [bottom.shape[1:]] * 2


def move_second(parts):
    top_send, top, bottom_send, bottom = parts
    top_got = exchange(top_send, "inner", 2)
    bottom_got = exchange(bottom_send, "inner", 1)
    rows = top.shape[0] + bottom.shape[0]
    return [top, top_got, bottom, bottom_got], join_second, [(rows, top.shape[1])]


def move_in(parts):
    return [parts[0], lax.ppermute(parts[0], "outer", [(0, 1), (3, 2)])], join_add, [parts[0].shape]


def move_across(parts):
    return [parts[0], lax.ppermute(parts[0], "outer", [(1, 2), (2, 1)])], join_add, [parts[0].shape]


def move_out(parts):
    return [parts[0], lax.ppermute(parts[0], "outer", [(1, 0), (2, 3)])], join_last, [parts[0].shape]


def move_any(parts):
    return [parts[0], lax.psum(parts[0], "outer")], lambda ids, ins, outs: join_last(ids, ins, outs), [parts[0].shape]


class Line:
    def __init__(self):
        inner = [move_section] + ([move_first, move_second] if lax.axis_size("inner") == 4 else [])
        place = lax.axis_index("outer")
        if lax.axis_size("outer") == 4:
            outer = [move_in, move_across, move_out]
            outside = ((place == 0) | (place == 3)).astype(jnp.int32)
        else:
            outer = [move_any]
            outside = jnp.ones((), jnp.int32)
        spot = lax.axis_index("inner")
        self.ids = jnp.stack([lax.axis_index("section"), spot % 2, spot // 2, outside]).astype(jnp.int32)
        self.moves = inner + outer
        self.running = []

    def add(self, send, keep):
        self.running.append({"at": 0, "parts": [send, keep], "pending": None})

    def settle(self):
        active = [item for item in self.running if item["pending"] is not None]
        if active:
            for item, parts in zip(active, join(self.ids, [item["pending"] for item in active])):
                item["parts"], item["pending"] = parts, None

    def advance(self, work=None):
        self.settle()
        active = [item for item in self.running if item["at"] < len(self.moves)]
        started = [self.moves[item["at"]](item["parts"]) for item in active]
        beside = work() if work is not None else ()
        beside, tied = lax.optimization_barrier((beside, [ins for ins, _, _ in started]))
        for item, ins, (_, function, shapes) in zip(active, tied, started):
            item["at"] += 1
            item["pending"] = (function, ins, shapes)
        return beside

    def done(self):
        return all(item["at"] == len(self.moves) for item in self.running)


def local(
    hidden_in, caption_len, region_len, cotangent, w_qkv, b_qv, w_out, b_out, ln_gain, ln_bias, w_up, b_up, w_down, b_down
):
    section = lax.axis_index("section")
    shards = lax.axis_size("inner")
    sec = section.astype(jnp.int32)[None]
    seqs_local, length, width = hidden_in.shape
    seqs = seqs_local // 2
    rows = seqs * length
    positions = jnp.arange(length, dtype=jnp.int32)[None, :]
    mine = lambda array: lax.dynamic_slice_in_dim(array, section * seqs, seqs, 0)
    caption, region = mine(caption_len)[:, None], mine(region_len)[:, None]
    valid = (positions < caption) | (positions >= CAP) & (positions < CAP + region)
    mask = jnp.concatenate([valid, valid], axis=1).astype(F32).T
    x = mine(hidden_in).reshape(rows, width)
    gy = jnp.where(valid[:, :, None], mine(cotangent), jnp.zeros((), BF16)).reshape(rows, width)

    blocks = w_up.shape[2] // width
    little = jnp.concatenate(
        [b_qv[0], b_out, ln_gain[0], ln_bias[0], b_down, b_up.reshape(blocks, width), jnp.zeros((8 - blocks, width), F32)]
    )
    little_other = exchange(little, "section", 1)
    big = (w_qkv[0], w_out[0], w_up[0], w_down[0])
    o_qkv = exchange(big[0], "section", 1)
    o_qkv, late_out, late_up = lax.optimization_barrier((o_qkv, big[1], big[2]))
    o_out, o_up = exchange(late_out, "section", 1), exchange(late_up, "section", 1)
    o_up, late_down = lax.optimization_barrier((o_up, big[3]))
    other = (o_qkv, o_out, o_up, exchange(late_down, "section", 1))

    smalls = [jnp.where(section == layer, little, little_other) for layer in (0, 1)]
    y_one, cache_one = layer_forward(0, sec, x, mask, big, other, smalls[0])
    y_two, cache_two = layer_forward(1, sec, y_one, mask, big, other, smalls[1])
    line = Line()
    gx_two, gx_two_low = layer_backward(line, 1, sec, gy, cache_two, big, other, smalls[1], shards)
    gx_one, gx_one_low = layer_backward(line, 0, sec, gx_two_low, cache_one, big, other, smalls[0], shards)

    def gather(for_zero, for_one):
        kept = jnp.where(section == 0, for_zero, for_one)
        got = exchange(jnp.where(section == 0, for_one, for_zero), "section", 1)
        return jnp.where(section == 0, kept, got), jnp.where(section == 0, got, kept)

    activations, input_grads = line.advance(
        lambda: (
            jnp.concatenate(gather(y_one, y_two), axis=0).reshape(seqs_local, length, width),
            jnp.concatenate(gather(gx_one, gx_two_low.astype(F32)), axis=0).reshape(seqs_local, length, width),
        )
    )
    while not line.done():
        line.advance()
    line.settle()
    sums = [item["parts"][0] for item in line.running]
    down, up, attend = [gather(one, two) for one, two in zip(sums[3:], sums[:3])]
    g_w_down = jnp.concatenate(down, axis=0).T.astype(F32)
    g_w_up = jnp.concatenate(up, axis=1).astype(F32)
    part = width // 2
    tall = width // shards
    matrix = [side[:tall] for side in attend]
    g_w_qkv = jnp.concatenate(
        [side[:, i * part : (i + 1) * part] for i in range(3) for side in matrix], axis=1
    ).astype(F32)
    g_w_out = jnp.concatenate([side[:, 3 * part :] for side in matrix], axis=1).astype(F32)
    rows = jnp.where(section == 0, sums[5][tall:, :width], sums[2][tall:, :width])
    place = lax.axis_index("inner")
    mine = lax.dynamic_slice_in_dim(rows, place * tall, tall, 1).astype(F32)
    up_row = pick(rows[11 : 11 + blocks].reshape(shards, width * blocks // shards), place, 0).astype(F32)
    return (
        activations[None],
        input_grads[None],
        g_w_qkv[None],
        jnp.stack([mine[15], mine[3]])[None],
        g_w_out[None],
        mine[10][None],
        jnp.stack([mine[8], mine[0]])[None],
        jnp.stack([mine[9], mine[1]])[None],
        g_w_up[None],
        up_row[None],
        g_w_down[None],
        mine[2][None],
    )


def solution(mesh):
    rows = ("inner", "outer")
    return jax.shard_map(
        local,
        mesh=mesh,
        in_specs=(
            P(rows, None, None),
            P(rows),
            P(rows),
            P(rows, None, None),
            P("section", None, None),
            P("section", None, None),
            P("section", None, None),
            P("section", None),
            P("section", None, None),
            P("section", None, None),
            P("section", None, None),
            P("section", None),
            P("section", None, None),
            P("section", None),
        ),
        out_specs=(
            P("section", rows, None, None),
            P("section", rows, None, None),
            P("section", "inner", None),
            P("section", None, "inner"),
            P("section", "inner", None),
            P("section", "inner"),
            P("section", None, "inner"),
            P("section", None, "inner"),
            P("section", "inner", None),
            P("section", "inner"),
            P("section", "inner", None),
            P("section", "inner"),
        ),
        check_vma=False,
    )
```

```python
import functools

import jax
import jax.numpy as jnp
from jax import lax
from jax.experimental import pallas as pl
from jax.experimental.pallas import tpu as pltpu
from jax.sharding import PartitionSpec as P

HEADS = 12
CAP = 28
EPS = 1e-12
SCALE = 0.125
VMEM = 30 * 1024 * 1024
F32 = jnp.float32
BF16 = jnp.bfloat16
B_Q, B_V, B_OUT, GAIN_ONE, GAIN_TWO, OFFSET_ONE, OFFSET_TWO, B_DOWN, B_UP = range(9)


def dot(left, right):
    return jnp.dot(left, right, preferred_element_type=F32)


def dot_t(left, right):
    return lax.dot_general(left, right, (((1,), (1,)), ((), ())), preferred_element_type=F32)


def t_dot(left, right):
    return lax.dot_general(left, right, (((0,), (0,)), ((), ())), preferred_element_type=F32)


def column_sum(values):
    return jnp.sum(values, axis=0, keepdims=True)


def standardize(summed):
    centre = jnp.mean(summed, axis=-1, keepdims=True)
    shifted = summed - centre
    spread = jnp.mean(shifted * shifted, axis=-1, keepdims=True)
    scale = lax.rsqrt(spread + EPS)
    return shifted * scale, scale


def norm_back(grad, hat, scale, gain):
    scaled = grad * gain
    return scale * (
        scaled
        - jnp.mean(scaled, axis=-1, keepdims=True)
        - hat * jnp.mean(scaled * hat, axis=-1, keepdims=True)
    )


def gauss_share(value):
    bell = jnp.exp2(value * value * -0.7213475204444817)
    part = 1.0 / (1.0 + 0.2316418882 * jnp.abs(value))
    tail = 0.5307027145
    for item in (-0.7265760135, 0.7107068705, -0.142248368, 0.127414796):
        tail = tail * part + item
    tail = tail * part * bell
    return jnp.where(value < 0.0, tail, 1.0 - tail), bell


def lane_halves():
    lane = lax.broadcasted_iota(jnp.int32, (1, 128), 1)
    lower = jnp.where(lane < 64, 1.0, 0.0)
    return lower.astype(BF16), (1.0 - lower).astype(BF16)


def two_heads(block, halves):
    return jnp.concatenate([block * halves[0], block * halves[1]], axis=0)


def sds(shape, dtype):
    return jax.ShapeDtypeStruct(shape, dtype)


class Mover:
    def __init__(self, sems):
        self.sems, self.used, self.outs = sems, 0, []

    def copy(self, source, target):
        self.used += 1
        return pltpu.make_async_copy(source, target, self.sems.at[self.used - 1])

    def load(self, source, target):
        self.last = self.copy(source, target)
        self.last.start()

    def choose(self, first, one, two, target):
        copy = self.copy(one, target)
        other = pltpu.make_async_copy(two, target, self.sems.at[self.used - 1])
        pl.when(first)(copy.start)
        pl.when(jnp.logical_not(first))(other.start)
        return copy

    def store(self, source, target):
        copy = self.copy(source, target)
        copy.start()
        self.outs.append(copy)

    def finish(self):
        for copy in self.outs:
            copy.wait()


class Operand:
    def __init__(self, ref, buffer, far):
        self.ref, self.buffer, self.far = ref, buffer, far

    def fetch(self, move, *index):
        if self.far:
            move.load(*(ref.at[index] if index else ref for ref in (self.ref, self.buffer)))
            return [move.last]
        return []

    def flush(self, move, *index):
        if self.far:
            move.store(*(ref.at[index] if index else ref for ref in (self.buffer, self.ref)))


NEAR, FAR, RAW, BOTH = "near", "far", "raw", "both"


def ready(waits):
    for item in waits:
        item.wait()


def call(kernel, ids, ins, outs, scratch, name, flops, nbytes):
    space = lambda kind: pltpu.VMEM if kind == NEAR else pltpu.HBM
    spread = [(shape, part) for shape, kind in outs for part in ((NEAR, RAW) if kind == BOTH else (kind,))]
    kinds = [kind for _, kind in ins] + [kind for _, kind in spread]
    shapes = [array for array, _ in ins] + [shape for shape, _ in spread]
    buffers = [pltpu.VMEM(shape.shape, shape.dtype) for shape, kind in zip(shapes, kinds) if kind == FAR]

    def body(ids_ref, *refs):
        count = len(kinds)
        spare = list(refs[count : count + len(buffers)])
        left = list(refs[:count])
        operands = []
        for _, kind in list(ins) + list(outs):
            ref = left.pop(0)
            if kind == BOTH:
                operands.append(Operand(left.pop(0), ref, True))
            else:
                operands.append(Operand(ref, spare.pop(0) if kind == FAR else ref, kind == FAR))
        kernel(ids_ref, *operands, *refs[count + len(buffers) :])

    results = pl.pallas_call(
        body,
        in_specs=[pl.BlockSpec(memory_space=pltpu.SMEM)]
        + [pl.BlockSpec(memory_space=space(kind)) for _, kind in ins],
        out_specs=[pl.BlockSpec(memory_space=space(kind)) for _, kind in spread],
        out_shape=[space(kind)(shape.shape, shape.dtype) for shape, kind in spread],
        scratch_shapes=buffers + [pltpu.VMEM(*item) for item in scratch] + [pltpu.SemaphoreType.DMA((64,))],
        compiler_params=pltpu.CompilerParams(vmem_limit_bytes=VMEM),
        cost_estimate=pl.CostEstimate(flops=flops, bytes_accessed=nbytes, transcendentals=0),
        name=name,
    )(ids, *(pltpu.with_memory_space_constraint(array, space(kind)) for array, kind in ins))
    results = list(results)
    return [(results.pop(0), results.pop(0)) if kind == BOTH else results.pop(0) for _, kind in outs]


def attend_phase(q, k, v, probs, ctx, mask, pairs):
    seqs = mask.shape[1]
    halves = lane_halves()
    feature = lax.broadcasted_iota(jnp.int32, (128, 128), 0)
    first_half = jnp.where(feature < 64, 1.0, 0.0).astype(BF16)
    second_half = jnp.where(feature < 64, 0.0, 1.0).astype(BF16)

    @pl.loop(*pairs)
    def _(pair):
        lanes = pl.ds(pl.multiple_of(pair * 128, 128), 128)
        for seq in range(seqs):
            rows = slice(seq * 128, seq * 128 + 128)
            seen = jnp.broadcast_to(mask[:, seq : seq + 1], (256, 128)) > 0.5
            scores = dot_t(two_heads(k[rows, lanes], halves), q[rows, lanes] * SCALE)
            scores = jnp.where(seen, scores, -1e30)
            parts = []
            for part in (scores[:128], scores[128:]):
                e = jnp.exp(part - jnp.max(part, axis=0, keepdims=True))
                parts.append(e * (1.0 / jnp.sum(e, axis=0, keepdims=True)))
            parts = jnp.concatenate(parts, axis=0)
            probs[seq, pair] = parts
            turned = v[rows, lanes].T
            turned = jnp.concatenate([turned * first_half, turned * second_half], axis=1)
            ctx[lanes, rows] = dot(turned, parts.astype(BF16)).astype(BF16)


def attend_kernel(layer, sec, x, w_a, w_b, small, mask, q, k, v, probs, ctx, w, sems):
    move = Mover(sems)
    mine = sec[0] == layer
    rows, width = x.buffer.shape
    waits = x.fetch(move) + small.fetch(move) + mask.fetch(move)
    parts = [
        move.choose(mine, w_a.ref.at[:, pl.ds(i * width, width)], w_b.ref.at[:, pl.ds(i * width, width)], w.at[i])
        for i in (1, 0, 2)
    ]
    ready(waits)
    x, small = x.buffer, small.buffer
    parts[0].wait()
    k.buffer[...] = dot(x[...], w[1]).astype(BF16)
    k.flush(move)
    parts[1].wait()
    q.buffer[...] = (dot(x[...], w[0]) + small[B_Q : B_Q + 1]).astype(BF16)
    q.flush(move)
    parts[2].wait()
    v.buffer[...] = (dot(x[...], w[2]) + small[B_V : B_V + 1]).astype(BF16)
    v.flush(move)
    half = width // 128 // 2
    for i in range(2):
        attend_phase(
            q.buffer, k.buffer, v.buffer, probs.buffer, ctx.buffer, mask.buffer, (i * half, i * half + half)
        )
        probs.flush(move, slice(None), pl.ds(i * half, half))
    ctx.flush(move)
    move.finish()


def attend_forward(layer, sec, x, x_kind, w_own, w_other, small, mask):
    rows, width = x.shape
    seqs = mask.shape[1]
    pairs = width // 128
    wide = sds((rows, width), BF16)
    return call(
        functools.partial(attend_kernel, layer),
        sec,
        [(x, x_kind), (w_own, RAW), (w_other, RAW), (small, FAR), (mask, FAR)],
        [(wide, FAR)] * 3 + [(sds((seqs, pairs, 256, 128), F32), FAR), (sds((width, rows), BF16), BOTH)],
        [((3, width, width), BF16)],
        "attend_forward",
        2 * rows * width * width * 4,
        12 << 20,
    )


def up_kernel(layer, sec, x, ctx, wo_a, wo_b, wu_a, wu_b, small, hat, scale, turned, act, slope, wo, wu, low, sems):
    move = Mover(sems)
    mine = sec[0] == layer
    blocks, _, wide = wu.shape
    waits = ctx.fetch(move) + [move.choose(mine, wo_a.ref, wo_b.ref, wo)] + small.fetch(move) + x.fetch(move)
    span = lambda i: pl.ds(i * wide, wide)
    parts = [move.choose(mine, wu_a.ref.at[:, span(i)], wu_b.ref.at[:, span(i)], wu.at[i]) for i in range(blocks)]
    ready(waits)
    small = small.buffer
    summed = x.buffer[...].astype(F32) + t_dot(ctx.buffer[...], wo[...]) + small[B_OUT : B_OUT + 1]
    unit, root = standardize(summed)
    hat.buffer[...] = unit
    hat.flush(move)
    scale.buffer[...] = jnp.broadcast_to(root, scale.buffer.shape)
    scale.flush(move)
    low[...] = (unit * small[GAIN_ONE : GAIN_ONE + 1] + small[OFFSET_ONE : OFFSET_ONE + 1]).astype(BF16)
    turned.buffer[...] = low[...].T
    turned.flush(move)
    for i in range(blocks):
        parts[i].wait()
        pre = dot(low[...], wu[i]) + small[B_UP + i : B_UP + i + 1]
        share, bell = gauss_share(pre)
        act.buffer[i] = (pre * share).astype(BF16)
        slope.buffer[i] = share + pre * 0.3989422804014327 * bell
        act.flush(move, i)
        slope.flush(move, i)
    move.finish()


def up_forward(layer, sec, x, x_kind, ctx, wo, wo_other, wu, wu_other, small):
    rows, width = x.shape
    blocks = wu.shape[1] // width
    wide = (rows, width)
    return call(
        functools.partial(up_kernel, layer),
        sec,
        [(x, x_kind), (ctx, NEAR), (wo, RAW), (wo_other, RAW), (wu, RAW), (wu_other, RAW), (small, FAR)],
        [
            (sds(wide, F32), BOTH),
            (sds((rows, 128), F32), FAR),
            (sds((width, rows), BF16), FAR),
            (sds((blocks,) + wide, BF16), BOTH if layer == 0 else NEAR),
            (sds((blocks,) + wide, F32), FAR),
        ],
        [((width, width), BF16), ((blocks, width, width), BF16), (wide, BF16)],
        "up_forward",
        2 * rows * width * width * (blocks + 1),
        20 << 20,
    )


def down_kernel(layer, sec, act, wd_a, wd_b, hat, small, y, two, scale, wd, total, sems):
    move = Mover(sems)
    mine = sec[0] == layer
    blocks, wide, _ = wd.shape
    parts = []
    for i in range(blocks):
        span = pl.ds(i * wide, wide)
        parts.append(act.fetch(move, i) + [move.choose(mine, wd_a.ref.at[span], wd_b.ref.at[span], wd.at[i])])
        if i == 0:
            waits = small.fetch(move) + hat.fetch(move)
    for i in range(blocks):
        ready(parts[i])
        product = dot(act.buffer[i], wd[i])
        total[...] = product if i == 0 else total[...] + product
    ready(waits)
    small = small.buffer
    normed = hat.buffer[...] * small[GAIN_ONE : GAIN_ONE + 1] + small[OFFSET_ONE : OFFSET_ONE + 1]
    unit, root = standardize(total[...] + normed + small[B_DOWN : B_DOWN + 1])
    y.buffer[...] = (unit * small[GAIN_TWO : GAIN_TWO + 1] + small[OFFSET_TWO : OFFSET_TWO + 1]).astype(BF16)
    y.flush(move)
    two.buffer[...] = unit
    two.flush(move)
    scale.buffer[...] = jnp.broadcast_to(root, scale.buffer.shape)
    scale.flush(move)
    move.finish()


def down_forward(layer, sec, act, wd, wd_other, hat, small, y_kind, two_kind):
    blocks, rows, width = act.shape
    wide = (rows, width)
    return call(
        functools.partial(down_kernel, layer),
        sec,
        [(act, NEAR), (wd, RAW), (wd_other, RAW), (hat, NEAR), (small, FAR)],
        [(sds(wide, BF16), y_kind), (sds(wide, F32), two_kind), (sds((rows, 128), F32), two_kind)],
        [((blocks, width, width), BF16), (wide, F32)],
        "down_forward",
        2 * rows * width * width * blocks,
        12 << 20,
    )


def down_grad_kernel(sec, gy, hat, scale, small, act, second, branch, sums, send, keep, turned, sems):
    move = Mover(sems)
    blocks = act.buffer.shape[0]
    tall = send.buffer.shape[1]
    waits = gy.fetch(move) + small.fetch(move) + scale.fetch(move) + hat.fetch(move)
    parts = [act.fetch(move, i) for i in range(blocks)]
    ready(waits)
    grad = gy.buffer[...].astype(F32)
    sums.buffer[0:1] = column_sum(grad * hat.buffer[...])
    sums.buffer[1:2] = column_sum(grad)
    unit = norm_back(grad, hat.buffer[...], scale.buffer[:, 0:1], small.buffer[GAIN_TWO : GAIN_TWO + 1])
    second.buffer[...] = unit
    second.flush(move)
    low = unit.astype(BF16)
    branch.buffer[...] = low
    branch.flush(move)
    sums.buffer[2:3] = column_sum(low.astype(F32))
    sums.buffer[3:] = jnp.zeros_like(sums.buffer[3:])
    sums.flush(move)
    turned[...] = branch.buffer[...].T
    for half, out in ((1 - sec[0], send), (sec[0], keep)):
        left = pl.ds(pl.multiple_of(half * tall, tall), tall)
        for i in range(blocks):
            if out is send:
                ready(parts[i])
            out.buffer[i] = dot(turned[left, :], act.buffer[i]).astype(BF16)
            out.flush(move, i)
    move.finish()


def down_grad(sec, gy, gy_kind, hat, scale, small, act, kind):
    rows, width = gy.shape
    blocks = act.shape[0]
    wide = (rows, width)
    part = sds((blocks, width // 2, width), BF16)
    return call(
        down_grad_kernel,
        sec,
        [(gy, gy_kind), (hat, kind), (scale, kind), (small, FAR), (act, kind)],
        [(sds(wide, F32), NEAR), (sds(wide, BF16), NEAR), (sds((8, width), F32), NEAR), (part, NEAR), (part, NEAR)],
        [((width, rows), BF16)],
        "down_grad",
        2 * rows * width * width * blocks,
        14 << 20,
    )


def up_grad_kernel(layer, last, sec, *refs):
    refs = list(refs)
    take = lambda count: [refs.pop(0) for _ in range(count)]
    branch, base, wd_a, wd_b, slope_h, low, wu_a, wu_b = take(8)
    if last:
        hat, scale, small, sums_in = take(4)
        first, attend, sums, out = take(4)
    else:
        first, sums, out = take(3)
    wd, wu, slope, pre, sems = refs
    move = Mover(sems)
    mine = sec[0] == layer
    half, wide, _ = wd.shape
    side = sec[0] if last else 1 - sec[0]
    at = [side * half + i for i in range(half)]
    span = [pl.ds(pl.multiple_of(place * wide, wide), wide) for place in at]
    parts = []
    early = branch.fetch(move)
    for i in range(half):
        move.load(slope_h.ref.at[at[i]], slope.at[i])
        parts.append(
            [
                move.last,
                move.choose(mine, wd_a.ref.at[span[i]], wd_b.ref.at[span[i]], wd.at[i]),
                move.choose(mine, wu_a.ref.at[:, span[i]], wu_b.ref.at[:, span[i]], wu.at[i]),
            ]
        )
        if i == 0:
            early += low.fetch(move)
    late = base.fetch(move)
    if last:
        late += hat.fetch(move) + scale.fetch(move) + small.fetch(move)
        sums.buffer[...] = sums_in.buffer[...]
    else:
        sums.buffer[...] = jnp.zeros_like(sums.buffer)
    ready(early)
    total = first.buffer
    shards, tall, _ = out.buffer.shape
    for i in range(half):
        ready(parts[i])
        pre[...] = (dot_t(branch.buffer[...], wd[i]) * slope[i]).astype(BF16)
        sums.buffer[pl.ds(3 + at[i], 1)] = column_sum(pre[...].astype(F32))
        block = dot(low.buffer[...], pre[...]).astype(BF16)
        for shard in range(shards):
            out.buffer[shard, :, i * wide : i * wide + wide] = block[shard * tall : shard * tall + tall]
        if i == 0:
            ready(late)
            total[...] = base.buffer[...] + dot_t(pre[...], wu[i])
        else:
            total[...] += dot_t(pre[...], wu[i])
    if last:
        grad = total[...]
        sums.buffer[0:1] = column_sum(grad * hat.buffer[...])
        sums.buffer[1:2] = column_sum(grad)
        unit = norm_back(grad, hat.buffer[...], scale.buffer[:, 0:1], small.buffer[GAIN_ONE : GAIN_ONE + 1])
        attend.buffer[...] = unit.astype(BF16)
        total[...] = unit
        sums.buffer[2:3] = column_sum(attend.buffer[...].astype(F32))
    move.finish()


def up_grad(layer, last, sec, branch, base, wd, wd_other, slope, low, wu, wu_other, shards, more=()):
    blocks, rows, width = slope.shape
    half = blocks // 2
    wide = (rows, width)
    part = sds((shards, width // shards, half * width), BF16)
    square = ((half, width, width), BF16)
    near = lambda *shapes: [(shape, NEAR) for shape in shapes]
    ins = [
        (branch, NEAR),
        (base, NEAR),
        (wd, RAW),
        (wd_other, RAW),
        (slope, RAW),
        (low, FAR),
        (wu, RAW),
        (wu_other, RAW),
    ]
    if last:
        hat, scale, small, sums = more
        ins += [(hat, FAR), (scale, FAR), (small, FAR), (sums, NEAR)]
        outs = near(sds(wide, F32), sds(wide, BF16), sds((8, width), F32), part)
    else:
        outs = near(sds(wide, F32), sds((8, width), F32), part)
    return call(
        functools.partial(up_grad_kernel, layer, last),
        sec,
        ins,
        outs,
        [square, square, ((half,) + wide, F32), (wide, BF16)],
        "up_grad_last" if last else "up_grad_first",
        3 * rows * width * width * blocks,
        15 << 20,
    )


def attend_grad_kernel(layer, last, sec, *refs):
    refs = list(refs)
    take = lambda count: [refs.pop(0) for _ in range(count)]
    attend, ctx, base, x, q_h, k_h, v_h, p_h, wo_a, wo_b, w_a, w_b, down, up = take(14)
    if last:
        gx, gx_low, out = take(3)
    else:
        total, turned, out = take(3)
    q, k, v, probs, wo, w, gc, grads, sems = refs
    move = Mover(sems)
    mine = sec[0] == layer
    rows_all, wide = q.shape
    width = 2 * wide
    seqs = probs.shape[0]
    shards = out.buffer.shape[0]
    tall = width // shards
    pairs = wide // 128
    side = sec[0] if last else 1 - sec[0]
    lanes_half = pl.ds(pl.multiple_of(side * wide, wide), wide)
    waits = attend.fetch(move) + [move.choose(mine, wo_a.ref.at[lanes_half], wo_b.ref.at[lanes_half], wo)]
    near = []
    for source, target in (
        (p_h.ref.at[:, pl.ds(side * pairs, pairs)], probs),
        (v_h.ref.at[:, lanes_half], v),
        (k_h.ref.at[:, lanes_half], k),
        (q_h.ref.at[:, lanes_half], q),
    ):
        move.load(source, target)
        near.append(move.last)
    later = x.fetch(move) + ctx.fetch(move) + down.fetch(move) + up.fetch(move)
    finals = base.fetch(move)
    for i in range(3):
        there = pl.ds(pl.multiple_of(i * width + side * wide, wide), wide)
        finals.append(move.choose(mine, w_a.ref.at[:, there], w_b.ref.at[:, there], w.at[:, pl.ds(i * wide, wide)]))
    ready(waits)
    gc[...] = dot_t(attend.buffer[...], wo[...]).astype(BF16)
    ready(near)
    halves = lane_halves()
    lower = lax.broadcasted_iota(jnp.int32, (128, 128), 1) < 64

    for pair in range(pairs):
        lanes = slice(pair * 128, pair * 128 + 128)
        for seq in range(seqs):
            rows = slice(seq * 128, seq * 128 + 128)

            def put(part, value):
                grads[rows, part * wide + pair * 128 : part * wide + pair * 128 + 128] = value.astype(BF16)

            grad = gc[rows, lanes]
            p = probs[seq, pair]
            full = dot(p.astype(BF16), grad)
            put(2, jnp.where(lower, full[:128], full[128:]))
            gp = dot_t(two_heads(v[rows, lanes], halves), grad)
            parts = []
            for part in (slice(0, 128), slice(128, 256)):
                g, pp = gp[part], p[part]
                parts.append(pp * (g - jnp.sum(g * pp, axis=0, keepdims=True)))
            gs = jnp.concatenate(parts, axis=0).astype(BF16)
            put(0, t_dot(gs, two_heads(k[rows, lanes] * SCALE, halves)))
            full = dot(gs, q[rows, lanes] * SCALE)
            put(1, jnp.where(lower, full[:128], full[128:]))
    ready(later)
    if last:
        turned = x
    else:
        turned.buffer[...] = x.buffer[...].T
    left = dot(turned.buffer[...], grads[...]).astype(BF16)
    right = dot(ctx.buffer[...], attend.buffer[:, lanes_half]).astype(BF16)
    little = jnp.concatenate([down.buffer[...], up.buffer[...]], axis=0).astype(BF16)
    zeros = jnp.zeros_like(little)
    b_q = column_sum(grads[:, 0:wide].astype(F32)).astype(BF16)
    b_v = column_sum(grads[:, 2 * wide :].astype(F32)).astype(BF16)
    pad = jnp.concatenate([b_q, b_v], axis=1)
    pad = jnp.concatenate([pad, jnp.zeros((15, width), BF16)], axis=0)
    for shard in range(shards):
        out.buffer[shard, :tall, 0 : 3 * wide] = left[shard * tall : shard * tall + tall]
        out.buffer[shard, :tall, 3 * wide :] = right[shard * tall : shard * tall + tall]
        out.buffer[shard, tall:, 0:width] = little
        out.buffer[shard, tall:, width:] = pad
    ready(finals)
    sum_all = base.buffer[...] + dot_t(grads[...], w[...])
    if last:
        gx.buffer[...] = sum_all
        gx.flush(move)
        gx_low.buffer[...] = sum_all.astype(BF16)
        gx_low.flush(move)
    else:
        total.buffer[...] = sum_all
    move.finish()


def attend_grad(layer, last, sec, attend, ctx, base, x, q, k, v, probs, wo, wo_other, w, w_other, down, up, shards, low_kind):
    rows, width = attend.shape
    seqs = probs.shape[0]
    wide = width // 2
    flat = (rows, width)
    part = (sds((shards, width // shards + 16, 2 * width), BF16), NEAR)
    if last:
        outs = [(sds(flat, F32), FAR), (sds(flat, BF16), low_kind), part]
    else:
        outs = [(sds(flat, F32), NEAR), (sds((width, rows), BF16), NEAR), part]
    half = ((rows, wide), BF16)
    return call(
        functools.partial(attend_grad_kernel, layer, last),
        sec,
        [(attend, NEAR), (ctx, FAR), (base, NEAR), (x, NEAR if last else FAR)]
        + [(item, RAW) for item in (q, k, v, probs, wo, wo_other, w, w_other)]
        + [(down, NEAR), (up, NEAR)],
        outs,
        [
            half,
            half,
            half,
            ((seqs, wide // 128) + probs.shape[2:], F32),
            ((wide, width), BF16),
            ((width, 3 * wide), BF16),
            half,
            ((rows, 3 * wide), BF16),
        ],
        "attend_grad_last" if last else "attend_grad_first",
        rows * width * width * 10,
        15 << 20,
    )


def layer_forward(layer, sec, x, front, big, other, small, far=None):
    w_qkv, w_out, w_up, w_down = big
    o_qkv, o_out, o_up, o_down = other
    x_kind = FAR if layer == 0 else NEAR
    q, k, v, probs, (ctx_near, ctx) = front
    (hat_near, hat_one), scale_one, low, act, slope = up_forward(
        layer, sec, x, x_kind, ctx_near, w_out, o_out, w_up, o_up, small
    )
    act_near, act = act if layer == 0 else (act, act)
    kinds = (BOTH, FAR) if layer == 0 else (FAR, NEAR)
    y, hat_two, scale_two = down_forward(layer, sec, act_near, w_down, o_down, hat_near, small, *kinds)
    x = x if far is None else far
    return y, (x, q, k, v, probs, ctx, hat_one, scale_one, low, act, slope, hat_two, scale_two)


def layer_backward(line, layer, sec, gy, cache, big, other, small, shards):
    w_qkv, w_out, w_up, w_down = big
    o_qkv, o_out, o_up, o_down = other
    x, q, k, v, probs, ctx, hat_one, scale_one, low, act, slope, hat_two, scale_two = cache
    kinds = (NEAR, FAR) if layer == 0 else (FAR, NEAR)
    second, branch, down, d_send, d_keep = line.advance(
        lambda: down_grad(sec, gy, kinds[0], hat_two, scale_two, small, act, kinds[1])
    )
    line.add(d_send, d_keep)
    up_ins = (w_down, o_down, slope, low, w_up, o_up, shards)
    part, up, u_send = line.advance(lambda: up_grad(layer, False, sec, branch, second, *up_ins))
    more = (hat_one, scale_one, small, up)
    line.add(u_send, None, layer == 0)
    first, attend, up, u_keep = line.advance(lambda: up_grad(layer, True, sec, branch, part, *up_ins, more))
    line.keep(u_keep)
    heads = (q, k, v, probs, w_out, o_out, w_qkv, o_qkv, down, up, shards)
    low_kind = FAR if layer == 0 else BOTH
    part, turned, a_send = line.advance(
        lambda: attend_grad(layer, False, sec, attend, ctx, first, x, *heads, low_kind)
    )
    line.add(a_send, None, layer == 0)
    gx, gx_low, a_keep = line.advance(
        lambda: attend_grad(layer, True, sec, attend, ctx, part, turned, *heads, low_kind)
    )
    line.keep(a_keep)
    return gx, gx_low


def exchange(array, axis, bit):
    length = lax.axis_size(axis)
    return lax.ppermute(array, axis, [(i, i ^ bit) for i in range(length)])


def pick(array, index, axis):
    return lax.dynamic_index_in_dim(array, index, axis, keepdims=False)


def split_at(rows):
    return (rows // 2 + 15) // 16 * 16


def join_section(ids, ins, outs):
    kept, got = ins
    top_send, top_keep, bottom_send, bottom_keep = outs
    low_bit, high_bit = ids[1], ids[2]
    cut = top_send.shape[1]
    for i in range(2):
        for out, shard in ((top_send, 2 * i + 1 - low_bit), (top_keep, 2 * i + low_bit)):
            out[i] = kept[shard, :cut] + got[shard, :cut]
        for out, shard in ((bottom_send, 2 * (1 - high_bit) + i), (bottom_keep, 2 * high_bit + i)):
            out[i] = kept[shard, cut:] + got[shard, cut:]


def join_first(ids, ins, outs):
    top, top_got, bottom, bottom_got = ins
    top_send, top_keep, bottom_send, bottom_keep = outs
    low_bit, high_bit = ids[1], ids[2]
    top_send[...] = top[1 - high_bit] + top_got[1 - high_bit]
    top_keep[...] = top[high_bit] + top_got[high_bit]
    bottom_send[...] = bottom[1 - low_bit] + bottom_got[1 - low_bit]
    bottom_keep[...] = bottom[low_bit] + bottom_got[low_bit]


def join_second(ids, ins, outs):
    top, top_got, bottom, bottom_got = ins
    cut = top.shape[0]
    outs[0][:cut] = top[...] + top_got[...]
    outs[0][cut:] = bottom[...] + bottom_got[...]


def join_add(ids, ins, outs):
    outs[0][...] = ins[0][...] + ins[1][...]


def join_split(ids, ins, outs):
    top, top_got, bottom, bottom_got = ins
    send, keep = outs
    cut, wide = top.shape[0], send.shape[1]
    for out, half in ((send, 1 - ids[3]), (keep, ids[3])):
        lanes = pl.ds(pl.multiple_of(half * wide, wide), wide)
        out[:cut] = top[:, lanes] + top_got[:, lanes]
        out[cut:] = bottom[:, lanes] + bottom_got[:, lanes]


def join_half(ids, ins, outs):
    kept, got = ins
    send, keep = outs
    wide = send.shape[1]
    for out, half in ((send, 1 - ids[4]), (keep, ids[4])):
        lanes = pl.ds(pl.multiple_of(half * wide, wide), wide)
        out[...] = kept[:, lanes] + got[:, lanes]


def join_last(ids, ins, outs):
    edge = ids[3] == ids[4]

    @pl.when(edge)
    def _():
        outs[0][...] = ins[1][...]

    @pl.when(jnp.logical_not(edge))
    def _():
        outs[0][...] = ins[0][...]


def join_sides(bit):
    def function(ids, ins, outs):
        wide = ins[0].shape[1]
        for part, half in ((ins[0], ids[bit]), (ins[1], 1 - ids[bit])):
            outs[0][:, pl.ds(pl.multiple_of(half * wide, wide), wide)] = part[...]

    return function


def join(ids, jobs):
    counts = [(len(ins), len(shapes)) for _, ins, shapes in jobs]
    n_in = sum(a for a, _ in counts)

    def kernel(ids_ref, *refs):
        at_in, at_out = 0, n_in
        for (function, _, _), (a, b) in zip(jobs, counts):
            function(ids_ref, refs[at_in : at_in + a], refs[at_out : at_out + b])
            at_in, at_out = at_in + a, at_out + b

    flat = [array for _, ins, _ in jobs for array in ins]
    shapes = [sds(shape, BF16) for _, _, shapes in jobs for shape in shapes]
    vmem = pl.BlockSpec(memory_space=pltpu.VMEM)
    outs = pl.pallas_call(
        kernel,
        in_specs=[pl.BlockSpec(memory_space=pltpu.SMEM)] + [vmem] * n_in,
        out_specs=[vmem] * len(shapes),
        out_shape=shapes,
        compiler_params=pltpu.CompilerParams(vmem_limit_bytes=VMEM),
        name="join_sums",
    )(ids, *flat)
    result = []
    for _, b in counts:
        result.append(outs[:b])
        outs = outs[b:]
    return result


TIMES = (1, 2, 2, 1, 1, 1, 1)


class Line:
    def __init__(self):
        self.plain = lax.axis_size("inner") != 4
        self.short = lax.axis_size("outer") == 4
        spot, place = lax.axis_index("inner"), lax.axis_index("outer")
        self.ids = jnp.stack([lax.axis_index("section"), spot % 2, spot // 2, place % 2, place // 2]).astype(jnp.int32)
        self.running = []

    def add(self, send, keep, late=False):
        self.running.append({"at": 0, "parts": [send, keep], "pending": None, "keep": keep, "late": late, "done": None, "flight": None})

    def keep(self, keep):
        self.running[-1]["keep"] = keep

    def start(self, item):
        at, parts = item["at"], item["parts"]
        item["at"] += 1
        if at == 0:
            got = exchange(parts[0], "section", 1)
            if self.plain:
                return [got], lambda tied: (join_add, [item["keep"], tied[0]], [item["keep"].shape])
            _, rows, columns = parts[0].shape
            cut = split_at(rows)
            shapes = [(2, cut, columns)] * 2 + [(2, rows - cut, columns)] * 2
            return [got], lambda tied: (join_section, [item["keep"], tied[0]], shapes)
        if self.plain:
            total = lax.psum_scatter(parts[0], "inner", scatter_dimension=0, tiled=False)
            item["done"] = lax.psum(total, "outer")
            return None
        if at == 1:
            top_send, top, bottom_send, bottom = parts
            gots = [exchange(top_send, "inner", 1), exchange(bottom_send, "inner", 2)]
            shapes = [top.shape[1:]] * 2 + [bottom.shape[1:]] * 2
            return gots, lambda tied: (join_first, [top, tied[0], bottom, tied[1]], shapes)
        halves = self.short and item["late"]
        if at == 2:
            top_send, top, bottom_send, bottom = parts
            gots = [exchange(top_send, "inner", 2), exchange(bottom_send, "inner", 1)]
            rows, columns = top.shape[0] + bottom.shape[0], top.shape[1]
            if halves:
                return gots, lambda tied: (
                    join_split, [top, tied[0], bottom, tied[1]], [(rows, columns // 2)] * 2
                )
            return gots, lambda tied: (join_second, [top, tied[0], bottom, tied[1]], [(rows, columns)])
        if not self.short:
            item["done"] = lax.psum(parts[0], "outer")
            return None
        rows, columns = parts[0].shape
        if not halves and at in (3, 4, 5):
            pairs = ([(0, 1), (3, 2)], [(1, 2), (2, 1)], [(1, 0), (2, 3)])[at - 3]
            got = lax.ppermute(parts[0], "outer", pairs)
            function = join_last if at == 5 else join_add
            return [got], lambda tied: (function, [parts[0], tied[0]], [(rows, columns)])
        if at == 3:
            send, keep = parts
            got = exchange(send, "outer", 1)
            return [got], lambda tied: (join_half, [keep, tied[0]], [(rows, columns // 2)] * 2)
        if at == 4:
            send, keep = parts
            got = exchange(send, "outer", 2)
            return [got], lambda tied: (join_add, [keep, tied[0]], [(rows, columns)])
        if halves and at in (5, 6):
            bit = 7 - at
            got = exchange(parts[0], "outer", bit)
            return [got], lambda tied: (join_sides(2 + bit), [parts[0], tied[0]], [(rows, 2 * columns)])
        item["done"] = parts[0]
        return None

    def settle(self, items):
        if items:
            for item, parts in zip(items, join(self.ids, [item["pending"]() for item in items])):
                item["parts"], item["pending"] = parts, None

    def advance(self, work):
        self.settle([item for item in self.running if item["pending"] is not None])
        for item in self.running:
            if item["done"] is None and item["flight"] is None:
                move = self.start(item)
                if move is not None:
                    item["flight"], item["left"] = move, TIMES[item["at"] - 1]
        flying = [item for item in self.running if item["flight"] is not None]
        for item in flying:
            item["left"] -= 1
        due = [item for item in flying if item["left"] == 0]
        beside, tied = lax.optimization_barrier((work(), [item["flight"][0] for item in due]))
        for item, gots in zip(due, tied):
            item["pending"], item["flight"] = functools.partial(item["flight"][1], gots), None
        return beside

    def finish(self):
        if not self.short or self.plain:
            for item in self.running:
                while item["done"] is None:
                    if item["flight"] is not None:
                        gots, after = item["flight"]
                        item["pending"], item["flight"] = functools.partial(after, gots), None
                    if item["pending"] is not None:
                        self.settle([item])
                    item["flight"] = self.start(item)
        while any(item["done"] is None for item in self.running):
            self.advance(lambda: ())
            for item in self.running:
                if item["flight"] is not None and item is self.running[-1]:
                    item["left"] = 1
        return [item["done"] for item in self.running]


def local(
    hidden_in, caption_len, region_len, cotangent, w_qkv, b_qv, w_out, b_out, ln_gain, ln_bias, w_up, b_up, w_down, b_down
):
    section = lax.axis_index("section")
    shards = lax.axis_size("inner")
    sec = section.astype(jnp.int32)[None]
    seqs_local, length, width = hidden_in.shape
    seqs = seqs_local // 2
    rows = seqs * length
    positions = jnp.arange(length, dtype=jnp.int32)[None, :]
    mine = lambda array: lax.dynamic_slice_in_dim(array, section * seqs, seqs, 0)
    caption, region = mine(caption_len)[:, None], mine(region_len)[:, None]
    valid = (positions < caption) | (positions >= CAP) & (positions < CAP + region)
    mask = jnp.concatenate([valid, valid], axis=1).astype(F32).T
    x = mine(hidden_in).reshape(rows, width)
    gy = jnp.where(valid[:, :, None], mine(cotangent), jnp.zeros((), BF16)).reshape(rows, width)

    blocks = w_up.shape[2] // width
    little = jnp.concatenate(
        [b_qv[0], b_out, ln_gain[0], ln_bias[0], b_down, b_up.reshape(blocks, width), jnp.zeros((8 - blocks, width), F32)]
    )
    little_other = exchange(little, "section", 1)
    big = (w_qkv[0], w_out[0], w_up[0], w_down[0])
    o_qkv = exchange(big[0], "section", 1)

    smalls = [jnp.where(section == layer, little, little_other) for layer in (0, 1)]
    o_qkv, smalls, mask, x, late_out, late_up = lax.optimization_barrier(
        (o_qkv, smalls, mask, x, big[1], big[2])
    )
    o_out, o_up = exchange(late_out, "section", 1), exchange(late_up, "section", 1)
    front = attend_forward(0, sec, x, FAR, big[0], o_qkv, smalls[0], mask)
    front, o_out, o_up, late_down = lax.optimization_barrier((front, o_out, o_up, big[3]))
    other = (o_qkv, o_out, o_up, exchange(late_down, "section", 1))
    y_one, cache_one = layer_forward(0, sec, x, front, big, other, smalls[0])
    y_near, y_one = y_one
    front = attend_forward(1, sec, y_near, NEAR, big[0], o_qkv, smalls[1], mask)
    y_two, cache_two = layer_forward(1, sec, y_near, front, big, other, smalls[1], y_one)
    line = Line()
    gx_two, (gx_two_near, gx_two_low) = layer_backward(line, 1, sec, gy, cache_two, big, other, smalls[1], shards)
    gx_one, gx_one_low = layer_backward(line, 0, sec, gx_two_near, cache_one, big, other, smalls[0], shards)

    def gather(for_zero, for_one):
        kept = jnp.where(section == 0, for_zero, for_one)
        got = exchange(jnp.where(section == 0, for_one, for_zero), "section", 1)
        return jnp.where(section == 0, kept, got), jnp.where(section == 0, got, kept)

    activations = jnp.concatenate(gather(y_one, y_two), axis=0).reshape(seqs_local, length, width)
    input_grads = jnp.concatenate(gather(gx_one, gx_two_low.astype(F32)), axis=0).reshape(
        seqs_local, length, width
    )
    sums = line.finish()
    down, up, attend = [gather(one, two) for one, two in zip(sums[3:], sums[:3])]
    g_w_down = jnp.concatenate(down, axis=0).T.astype(F32)
    g_w_up = jnp.concatenate(up, axis=1).astype(F32)
    part = width // 2
    tall = width // shards
    matrix = [side[:tall] for side in attend]
    g_w_qkv = jnp.concatenate(
        [side[:, i * part : (i + 1) * part] for i in range(3) for side in matrix], axis=1
    ).astype(F32)
    g_w_out = jnp.concatenate([side[:, 3 * part :] for side in matrix], axis=1).astype(F32)
    rows = attend[0][tall:, :width]
    b_q, b_v = [
        jnp.concatenate([side[tall, width + i * part : width + (i + 1) * part] for side in attend]) for i in range(2)
    ]
    rows = jnp.concatenate([rows, b_q[None], b_v[None]], axis=0)
    place = lax.axis_index("inner")
    mine = lax.dynamic_slice_in_dim(rows, place * tall, tall, 1).astype(F32)
    up_row = pick(rows[11 : 11 + blocks].reshape(shards, width * blocks // shards), place, 0).astype(F32)
    return (
        activations[None],
        input_grads[None],
        g_w_qkv[None],
        mine[16:18][None],
        g_w_out[None],
        mine[10][None],
        jnp.stack([mine[8], mine[0]])[None],
        jnp.stack([mine[9], mine[1]])[None],
        g_w_up[None],
        up_row[None],
        g_w_down[None],
        mine[2][None],
    )


def solution(mesh):
    rows = ("inner", "outer")
    return jax.shard_map(
        local,
        mesh=mesh,
        in_specs=(
            P(rows, None, None),
            P(rows),
            P(rows),
            P(rows, None, None),
            P("section", None, None),
            P("section", None, None),
            P("section", None, None),
            P("section", None),
            P("section", None, None),
            P("section", None, None),
            P("section", None, None),
            P("section", None),
            P("section", None, None),
            P("section", None),
        ),
        out_specs=(
            P("section", rows, None, None),
            P("section", rows, None, None),
            P("section", "inner", None),
            P("section", None, "inner"),
            P("section", "inner", None),
            P("section", "inner"),
            P("section", None, "inner"),
            P("section", None, "inner"),
            P("section", "inner", None),
            P("section", "inner"),
            P("section", "inner", None),
            P("section", "inner"),
        ),
        check_vma=False,
    )
```

```python
import functools

import jax
import jax.numpy as jnp
from jax import lax
from jax.experimental import pallas as pl
from jax.experimental.pallas import tpu as pltpu
from jax.sharding import PartitionSpec as P

HEADS = 12
CAP = 28
EPS = 1e-12
SCALE = 0.125
VMEM = 30 * 1024 * 1024
F32 = jnp.float32
BF16 = jnp.bfloat16
B_Q, B_V, B_OUT, GAIN_ONE, GAIN_TWO, OFFSET_ONE, OFFSET_TWO, B_DOWN, B_UP = range(9)


def dot(left, right):
    return jnp.dot(left, right, preferred_element_type=F32)


def dot_t(left, right):
    return lax.dot_general(left, right, (((1,), (1,)), ((), ())), preferred_element_type=F32)


def t_dot(left, right):
    return lax.dot_general(left, right, (((0,), (0,)), ((), ())), preferred_element_type=F32)


def column_sum(values):
    return jnp.sum(values, axis=0, keepdims=True)


def standardize(summed):
    centre = jnp.mean(summed, axis=-1, keepdims=True)
    shifted = summed - centre
    spread = jnp.mean(shifted * shifted, axis=-1, keepdims=True)
    scale = lax.rsqrt(spread + EPS)
    return shifted * scale, scale


def norm_back(grad, hat, scale, gain):
    scaled = grad * gain
    return scale * (
        scaled
        - jnp.mean(scaled, axis=-1, keepdims=True)
        - hat * jnp.mean(scaled * hat, axis=-1, keepdims=True)
    )


def gauss_share(value):
    bell = jnp.exp2(value * value * -0.7213475204444817)
    part = 1.0 / (1.0 + 0.2316418882 * jnp.abs(value))
    tail = 0.5307027145
    for item in (-0.7265760135, 0.7107068705, -0.142248368, 0.127414796):
        tail = tail * part + item
    tail = tail * part * bell
    return jnp.where(value < 0.0, tail, 1.0 - tail), bell


def lane_halves():
    lane = lax.broadcasted_iota(jnp.int32, (1, 128), 1)
    lower = jnp.where(lane < 64, 1.0, 0.0)
    return lower.astype(BF16), (1.0 - lower).astype(BF16)


def two_heads(block, halves):
    return jnp.concatenate([block * halves[0], block * halves[1]], axis=0)


def sds(shape, dtype):
    return jax.ShapeDtypeStruct(shape, dtype)


class Mover:
    def __init__(self, sems):
        self.sems, self.used, self.outs = sems, 0, []

    def copy(self, source, target):
        self.used += 1
        return pltpu.make_async_copy(source, target, self.sems.at[self.used - 1])

    def load(self, source, target):
        self.last = self.copy(source, target)
        self.last.start()

    def choose(self, first, one, two, target):
        copy = self.copy(one, target)
        other = pltpu.make_async_copy(two, target, self.sems.at[self.used - 1])
        pl.when(first)(copy.start)
        pl.when(jnp.logical_not(first))(other.start)
        return copy

    def store(self, source, target):
        copy = self.copy(source, target)
        copy.start()
        self.outs.append(copy)

    def finish(self):
        for copy in self.outs:
            copy.wait()


class Operand:
    def __init__(self, ref, buffer, far):
        self.ref, self.buffer, self.far = ref, buffer, far

    def fetch(self, move, *index):
        if self.far:
            move.load(*(ref.at[index] if index else ref for ref in (self.ref, self.buffer)))
            return [move.last]
        return []

    def flush(self, move, *index):
        if self.far:
            move.store(*(ref.at[index] if index else ref for ref in (self.buffer, self.ref)))


NEAR, FAR, RAW, BOTH = "near", "far", "raw", "both"


def ready(waits):
    for item in waits:
        item.wait()


def call(kernel, ids, ins, outs, scratch, name, flops, nbytes):
    space = lambda kind: pltpu.VMEM if kind == NEAR else pltpu.HBM
    spread = [(shape, part) for shape, kind in outs for part in ((NEAR, RAW) if kind == BOTH else (kind,))]
    kinds = [kind for _, kind in ins] + [kind for _, kind in spread]
    shapes = [array for array, _ in ins] + [shape for shape, _ in spread]
    buffers = [pltpu.VMEM(shape.shape, shape.dtype) for shape, kind in zip(shapes, kinds) if kind == FAR]

    def body(ids_ref, *refs):
        count = len(kinds)
        spare = list(refs[count : count + len(buffers)])
        left = list(refs[:count])
        operands = []
        for _, kind in list(ins) + list(outs):
            ref = left.pop(0)
            if kind == BOTH:
                operands.append(Operand(left.pop(0), ref, True))
            else:
                operands.append(Operand(ref, spare.pop(0) if kind == FAR else ref, kind == FAR))
        kernel(ids_ref, *operands, *refs[count + len(buffers) :])

    results = pl.pallas_call(
        body,
        in_specs=[pl.BlockSpec(memory_space=pltpu.SMEM)]
        + [pl.BlockSpec(memory_space=space(kind)) for _, kind in ins],
        out_specs=[pl.BlockSpec(memory_space=space(kind)) for _, kind in spread],
        out_shape=[space(kind)(shape.shape, shape.dtype) for shape, kind in spread],
        scratch_shapes=buffers + [pltpu.VMEM(*item) for item in scratch] + [pltpu.SemaphoreType.DMA((64,))],
        compiler_params=pltpu.CompilerParams(vmem_limit_bytes=VMEM),
        cost_estimate=pl.CostEstimate(flops=flops, bytes_accessed=nbytes, transcendentals=0),
        name=name,
    )(ids, *(pltpu.with_memory_space_constraint(array, space(kind)) for array, kind in ins))
    results = list(results)
    return [(results.pop(0), results.pop(0)) if kind == BOTH else results.pop(0) for _, kind in outs]


def attend_phase(q, k, v, probs, ctx, mask, pairs):
    seqs = mask.shape[1]
    halves = lane_halves()
    feature = lax.broadcasted_iota(jnp.int32, (128, 128), 0)
    first_half = jnp.where(feature < 64, 1.0, 0.0).astype(BF16)
    second_half = jnp.where(feature < 64, 0.0, 1.0).astype(BF16)

    @pl.loop(*pairs)
    def _(pair):
        lanes = pl.ds(pl.multiple_of(pair * 128, 128), 128)
        for seq in range(seqs):
            rows = slice(seq * 128, seq * 128 + 128)
            seen = jnp.broadcast_to(mask[:, seq : seq + 1], (256, 128)) > 0.5
            scores = dot_t(two_heads(k[rows, lanes], halves), q[rows, lanes] * SCALE)
            scores = jnp.where(seen, scores, -1e30)
            parts = []
            for part in (scores[:128], scores[128:]):
                e = jnp.exp(part - jnp.max(part, axis=0, keepdims=True))
                parts.append(e * (1.0 / jnp.sum(e, axis=0, keepdims=True)))
            parts = jnp.concatenate(parts, axis=0)
            probs[seq, pair] = parts
            turned = v[rows, lanes].T
            turned = jnp.concatenate([turned * first_half, turned * second_half], axis=1)
            ctx[lanes, rows] = dot(turned, parts.astype(BF16)).astype(BF16)


def attend_kernel(layer, sec, x, w_a, w_b, small, mask, q, k, v, probs, ctx, w, sems):
    move = Mover(sems)
    mine = sec[0] == layer
    rows, width = x.buffer.shape
    waits = x.fetch(move) + small.fetch(move) + mask.fetch(move)
    parts = [
        move.choose(mine, w_a.ref.at[:, pl.ds(i * width, width)], w_b.ref.at[:, pl.ds(i * width, width)], w.at[i])
        for i in (1, 0, 2)
    ]
    ready(waits)
    x, small = x.buffer, small.buffer
    parts[0].wait()
    k.buffer[...] = dot(x[...], w[1]).astype(BF16)
    k.flush(move)
    parts[1].wait()
    q.buffer[...] = (dot(x[...], w[0]) + small[B_Q : B_Q + 1]).astype(BF16)
    q.flush(move)
    parts[2].wait()
    v.buffer[...] = (dot(x[...], w[2]) + small[B_V : B_V + 1]).astype(BF16)
    v.flush(move)
    half = width // 128 // 2
    for i in range(2):
        attend_phase(
            q.buffer, k.buffer, v.buffer, probs.buffer, ctx.buffer, mask.buffer, (i * half, i * half + half)
        )
        probs.flush(move, slice(None), pl.ds(i * half, half))
    ctx.flush(move)
    move.finish()


def attend_forward(layer, sec, x, x_kind, w_own, w_other, small, mask):
    rows, width = x.shape
    seqs = mask.shape[1]
    pairs = width // 128
    wide = sds((rows, width), BF16)
    return call(
        functools.partial(attend_kernel, layer),
        sec,
        [(x, x_kind), (w_own, RAW), (w_other, RAW), (small, FAR), (mask, FAR)],
        [(wide, FAR)] * 3 + [(sds((seqs, pairs, 256, 128), F32), FAR), (sds((width, rows), BF16), BOTH)],
        [((3, width, width), BF16)],
        "attend_forward",
        2 * rows * width * width * 4,
        12 << 20,
    )


def up_kernel(layer, sec, x, ctx, wo_a, wo_b, wu_a, wu_b, small, hat, scale, turned, act, slope, wo, wu, low, sems):
    move = Mover(sems)
    mine = sec[0] == layer
    blocks, _, wide = wu.shape
    waits = ctx.fetch(move) + [move.choose(mine, wo_a.ref, wo_b.ref, wo)] + small.fetch(move) + x.fetch(move)
    span = lambda i: pl.ds(i * wide, wide)
    parts = [move.choose(mine, wu_a.ref.at[:, span(i)], wu_b.ref.at[:, span(i)], wu.at[i]) for i in range(blocks)]
    ready(waits)
    small = small.buffer
    summed = x.buffer[...].astype(F32) + t_dot(ctx.buffer[...], wo[...]) + small[B_OUT : B_OUT + 1]
    unit, root = standardize(summed)
    hat.buffer[...] = unit
    hat.flush(move)
    scale.buffer[...] = jnp.broadcast_to(root, scale.buffer.shape)
    scale.flush(move)
    low[...] = (unit * small[GAIN_ONE : GAIN_ONE + 1] + small[OFFSET_ONE : OFFSET_ONE + 1]).astype(BF16)
    turned.buffer[...] = low[...].T
    turned.flush(move)
    for i in range(blocks):
        parts[i].wait()
        pre = dot(low[...], wu[i]) + small[B_UP + i : B_UP + i + 1]
        share, bell = gauss_share(pre)
        act.buffer[i] = (pre * share).astype(BF16)
        slope.buffer[i] = share + pre * 0.3989422804014327 * bell
        act.flush(move, i)
        slope.flush(move, i)
    move.finish()


def up_forward(layer, sec, x, x_kind, ctx, wo, wo_other, wu, wu_other, small):
    rows, width = x.shape
    blocks = wu.shape[1] // width
    wide = (rows, width)
    return call(
        functools.partial(up_kernel, layer),
        sec,
        [(x, x_kind), (ctx, NEAR), (wo, RAW), (wo_other, RAW), (wu, RAW), (wu_other, RAW), (small, FAR)],
        [
            (sds(wide, F32), BOTH),
            (sds((rows, 128), F32), FAR),
            (sds((width, rows), BF16), FAR),
            (sds((blocks,) + wide, BF16), BOTH if layer == 0 else NEAR),
            (sds((blocks,) + wide, F32), FAR),
        ],
        [((width, width), BF16), ((blocks, width, width), BF16), (wide, BF16)],
        "up_forward",
        2 * rows * width * width * (blocks + 1),
        20 << 20,
    )


def down_kernel(layer, sec, act, wd_a, wd_b, hat, small, y, two, scale, wd, total, sems):
    move = Mover(sems)
    mine = sec[0] == layer
    blocks, wide, _ = wd.shape
    parts = []
    for i in range(blocks):
        span = pl.ds(i * wide, wide)
        parts.append(act.fetch(move, i) + [move.choose(mine, wd_a.ref.at[span], wd_b.ref.at[span], wd.at[i])])
        if i == 0:
            waits = small.fetch(move) + hat.fetch(move)
    for i in range(blocks):
        ready(parts[i])
        product = dot(act.buffer[i], wd[i])
        total[...] = product if i == 0 else total[...] + product
    ready(waits)
    small = small.buffer
    normed = hat.buffer[...] * small[GAIN_ONE : GAIN_ONE + 1] + small[OFFSET_ONE : OFFSET_ONE + 1]
    unit, root = standardize(total[...] + normed + small[B_DOWN : B_DOWN + 1])
    y.buffer[...] = (unit * small[GAIN_TWO : GAIN_TWO + 1] + small[OFFSET_TWO : OFFSET_TWO + 1]).astype(BF16)
    y.flush(move)
    two.buffer[...] = unit
    two.flush(move)
    scale.buffer[...] = jnp.broadcast_to(root, scale.buffer.shape)
    scale.flush(move)
    move.finish()


def down_forward(layer, sec, act, wd, wd_other, hat, small, y_kind, two_kind):
    blocks, rows, width = act.shape
    wide = (rows, width)
    return call(
        functools.partial(down_kernel, layer),
        sec,
        [(act, NEAR), (wd, RAW), (wd_other, RAW), (hat, NEAR), (small, FAR)],
        [(sds(wide, BF16), y_kind), (sds(wide, F32), two_kind), (sds((rows, 128), F32), two_kind)],
        [((blocks, width, width), BF16), (wide, F32)],
        "down_forward",
        2 * rows * width * width * blocks,
        12 << 20,
    )


def down_grad_kernel(sec, gy, hat, scale, small, act, second, branch, sums, send, keep, turned, sems):
    move = Mover(sems)
    blocks = act.buffer.shape[0]
    low_rows, wide = send.buffer.shape[1], act.buffer.shape[2]
    tall = 2 * low_rows
    waits = gy.fetch(move) + small.fetch(move) + scale.fetch(move) + hat.fetch(move)
    parts = [act.fetch(move, i) for i in range(blocks)]
    ready(waits)
    grad = gy.buffer[...].astype(F32)
    sums.buffer[0:1] = column_sum(grad * hat.buffer[...])
    sums.buffer[1:2] = column_sum(grad)
    unit = norm_back(grad, hat.buffer[...], scale.buffer[:, 0:1], small.buffer[GAIN_TWO : GAIN_TWO + 1])
    second.buffer[...] = unit
    second.flush(move)
    low = unit.astype(BF16)
    branch.buffer[...] = low
    branch.flush(move)
    sums.buffer[2:3] = column_sum(low.astype(F32))
    sums.buffer[3:] = jnp.zeros_like(sums.buffer[3:])
    sums.flush(move)
    turned[...] = branch.buffer[...].T
    for half, out in ((1 - sec[0], send), (sec[0], keep)):
        left = pl.ds(pl.multiple_of(half * tall, tall), tall)
        for i in range(blocks):
            if out is send:
                ready(parts[i])
            block = dot(turned[left, :], act.buffer[i]).astype(BF16)
            out.buffer[i, :, :wide] = block[:low_rows]
            out.buffer[i, :, wide:] = block[low_rows:]
    move.finish()


def down_grad(sec, gy, gy_kind, hat, scale, small, act, kind):
    rows, width = gy.shape
    blocks = act.shape[0]
    wide = (rows, width)
    part = sds((blocks, width // 4, 2 * width), BF16)
    return call(
        down_grad_kernel,
        sec,
        [(gy, gy_kind), (hat, kind), (scale, kind), (small, FAR), (act, kind)],
        [(sds(wide, F32), NEAR), (sds(wide, BF16), NEAR), (sds((8, width), F32), NEAR), (part, NEAR), (part, NEAR)],
        [((width, rows), BF16)],
        "down_grad",
        2 * rows * width * width * blocks,
        14 << 20,
    )


def up_grad_kernel(layer, last, sec, *refs):
    refs = list(refs)
    take = lambda count: [refs.pop(0) for _ in range(count)]
    branch, base, wd_a, wd_b, slope_h, low, wu_a, wu_b = take(8)
    if last:
        hat, scale, small, sums_in = take(4)
        first, attend, sums, out = take(4)
    else:
        first, sums, out = take(3)
    wd, wu, slope, pre, sems = refs
    move = Mover(sems)
    mine = sec[0] == layer
    half, wide, _ = wd.shape
    side = sec[0] if last else 1 - sec[0]
    at = [side * half + i for i in range(half)]
    span = [pl.ds(pl.multiple_of(place * wide, wide), wide) for place in at]
    parts = []
    early = branch.fetch(move)
    for i in range(half):
        move.load(slope_h.ref.at[at[i]], slope.at[i])
        parts.append(
            [
                move.last,
                move.choose(mine, wd_a.ref.at[span[i]], wd_b.ref.at[span[i]], wd.at[i]),
                move.choose(mine, wu_a.ref.at[:, span[i]], wu_b.ref.at[:, span[i]], wu.at[i]),
            ]
        )
        if i == 0:
            early += low.fetch(move)
    late = base.fetch(move)
    if last:
        late += hat.fetch(move) + scale.fetch(move) + small.fetch(move)
        sums.buffer[...] = sums_in.buffer[...]
    else:
        sums.buffer[...] = jnp.zeros_like(sums.buffer)
    ready(early)
    total = first.buffer
    shards, tall, _ = out.buffer.shape
    for i in range(half):
        ready(parts[i])
        pre[...] = (dot_t(branch.buffer[...], wd[i]) * slope[i]).astype(BF16)
        sums.buffer[pl.ds(3 + at[i], 1)] = column_sum(pre[...].astype(F32))
        block = dot(low.buffer[...], pre[...]).astype(BF16)
        for shard in range(shards):
            out.buffer[shard, :, i * wide : i * wide + wide] = block[shard * tall : shard * tall + tall]
        if i == 0:
            ready(late)
            total[...] = base.buffer[...] + dot_t(pre[...], wu[i])
        else:
            total[...] += dot_t(pre[...], wu[i])
    if last:
        grad = total[...]
        sums.buffer[0:1] = column_sum(grad * hat.buffer[...])
        sums.buffer[1:2] = column_sum(grad)
        unit = norm_back(grad, hat.buffer[...], scale.buffer[:, 0:1], small.buffer[GAIN_ONE : GAIN_ONE + 1])
        attend.buffer[...] = unit.astype(BF16)
        total[...] = unit
        sums.buffer[2:3] = column_sum(attend.buffer[...].astype(F32))
    move.finish()


def up_grad(layer, last, sec, branch, base, wd, wd_other, slope, low, wu, wu_other, shards, more=()):
    blocks, rows, width = slope.shape
    half = blocks // 2
    wide = (rows, width)
    part = sds((shards, width // shards, half * width), BF16)
    square = ((half, width, width), BF16)
    near = lambda *shapes: [(shape, NEAR) for shape in shapes]
    ins = [
        (branch, NEAR),
        (base, NEAR),
        (wd, RAW),
        (wd_other, RAW),
        (slope, RAW),
        (low, FAR),
        (wu, RAW),
        (wu_other, RAW),
    ]
    if last:
        hat, scale, small, sums = more
        ins += [(hat, FAR), (scale, FAR), (small, FAR), (sums, NEAR)]
        outs = near(sds(wide, F32), sds(wide, BF16), sds((8, width), F32), part)
    else:
        outs = near(sds(wide, F32), sds((8, width), F32), part)
    return call(
        functools.partial(up_grad_kernel, layer, last),
        sec,
        ins,
        outs,
        [square, square, ((half,) + wide, F32), (wide, BF16)],
        "up_grad_last" if last else "up_grad_first",
        3 * rows * width * width * blocks,
        15 << 20,
    )


def attend_grad_kernel(layer, last, sec, *refs):
    refs = list(refs)
    take = lambda count: [refs.pop(0) for _ in range(count)]
    attend, ctx, base, x, q_h, k_h, v_h, p_h, wo_a, wo_b, w_a, w_b, down, up = take(14)
    if last:
        gx, gx_low, out = take(3)
    else:
        total, turned, out = take(3)
    q, k, v, probs, wo, w, gc, grads, sems = refs
    move = Mover(sems)
    mine = sec[0] == layer
    rows_all, wide = q.shape
    width = 2 * wide
    seqs = probs.shape[0]
    shards = out.buffer.shape[0]
    tall = width // shards
    pairs = wide // 128
    side = sec[0] if last else 1 - sec[0]
    lanes_half = pl.ds(pl.multiple_of(side * wide, wide), wide)
    waits = attend.fetch(move) + [move.choose(mine, wo_a.ref.at[lanes_half], wo_b.ref.at[lanes_half], wo)]
    near = []
    for source, target in (
        (p_h.ref.at[:, pl.ds(side * pairs, pairs)], probs),
        (v_h.ref.at[:, lanes_half], v),
        (k_h.ref.at[:, lanes_half], k),
        (q_h.ref.at[:, lanes_half], q),
    ):
        move.load(source, target)
        near.append(move.last)
    later = x.fetch(move) + ctx.fetch(move) + down.fetch(move) + up.fetch(move)
    finals = base.fetch(move)
    for i in range(3):
        there = pl.ds(pl.multiple_of(i * width + side * wide, wide), wide)
        finals.append(move.choose(mine, w_a.ref.at[:, there], w_b.ref.at[:, there], w.at[:, pl.ds(i * wide, wide)]))
    ready(waits)
    gc[...] = dot_t(attend.buffer[...], wo[...]).astype(BF16)
    ready(near)
    halves = lane_halves()
    lower = lax.broadcasted_iota(jnp.int32, (128, 128), 1) < 64

    for pair in range(pairs):
        lanes = slice(pair * 128, pair * 128 + 128)
        for seq in range(seqs):
            rows = slice(seq * 128, seq * 128 + 128)

            def put(part, value):
                grads[rows, part * wide + pair * 128 : part * wide + pair * 128 + 128] = value.astype(BF16)

            grad = gc[rows, lanes]
            p = probs[seq, pair]
            full = dot(p.astype(BF16), grad)
            put(2, jnp.where(lower, full[:128], full[128:]))
            gp = dot_t(two_heads(v[rows, lanes], halves), grad)
            parts = []
            for part in (slice(0, 128), slice(128, 256)):
                g, pp = gp[part], p[part]
                parts.append(pp * (g - jnp.sum(g * pp, axis=0, keepdims=True)))
            gs = jnp.concatenate(parts, axis=0).astype(BF16)
            put(0, t_dot(gs, two_heads(k[rows, lanes] * SCALE, halves)))
            full = dot(gs, q[rows, lanes] * SCALE)
            put(1, jnp.where(lower, full[:128], full[128:]))
    ready(later)
    if last:
        turned = x
    else:
        turned.buffer[...] = x.buffer[...].T
    left = dot(turned.buffer[...], grads[...]).astype(BF16)
    right = dot(ctx.buffer[...], attend.buffer[:, lanes_half]).astype(BF16)
    little = jnp.concatenate([down.buffer[...], up.buffer[...]], axis=0).astype(BF16)
    zeros = jnp.zeros_like(little)
    b_q = column_sum(grads[:, 0:wide].astype(F32)).astype(BF16)
    b_v = column_sum(grads[:, 2 * wide :].astype(F32)).astype(BF16)
    pad = jnp.concatenate([b_q, b_v], axis=1)
    pad = jnp.concatenate([pad, jnp.zeros((15, width), BF16)], axis=0)
    for shard in range(shards):
        out.buffer[shard, :tall, 0 : 3 * wide] = left[shard * tall : shard * tall + tall]
        out.buffer[shard, :tall, 3 * wide :] = right[shard * tall : shard * tall + tall]
        out.buffer[shard, tall:, 0:width] = little
        out.buffer[shard, tall:, width:] = pad
    ready(finals)
    sum_all = base.buffer[...] + dot_t(grads[...], w[...])
    if last:
        gx.buffer[...] = sum_all
        gx.flush(move)
        gx_low.buffer[...] = sum_all.astype(BF16)
        gx_low.flush(move)
    else:
        total.buffer[...] = sum_all
    move.finish()


def attend_grad(layer, last, sec, attend, ctx, base, x, q, k, v, probs, wo, wo_other, w, w_other, down, up, shards, low_kind):
    rows, width = attend.shape
    seqs = probs.shape[0]
    wide = width // 2
    flat = (rows, width)
    part = (sds((shards, width // shards + 16, 2 * width), BF16), NEAR)
    if last:
        outs = [(sds(flat, F32), FAR), (sds(flat, BF16), low_kind), part]
    else:
        outs = [(sds(flat, F32), NEAR), (sds((width, rows), BF16), NEAR), part]
    half = ((rows, wide), BF16)
    return call(
        functools.partial(attend_grad_kernel, layer, last),
        sec,
        [(attend, NEAR), (ctx, FAR), (base, NEAR), (x, NEAR if last else FAR)]
        + [(item, RAW) for item in (q, k, v, probs, wo, wo_other, w, w_other)]
        + [(down, NEAR), (up, NEAR)],
        outs,
        [
            half,
            half,
            half,
            ((seqs, wide // 128) + probs.shape[2:], F32),
            ((wide, width), BF16),
            ((width, 3 * wide), BF16),
            half,
            ((rows, 3 * wide), BF16),
        ],
        "attend_grad_last" if last else "attend_grad_first",
        rows * width * width * 10,
        15 << 20,
    )


def up_whole_kernel(
    layer, sec, branch, second, wd_a, wd_b, slope, low, wu_a, wu_b, hat, scale, small,
    first, attend, sums, send, keep, wd, wu, pre, sems,
):
    move = Mover(sems)
    mine = sec[0] == layer
    blocks, wide, _ = wd.shape
    half = blocks // 2
    at = [lax.rem(i + half * (1 - sec[0]), blocks) for i in range(blocks)]
    span = [pl.ds(pl.multiple_of(place * wide, wide), wide) for place in at]
    parts = []
    early = branch.fetch(move)
    for i in range(blocks):
        parts.append(
            [move.choose(mine, wd_a.ref.at[span[i]], wd_b.ref.at[span[i]], wd.at[i])]
            + slope.fetch(move, at[i])
            + [move.choose(mine, wu_a.ref.at[:, span[i]], wu_b.ref.at[:, span[i]], wu.at[i])]
        )
        if i == 0:
            early += low.fetch(move)
    late = second.fetch(move) + hat.fetch(move) + scale.fetch(move) + small.fetch(move)
    ready(early)
    branch, low, total = branch.buffer, low.buffer, first.buffer
    for i in range(blocks):
        ready(parts[i])
        pre[...] = (dot_t(branch[...], wd[i]) * slope.buffer[at[i]]).astype(BF16)
        sums.buffer[pl.ds(3 + at[i], 1)] = column_sum(pre[...].astype(F32))
        out, place = (send, i) if i < half else (keep, i - half)
        block = dot(low[...], pre[...]).astype(BF16)
        shards, tall, _ = out.buffer.shape
        for shard in range(shards):
            out.buffer[shard, :, place * wide : place * wide + wide] = block[shard * tall : shard * tall + tall]
        if i == 0:
            ready(late)
            total[...] = second.buffer[...] + dot_t(pre[...], wu[i])
        else:
            total[...] += dot_t(pre[...], wu[i])
    grad = total[...]
    sums.buffer[0:1] = column_sum(grad * hat.buffer[...])
    sums.buffer[1:2] = column_sum(grad)
    unit = norm_back(grad, hat.buffer[...], scale.buffer[:, 0:1], small.buffer[GAIN_ONE : GAIN_ONE + 1])
    attend.buffer[...] = unit.astype(BF16)
    attend.flush(move)
    total[...] = unit
    first.flush(move)
    sums.buffer[2:3] = column_sum(attend.buffer[...].astype(F32))
    sums.buffer[3 + blocks :] = jnp.zeros_like(sums.buffer[3 + blocks :])
    sums.flush(move)
    move.finish()


def up_whole(layer, sec, branch, second, wd, wd_other, slope, low, wu, wu_other, hat, scale, small, shards):
    blocks, rows, width = slope.shape
    wide = (rows, width)
    part = sds((shards, width // shards, blocks * width // 2), BF16)
    square = ((blocks, width, width), BF16)
    return call(
        functools.partial(up_whole_kernel, layer),
        sec,
        [
            (branch, NEAR),
            (second, NEAR),
            (wd, RAW),
            (wd_other, RAW),
            (slope, FAR),
            (low, FAR),
            (wu, RAW),
            (wu_other, RAW),
            (hat, FAR),
            (scale, FAR),
            (small, FAR),
        ],
        [(sds(wide, F32), NEAR), (sds(wide, BF16), NEAR), (sds((8, width), F32), NEAR), (part, NEAR), (part, NEAR)],
        [square, square, (wide, BF16)],
        "up_grad",
        6 * rows * width * width * blocks,
        30 << 20,
    )


def attend_whole_kernel(
    layer, shards, sec, attend, ctx, first, x, q, k, v, probs, wo_a, wo_b, w_a, w_b, down, up,
    gx, gx_low, send, keep, turned, wo, w, gc, grads, sems,
):
    move = Mover(sems)
    mine = sec[0] == layer
    rows_all, width = x.buffer.shape
    seqs = probs.buffer.shape[0]
    wide = width // 2
    tall = width // shards
    pairs = wide // 128
    waits = attend.fetch(move) + [move.choose(mine, wo_a.ref, wo_b.ref, wo)]
    near = probs.fetch(move) + v.fetch(move) + k.fetch(move) + q.fetch(move)
    later = x.fetch(move) + ctx.fetch(move) + down.fetch(move) + up.fetch(move)
    last = [
        move.choose(mine, w_a.ref.at[:, pl.ds(i * width, width)], w_b.ref.at[:, pl.ds(i * width, width)], w.at[i])
        for i in range(3)
    ] + first.fetch(move)
    ready(waits)
    attend, q, k, v, probs = (item.buffer for item in (attend, q, k, v, probs))
    gc[...] = dot_t(attend[...], wo[...]).astype(BF16)
    ready(near)
    halves = lane_halves()
    lower = lax.broadcasted_iota(jnp.int32, (128, 128), 1) < 64

    def attention(first_pair):
        @pl.loop(0, pairs)
        def _(index):
            pair = first_pair + index
            lanes = pl.ds(pl.multiple_of(pair * 128, 128), 128)
            for seq in range(seqs):
                rows = slice(seq * 128, seq * 128 + 128)
                grad = gc[rows, lanes]
                p = probs[seq, pair]
                full = dot(p.astype(BF16), grad)
                grads[2, rows, lanes] = jnp.where(lower, full[:128], full[128:]).astype(BF16)
                gp = dot_t(two_heads(v[rows, lanes], halves), grad)
                parts = []
                for side in (slice(0, 128), slice(128, 256)):
                    g, pp = gp[side], p[side]
                    parts.append(pp * (g - jnp.sum(g * pp, axis=0, keepdims=True)))
                gs = jnp.concatenate(parts, axis=0).astype(BF16)
                grads[0, rows, lanes] = t_dot(gs, two_heads(k[rows, lanes] * SCALE, halves)).astype(BF16)
                full = dot(gs, q[rows, lanes] * SCALE)
                grads[1, rows, lanes] = jnp.where(lower, full[:128], full[128:]).astype(BF16)

    def products(half, out):
        lanes = pl.ds(pl.multiple_of(half * wide, wide), wide)
        for part in range(4):
            if part < 3:
                block = dot(turned[...], grads[part, :, lanes]).astype(BF16)
            else:
                block = dot(ctx.buffer[...], attend[:, lanes]).astype(BF16)
            for shard in range(shards):
                out.buffer[shard, :tall, part * wide : part * wide + wide] = block[shard * tall : shard * tall + tall]

    attention((1 - sec[0]) * pairs)
    ready(later)
    turned[...] = x.buffer[...].T
    products(1 - sec[0], send)
    attention(sec[0] * pairs)
    products(sec[0], keep)
    little = jnp.concatenate([down.buffer[...], up.buffer[...]], axis=0).astype(BF16)
    for half, out in ((1 - sec[0], send), (sec[0], keep)):
        lanes = pl.ds(pl.multiple_of(half * wide, wide), wide)
        pad = [column_sum(grads[part, :, lanes].astype(F32)).astype(BF16) for part in (0, 2)]
        pad = jnp.concatenate([jnp.concatenate(pad, axis=1), jnp.zeros((15, width), BF16)], axis=0)
        for shard in range(shards):
            out.buffer[shard, tall:, 0:width] = little
            out.buffer[shard, tall:, width:] = pad
    ready(last)
    total = first.buffer[...] + dot_t(grads[0], w[0]) + dot_t(grads[1], w[1]) + dot_t(grads[2], w[2])
    gx.buffer[...] = total
    gx.flush(move)
    gx_low.buffer[...] = total.astype(BF16)
    gx_low.flush(move)
    move.finish()


def attend_whole(layer, sec, attend, ctx, first, x, q, k, v, probs, wo, wo_other, w, w_other, down, up, shards, low_kind):
    rows, width = x.shape
    wide = (rows, width)
    part = sds((shards, width // shards + 16, 2 * width), BF16)
    return call(
        functools.partial(attend_whole_kernel, layer, shards),
        sec,
        [(attend, NEAR), (ctx, FAR), (first, NEAR)]
        + [(item, FAR) for item in (x, q, k, v, probs)]
        + [(wo, RAW), (wo_other, RAW), (w, RAW), (w_other, RAW), (down, NEAR), (up, NEAR)],
        [(sds(wide, F32), FAR), (sds(wide, BF16), low_kind), (part, NEAR), (part, NEAR)],
        [((width, rows), BF16), ((width, width), BF16), ((3, width, width), BF16), (wide, BF16), ((3,) + wide, BF16)],
        "attend_grad",
        2 * rows * width * width * 10,
        30 << 20,
    )


def layer_forward(layer, sec, x, front, big, other, small, far=None):
    w_qkv, w_out, w_up, w_down = big
    o_qkv, o_out, o_up, o_down = other
    x_kind = FAR if layer == 0 else NEAR
    q, k, v, probs, (ctx_near, ctx) = front
    (hat_near, hat_one), scale_one, low, act, slope = up_forward(
        layer, sec, x, x_kind, ctx_near, w_out, o_out, w_up, o_up, small
    )
    act_near, act = act if layer == 0 else (act, act)
    kinds = (BOTH, FAR) if layer == 0 else (FAR, NEAR)
    y, hat_two, scale_two = down_forward(layer, sec, act_near, w_down, o_down, hat_near, small, *kinds)
    x = x if far is None else far
    return y, (x, q, k, v, probs, ctx, hat_one, scale_one, low, act, slope, hat_two, scale_two)


class Backward:
    def __init__(self, line, layer, sec, cache, big, other, small, shards):
        self.line, self.layer, self.sec, self.small, self.shards = line, layer, sec, small, shards
        self.cache, self.weights, self.made = cache, tuple(zip(big, other)), {}

    def down(self, gy):
        act, _, hat_two, scale_two = self.cache[-4:]
        kinds = (NEAR, FAR) if self.layer == 0 else (FAR, NEAR)
        second, branch, sums, send, keep = down_grad(
            self.line.sec, gy, kinds[0], hat_two, scale_two, self.small, act, kinds[1]
        )
        self.made.update(second=second, branch=branch, down_sums=sums)
        self.line.add(send, keep)

    def up_inputs(self):
        (w_up, o_up), (w_down, o_down) = self.weights[2:]
        low, _, slope = self.cache[-5:-2]
        return w_down, o_down, slope, low, w_up, o_up, self.shards

    def up_first(self):
        made = self.made
        made["part"], made["up_sums"], send = up_grad(
            self.layer, False, self.line.sec, made["branch"], made["second"], *self.up_inputs()
        )
        self.up_chunk = self.line.add(send, None)

    def up_last(self):
        made = self.made
        hat_one, scale_one = self.cache[-7:-5]
        more = (hat_one, scale_one, self.small, made["up_sums"])
        made["first"], made["attend"], made["up_sums"], self.up_chunk.keep = up_grad(
            self.layer, True, self.line.sec, made["branch"], made["part"], *self.up_inputs(), more
        )

    def up(self):
        made = self.made
        hat_one, scale_one = self.cache[-7:-5]
        ins = self.up_inputs()
        made["first"], made["attend"], made["up_sums"], send, keep = up_whole(
            self.layer, self.line.sec, made["branch"], made["second"], *ins[:-1], hat_one, scale_one, self.small, ins[-1]
        )
        self.line.add(send, keep)

    def attention(self):
        made = self.made
        made["gx"], made["gx_low"], send, keep = attend_whole(
            self.layer, self.line.sec, made["attend"], self.cache[5], made["first"], self.cache[0], *self.heads()
        )
        self.line.add(send, keep)

    def heads(self):
        q, k, v, probs = self.cache[1:5]
        (w_qkv, o_qkv), (w_out, o_out) = self.weights[:2]
        low_kind = FAR if self.layer == 0 else BOTH
        sums = (self.made["down_sums"], self.made["up_sums"])
        return (q, k, v, probs, w_out, o_out, w_qkv, o_qkv) + sums + (self.shards, low_kind)

    def attend_first(self):
        made = self.made
        made["part"], made["turned"], send = attend_grad(
            self.layer, False, self.line.sec, made["attend"], self.cache[5], made["first"], self.cache[0], *self.heads()
        )
        self.attend_chunk = self.line.add(send, None)

    def attend_last(self):
        made = self.made
        made["gx"], made["gx_low"], self.attend_chunk.keep = attend_grad(
            self.layer, True, self.line.sec, made["attend"], self.cache[5], made["part"], made["turned"], *self.heads()
        )


def exchange(array, axis, bit):
    length = lax.axis_size(axis)
    return lax.ppermute(array, axis, [(i, i ^ bit) for i in range(length)])


def pick(array, index, axis):
    return lax.dynamic_index_in_dim(array, index, axis, keepdims=False)


def split_at(rows):
    return (rows // 2 + 15) // 16 * 16


class Sums:
    def __init__(self, columns):
        self.columns, self.ins, self.outs, self.code = columns, [], [], []
        self.rows = {}

    def use(self, array):
        for index, known in enumerate(self.ins):
            if known is array:
                return index
        self.ins.append(array)
        return len(self.ins) - 1

    def result(self, shape):
        self.outs.append(sds(tuple(shape) + (self.columns,), BF16))
        return len(self.outs) - 1

    def region(self, way, rows):
        first = self.rows.get(way, 0)
        self.rows[way] = first + rows
        return first

    def run(self, ids):
        ways = sorted(self.rows)
        shapes = self.outs + [sds((self.rows[way], self.columns), BF16) for way in ways]
        n_in, n_out = len(self.ins), len(self.outs)

        def kernel(ids_ref, *refs):
            sends = dict(zip(ways, refs[n_in + n_out :]))
            for code in self.code:
                code(ids_ref, refs[:n_in], refs[n_in : n_in + n_out], sends)

        vmem = pl.BlockSpec(memory_space=pltpu.VMEM)
        results = pl.pallas_call(
            kernel,
            in_specs=[pl.BlockSpec(memory_space=pltpu.SMEM)] + [vmem] * n_in,
            out_specs=[vmem] * len(shapes),
            out_shape=shapes,
            compiler_params=pltpu.CompilerParams(vmem_limit_bytes=VMEM),
            name="join_sums",
        )(ids, *self.ins)
        return results[:n_out], dict(zip(ways, results[n_out:]))


def at_rows(first, index, count):
    return pl.ds(pl.multiple_of(first + index * count, 16), count)


def sum_section(sums, chunk):
    kept, got = sums.use(chunk.keep), sums.use(chunk.got["section"])
    _, rows, _ = chunk.keep.shape
    cut = chunk.cut
    rest = rows - cut
    top, bottom = sums.result((2, cut)), sums.result((2, rest))
    chunk.first = {"x": sums.region("x", 2 * cut), "y": sums.region("y", 2 * rest)}
    to_x, to_y = chunk.first["x"], chunk.first["y"]

    def code(ids, ins, outs, sends):
        low, high = ids[1], ids[2]
        for i in range(2):
            add = lambda shard, lines: ins[kept][shard, lines] + ins[got][shard, lines]
            sends["x"][to_x + i * cut : to_x + i * cut + cut] = add(2 * i + 1 - low, slice(0, cut))
            outs[top][i] = add(2 * i + low, slice(0, cut))
            sends["y"][to_y + i * rest : to_y + i * rest + rest] = add(2 * (1 - high) + i, slice(cut, rows))
            outs[bottom][i] = add(2 * high + i, slice(cut, rows))

    sums.code.append(code)
    return [top, bottom]


def sum_first(sums, chunk):
    top, bottom = (sums.use(item) for item in chunk.kept)
    got_x, got_y = sums.use(chunk.got["x"]), sums.use(chunk.got["y"])
    at_x, at_y = chunk.first["x"], chunk.first["y"]
    cut, rest = chunk.kept[0].shape[1], chunk.kept[1].shape[1]
    new_top, new_bottom = sums.result((cut,)), sums.result((rest,))
    chunk.first = {"y": sums.region("y", cut), "x": sums.region("x", rest)}
    to_x, to_y = chunk.first["x"], chunk.first["y"]

    def code(ids, ins, outs, sends):
        low, high = ids[1], ids[2]
        upper = lambda i: ins[top][i] + ins[got_x][at_rows(at_x, i, cut)]
        lower = lambda i: ins[bottom][i] + ins[got_y][at_rows(at_y, i, rest)]
        sends["y"][to_y : to_y + cut] = upper(1 - high)
        outs[new_top][...] = upper(high)
        sends["x"][to_x : to_x + rest] = lower(1 - low)
        outs[new_bottom][...] = lower(low)

    sums.code.append(code)
    return [new_top, new_bottom]


def sum_second(sums, chunk):
    top, bottom = (sums.use(item) for item in chunk.kept)
    got_x, got_y = sums.use(chunk.got["x"]), sums.use(chunk.got["y"])
    at_x, at_y = chunk.first["x"], chunk.first["y"]
    cut, rest = chunk.kept[0].shape[0], chunk.kept[1].shape[0]
    part = sums.result((cut + rest,))
    onward = chunk.line.short
    if onward:
        sums.rows["ends"] = max(sums.rows.get("ends", 0), cut + rest)

    def code(ids, ins, outs, sends):
        outs[part][:cut] = ins[top][...] + ins[got_y][at_y : at_y + cut]
        outs[part][cut:] = ins[bottom][...] + ins[got_x][at_x : at_x + rest]
        if onward:

            @pl.when(ids[3] == 1)
            def _():
                sends["ends"][: cut + rest] = outs[part][...]

    sums.code.append(code)
    return [part]


def sum_ends(sums, chunk):
    part, got = sums.use(chunk.kept[0]), sums.use(chunk.got["ends"])
    rows = chunk.kept[0].shape[0]
    chunk.first = {"middle": sums.region("middle", rows)}
    to = chunk.first["middle"]

    def code(ids, ins, outs, sends):
        sends["middle"][to : to + rows] = ins[part][...] + ins[got][:rows]

    sums.code.append(code)
    return []


def sum_middle(sums, chunk):
    sent, got = sums.use(chunk.sent["middle"]), sums.use(chunk.got["middle"])
    at, rows = chunk.first["middle"], chunk.rows
    whole = sums.result((rows,))
    sums.rows["ends"] = max(sums.rows.get("ends", 0), rows)

    def code(ids, ins, outs, sends):
        outs[whole][...] = ins[sent][at : at + rows] + ins[got][at : at + rows]

        @pl.when(ids[3] == 0)
        def _():
            sends["ends"][:rows] = outs[whole][...]

    sums.code.append(code)
    return [whole]


def sum_last(sums, chunk):
    whole, got = sums.use(chunk.kept[0]), sums.use(chunk.got["ends"])
    rows = chunk.rows
    result = sums.result((rows,))

    def code(ids, ins, outs, sends):
        @pl.when(ids[3] == 1)
        def _():
            outs[result][...] = ins[got][:rows]

        @pl.when(ids[3] == 0)
        def _():
            outs[result][...] = ins[whole][...]

    sums.code.append(code)
    return [result]


class Chunk:
    def __init__(self, line, send, keep):
        self.line, self.send, self.keep = line, send, keep
        self.at, self.kept, self.got, self.sent, self.done = 0, [], {}, {}, None
        self.rows = send.shape[1]
        self.cut = split_at(self.rows)


class Line:
    def __init__(self, sec):
        self.sec = sec
        self.square = lax.axis_size("inner") == 4
        self.short = lax.axis_size("outer") == 4
        spot, place = lax.axis_index("inner"), lax.axis_index("outer")
        outside = (place == 0) | (place == lax.axis_size("outer") - 1)
        self.ids = jnp.stack([lax.axis_index("section"), spot % 2, spot // 2, outside]).astype(jnp.int32)
        self.chunks, self.made = [], {}
        self.sums = (sum_section, sum_first, sum_second, sum_ends, sum_middle, sum_last)

    def add(self, send, keep):
        chunk = Chunk(self, send, keep)
        self.chunks.append(chunk)
        return chunk

    def move(self, way, array):
        if way == "section":
            return exchange(array, "section", 1)
        if way in ("x", "y"):
            return exchange(array, "inner", 1 if way == "x" else 2)
        return lax.ppermute(array, "outer", [(0, 1), (1, 0), (2, 3), (3, 2)] if way == "ends" else [(1, 2), (2, 1)])

    def advance(self, owner, *works):
        moving = [chunk for chunk in self.chunks if chunk.done is None and chunk.at > 0]
        sends = {}
        if moving and self.square:
            sums = Sums(moving[0].send.shape[-1])
            places = [self.sums[chunk.at - 1](sums, chunk) for chunk in moving]
            outs, sends = sums.run(self.ids)
            for chunk, place in zip(moving, places):
                chunk.kept, chunk.sent = [outs[index] for index in place], sends
        for chunk in moving:
            chunk.at += 1
            if not self.square:
                half = chunk.keep.astype(F32) + chunk.got["section"].astype(F32)
                half = lax.psum_scatter(half.astype(BF16), "inner", scatter_dimension=0, tiled=False)
                chunk.done = lax.psum(half, "outer")
            elif chunk.at == 4 and not self.short:
                chunk.done = lax.psum(chunk.kept[0], "outer")
            elif chunk.at == 7:
                chunk.done = chunk.kept[0]
        new = [chunk for chunk in self.chunks if chunk.at == 0]
        gots = {way: self.move(way, array) for way, array in sends.items()}
        arrived = [self.move("section", chunk.send) for chunk in new]
        for work in works:
            work()
        fresh = [chunk for chunk in self.chunks if chunk not in new and chunk.at == 0]
        late = [chunk for chunk in self.chunks if chunk.keep is not None and chunk.at == 0]
        owner.made, parts, keeps, gots, arrived = lax.optimization_barrier(
            (owner.made, [chunk.send for chunk in fresh], [chunk.keep for chunk in late], gots, arrived)
        )
        for chunk, part in zip(fresh, parts):
            chunk.send = part
        for chunk, part in zip(late, keeps):
            chunk.keep = part
        for chunk in moving:
            chunk.got = gots
        for chunk, part in zip(new, arrived):
            chunk.at, chunk.got = 1, {"section": part}

    def finish(self):
        while any(chunk.done is None for chunk in self.chunks):
            self.advance(self)
        return [chunk.done for chunk in self.chunks]


def local(
    hidden_in, caption_len, region_len, cotangent, w_qkv, b_qv, w_out, b_out, ln_gain, ln_bias, w_up, b_up, w_down, b_down
):
    section = lax.axis_index("section")
    shards = lax.axis_size("inner")
    sec = section.astype(jnp.int32)[None]
    seqs_local, length, width = hidden_in.shape
    seqs = seqs_local // 2
    rows = seqs * length
    positions = jnp.arange(length, dtype=jnp.int32)[None, :]
    mine = lambda array: lax.dynamic_slice_in_dim(array, section * seqs, seqs, 0)
    caption, region = mine(caption_len)[:, None], mine(region_len)[:, None]
    valid = (positions < caption) | (positions >= CAP) & (positions < CAP + region)
    mask = jnp.concatenate([valid, valid], axis=1).astype(F32).T
    x = mine(hidden_in).reshape(rows, width)
    gy = jnp.where(valid[:, :, None], mine(cotangent), jnp.zeros((), BF16)).reshape(rows, width)

    blocks = w_up.shape[2] // width
    little = jnp.concatenate(
        [b_qv[0], b_out, ln_gain[0], ln_bias[0], b_down, b_up.reshape(blocks, width), jnp.zeros((8 - blocks, width), F32)]
    )
    little_other = exchange(little, "section", 1)
    big = (w_qkv[0], w_out[0], w_up[0], w_down[0])
    o_qkv = exchange(big[0], "section", 1)

    smalls = [jnp.where(section == layer, little, little_other) for layer in (0, 1)]
    o_qkv, smalls, mask, x, late_out, late_up = lax.optimization_barrier(
        (o_qkv, smalls, mask, x, big[1], big[2])
    )
    o_out, o_up = exchange(late_out, "section", 1), exchange(late_up, "section", 1)
    front = attend_forward(0, sec, x, FAR, big[0], o_qkv, smalls[0], mask)
    front, o_out, o_up, late_down = lax.optimization_barrier((front, o_out, o_up, big[3]))
    other = (o_qkv, o_out, o_up, exchange(late_down, "section", 1))
    y_one, cache_one = layer_forward(0, sec, x, front, big, other, smalls[0])
    y_near, y_one = y_one
    front = attend_forward(1, sec, y_near, NEAR, big[0], o_qkv, smalls[1], mask)
    y_two, cache_two = layer_forward(1, sec, y_near, front, big, other, smalls[1], y_one)
    line = Line(sec)
    two = Backward(line, 1, sec, cache_two, big, other, smalls[1], shards)
    one = Backward(line, 0, sec, cache_one, big, other, smalls[0], shards)
    line.advance(two, lambda: two.down(gy))
    line.advance(two, two.up_first)
    line.advance(two, two.up_last)
    line.advance(two, two.attention)
    gx_two_near, gx_two_low = two.made["gx_low"]
    line.advance(one, lambda: one.down(gx_two_near))
    line.advance(one, one.up)
    line.advance(one, one.attention)
    gx_one = one.made["gx"]

    def gather(for_zero, for_one):
        kept = jnp.where(section == 0, for_zero, for_one)
        got = exchange(jnp.where(section == 0, for_one, for_zero), "section", 1)
        return jnp.where(section == 0, kept, got), jnp.where(section == 0, got, kept)

    activations = jnp.concatenate(gather(y_one, y_two), axis=0).reshape(seqs_local, length, width)
    input_grads = jnp.concatenate(gather(gx_one, gx_two_low.astype(F32)), axis=0).reshape(
        seqs_local, length, width
    )
    sums = line.finish()
    down, up, attend = [gather(one, two) for one, two in zip(sums[3:], sums[:3])]
    g_w_down = jnp.concatenate(
        [side[:, i * width : (i + 1) * width] for side in down for i in range(2)], axis=0
    ).T.astype(F32)
    g_w_up = jnp.concatenate(up, axis=1).astype(F32)
    part = width // 2
    tall = width // shards
    matrix = [side[:tall] for side in attend]
    g_w_qkv = jnp.concatenate(
        [side[:, i * part : (i + 1) * part] for i in range(3) for side in matrix], axis=1
    ).astype(F32)
    g_w_out = jnp.concatenate([side[:, 3 * part :] for side in matrix], axis=1).astype(F32)
    rows = attend[0][tall:, :width]
    b_q, b_v = [
        jnp.concatenate([side[tall, width + i * part : width + (i + 1) * part] for side in attend]) for i in range(2)
    ]
    rows = jnp.concatenate([rows, b_q[None], b_v[None]], axis=0)
    place = lax.axis_index("inner")
    mine = lax.dynamic_slice_in_dim(rows, place * tall, tall, 1).astype(F32)
    up_row = pick(rows[11 : 11 + blocks].reshape(shards, width * blocks // shards), place, 0).astype(F32)
    return (
        activations[None],
        input_grads[None],
        g_w_qkv[None],
        mine[16:18][None],
        g_w_out[None],
        mine[10][None],
        jnp.stack([mine[8], mine[0]])[None],
        jnp.stack([mine[9], mine[1]])[None],
        g_w_up[None],
        up_row[None],
        g_w_down[None],
        mine[2][None],
    )


def solution(mesh):
    rows = ("inner", "outer")
    return jax.shard_map(
        local,
        mesh=mesh,
        in_specs=(
            P(rows, None, None),
            P(rows),
            P(rows),
            P(rows, None, None),
            P("section", None, None),
            P("section", None, None),
            P("section", None, None),
            P("section", None),
            P("section", None, None),
            P("section", None, None),
            P("section", None, None),
            P("section", None),
            P("section", None, None),
            P("section", None),
        ),
        out_specs=(
            P("section", rows, None, None),
            P("section", rows, None, None),
            P("section", "inner", None),
            P("section", None, "inner"),
            P("section", "inner", None),
            P("section", "inner"),
            P("section", None, "inner"),
            P("section", None, "inner"),
            P("section", "inner", None),
            P("section", "inner"),
            P("section", "inner", None),
            P("section", "inner"),
        ),
        check_vma=False,
    )
```

```python
import functools
import math

import jax
import jax.numpy as jnp
from jax import lax
from jax.experimental import pallas as pl
from jax.experimental.pallas import tpu as pltpu
from jax.sharding import PartitionSpec as P

HEADS = 12
CAP = 28
EPS = 1e-12
SCALE = 0.125
SPARE = 8 * 1024 * 1024
F32 = jnp.float32
BF16 = jnp.bfloat16
B_Q, B_V, B_OUT, GAIN_ONE, GAIN_TWO, OFFSET_ONE, OFFSET_TWO, B_DOWN, B_UP = range(9)


def dot(left, right):
    return jnp.dot(left, right, preferred_element_type=F32)


def dot_t(left, right):
    return lax.dot_general(left, right, (((1,), (1,)), ((), ())), preferred_element_type=F32)


def t_dot(left, right):
    return lax.dot_general(left, right, (((0,), (0,)), ((), ())), preferred_element_type=F32)


def column_sum(values):
    return jnp.sum(values, axis=0, keepdims=True)


def standardize(summed):
    centre = jnp.mean(summed, axis=-1, keepdims=True)
    shifted = summed - centre
    spread = jnp.mean(shifted * shifted, axis=-1, keepdims=True)
    scale = lax.rsqrt(spread + EPS)
    return shifted * scale, scale


def norm_back(grad, hat, scale, gain):
    scaled = grad * gain
    return scale * (
        scaled
        - jnp.mean(scaled, axis=-1, keepdims=True)
        - hat * jnp.mean(scaled * hat, axis=-1, keepdims=True)
    )


def gauss_share(value):
    bell = jnp.exp2(value * value * -0.7213475204444817)
    part = 1.0 / (1.0 + 0.2316418882 * jnp.abs(value))
    tail = 0.5307027145
    for item in (-0.7265760135, 0.7107068705, -0.142248368, 0.127414796):
        tail = tail * part + item
    tail = tail * part * bell
    return jnp.where(value < 0.0, tail, 1.0 - tail), bell


def lane_halves():
    lane = lax.broadcasted_iota(jnp.int32, (1, 128), 1)
    lower = jnp.where(lane < 64, 1.0, 0.0)
    return lower.astype(BF16), (1.0 - lower).astype(BF16)


def two_heads(block, halves):
    return jnp.concatenate([block * halves[0], block * halves[1]], axis=0)


def sds(shape, dtype):
    return jax.ShapeDtypeStruct(shape, dtype)


class Mover:
    def __init__(self, sems):
        self.sems, self.used, self.outs = sems, 0, []

    def copy(self, source, target):
        self.used += 1
        return pltpu.make_async_copy(source, target, self.sems.at[self.used - 1])

    def load(self, source, target):
        self.last = self.copy(source, target)
        self.last.start()

    def choose(self, first, one, two, target):
        copy = self.copy(one, target)
        other = pltpu.make_async_copy(two, target, self.sems.at[self.used - 1])
        pl.when(first)(copy.start)
        pl.when(jnp.logical_not(first))(other.start)
        return copy

    def store(self, source, target):
        copy = self.copy(source, target)
        copy.start()
        self.outs.append(copy)

    def finish(self):
        for copy in self.outs:
            copy.wait()


class Operand:
    def __init__(self, ref, buffer, far):
        self.ref, self.buffer, self.far = ref, buffer, far

    def fetch(self, move, *index):
        if self.far:
            move.load(*(ref.at[index] if index else ref for ref in (self.ref, self.buffer)))
            return [move.last]
        return []

    def flush(self, move, *index):
        if self.far:
            move.store(*(ref.at[index] if index else ref for ref in (self.buffer, self.ref)))


NEAR, FAR, RAW, BOTH, FREE = "near", "far", "raw", "both", "free"


def ready(waits):
    for item in waits:
        item.wait()


def call(kernel, ids, ins, outs, scratch, name, flops, nbytes):
    space = lambda kind: {NEAR: pltpu.VMEM, FREE: pl.ANY}.get(kind, pltpu.HBM)
    spread = [(shape, part) for shape, kind in outs for part in ((NEAR, RAW) if kind == BOTH else (kind,))]
    kinds = [kind for _, kind in ins] + [kind for _, kind in spread]
    shapes = [array for array, _ in ins] + [shape for shape, _ in spread]
    buffers = [pltpu.VMEM(shape.shape, shape.dtype) for shape, kind in zip(shapes, kinds) if kind == FAR]

    def body(ids_ref, *refs):
        count = len(kinds)
        spare = list(refs[count : count + len(buffers)])
        left = list(refs[:count])
        operands = []
        for _, kind in list(ins) + list(outs):
            ref = left.pop(0)
            if kind == BOTH:
                operands.append(Operand(left.pop(0), ref, True))
            else:
                operands.append(Operand(ref, spare.pop(0) if kind == FAR else ref, kind == FAR))
        kernel(ids_ref, *operands, *refs[count + len(buffers) :])

    size = lambda shape, dtype: math.prod(shape) * jnp.dtype(dtype).itemsize
    limit = SPARE + sum(size(*item) for item in scratch)
    limit += sum(size(shape.shape, shape.dtype) for shape, kind in zip(shapes, kinds) if kind == FAR)
    results = pl.pallas_call(
        body,
        in_specs=[pl.BlockSpec(memory_space=pltpu.SMEM)]
        + [pl.BlockSpec(memory_space=space(kind)) for _, kind in ins],
        out_specs=[pl.BlockSpec(memory_space=space(kind)) for _, kind in spread],
        out_shape=[space(kind)(shape.shape, shape.dtype) for shape, kind in spread],
        scratch_shapes=buffers + [pltpu.VMEM(*item) for item in scratch] + [pltpu.SemaphoreType.DMA((64,))],
        compiler_params=pltpu.CompilerParams(vmem_limit_bytes=limit),
        cost_estimate=pl.CostEstimate(flops=flops, bytes_accessed=nbytes, transcendentals=0),
        name=name,
    )(ids, *(pltpu.with_memory_space_constraint(array, space(kind)) for array, kind in ins))
    results = list(results)
    return [(results.pop(0), results.pop(0)) if kind == BOTH else results.pop(0) for _, kind in outs]


def attend_phase(q, k, v, probs, ctx, mask, pairs):
    seqs = mask.shape[1]
    halves = lane_halves()
    feature = lax.broadcasted_iota(jnp.int32, (128, 128), 0)
    first_half = jnp.where(feature < 64, 1.0, 0.0).astype(BF16)
    second_half = jnp.where(feature < 64, 0.0, 1.0).astype(BF16)

    for seq in range(seqs):
        rows = slice(seq * 128, seq * 128 + 128)
        seen = jnp.broadcast_to(mask[:, seq : seq + 1], (256, 128)) > 0.5
        for pair in range(*pairs):
            lanes = slice(pair * 128, pair * 128 + 128)
            scores = dot_t(two_heads(k[rows, lanes], halves), q[rows, lanes] * SCALE)
            scores = jnp.where(seen, scores, -1e30)
            parts = []
            for part in (scores[:128], scores[128:]):
                e = jnp.exp(part - jnp.max(part, axis=0, keepdims=True))
                parts.append(e * (1.0 / jnp.sum(e, axis=0, keepdims=True)))
            parts = jnp.concatenate(parts, axis=0)
            probs[seq, pair] = parts
            turned = v[rows, lanes].T
            turned = jnp.concatenate([turned * first_half, turned * second_half], axis=1)
            ctx[lanes, rows] = dot(turned, parts.astype(BF16)).astype(BF16)


def attend_kernel(layer, sec, x, w_a, w_b, small, mask, q, k, v, probs, ctx, w, sems):
    move = Mover(sems)
    mine = sec[0] == layer
    rows, width = x.buffer.shape
    waits = x.fetch(move) + small.fetch(move) + mask.fetch(move)
    parts = [
        move.choose(mine, w_a.ref.at[:, pl.ds(i * width, width)], w_b.ref.at[:, pl.ds(i * width, width)], w.at[i])
        for i in (1, 0, 2)
    ]
    ready(waits)
    x, small = x.buffer, small.buffer
    parts[0].wait()
    k.buffer[...] = dot(x[...], w[1]).astype(BF16)
    k.flush(move)
    parts[1].wait()
    q.buffer[...] = (dot(x[...], w[0]) + small[B_Q : B_Q + 1]).astype(BF16)
    q.flush(move)
    parts[2].wait()
    v.buffer[...] = (dot(x[...], w[2]) + small[B_V : B_V + 1]).astype(BF16)
    v.flush(move)
    half = width // 128 // 2
    for i in range(2):
        attend_phase(
            q.buffer, k.buffer, v.buffer, probs.buffer, ctx.buffer, mask.buffer, (i * half, i * half + half)
        )
        probs.flush(move, slice(None), pl.ds(i * half, half))
    ctx.flush(move)
    move.finish()


def attend_forward(layer, sec, x, x_kind, w_own, w_other, small, mask):
    rows, width = x.shape
    seqs = mask.shape[1]
    pairs = width // 128
    wide = sds((rows, width), BF16)
    return call(
        functools.partial(attend_kernel, layer),
        sec,
        [(x, x_kind), (w_own, RAW), (w_other, RAW), (small, FAR), (mask, FAR)],
        [(wide, FAR)] * 3 + [(sds((seqs, pairs, 256, 128), F32), FAR), (sds((width, rows), BF16), BOTH)],
        [((3, width, width), BF16)],
        "attend_forward",
        2 * rows * width * width * 4,
        12 << 20,
    )


def up_kernel(layer, sec, x, ctx, wo_a, wo_b, wu_a, wu_b, small, hat, scale, turned, act, slope, wo, wu, low, sems):
    move = Mover(sems)
    mine = sec[0] == layer
    blocks, _, wide = wu.shape
    waits = ctx.fetch(move) + [move.choose(mine, wo_a.ref, wo_b.ref, wo)] + small.fetch(move) + x.fetch(move)
    span = lambda i: pl.ds(i * wide, wide)
    parts = [move.choose(mine, wu_a.ref.at[:, span(i)], wu_b.ref.at[:, span(i)], wu.at[i]) for i in range(blocks)]
    ready(waits)
    small = small.buffer
    summed = x.buffer[...].astype(F32) + t_dot(ctx.buffer[...], wo[...]) + small[B_OUT : B_OUT + 1]
    unit, root = standardize(summed)
    hat.buffer[...] = unit
    hat.flush(move)
    scale.buffer[...] = jnp.broadcast_to(root, scale.buffer.shape)
    scale.flush(move)
    low[...] = (unit * small[GAIN_ONE : GAIN_ONE + 1] + small[OFFSET_ONE : OFFSET_ONE + 1]).astype(BF16)
    turned.buffer[...] = low[...].T
    turned.flush(move)
    for i in range(blocks):
        parts[i].wait()
        pre = dot(low[...], wu[i]) + small[B_UP + i : B_UP + i + 1]
        share, bell = gauss_share(pre)
        act.buffer[i] = (pre * share).astype(BF16)
        slope.buffer[i] = share + pre * 0.3989422804014327 * bell
        act.flush(move, i)
        slope.flush(move, i)
    move.finish()


def up_forward(layer, sec, x, x_kind, ctx, wo, wo_other, wu, wu_other, small):
    rows, width = x.shape
    blocks = wu.shape[1] // width
    wide = (rows, width)
    other_kind = FREE if layer == 0 else RAW
    return call(
        functools.partial(up_kernel, layer),
        sec,
        [(x, x_kind), (ctx, NEAR), (wo, RAW), (wo_other, other_kind), (wu, RAW), (wu_other, other_kind), (small, FAR)],
        [
            (sds(wide, F32), BOTH),
            (sds((rows, 128), F32), FAR),
            (sds((width, rows), BF16), FAR),
            (sds((blocks,) + wide, BF16), BOTH if layer == 0 else NEAR),
            (sds((blocks,) + wide, F32), FAR),
        ],
        [((width, width), BF16), ((blocks, width, width), BF16), (wide, BF16)],
        "up_forward",
        2 * rows * width * width * (blocks + 1),
        20 << 20,
    )


def down_kernel(layer, sec, act, wd_a, wd_b, hat, small, y, two, scale, wd, total, sems):
    move = Mover(sems)
    mine = sec[0] == layer
    blocks, wide, _ = wd.shape
    parts = []
    for i in range(blocks):
        span = pl.ds(i * wide, wide)
        parts.append(act.fetch(move, i) + [move.choose(mine, wd_a.ref.at[span], wd_b.ref.at[span], wd.at[i])])
        if i == 0:
            waits = small.fetch(move) + hat.fetch(move)
    for i in range(blocks):
        ready(parts[i])
        product = dot(act.buffer[i], wd[i])
        total[...] = product if i == 0 else total[...] + product
    ready(waits)
    small = small.buffer
    normed = hat.buffer[...] * small[GAIN_ONE : GAIN_ONE + 1] + small[OFFSET_ONE : OFFSET_ONE + 1]
    unit, root = standardize(total[...] + normed + small[B_DOWN : B_DOWN + 1])
    y.buffer[...] = (unit * small[GAIN_TWO : GAIN_TWO + 1] + small[OFFSET_TWO : OFFSET_TWO + 1]).astype(BF16)
    y.flush(move)
    two.buffer[...] = unit
    two.flush(move)
    scale.buffer[...] = jnp.broadcast_to(root, scale.buffer.shape)
    scale.flush(move)
    move.finish()


def down_forward(layer, sec, act, wd, wd_other, hat, small, y_kind, two_kind):
    blocks, rows, width = act.shape
    wide = (rows, width)
    return call(
        functools.partial(down_kernel, layer),
        sec,
        [(act, NEAR), (wd, RAW), (wd_other, FREE if layer == 0 else RAW), (hat, NEAR), (small, FAR)],
        [(sds(wide, BF16), y_kind), (sds(wide, F32), two_kind), (sds((rows, 128), F32), two_kind)],
        [((blocks, width, width), BF16), (wide, F32)],
        "down_forward",
        2 * rows * width * width * blocks,
        12 << 20,
    )


def down_grad_kernel(sec, gy, hat, scale, small, act, second, branch, sums, send, keep, turned, sems):
    move = Mover(sems)
    blocks = act.buffer.shape[0]
    low_rows, wide = send.buffer.shape[1], act.buffer.shape[2]
    tall = 2 * low_rows
    waits = gy.fetch(move) + small.fetch(move) + scale.fetch(move) + hat.fetch(move)
    parts = [act.fetch(move, i) for i in range(blocks)]
    ready(waits)
    grad = gy.buffer[...].astype(F32)
    sums.buffer[0:1] = column_sum(grad * hat.buffer[...])
    sums.buffer[1:2] = column_sum(grad)
    unit = norm_back(grad, hat.buffer[...], scale.buffer[:, 0:1], small.buffer[GAIN_TWO : GAIN_TWO + 1])
    second.buffer[...] = unit
    second.flush(move)
    low = unit.astype(BF16)
    branch.buffer[...] = low
    branch.flush(move)
    sums.buffer[2:3] = column_sum(low.astype(F32))
    sums.buffer[3:] = jnp.zeros_like(sums.buffer[3:])
    sums.flush(move)
    turned[...] = branch.buffer[...].T
    for half, out in ((1 - sec[0], send), (sec[0], keep)):
        left = pl.ds(pl.multiple_of(half * tall, tall), tall)
        for i in range(blocks):
            if out is send:
                ready(parts[i])
            block = dot(turned[left, :], act.buffer[i]).astype(BF16)
            out.buffer[i, :, :wide] = block[:low_rows]
            out.buffer[i, :, wide:] = block[low_rows:]
    move.finish()


def down_grad(sec, gy, gy_kind, hat, scale, small, act, kind):
    rows, width = gy.shape
    blocks = act.shape[0]
    wide = (rows, width)
    part = sds((blocks, width // 4, 2 * width), BF16)
    return call(
        down_grad_kernel,
        sec,
        [(gy, gy_kind), (hat, kind), (scale, kind), (small, FAR), (act, kind)],
        [(sds(wide, F32), NEAR), (sds(wide, BF16), NEAR), (sds((8, width), F32), NEAR), (part, NEAR), (part, NEAR)],
        [((width, rows), BF16)],
        "down_grad",
        2 * rows * width * width * blocks,
        14 << 20,
    )


def up_grad_kernel(layer, last, sec, *refs):
    refs = list(refs)
    take = lambda count: [refs.pop(0) for _ in range(count)]
    branch, base, wd_a, wd_b, slope_h, low, wu_a, wu_b = take(8)
    if last:
        hat, scale, small, sums_in = take(4)
        first, attend, sums, out = take(4)
    else:
        first, sums, out = take(3)
    wd, wu, slope, pre, sems = refs
    move = Mover(sems)
    mine = sec[0] == layer
    half, wide, _ = wd.shape
    side = sec[0] if last else 1 - sec[0]
    at = [side * half + i for i in range(half)]
    span = [pl.ds(pl.multiple_of(place * wide, wide), wide) for place in at]
    parts = []
    early = branch.fetch(move)
    for i in range(half):
        move.load(slope_h.ref.at[at[i]], slope.at[i])
        parts.append(
            [
                move.last,
                move.choose(mine, wd_a.ref.at[span[i]], wd_b.ref.at[span[i]], wd.at[i]),
                move.choose(mine, wu_a.ref.at[:, span[i]], wu_b.ref.at[:, span[i]], wu.at[i]),
            ]
        )
        if i == 0:
            early += low.fetch(move)
    late = base.fetch(move)
    if last:
        late += hat.fetch(move) + scale.fetch(move) + small.fetch(move)
        sums.buffer[...] = sums_in.buffer[...]
    else:
        sums.buffer[...] = jnp.zeros_like(sums.buffer)
    ready(early)
    total = first.buffer
    shards, tall, _ = out.buffer.shape
    for i in range(half):
        ready(parts[i])
        pre[...] = (dot_t(branch.buffer[...], wd[i]) * slope[i]).astype(BF16)
        sums.buffer[pl.ds(3 + at[i], 1)] = column_sum(pre[...].astype(F32))
        block = dot(low.buffer[...], pre[...]).astype(BF16)
        for shard in range(shards):
            out.buffer[shard, :, i * wide : i * wide + wide] = block[shard * tall : shard * tall + tall]
        if i == 0:
            ready(late)
            total[...] = base.buffer[...] + dot_t(pre[...], wu[i])
        else:
            total[...] += dot_t(pre[...], wu[i])
    if last:
        grad = total[...]
        sums.buffer[0:1] = column_sum(grad * hat.buffer[...])
        sums.buffer[1:2] = column_sum(grad)
        unit = norm_back(grad, hat.buffer[...], scale.buffer[:, 0:1], small.buffer[GAIN_ONE : GAIN_ONE + 1])
        attend.buffer[...] = unit.astype(BF16)
        total[...] = unit
        sums.buffer[2:3] = column_sum(attend.buffer[...].astype(F32))
    move.finish()


def up_grad(layer, last, sec, branch, base, wd, wd_other, slope, low, wu, wu_other, shards, more=()):
    blocks, rows, width = slope.shape
    half = blocks // 2
    wide = (rows, width)
    part = sds((shards, width // shards, half * width), BF16)
    square = ((half, width, width), BF16)
    near = lambda *shapes: [(shape, NEAR) for shape in shapes]
    ins = [
        (branch, NEAR),
        (base, NEAR),
        (wd, RAW),
        (wd_other, RAW),
        (slope, RAW),
        (low, FAR),
        (wu, RAW),
        (wu_other, RAW),
    ]
    if last:
        hat, scale, small, sums = more
        ins += [(hat, FAR), (scale, FAR), (small, FAR), (sums, NEAR)]
        outs = near(sds(wide, F32), sds(wide, BF16), sds((8, width), F32), part)
    else:
        outs = near(sds(wide, F32), sds((8, width), F32), part)
    return call(
        functools.partial(up_grad_kernel, layer, last),
        sec,
        ins,
        outs,
        [square, square, ((half,) + wide, F32), (wide, BF16)],
        "up_grad_last" if last else "up_grad_first",
        3 * rows * width * width * blocks,
        15 << 20,
    )


def attend_grad_kernel(layer, last, sec, *refs):
    refs = list(refs)
    take = lambda count: [refs.pop(0) for _ in range(count)]
    attend, ctx, base, x, q_h, k_h, v_h, p_h, wo_a, wo_b, w_a, w_b, down, up = take(14)
    if last:
        gx, gx_low, out = take(3)
    else:
        total, turned, out = take(3)
    q, k, v, probs, wo, w, gc, grads, sems = refs
    move = Mover(sems)
    mine = sec[0] == layer
    rows_all, wide = q.shape
    width = 2 * wide
    seqs = probs.shape[0]
    shards = out.buffer.shape[0]
    tall = width // shards
    pairs = wide // 128
    side = sec[0] if last else 1 - sec[0]
    lanes_half = pl.ds(pl.multiple_of(side * wide, wide), wide)
    waits = attend.fetch(move) + [move.choose(mine, wo_a.ref.at[lanes_half], wo_b.ref.at[lanes_half], wo)]
    near = []
    for source, target in (
        (p_h.ref.at[:, pl.ds(side * pairs, pairs)], probs),
        (v_h.ref.at[:, lanes_half], v),
        (k_h.ref.at[:, lanes_half], k),
        (q_h.ref.at[:, lanes_half], q),
    ):
        move.load(source, target)
        near.append(move.last)
    later = x.fetch(move) + ctx.fetch(move) + down.fetch(move) + up.fetch(move)
    finals = base.fetch(move)
    for i in range(3):
        there = pl.ds(pl.multiple_of(i * width + side * wide, wide), wide)
        finals.append(move.choose(mine, w_a.ref.at[:, there], w_b.ref.at[:, there], w.at[:, pl.ds(i * wide, wide)]))
    ready(waits)
    gc[...] = dot_t(attend.buffer[...], wo[...]).astype(BF16)
    ready(near)
    halves = lane_halves()
    lower = lax.broadcasted_iota(jnp.int32, (128, 128), 1) < 64

    for pair in range(pairs):
        lanes = slice(pair * 128, pair * 128 + 128)
        for seq in range(seqs):
            rows = slice(seq * 128, seq * 128 + 128)

            def put(part, value):
                grads[rows, part * wide + pair * 128 : part * wide + pair * 128 + 128] = value.astype(BF16)

            grad = gc[rows, lanes]
            p = probs[seq, pair]
            full = dot(p.astype(BF16), grad)
            put(2, jnp.where(lower, full[:128], full[128:]))
            gp = dot_t(two_heads(v[rows, lanes], halves), grad)
            parts = []
            for part in (slice(0, 128), slice(128, 256)):
                g, pp = gp[part], p[part]
                parts.append(pp * (g - jnp.sum(g * pp, axis=0, keepdims=True)))
            gs = jnp.concatenate(parts, axis=0).astype(BF16)
            put(0, t_dot(gs, two_heads(k[rows, lanes] * SCALE, halves)))
            full = dot(gs, q[rows, lanes] * SCALE)
            put(1, jnp.where(lower, full[:128], full[128:]))
    ready(later)
    if last:
        turned = x
    else:
        turned.buffer[...] = x.buffer[...].T
    left = dot(turned.buffer[...], grads[...]).astype(BF16)
    right = dot(ctx.buffer[...], attend.buffer[:, lanes_half]).astype(BF16)
    little = jnp.concatenate([down.buffer[...], up.buffer[...]], axis=0).astype(BF16)
    zeros = jnp.zeros_like(little)
    b_q = column_sum(grads[:, 0:wide].astype(F32)).astype(BF16)
    b_v = column_sum(grads[:, 2 * wide :].astype(F32)).astype(BF16)
    pad = jnp.concatenate([b_q, b_v], axis=1)
    pad = jnp.concatenate([pad, jnp.zeros((15, width), BF16)], axis=0)
    for shard in range(shards):
        out.buffer[shard, :tall, 0 : 3 * wide] = left[shard * tall : shard * tall + tall]
        out.buffer[shard, :tall, 3 * wide :] = right[shard * tall : shard * tall + tall]
        out.buffer[shard, tall:, 0:width] = little
        out.buffer[shard, tall:, width:] = pad
    ready(finals)
    sum_all = base.buffer[...] + dot_t(grads[...], w[...])
    if last:
        gx.buffer[...] = sum_all
        gx.flush(move)
        gx_low.buffer[...] = sum_all.astype(BF16)
        gx_low.flush(move)
    else:
        total.buffer[...] = sum_all
    move.finish()


def attend_grad(layer, last, sec, attend, ctx, base, x, q, k, v, probs, wo, wo_other, w, w_other, down, up, shards, low_kind):
    rows, width = attend.shape
    seqs = probs.shape[0]
    wide = width // 2
    flat = (rows, width)
    part = (sds((shards, width // shards + 16, 2 * width), BF16), NEAR)
    if last:
        outs = [(sds(flat, F32), FAR), (sds(flat, BF16), low_kind), part]
    else:
        outs = [(sds(flat, F32), NEAR), (sds((width, rows), BF16), NEAR), part]
    half = ((rows, wide), BF16)
    return call(
        functools.partial(attend_grad_kernel, layer, last),
        sec,
        [(attend, NEAR), (ctx, FAR), (base, NEAR), (x, NEAR if last else FAR)]
        + [(item, RAW) for item in (q, k, v, probs, wo, wo_other, w, w_other)]
        + [(down, NEAR), (up, NEAR)],
        outs,
        [
            half,
            half,
            half,
            ((seqs, wide // 128) + probs.shape[2:], F32),
            ((wide, width), BF16),
            ((width, 3 * wide), BF16),
            half,
            ((rows, 3 * wide), BF16),
        ],
        "attend_grad_last" if last else "attend_grad_first",
        rows * width * width * 10,
        15 << 20,
    )


def up_whole_kernel(
    layer, sec, branch, second, wd_a, wd_b, slope, low, wu_a, wu_b, hat, scale, small,
    first, attend, sums, send, keep, wd, wu, pre, sems,
):
    move = Mover(sems)
    mine = sec[0] == layer
    blocks, wide, _ = wd.shape
    half = blocks // 2
    at = [lax.rem(i + half * (1 - sec[0]), blocks) for i in range(blocks)]
    span = [pl.ds(pl.multiple_of(place * wide, wide), wide) for place in at]
    parts = []
    early = branch.fetch(move)
    for i in range(blocks):
        parts.append(
            [move.choose(mine, wd_a.ref.at[span[i]], wd_b.ref.at[span[i]], wd.at[i])]
            + slope.fetch(move, at[i])
            + [move.choose(mine, wu_a.ref.at[:, span[i]], wu_b.ref.at[:, span[i]], wu.at[i])]
        )
        if i == 0:
            early += low.fetch(move)
    late = second.fetch(move) + hat.fetch(move) + scale.fetch(move) + small.fetch(move)
    ready(early)
    branch, low, total = branch.buffer, low.buffer, first.buffer
    for i in range(blocks):
        ready(parts[i])
        pre[...] = (dot_t(branch[...], wd[i]) * slope.buffer[at[i]]).astype(BF16)
        sums.buffer[pl.ds(3 + at[i], 1)] = column_sum(pre[...].astype(F32))
        out, place = (send, i) if i < half else (keep, i - half)
        block = dot(low[...], pre[...]).astype(BF16)
        shards, tall, _ = out.buffer.shape
        for shard in range(shards):
            out.buffer[shard, :, place * wide : place * wide + wide] = block[shard * tall : shard * tall + tall]
        if i == 0:
            ready(late)
            total[...] = second.buffer[...] + dot_t(pre[...], wu[i])
        else:
            total[...] += dot_t(pre[...], wu[i])
    grad = total[...]
    sums.buffer[0:1] = column_sum(grad * hat.buffer[...])
    sums.buffer[1:2] = column_sum(grad)
    unit = norm_back(grad, hat.buffer[...], scale.buffer[:, 0:1], small.buffer[GAIN_ONE : GAIN_ONE + 1])
    attend.buffer[...] = unit.astype(BF16)
    attend.flush(move)
    total[...] = unit
    first.flush(move)
    sums.buffer[2:3] = column_sum(attend.buffer[...].astype(F32))
    sums.buffer[3 + blocks :] = jnp.zeros_like(sums.buffer[3 + blocks :])
    sums.flush(move)
    move.finish()


def up_whole(layer, sec, branch, second, wd, wd_other, slope, low, wu, wu_other, hat, scale, small, shards):
    blocks, rows, width = slope.shape
    wide = (rows, width)
    part = sds((shards, width // shards, blocks * width // 2), BF16)
    square = ((blocks, width, width), BF16)
    return call(
        functools.partial(up_whole_kernel, layer),
        sec,
        [
            (branch, NEAR),
            (second, NEAR),
            (wd, RAW),
            (wd_other, RAW),
            (slope, FAR),
            (low, FAR),
            (wu, RAW),
            (wu_other, RAW),
            (hat, FAR),
            (scale, FAR),
            (small, FAR),
        ],
        [(sds(wide, F32), NEAR), (sds(wide, BF16), NEAR), (sds((8, width), F32), NEAR), (part, NEAR), (part, NEAR)],
        [square, square, (wide, BF16)],
        "up_grad",
        6 * rows * width * width * blocks,
        30 << 20,
    )


def attend_whole_kernel(
    layer, shards, sec, attend, ctx, first, x, q, k, v, probs, wo_a, wo_b, w_a, w_b, down, up,
    gx, gx_low, send, keep, turned, wo, w, gc, grads, sems,
):
    move = Mover(sems)
    mine = sec[0] == layer
    rows_all, width = x.buffer.shape
    seqs = probs.buffer.shape[0]
    wide = width // 2
    tall = width // shards
    pairs = wide // 128
    waits = attend.fetch(move) + [move.choose(mine, wo_a.ref, wo_b.ref, wo)]
    near = probs.fetch(move) + v.fetch(move) + k.fetch(move) + q.fetch(move)
    later = x.fetch(move) + ctx.fetch(move) + down.fetch(move) + up.fetch(move)
    last = [
        move.choose(mine, w_a.ref.at[:, pl.ds(i * width, width)], w_b.ref.at[:, pl.ds(i * width, width)], w.at[i])
        for i in range(3)
    ] + first.fetch(move)
    ready(waits)
    attend, q, k, v, probs = (item.buffer for item in (attend, q, k, v, probs))
    gc[...] = dot_t(attend[...], wo[...]).astype(BF16)
    ready(near)
    halves = lane_halves()
    lower = lax.broadcasted_iota(jnp.int32, (128, 128), 1) < 64

    def attention(first_pair):
        @pl.loop(0, pairs)
        def _(index):
            pair = first_pair + index
            lanes = pl.ds(pl.multiple_of(pair * 128, 128), 128)
            for seq in range(seqs):
                rows = slice(seq * 128, seq * 128 + 128)
                grad = gc[rows, lanes]
                p = probs[seq, pair]
                full = dot(p.astype(BF16), grad)
                grads[2, rows, lanes] = jnp.where(lower, full[:128], full[128:]).astype(BF16)
                gp = dot_t(two_heads(v[rows, lanes], halves), grad)
                parts = []
                for side in (slice(0, 128), slice(128, 256)):
                    g, pp = gp[side], p[side]
                    parts.append(pp * (g - jnp.sum(g * pp, axis=0, keepdims=True)))
                gs = jnp.concatenate(parts, axis=0).astype(BF16)
                grads[0, rows, lanes] = t_dot(gs, two_heads(k[rows, lanes] * SCALE, halves)).astype(BF16)
                full = dot(gs, q[rows, lanes] * SCALE)
                grads[1, rows, lanes] = jnp.where(lower, full[:128], full[128:]).astype(BF16)

    def products(half, out):
        lanes = pl.ds(pl.multiple_of(half * wide, wide), wide)
        for part in range(4):
            if part < 3:
                block = dot(turned[...], grads[part, :, lanes]).astype(BF16)
            else:
                block = dot(ctx.buffer[...], attend[:, lanes]).astype(BF16)
            for shard in range(shards):
                out.buffer[shard, :tall, part * wide : part * wide + wide] = block[shard * tall : shard * tall + tall]

    attention((1 - sec[0]) * pairs)
    ready(later)
    turned[...] = x.buffer[...].T
    products(1 - sec[0], send)
    attention(sec[0] * pairs)
    products(sec[0], keep)
    little = jnp.concatenate([down.buffer[...], up.buffer[...]], axis=0).astype(BF16)
    for half, out in ((1 - sec[0], send), (sec[0], keep)):
        lanes = pl.ds(pl.multiple_of(half * wide, wide), wide)
        pad = [column_sum(grads[part, :, lanes].astype(F32)).astype(BF16) for part in (0, 2)]
        pad = jnp.concatenate([jnp.concatenate(pad, axis=1), jnp.zeros((15, width), BF16)], axis=0)
        for shard in range(shards):
            out.buffer[shard, tall:, 0:width] = little
            out.buffer[shard, tall:, width:] = pad
    ready(last)
    total = first.buffer[...] + dot_t(grads[0], w[0]) + dot_t(grads[1], w[1]) + dot_t(grads[2], w[2])
    gx.buffer[...] = total
    gx.flush(move)
    gx_low.buffer[...] = total.astype(BF16)
    gx_low.flush(move)
    move.finish()


def attend_whole(layer, sec, attend, ctx, first, x, q, k, v, probs, wo, wo_other, w, w_other, down, up, shards, low_kind):
    rows, width = x.shape
    wide = (rows, width)
    part = sds((shards, width // shards + 16, 2 * width), BF16)
    return call(
        functools.partial(attend_whole_kernel, layer, shards),
        sec,
        [(attend, NEAR), (ctx, FAR), (first, NEAR)]
        + [(item, FAR) for item in (x, q, k, v, probs)]
        + [(wo, RAW), (wo_other, RAW), (w, RAW), (w_other, RAW), (down, NEAR), (up, NEAR)],
        [(sds(wide, F32), FAR), (sds(wide, BF16), low_kind), (part, NEAR), (part, NEAR)],
        [((width, rows), BF16), ((width, width), BF16), ((3, width, width), BF16), (wide, BF16), ((3,) + wide, BF16)],
        "attend_grad",
        2 * rows * width * width * 10,
        30 << 20,
    )


def layer_forward(layer, sec, x, front, big, other, small, far=None):
    w_qkv, w_out, w_up, w_down = big
    o_qkv, o_out, o_up, o_down = other
    x_kind = FAR if layer == 0 else NEAR
    q, k, v, probs, (ctx_near, ctx) = front
    (hat_near, hat_one), scale_one, low, act, slope = up_forward(
        layer, sec, x, x_kind, ctx_near, w_out, o_out, w_up, o_up, small
    )
    act_near, act = act if layer == 0 else (act, act)
    kinds = (BOTH, FAR) if layer == 0 else (FAR, NEAR)
    y, hat_two, scale_two = down_forward(layer, sec, act_near, w_down, o_down, hat_near, small, *kinds)
    x = x if far is None else far
    return y, (x, q, k, v, probs, ctx, hat_one, scale_one, low, act, slope, hat_two, scale_two)


class Backward:
    def __init__(self, line, layer, sec, cache, big, other, small, shards):
        self.line, self.layer, self.sec, self.small, self.shards = line, layer, sec, small, shards
        self.cache, self.weights, self.made = cache, tuple(zip(big, other)), {}

    def down(self, gy):
        act, _, hat_two, scale_two = self.cache[-4:]
        kinds = (NEAR, FAR) if self.layer == 0 else (FAR, NEAR)
        second, branch, sums, send, keep = down_grad(
            self.line.sec, gy, kinds[0], hat_two, scale_two, self.small, act, kinds[1]
        )
        self.made.update(second=second, branch=branch, down_sums=sums)
        self.line.add(send, keep)

    def up_inputs(self):
        (w_up, o_up), (w_down, o_down) = self.weights[2:]
        low, _, slope = self.cache[-5:-2]
        return w_down, o_down, slope, low, w_up, o_up, self.shards

    def up_first(self):
        made = self.made
        made["part"], made["up_sums"], send = up_grad(
            self.layer, False, self.line.sec, made["branch"], made["second"], *self.up_inputs()
        )
        self.up_chunk = self.line.add(send, None)

    def up_last(self):
        made = self.made
        hat_one, scale_one = self.cache[-7:-5]
        more = (hat_one, scale_one, self.small, made["up_sums"])
        made["first"], made["attend"], made["up_sums"], self.up_chunk.keep = up_grad(
            self.layer, True, self.line.sec, made["branch"], made["part"], *self.up_inputs(), more
        )

    def up(self):
        made = self.made
        hat_one, scale_one = self.cache[-7:-5]
        ins = self.up_inputs()
        made["first"], made["attend"], made["up_sums"], send, keep = up_whole(
            self.layer, self.line.sec, made["branch"], made["second"], *ins[:-1], hat_one, scale_one, self.small, ins[-1]
        )
        self.line.add(send, keep)

    def attention(self):
        made = self.made
        made["gx"], made["gx_low"], send, keep = attend_whole(
            self.layer, self.line.sec, made["attend"], self.cache[5], made["first"], self.cache[0], *self.heads()
        )
        self.line.add(send, keep)

    def heads(self):
        q, k, v, probs = self.cache[1:5]
        (w_qkv, o_qkv), (w_out, o_out) = self.weights[:2]
        low_kind = FAR if self.layer == 0 else BOTH
        sums = (self.made["down_sums"], self.made["up_sums"])
        return (q, k, v, probs, w_out, o_out, w_qkv, o_qkv) + sums + (self.shards, low_kind)

    def attend_first(self):
        made = self.made
        made["part"], made["turned"], send = attend_grad(
            self.layer, False, self.line.sec, made["attend"], self.cache[5], made["first"], self.cache[0], *self.heads()
        )
        self.attend_chunk = self.line.add(send, None)

    def attend_last(self):
        made = self.made
        made["gx"], made["gx_low"], self.attend_chunk.keep = attend_grad(
            self.layer, True, self.line.sec, made["attend"], self.cache[5], made["part"], made["turned"], *self.heads()
        )


def exchange(array, axis, bit):
    length = lax.axis_size(axis)
    return lax.ppermute(array, axis, [(i, i ^ bit) for i in range(length)])


def pick(array, index, axis):
    return lax.dynamic_index_in_dim(array, index, axis, keepdims=False)


def split_at(rows):
    return (rows // 2 + 15) // 16 * 16


class Sums:
    def __init__(self, columns):
        self.columns, self.ins, self.outs, self.code = columns, [], [], []
        self.rows = {}

    def use(self, array):
        for index, known in enumerate(self.ins):
            if known is array:
                return index
        self.ins.append(array)
        return len(self.ins) - 1

    def result(self, shape):
        self.outs.append(sds(tuple(shape) + (self.columns,), BF16))
        return len(self.outs) - 1

    def region(self, way, rows):
        first = self.rows.get(way, 0)
        self.rows[way] = first + rows
        return first

    def run(self, ids):
        ways = sorted(self.rows)
        shapes = self.outs + [sds((self.rows[way], self.columns), BF16) for way in ways]
        n_in, n_out = len(self.ins), len(self.outs)

        def kernel(ids_ref, *refs):
            sends = dict(zip(ways, refs[n_in + n_out :]))
            for code in self.code:
                code(ids_ref, refs[:n_in], refs[n_in : n_in + n_out], sends)

        vmem = pl.BlockSpec(memory_space=pltpu.VMEM)
        results = pl.pallas_call(
            kernel,
            in_specs=[pl.BlockSpec(memory_space=pltpu.SMEM)] + [vmem] * n_in,
            out_specs=[vmem] * len(shapes),
            out_shape=shapes,
            compiler_params=pltpu.CompilerParams(vmem_limit_bytes=SPARE),
            name="join_sums",
        )(ids, *self.ins)
        return results[:n_out], dict(zip(ways, results[n_out:]))


def at_rows(first, index, count):
    return pl.ds(pl.multiple_of(first + index * count, 16), count)


def sum_section(sums, chunk):
    kept, got = sums.use(chunk.keep), sums.use(chunk.got["section"])
    _, rows, _ = chunk.keep.shape
    cut = chunk.cut
    rest = rows - cut
    top, bottom = sums.result((2, cut)), sums.result((2, rest))
    chunk.first = {"x": sums.region("x", 2 * cut), "y": sums.region("y", 2 * rest)}
    to_x, to_y = chunk.first["x"], chunk.first["y"]

    def code(ids, ins, outs, sends):
        low, high = ids[1], ids[2]
        for i in range(2):
            add = lambda shard, lines: ins[kept][shard, lines] + ins[got][shard, lines]
            sends["x"][to_x + i * cut : to_x + i * cut + cut] = add(2 * i + 1 - low, slice(0, cut))
            outs[top][i] = add(2 * i + low, slice(0, cut))
            sends["y"][to_y + i * rest : to_y + i * rest + rest] = add(2 * (1 - high) + i, slice(cut, rows))
            outs[bottom][i] = add(2 * high + i, slice(cut, rows))

    sums.code.append(code)
    return [top, bottom]


def sum_first(sums, chunk):
    top, bottom = (sums.use(item) for item in chunk.kept)
    got_x, got_y = sums.use(chunk.got["x"]), sums.use(chunk.got["y"])
    at_x, at_y = chunk.first["x"], chunk.first["y"]
    cut, rest = chunk.kept[0].shape[1], chunk.kept[1].shape[1]
    new_top, new_bottom = sums.result((cut,)), sums.result((rest,))
    chunk.first = {"y": sums.region("y", cut), "x": sums.region("x", rest)}
    to_x, to_y = chunk.first["x"], chunk.first["y"]

    def code(ids, ins, outs, sends):
        low, high = ids[1], ids[2]
        upper = lambda i: ins[top][i] + ins[got_x][at_rows(at_x, i, cut)]
        lower = lambda i: ins[bottom][i] + ins[got_y][at_rows(at_y, i, rest)]
        sends["y"][to_y : to_y + cut] = upper(1 - high)
        outs[new_top][...] = upper(high)
        sends["x"][to_x : to_x + rest] = lower(1 - low)
        outs[new_bottom][...] = lower(low)

    sums.code.append(code)
    return [new_top, new_bottom]


def sum_second(sums, chunk):
    top, bottom = (sums.use(item) for item in chunk.kept)
    got_x, got_y = sums.use(chunk.got["x"]), sums.use(chunk.got["y"])
    at_x, at_y = chunk.first["x"], chunk.first["y"]
    cut, rest = chunk.kept[0].shape[0], chunk.kept[1].shape[0]
    part = sums.result((cut + rest,))
    onward = chunk.line.short
    if onward:
        sums.rows["ends"] = max(sums.rows.get("ends", 0), cut + rest)

    def code(ids, ins, outs, sends):
        outs[part][:cut] = ins[top][...] + ins[got_y][at_y : at_y + cut]
        outs[part][cut:] = ins[bottom][...] + ins[got_x][at_x : at_x + rest]
        if onward:

            @pl.when(ids[3] == 1)
            def _():
                sends["ends"][: cut + rest] = outs[part][...]

    sums.code.append(code)
    return [part]


def sum_ends(sums, chunk):
    part, got = sums.use(chunk.kept[0]), sums.use(chunk.got["ends"])
    rows = chunk.kept[0].shape[0]
    chunk.first = {"middle": sums.region("middle", rows)}
    to = chunk.first["middle"]

    def code(ids, ins, outs, sends):
        sends["middle"][to : to + rows] = ins[part][...] + ins[got][:rows]

    sums.code.append(code)
    return []


def sum_middle(sums, chunk):
    sent, got = sums.use(chunk.sent["middle"]), sums.use(chunk.got["middle"])
    at, rows = chunk.first["middle"], chunk.rows
    whole = sums.result((rows,))
    sums.rows["ends"] = max(sums.rows.get("ends", 0), rows)

    def code(ids, ins, outs, sends):
        outs[whole][...] = ins[sent][at : at + rows] + ins[got][at : at + rows]

        @pl.when(ids[3] == 0)
        def _():
            sends["ends"][:rows] = outs[whole][...]

    sums.code.append(code)
    return [whole]


def sum_last(sums, chunk):
    whole, got = sums.use(chunk.kept[0]), sums.use(chunk.got["ends"])
    rows = chunk.rows
    results = [sums.result((rows,))]
    if chunk.partner is not None:
        other = sums.use(chunk.partner.done[0])
        results.append(sums.result((rows,)))

    def code(ids, ins, outs, sends):
        def put(value, outer):
            if chunk.partner is None:
                outs[results[0]][...] = value(slice(None))
                return
            for first, (to_value, to_other) in ((0, results), (1, results[::-1])):

                @pl.when((ids[0] == first) & (ids[3] == outer))
                def _():
                    outs[to_value][...] = value(slice(None))
                    outs[to_other][...] = ins[other][...]

        if chunk.partner is None:
            pl.when(ids[3] == 1)(lambda: put(lambda _: ins[got][:rows], 1))
            pl.when(ids[3] == 0)(lambda: put(lambda _: ins[whole][...], 0))
        else:
            put(lambda _: ins[got][:rows], 1)
            put(lambda _: ins[whole][...], 0)

    sums.code.append(code)
    return results


class Chunk:
    def __init__(self, line, send, keep, partner):
        self.line, self.send, self.keep, self.partner = line, send, keep, partner
        self.at, self.kept, self.got, self.sent, self.done = 0, [], {}, {}, None
        self.rows = send.shape[1]
        self.cut = split_at(self.rows)


class Line:
    def __init__(self, sec):
        self.sec = sec
        self.square = lax.axis_size("inner") == 4
        self.short = lax.axis_size("outer") == 4
        spot, place = lax.axis_index("inner"), lax.axis_index("outer")
        outside = (place == 0) | (place == lax.axis_size("outer") - 1)
        self.ids = jnp.stack([lax.axis_index("section"), spot % 2, spot // 2, outside, spot]).astype(jnp.int32)
        self.chunks, self.made = [], {}
        self.sums = (sum_section, sum_first, sum_second, sum_ends, sum_middle, sum_last)

    def add(self, send, keep):
        count = len(self.chunks)
        chunk = Chunk(self, send, keep, self.chunks[count - 3] if count >= 3 else None)
        self.chunks.append(chunk)
        return chunk

    def move(self, way, array):
        if way == "section":
            return exchange(array, "section", 1)
        if way in ("x", "y"):
            return exchange(array, "inner", 1 if way == "x" else 2)
        return lax.ppermute(array, "outer", [(0, 1), (1, 0), (2, 3), (3, 2)] if way == "ends" else [(1, 2), (2, 1)])

    def advance(self, owner, *works):
        moving = [chunk for chunk in self.chunks if chunk.done is None and chunk.at > 0]
        sends = {}
        if moving and self.square:
            sums = Sums(moving[0].send.shape[-1])
            places = [self.sums[chunk.at - 1](sums, chunk) for chunk in moving]
            outs, sends = sums.run(self.ids)
            for chunk, place in zip(moving, places):
                chunk.kept, chunk.sent = [outs[index] for index in place], sends
        for chunk in moving:
            chunk.at += 1
            if not self.square:
                half = chunk.keep.astype(F32) + chunk.got["section"].astype(F32)
                half = lax.psum_scatter(half.astype(BF16), "inner", scatter_dimension=0, tiled=False)
                chunk.done = [lax.psum(half, "outer")]
            elif chunk.at == 4 and not self.short:
                chunk.done = [lax.psum(chunk.kept[0], "outer")]
            elif chunk.at == 7:
                chunk.done = chunk.kept
        new = [chunk for chunk in self.chunks if chunk.at == 0]
        gots = {way: self.move(way, array) for way, array in sends.items()}
        arrived = [self.move("section", chunk.send) for chunk in new]
        for work in works:
            work()
        fresh = [chunk for chunk in self.chunks if chunk not in new and chunk.at == 0]
        late = [chunk for chunk in self.chunks if chunk.keep is not None and chunk.at == 0]
        owner.made, parts, keeps, gots, arrived = lax.optimization_barrier(
            (owner.made, [chunk.send for chunk in fresh], [chunk.keep for chunk in late], gots, arrived)
        )
        for chunk, part in zip(fresh, parts):
            chunk.send = part
        for chunk, part in zip(late, keeps):
            chunk.keep = part
        for chunk in moving:
            chunk.got = gots
        for chunk, part in zip(new, arrived):
            chunk.at, chunk.got = 1, {"section": part}

    def finish(self):
        while any(chunk.done is None for chunk in self.chunks):
            self.advance(self)
        pairs = []
        for chunk in self.chunks[3:]:
            if len(chunk.done) == 1:
                two, one = chunk.partner.done[0], chunk.done[0]
                mine, send = (jnp.where(self.ids[0] == 0, *item) for item in ((one, two), (two, one)))
            else:
                mine, send = chunk.done
            pairs.append((mine, exchange(send, "section", 1)))
        return pairs


def assemble_kernel(sec, y_one, y_two, y_got, one, two_low, got, y_out, g_out, y, low, wide, sems):
    move = Mover(sems)
    first = sec[0] == 0
    loads = [
        move.choose(first, y_one.ref, y_got.ref, y.at[0]),
        move.choose(first, y_got.ref, y_two.ref, y.at[1]),
        move.choose(first, one.ref, got.ref, wide.at[0]),
    ]
    move.load(two_low.ref, low)
    loads.append(move.last)
    pl.when(first)(lambda: move.choose(first, got.ref, got.ref, wide.at[1]).wait())
    ready(loads)
    move.used += 1

    @pl.when(jnp.logical_not(first))
    def _():
        wide[1] = low[...].astype(F32)

    move.store(y, y_out.ref)
    move.store(wide, g_out.ref)
    move.finish()


def assemble(sec, y_one, y_two, y_got, one, two_low, got):
    flat = one.shape
    return call(
        assemble_kernel,
        sec,
        [(item, RAW) for item in (y_one, y_two, y_got, one, two_low, got)],
        [(sds((2,) + flat, BF16), RAW), (sds((2,) + flat, F32), RAW)],
        [((2,) + flat, BF16), (flat, BF16), ((2,) + flat, F32)],
        "assemble",
        1000,
        10 << 20,
    )


class Rest:
    def __init__(self, sec):
        self.sec, self.made = sec, {}

    def send(self, one, two_low):
        low = two_low.astype(F32)
        self.made["got"] = exchange(jnp.where(self.sec[0] == 0, low, one), "section", 1)

    def assemble(self, y_one, y_two, one, two_low):
        self.made["outs"] = assemble(self.sec, y_one, y_two, self.made["y"], one, two_low, self.made["got"])


def last_kernel(ids, up_mine, up_got, mine, got, qkv, out, b_qv, b_out, gain, offset, b_up, b_down, w_up, sems):
    move = Mover(sems)
    up_wide = w_up.buffer.shape[1] // 2
    for half, side in ((ids[0], up_mine), (1 - ids[0], up_got)):
        w_up.buffer[:, pl.ds(pl.multiple_of(half * up_wide, up_wide), up_wide)] = side.buffer[...].astype(F32)
    w_up.flush(move)
    mine, got = mine.buffer, got.buffer
    tall, wide = qkv.buffer.shape[0], out.buffer.shape[1] // 2
    for half, side in ((ids[0], mine), (1 - ids[0], got)):
        for part in range(4):
            block = side[:tall, part * wide : part * wide + wide].astype(F32)
            target, first = (qkv, 2 * part * wide) if part < 3 else (out, 0)
            lanes = pl.ds(pl.multiple_of(first + half * wide, wide), wide)
            target.buffer[:, lanes] = block
    qkv.flush(move)
    out.flush(move)
    rows = mine[tall:, : 2 * wide].astype(F32)
    own, other = (side[tall : tall + 1, 2 * wide :].astype(F32) for side in (mine, got))

    def write(first_half, place):
        left, right = (own, other) if first_half else (other, own)
        span = slice(place * tall, place * tall + tall)
        for row in range(2):
            bias = jnp.concatenate([side[:, row * wide : row * wide + wide] for side in (left, right)], axis=1)
            b_qv.buffer[row : row + 1, :] = bias[:, span]
        b_out.buffer[...] = rows[10:11, span]
        gain.buffer[0:1, :] = rows[8:9, span]
        gain.buffer[1:2, :] = rows[0:1, span]
        offset.buffer[0:1, :] = rows[9:10, span]
        offset.buffer[1:2, :] = rows[1:2, span]
        b_up.buffer[...] = rows[11 + place : 12 + place]
        b_down.buffer[...] = rows[2:3, span]

    for first_half in (True, False):
        for place in range(2 * wide // tall):
            here = (ids[0] == (0 if first_half else 1)) & (ids[4] == place)
            pl.when(here)(functools.partial(write, first_half, place))
    for item in (b_qv, b_out, gain, offset, b_up, b_down):
        item.flush(move)
    move.finish()


def last(ids, up, attend, width, shards):
    tall = width // shards
    shapes = [(tall, 3 * width), (tall, width), (2, tall), (1, tall), (2, tall), (2, tall), (1, width), (1, tall)]
    shapes.append((tall, 2 * up[0].shape[1]))
    return call(
        last_kernel,
        ids,
        [(item, NEAR) for item in (*up, *attend)],
        [(sds(shape, F32), FAR) for shape in shapes],
        [],
        "last",
        1000,
        5 << 20,
    )


def local(
    hidden_in, caption_len, region_len, cotangent, w_qkv, b_qv, w_out, b_out, ln_gain, ln_bias, w_up, b_up, w_down, b_down
):
    section = lax.axis_index("section")
    shards = lax.axis_size("inner")
    sec = section.astype(jnp.int32)[None]
    seqs_local, length, width = hidden_in.shape
    seqs = seqs_local // 2
    rows = seqs * length
    positions = jnp.arange(length, dtype=jnp.int32)[None, :]
    mine = lambda array: lax.dynamic_slice_in_dim(array, section * seqs, seqs, 0)
    caption, region = mine(caption_len)[:, None], mine(region_len)[:, None]
    valid = (positions < caption) | (positions >= CAP) & (positions < CAP + region)
    mask = jnp.concatenate([valid, valid], axis=1).astype(F32).T
    x = mine(hidden_in).reshape(rows, width)
    gy = jnp.where(valid[:, :, None], mine(cotangent), jnp.zeros((), BF16)).reshape(rows, width)

    blocks = w_up.shape[2] // width
    little = jnp.concatenate(
        [b_qv[0], b_out, ln_gain[0], ln_bias[0], b_down, b_up.reshape(blocks, width), jnp.zeros((8 - blocks, width), F32)]
    )
    little_other = exchange(little, "section", 1)
    big = (w_qkv[0], w_out[0], w_up[0], w_down[0])
    o_qkv = exchange(big[0], "section", 1)

    smalls = [jnp.where(section == layer, little, little_other) for layer in (0, 1)]
    o_qkv, smalls, mask, x, late_out, late_up = lax.optimization_barrier(
        (o_qkv, smalls, mask, x, big[1], big[2])
    )
    o_out, o_up = exchange(late_out, "section", 1), exchange(late_up, "section", 1)
    front = attend_forward(0, sec, x, FAR, big[0], o_qkv, smalls[0], mask)
    front, o_out, o_up, late_down = lax.optimization_barrier((front, o_out, o_up, big[3]))
    other = (o_qkv, o_out, o_up, exchange(late_down, "section", 1))
    y_one, cache_one = layer_forward(0, sec, x, front, big, other, smalls[0])
    y_near, y_one = y_one
    front = attend_forward(1, sec, y_near, NEAR, big[0], o_qkv, smalls[1], mask)
    y_two, cache_two = layer_forward(1, sec, y_near, front, big, other, smalls[1], y_one)
    line = Line(sec)
    two = Backward(line, 1, sec, cache_two, big, other, smalls[1], shards)
    one = Backward(line, 0, sec, cache_one, big, other, smalls[0], shards)
    exchanged_y = exchange(jnp.where(section == 0, y_two, y_one), "section", 1)
    line.advance(two, lambda: two.down(gy))
    line.advance(two, two.up_first)
    line.advance(two, two.up_last)
    line.advance(two, two.attention)
    gx_two_near, gx_two_low = two.made["gx_low"]
    line.advance(one, lambda: one.down(gx_two_near))
    line.advance(one, one.up)
    line.advance(one, one.attention)
    gx_one = one.made["gx"]

    rest = Rest(sec)
    rest.made["y"] = exchanged_y
    for _ in range(3):
        line.advance(line)
    line.advance(rest, lambda: rest.send(gx_one, gx_two_low))
    line.advance(rest, lambda: rest.assemble(y_one, y_two, gx_one, gx_two_low))
    activations, input_grads = rest.made["outs"]
    activations = activations.reshape(seqs_local, length, width)
    input_grads = input_grads.reshape(seqs_local, length, width)
    down, up, attend = line.finish()
    g_w_qkv, g_w_out, g_b_qv, g_b_out, g_gain, g_offset, g_b_up, g_b_down, g_w_up = last(
        line.ids, up, attend, width, shards
    )
    mine, got = down
    down = (jnp.where(section == 0, mine, got), jnp.where(section == 0, got, mine))
    g_w_down = jnp.concatenate(
        [side[:, i * width : (i + 1) * width] for side in down for i in range(2)], axis=0
    ).T.astype(F32)
    return (
        activations[None],
        input_grads[None],
        g_w_qkv[None],
        g_b_qv[None],
        g_w_out[None],
        g_b_out,
        g_gain[None],
        g_offset[None],
        g_w_up[None],
        g_b_up,
        g_w_down[None],
        g_b_down,
    )


def solution(mesh):
    rows = ("inner", "outer")
    return jax.shard_map(
        local,
        mesh=mesh,
        in_specs=(
            P(rows, None, None),
            P(rows),
            P(rows),
            P(rows, None, None),
            P("section", None, None),
            P("section", None, None),
            P("section", None, None),
            P("section", None),
            P("section", None, None),
            P("section", None, None),
            P("section", None, None),
            P("section", None),
            P("section", None, None),
            P("section", None),
        ),
        out_specs=(
            P("section", rows, None, None),
            P("section", rows, None, None),
            P("section", "inner", None),
            P("section", None, "inner"),
            P("section", "inner", None),
            P("section", "inner"),
            P("section", None, "inner"),
            P("section", None, "inner"),
            P("section", "inner", None),
            P("section", "inner"),
            P("section", "inner", None),
            P("section", "inner"),
        ),
        check_vma=False,
    )
```

```python
import functools
import math

import jax
import jax.numpy as jnp
from jax import lax
from jax.experimental import pallas as pl
from jax.experimental.pallas import tpu as pltpu
from jax.sharding import PartitionSpec as P

HEADS = 12
CAP = 28
EPS = 1e-12
SCALE = 0.125
SPARE = 8 * 1024 * 1024
F32 = jnp.float32
BF16 = jnp.bfloat16
B_Q, B_V, B_OUT, GAIN_ONE, GAIN_TWO, OFFSET_ONE, OFFSET_TWO, B_DOWN, B_UP = range(9)


def dot(left, right):
    return jnp.dot(left, right, preferred_element_type=F32)


def dot_t(left, right):
    return lax.dot_general(left, right, (((1,), (1,)), ((), ())), preferred_element_type=F32)


def t_dot(left, right):
    return lax.dot_general(left, right, (((0,), (0,)), ((), ())), preferred_element_type=F32)


def column_sum(values):
    return jnp.sum(values, axis=0, keepdims=True)


def standardize(summed):
    centre = jnp.mean(summed, axis=-1, keepdims=True)
    shifted = summed - centre
    spread = jnp.mean(shifted * shifted, axis=-1, keepdims=True)
    scale = lax.rsqrt(spread + EPS)
    return shifted * scale, scale


def norm_back(grad, hat, scale, gain):
    scaled = grad * gain
    return scale * (
        scaled
        - jnp.mean(scaled, axis=-1, keepdims=True)
        - hat * jnp.mean(scaled * hat, axis=-1, keepdims=True)
    )


def gauss_share(value):
    bell = jnp.exp2(value * value * -0.7213475204444817)
    part = 1.0 / (1.0 + 0.2316418882 * jnp.abs(value))
    tail = 0.5307027145
    for item in (-0.7265760135, 0.7107068705, -0.142248368, 0.127414796):
        tail = tail * part + item
    tail = tail * part * bell
    return jnp.where(value < 0.0, tail, 1.0 - tail), bell


def lane_halves():
    lane = lax.broadcasted_iota(jnp.int32, (1, 128), 1)
    lower = jnp.where(lane < 64, 1.0, 0.0)
    return lower.astype(BF16), (1.0 - lower).astype(BF16)


def two_heads(block, halves):
    return jnp.concatenate([block * halves[0], block * halves[1]], axis=0)


def sds(shape, dtype):
    return jax.ShapeDtypeStruct(shape, dtype)


class Mover:
    def __init__(self, sems):
        self.sems, self.used, self.outs = sems, 0, []

    def copy(self, source, target):
        self.used += 1
        return pltpu.make_async_copy(source, target, self.sems.at[self.used - 1])

    def load(self, source, target):
        self.last = self.copy(source, target)
        self.last.start()

    def choose(self, first, one, two, target):
        copy = self.copy(one, target)
        other = pltpu.make_async_copy(two, target, self.sems.at[self.used - 1])
        pl.when(first)(copy.start)
        pl.when(jnp.logical_not(first))(other.start)
        return copy

    def store(self, source, target):
        copy = self.copy(source, target)
        copy.start()
        self.outs.append(copy)

    def finish(self):
        for copy in self.outs:
            copy.wait()


class Operand:
    def __init__(self, ref, buffer, far):
        self.ref, self.buffer, self.far = ref, buffer, far

    def fetch(self, move, *index):
        if self.far:
            move.load(*(ref.at[index] if index else ref for ref in (self.ref, self.buffer)))
            return [move.last]
        return []

    def flush(self, move, *index):
        if self.far:
            move.store(*(ref.at[index] if index else ref for ref in (self.buffer, self.ref)))


NEAR, FAR, RAW, BOTH, FREE = "near", "far", "raw", "both", "free"


def run(*parts):
    for part in parts:
        next(part)
    for part in parts:
        for _ in part:
            pass


def ready(waits):
    for item in waits:
        item.wait()


def call(kernel, ids, ins, outs, scratch, name, flops, nbytes):
    space = lambda kind: {NEAR: pltpu.VMEM, FREE: pl.ANY}.get(kind, pltpu.HBM)
    spread = [(shape, part) for shape, kind in outs for part in ((NEAR, RAW) if kind == BOTH else (kind,))]
    kinds = [kind for _, kind in ins] + [kind for _, kind in spread]
    shapes = [array for array, _ in ins] + [shape for shape, _ in spread]
    buffers = [pltpu.VMEM(shape.shape, shape.dtype) for shape, kind in zip(shapes, kinds) if kind == FAR]

    def body(ids_ref, *refs):
        count = len(kinds)
        spare = list(refs[count : count + len(buffers)])
        left = list(refs[:count])
        operands = []
        for _, kind in list(ins) + list(outs):
            ref = left.pop(0)
            if kind == BOTH:
                operands.append(Operand(left.pop(0), ref, True))
            else:
                operands.append(Operand(ref, spare.pop(0) if kind == FAR else ref, kind == FAR))
        kernel(ids_ref, *operands, *refs[count + len(buffers) :])

    size = lambda shape, dtype: math.prod(shape) * jnp.dtype(dtype).itemsize
    limit = SPARE + sum(size(*item) for item in scratch)
    limit += sum(size(shape.shape, shape.dtype) for shape, kind in zip(shapes, kinds) if kind == FAR)
    results = pl.pallas_call(
        body,
        in_specs=[pl.BlockSpec(memory_space=pltpu.SMEM)]
        + [pl.BlockSpec(memory_space=space(kind)) for _, kind in ins],
        out_specs=[pl.BlockSpec(memory_space=space(kind)) for _, kind in spread],
        out_shape=[space(kind)(shape.shape, shape.dtype) for shape, kind in spread],
        scratch_shapes=buffers + [pltpu.VMEM(*item) for item in scratch] + [pltpu.SemaphoreType.DMA((64,))],
        compiler_params=pltpu.CompilerParams(vmem_limit_bytes=limit),
        cost_estimate=pl.CostEstimate(flops=flops, bytes_accessed=nbytes, transcendentals=0),
        name=name,
    )(ids, *(pltpu.with_memory_space_constraint(array, space(kind)) for array, kind in ins))
    results = list(results)
    return [(results.pop(0), results.pop(0)) if kind == BOTH else results.pop(0) for _, kind in outs]


def attend_phase(q, k, v, probs, ctx, mask, pairs):
    seqs = mask.shape[1]
    halves = lane_halves()
    feature = lax.broadcasted_iota(jnp.int32, (128, 128), 0)
    first_half = jnp.where(feature < 64, 1.0, 0.0).astype(BF16)
    second_half = jnp.where(feature < 64, 0.0, 1.0).astype(BF16)

    for seq in range(seqs):
        rows = slice(seq * 128, seq * 128 + 128)
        seen = jnp.broadcast_to(mask[:, seq : seq + 1], (256, 128)) > 0.5
        for pair in range(*pairs):
            lanes = slice(pair * 128, pair * 128 + 128)
            scores = dot_t(two_heads(k[rows, lanes], halves), q[rows, lanes] * SCALE)
            scores = jnp.where(seen, scores, -1e30)
            parts = []
            for part in (scores[:128], scores[128:]):
                e = jnp.exp(part - jnp.max(part, axis=0, keepdims=True))
                parts.append(e * (1.0 / jnp.sum(e, axis=0, keepdims=True)))
            parts = jnp.concatenate(parts, axis=0)
            probs[seq, pair] = parts
            turned = v[rows, lanes].T
            turned = jnp.concatenate([turned * first_half, turned * second_half], axis=1)
            ctx[lanes, rows] = dot(turned, parts.astype(BF16)).astype(BF16)


def attend_steps(move, layer, sec, x, w_a, w_b, small, mask, q, k, v, probs, ctx, w):
    mine = sec[0] == layer
    rows, width = x.buffer.shape
    waits = x.fetch(move) + small.fetch(move) + mask.fetch(move)
    parts = [
        move.choose(mine, w_a.ref.at[:, pl.ds(i * width, width)], w_b.ref.at[:, pl.ds(i * width, width)], w.at[i])
        for i in (1, 0, 2)
    ]
    yield
    ready(waits)
    x, small = x.buffer, small.buffer
    parts[0].wait()
    k.buffer[...] = dot(x[...], w[1]).astype(BF16)
    k.flush(move)
    parts[1].wait()
    q.buffer[...] = (dot(x[...], w[0]) + small[B_Q : B_Q + 1]).astype(BF16)
    q.flush(move)
    parts[2].wait()
    v.buffer[...] = (dot(x[...], w[2]) + small[B_V : B_V + 1]).astype(BF16)
    v.flush(move)
    half = width // 128 // 2
    for i in range(2):
        attend_phase(
            q.buffer, k.buffer, v.buffer, probs.buffer, ctx.buffer, mask.buffer, (i * half, i * half + half)
        )
        probs.flush(move, slice(None), pl.ds(i * half, half))
    ctx.flush(move)


def attend_kernel(layer, sec, *refs):
    move = Mover(refs[-1])
    run(attend_steps(move, layer, sec, *refs[:-1]))
    move.finish()


def attend_forward(layer, sec, x, x_kind, w_own, w_other, small, mask):
    rows, width = x.shape
    seqs = mask.shape[1]
    pairs = width // 128
    wide = sds((rows, width), BF16)
    return call(
        functools.partial(attend_kernel, layer),
        sec,
        [(x, x_kind), (w_own, RAW), (w_other, RAW), (small, FAR), (mask, FAR)],
        [(wide, FAR)] * 3 + [(sds((seqs, pairs, 256, 128), F32), FAR), (sds((width, rows), BF16), BOTH)],
        [((3, width, width), BF16)],
        "attend_forward",
        2 * rows * width * width * 4,
        12 << 20,
    )


def up_kernel(layer, sec, x, ctx, wo_a, wo_b, wu_a, wu_b, small, hat, scale, turned, act, slope, wo, wu, low, sems):
    move = Mover(sems)
    mine = sec[0] == layer
    blocks, _, wide = wu.shape
    waits = ctx.fetch(move) + [move.choose(mine, wo_a.ref, wo_b.ref, wo)] + small.fetch(move) + x.fetch(move)
    span = lambda i: pl.ds(i * wide, wide)
    parts = [move.choose(mine, wu_a.ref.at[:, span(i)], wu_b.ref.at[:, span(i)], wu.at[i]) for i in range(blocks)]
    ready(waits)
    small = small.buffer
    summed = x.buffer[...].astype(F32) + t_dot(ctx.buffer[...], wo[...]) + small[B_OUT : B_OUT + 1]
    unit, root = standardize(summed)
    hat.buffer[...] = unit
    hat.flush(move)
    scale.buffer[...] = jnp.broadcast_to(root, scale.buffer.shape)
    scale.flush(move)
    low[...] = (unit * small[GAIN_ONE : GAIN_ONE + 1] + small[OFFSET_ONE : OFFSET_ONE + 1]).astype(BF16)
    turned.buffer[...] = low[...].T
    turned.flush(move)
    for i in range(blocks):
        parts[i].wait()
        pre = dot(low[...], wu[i]) + small[B_UP + i : B_UP + i + 1]
        share, bell = gauss_share(pre)
        act.buffer[i] = (pre * share).astype(BF16)
        slope.buffer[i] = share + pre * 0.3989422804014327 * bell
        act.flush(move, i)
        slope.flush(move, i)
    move.finish()


def up_forward(layer, sec, x, x_kind, ctx, wo, wo_other, wu, wu_other, small):
    rows, width = x.shape
    blocks = wu.shape[1] // width
    wide = (rows, width)
    other_kind = FREE if layer == 0 else RAW
    return call(
        functools.partial(up_kernel, layer),
        sec,
        [(x, x_kind), (ctx, NEAR), (wo, RAW), (wo_other, other_kind), (wu, RAW), (wu_other, other_kind), (small, FAR)],
        [
            (sds(wide, F32), BOTH),
            (sds((rows, 128), F32), FAR),
            (sds((width, rows), BF16), FAR),
            (sds((blocks,) + wide, BF16), BOTH if layer == 0 else NEAR),
            (sds((blocks,) + wide, F32), FAR),
        ],
        [((width, width), BF16), ((blocks, width, width), BF16), (wide, BF16)],
        "up_forward",
        2 * rows * width * width * (blocks + 1),
        20 << 20,
    )


def down_kernel(layer, sec, act, wd_a, wd_b, hat, small, y, two, scale, wd, total, sems):
    move = Mover(sems)
    mine = sec[0] == layer
    blocks, wide, _ = wd.shape
    parts = []
    for i in range(blocks):
        span = pl.ds(i * wide, wide)
        parts.append(act.fetch(move, i) + [move.choose(mine, wd_a.ref.at[span], wd_b.ref.at[span], wd.at[i])])
        if i == 0:
            waits = small.fetch(move) + hat.fetch(move)
    for i in range(blocks):
        ready(parts[i])
        product = dot(act.buffer[i], wd[i])
        total[...] = product if i == 0 else total[...] + product
    ready(waits)
    small = small.buffer
    normed = hat.buffer[...] * small[GAIN_ONE : GAIN_ONE + 1] + small[OFFSET_ONE : OFFSET_ONE + 1]
    unit, root = standardize(total[...] + normed + small[B_DOWN : B_DOWN + 1])
    y.buffer[...] = (unit * small[GAIN_TWO : GAIN_TWO + 1] + small[OFFSET_TWO : OFFSET_TWO + 1]).astype(BF16)
    y.flush(move)
    two.buffer[...] = unit
    two.flush(move)
    scale.buffer[...] = jnp.broadcast_to(root, scale.buffer.shape)
    scale.flush(move)
    move.finish()


def down_forward(layer, sec, act, wd, wd_other, hat, small, y_kind, two_kind):
    blocks, rows, width = act.shape
    wide = (rows, width)
    return call(
        functools.partial(down_kernel, layer),
        sec,
        [(act, NEAR), (wd, RAW), (wd_other, FREE if layer == 0 else RAW), (hat, NEAR), (small, FAR)],
        [(sds(wide, BF16), y_kind), (sds(wide, F32), two_kind), (sds((rows, 128), F32), two_kind)],
        [((blocks, width, width), BF16), (wide, F32)],
        "down_forward",
        2 * rows * width * width * blocks,
        12 << 20,
    )


def up_down_steps(
    move, layer, sec, x, ctx, wo_a, wo_b, wu_a, wu_b, wd_a, wd_b, small,
    hat, scale, turned, act, slope, y, two, scale_two, wo, wu, wd, low, total,
):
    mine = sec[0] == layer
    blocks, _, wide = wu.shape
    waits = ctx.fetch(move) + [move.choose(mine, wo_a.ref, wo_b.ref, wo)] + small.fetch(move) + x.fetch(move)
    ups, downs = [], []
    for i in range(blocks):
        span = pl.ds(i * wide, wide)
        ups.append(move.choose(mine, wu_a.ref.at[:, span], wu_b.ref.at[:, span], wu.at[i]))
        downs.append(move.choose(mine, wd_a.ref.at[span], wd_b.ref.at[span], wd.at[i]))
    yield
    ready(waits)
    small = small.buffer
    summed = x.buffer[...].astype(F32) + t_dot(ctx.buffer[...], wo[...]) + small[B_OUT : B_OUT + 1]
    unit, root = standardize(summed)
    hat.buffer[...] = unit
    hat.flush(move)
    scale.buffer[...] = jnp.broadcast_to(root, scale.buffer.shape)
    scale.flush(move)
    normed = unit * small[GAIN_ONE : GAIN_ONE + 1] + small[OFFSET_ONE : OFFSET_ONE + 1]
    total[...] = normed + small[B_DOWN : B_DOWN + 1]
    low[...] = normed.astype(BF16)
    turned.buffer[...] = low[...].T
    turned.flush(move)
    for i in range(blocks):
        ups[i].wait()
        pre = dot(low[...], wu[i]) + small[B_UP + i : B_UP + i + 1]
        share, bell = gauss_share(pre)
        act.buffer[i] = (pre * share).astype(BF16)
        slope.buffer[i] = share + pre * 0.3989422804014327 * bell
        slope.flush(move, i)
        downs[i].wait()
        total[...] += dot(act.buffer[i], wd[i])
    unit, root = standardize(total[...])
    y.buffer[...] = (unit * small[GAIN_TWO : GAIN_TWO + 1] + small[OFFSET_TWO : OFFSET_TWO + 1]).astype(BF16)
    y.flush(move)
    two.buffer[...] = unit
    scale_two.buffer[...] = jnp.broadcast_to(root, scale_two.buffer.shape)


def down_grad_steps(move, sec, gy, hat, scale, small, act, second, branch, sums, send, keep, turned):
    blocks = act.buffer.shape[0]
    low_rows, wide = send.buffer.shape[1], act.buffer.shape[2]
    tall = 2 * low_rows
    waits = gy.fetch(move) + small.fetch(move) + scale.fetch(move) + hat.fetch(move)
    parts = [act.fetch(move, i) for i in range(blocks)]
    yield
    ready(waits)
    grad = gy.buffer[...].astype(F32)
    sums.buffer[0:1] = column_sum(grad * hat.buffer[...])
    sums.buffer[1:2] = column_sum(grad)
    unit = norm_back(grad, hat.buffer[...], scale.buffer[:, 0:1], small.buffer[GAIN_TWO : GAIN_TWO + 1])
    second.buffer[...] = unit
    second.flush(move)
    low = unit.astype(BF16)
    branch.buffer[...] = low
    branch.flush(move)
    sums.buffer[2:3] = column_sum(low.astype(F32))
    sums.buffer[3:] = jnp.zeros_like(sums.buffer[3:])
    sums.flush(move)
    turned[...] = branch.buffer[...].T
    for half, out in ((1 - sec[0], send), (sec[0], keep)):
        left = pl.ds(pl.multiple_of(half * tall, tall), tall)
        for i in range(blocks):
            if out is send:
                ready(parts[i])
            block = dot(turned[left, :], act.buffer[i]).astype(BF16)
            out.buffer[i, :, :wide] = block[:low_rows]
            out.buffer[i, :, wide:] = block[low_rows:]
            out.flush(move, i)


def down_grad_kernel(sec, *refs):
    move = Mover(refs[-1])
    run(down_grad_steps(move, sec, *refs[:-1]))
    move.finish()


def down_grad(sec, gy, gy_kind, hat, scale, small, act, kind):
    rows, width = gy.shape
    blocks = act.shape[0]
    wide = (rows, width)
    part = sds((blocks, width // 4, 2 * width), BF16)
    return call(
        down_grad_kernel,
        sec,
        [(gy, gy_kind), (hat, kind), (scale, kind), (small, FAR), (act, kind)],
        [(sds(wide, F32), NEAR), (sds(wide, BF16), NEAR), (sds((8, width), F32), NEAR), (part, NEAR), (part, FAR if kind == NEAR else NEAR)],
        [((width, rows), BF16)],
        "down_grad",
        2 * rows * width * width * blocks,
        14 << 20,
    )


def up_grad_kernel(layer, last, sec, *refs):
    refs = list(refs)
    take = lambda count: [refs.pop(0) for _ in range(count)]
    branch, base, wd_a, wd_b, slope_h, low, wu_a, wu_b = take(8)
    if last:
        hat, scale, small, sums_in = take(4)
        first, attend, sums, out = take(4)
    else:
        first, sums, out = take(3)
    wd, wu, slope, pre, sems = refs
    move = Mover(sems)
    mine = sec[0] == layer
    half, wide, _ = wd.shape
    side = sec[0] if last else 1 - sec[0]
    at = [side * half + i for i in range(half)]
    span = [pl.ds(pl.multiple_of(place * wide, wide), wide) for place in at]
    parts = []
    early = branch.fetch(move)
    for i in range(half):
        move.load(slope_h.ref.at[at[i]], slope.at[i])
        parts.append(
            [
                move.last,
                move.choose(mine, wd_a.ref.at[span[i]], wd_b.ref.at[span[i]], wd.at[i]),
                move.choose(mine, wu_a.ref.at[:, span[i]], wu_b.ref.at[:, span[i]], wu.at[i]),
            ]
        )
        if i == 0:
            early += low.fetch(move)
    late = base.fetch(move)
    if last:
        late += hat.fetch(move) + scale.fetch(move) + small.fetch(move)
        sums.buffer[...] = sums_in.buffer[...]
    else:
        sums.buffer[...] = jnp.zeros_like(sums.buffer)
    ready(early)
    total = first.buffer
    shards, tall, _ = out.buffer.shape
    for i in range(half):
        ready(parts[i])
        pre[...] = (dot_t(branch.buffer[...], wd[i]) * slope[i]).astype(BF16)
        sums.buffer[pl.ds(3 + at[i], 1)] = column_sum(pre[...].astype(F32))
        block = dot(low.buffer[...], pre[...]).astype(BF16)
        for shard in range(shards):
            out.buffer[shard, :, i * wide : i * wide + wide] = block[shard * tall : shard * tall + tall]
        if i == 0:
            ready(late)
            total[...] = base.buffer[...] + dot_t(pre[...], wu[i])
        else:
            total[...] += dot_t(pre[...], wu[i])
    if last:
        grad = total[...]
        sums.buffer[0:1] = column_sum(grad * hat.buffer[...])
        sums.buffer[1:2] = column_sum(grad)
        unit = norm_back(grad, hat.buffer[...], scale.buffer[:, 0:1], small.buffer[GAIN_ONE : GAIN_ONE + 1])
        attend.buffer[...] = unit.astype(BF16)
        total[...] = unit
        sums.buffer[2:3] = column_sum(attend.buffer[...].astype(F32))
    move.finish()


def up_grad(layer, last, sec, branch, base, wd, wd_other, slope, low, wu, wu_other, shards, more=()):
    blocks, rows, width = slope.shape
    half = blocks // 2
    wide = (rows, width)
    part = sds((shards, width // shards, half * width), BF16)
    square = ((half, width, width), BF16)
    near = lambda *shapes: [(shape, NEAR) for shape in shapes]
    ins = [
        (branch, NEAR),
        (base, NEAR),
        (wd, RAW),
        (wd_other, RAW),
        (slope, RAW),
        (low, FAR),
        (wu, RAW),
        (wu_other, RAW),
    ]
    if last:
        hat, scale, small, sums = more
        ins += [(hat, FAR), (scale, FAR), (small, FAR), (sums, NEAR)]
        outs = near(sds(wide, F32), sds(wide, BF16), sds((8, width), F32), part)
    else:
        outs = near(sds(wide, F32), sds((8, width), F32), part)
    return call(
        functools.partial(up_grad_kernel, layer, last),
        sec,
        ins,
        outs,
        [square, square, ((half,) + wide, F32), (wide, BF16)],
        "up_grad_last" if last else "up_grad_first",
        3 * rows * width * width * blocks,
        15 << 20,
    )


def attend_grad_kernel(layer, last, sec, *refs):
    refs = list(refs)
    take = lambda count: [refs.pop(0) for _ in range(count)]
    attend, ctx, base, x, q_h, k_h, v_h, p_h, wo_a, wo_b, w_a, w_b, down, up = take(14)
    if last:
        gx, gx_low, out = take(3)
    else:
        total, turned, out = take(3)
    q, k, v, probs, wo, w, gc, grads, sems = refs
    move = Mover(sems)
    mine = sec[0] == layer
    rows_all, wide = q.shape
    width = 2 * wide
    seqs = probs.shape[0]
    shards = out.buffer.shape[0]
    tall = width // shards
    pairs = wide // 128
    side = sec[0] if last else 1 - sec[0]
    lanes_half = pl.ds(pl.multiple_of(side * wide, wide), wide)
    waits = attend.fetch(move) + [move.choose(mine, wo_a.ref.at[lanes_half], wo_b.ref.at[lanes_half], wo)]
    near = []
    for source, target in (
        (p_h.ref.at[:, pl.ds(side * pairs, pairs)], probs),
        (v_h.ref.at[:, lanes_half], v),
        (k_h.ref.at[:, lanes_half], k),
        (q_h.ref.at[:, lanes_half], q),
    ):
        move.load(source, target)
        near.append(move.last)
    later = x.fetch(move) + ctx.fetch(move) + down.fetch(move) + up.fetch(move)
    finals = base.fetch(move)
    for i in range(3):
        there = pl.ds(pl.multiple_of(i * width + side * wide, wide), wide)
        finals.append(move.choose(mine, w_a.ref.at[:, there], w_b.ref.at[:, there], w.at[:, pl.ds(i * wide, wide)]))
    ready(waits)
    gc[...] = dot_t(attend.buffer[...], wo[...]).astype(BF16)
    ready(near)
    halves = lane_halves()
    lower = lax.broadcasted_iota(jnp.int32, (128, 128), 1) < 64

    for pair in range(pairs):
        lanes = slice(pair * 128, pair * 128 + 128)
        for seq in range(seqs):
            rows = slice(seq * 128, seq * 128 + 128)

            def put(part, value):
                grads[rows, part * wide + pair * 128 : part * wide + pair * 128 + 128] = value.astype(BF16)

            grad = gc[rows, lanes]
            p = probs[seq, pair]
            full = dot(p.astype(BF16), grad)
            put(2, jnp.where(lower, full[:128], full[128:]))
            gp = dot_t(two_heads(v[rows, lanes], halves), grad)
            parts = []
            for part in (slice(0, 128), slice(128, 256)):
                g, pp = gp[part], p[part]
                parts.append(pp * (g - jnp.sum(g * pp, axis=0, keepdims=True)))
            gs = jnp.concatenate(parts, axis=0).astype(BF16)
            put(0, t_dot(gs, two_heads(k[rows, lanes] * SCALE, halves)))
            full = dot(gs, q[rows, lanes] * SCALE)
            put(1, jnp.where(lower, full[:128], full[128:]))
    ready(later)
    if last:
        turned = x
    else:
        turned.buffer[...] = x.buffer[...].T
    left = dot(turned.buffer[...], grads[...]).astype(BF16)
    right = dot(ctx.buffer[...], attend.buffer[:, lanes_half]).astype(BF16)
    little = jnp.concatenate([down.buffer[...], up.buffer[...]], axis=0).astype(BF16)
    zeros = jnp.zeros_like(little)
    b_q = column_sum(grads[:, 0:wide].astype(F32)).astype(BF16)
    b_v = column_sum(grads[:, 2 * wide :].astype(F32)).astype(BF16)
    pad = jnp.concatenate([b_q, b_v], axis=1)
    pad = jnp.concatenate([pad, jnp.zeros((15, width), BF16)], axis=0)
    for shard in range(shards):
        out.buffer[shard, :tall, 0 : 3 * wide] = left[shard * tall : shard * tall + tall]
        out.buffer[shard, :tall, 3 * wide :] = right[shard * tall : shard * tall + tall]
        out.buffer[shard, tall:, 0:width] = little
        out.buffer[shard, tall:, width:] = pad
    ready(finals)
    sum_all = base.buffer[...] + dot_t(grads[...], w[...])
    if last:
        gx.buffer[...] = sum_all
        gx.flush(move)
        gx_low.buffer[...] = sum_all.astype(BF16)
        gx_low.flush(move)
    else:
        total.buffer[...] = sum_all
    move.finish()


def attend_grad(layer, last, sec, attend, ctx, base, x, q, k, v, probs, wo, wo_other, w, w_other, down, up, shards, low_kind):
    rows, width = attend.shape
    seqs = probs.shape[0]
    wide = width // 2
    flat = (rows, width)
    part = (sds((shards, width // shards + 16, 2 * width), BF16), NEAR)
    if last:
        outs = [(sds(flat, F32), FAR), (sds(flat, BF16), low_kind), part]
    else:
        outs = [(sds(flat, F32), NEAR), (sds((width, rows), BF16), NEAR), part]
    half = ((rows, wide), BF16)
    return call(
        functools.partial(attend_grad_kernel, layer, last),
        sec,
        [(attend, NEAR), (ctx, FAR), (base, NEAR), (x, NEAR if last else FAR)]
        + [(item, RAW) for item in (q, k, v, probs, wo, wo_other, w, w_other)]
        + [(down, NEAR), (up, NEAR)],
        outs,
        [
            half,
            half,
            half,
            ((seqs, wide // 128) + probs.shape[2:], F32),
            ((wide, width), BF16),
            ((width, 3 * wide), BF16),
            half,
            ((rows, 3 * wide), BF16),
        ],
        "attend_grad_last" if last else "attend_grad_first",
        rows * width * width * 10,
        15 << 20,
    )


def second_kernel(sec, *refs):
    refs = list(refs)
    take = lambda count: [refs.pop(0) for _ in range(count)]
    inside = lambda item: Operand(None, item, False)
    x, w_a, w_b, small, mask = take(5)
    weights, (gy,) = take(6), take(1)
    q, k, v, probs, ctx, hat, scale, turned, slope, y = take(10)
    second, branch, sums, send, keep = take(5)
    w, wo, wu, wd, low, total, act, two, scale_two, branch_turned, sems = refs
    move = Mover(sems)
    near = inside(small.buffer)
    act, two, scale_two = inside(act), inside(two), inside(scale_two)
    run(
        attend_steps(move, 1, sec, x, w_a, w_b, small, mask, q, k, v, probs, ctx, w),
        up_down_steps(
            move, 1, sec, x, inside(ctx.buffer), *weights, near,
            hat, scale, turned, act, slope, y, two, scale_two, wo, wu, wd, low, total,
        ),
        down_grad_steps(move, sec, gy, two, scale_two, near, act, second, branch, sums, send, keep, branch_turned),
    )
    move.finish()


def second_layer(sec, x, mask, big, other, small, gy):
    rows, width = x.shape
    seqs = mask.shape[1]
    pairs = width // 128
    (w, w_other), (wo, wo_other), (wu, wu_other), (wd, wd_other) = zip(big, other)
    blocks = wu.shape[1] // width
    wide = (rows, width)
    part = sds((blocks, width // 4, 2 * width), BF16)
    square = lambda count: ((count, width, width), BF16)
    return call(
        second_kernel,
        sec,
        [(x, NEAR), (w, RAW), (w_other, RAW), (small, FAR), (mask, FAR)]
        + [(item, RAW) for item in (wo, wo_other, wu, wu_other, wd, wd_other)]
        + [(gy, FAR)],
        [(sds(wide, BF16), FAR)] * 3
        + [
            (sds((seqs, pairs, 256, 128), F32), FAR),
            (sds((width, rows), BF16), FAR),
            (sds(wide, F32), FAR),
            (sds((rows, 128), F32), FAR),
            (sds((width, rows), BF16), FAR),
            (sds((blocks,) + wide, F32), FAR),
            (sds(wide, BF16), FAR),
            (sds(wide, F32), NEAR),
            (sds(wide, BF16), NEAR),
            (sds((8, width), F32), NEAR),
            (part, NEAR),
            (part, FAR),
        ],
        [
            square(3),
            ((width, width), BF16),
            square(blocks),
            square(blocks),
            (wide, BF16),
            (wide, F32),
            ((blocks,) + wide, BF16),
            (wide, F32),
            ((rows, 128), F32),
            ((width, rows), BF16),
        ],
        "second_layer",
        2 * rows * width * width * (3 * blocks + 5),
        50 << 20,
    )


def up_whole_kernel(
    layer, sec, branch, second, wd_a, wd_b, slope, low, wu_a, wu_b, hat, scale, small,
    first, attend, sums, send, keep, wd, wu, pre, sems,
):
    move = Mover(sems)
    mine = sec[0] == layer
    blocks, wide, _ = wd.shape
    half = blocks // 2
    at = [lax.rem(i + half * (1 - sec[0]), blocks) for i in range(blocks)]
    span = [pl.ds(pl.multiple_of(place * wide, wide), wide) for place in at]
    parts = []
    early = branch.fetch(move)
    for i in range(blocks):
        parts.append(
            [move.choose(mine, wd_a.ref.at[span[i]], wd_b.ref.at[span[i]], wd.at[i])]
            + slope.fetch(move, at[i])
            + [move.choose(mine, wu_a.ref.at[:, span[i]], wu_b.ref.at[:, span[i]], wu.at[i])]
        )
        if i == 0:
            early += low.fetch(move)
    late = second.fetch(move) + hat.fetch(move) + scale.fetch(move) + small.fetch(move)
    ready(early)
    branch, low, total = branch.buffer, low.buffer, first.buffer
    for i in range(blocks):
        ready(parts[i])
        pre[...] = (dot_t(branch[...], wd[i]) * slope.buffer[at[i]]).astype(BF16)
        sums.buffer[pl.ds(3 + at[i], 1)] = column_sum(pre[...].astype(F32))
        out, place = (send, i) if i < half else (keep, i - half)
        block = dot(low[...], pre[...]).astype(BF16)
        shards, tall, _ = out.buffer.shape
        for shard in range(shards):
            out.buffer[shard, :, place * wide : place * wide + wide] = block[shard * tall : shard * tall + tall]
        if i == 0:
            ready(late)
            total[...] = second.buffer[...] + dot_t(pre[...], wu[i])
        else:
            total[...] += dot_t(pre[...], wu[i])
    grad = total[...]
    sums.buffer[0:1] = column_sum(grad * hat.buffer[...])
    sums.buffer[1:2] = column_sum(grad)
    unit = norm_back(grad, hat.buffer[...], scale.buffer[:, 0:1], small.buffer[GAIN_ONE : GAIN_ONE + 1])
    attend.buffer[...] = unit.astype(BF16)
    attend.flush(move)
    total[...] = unit
    first.flush(move)
    sums.buffer[2:3] = column_sum(attend.buffer[...].astype(F32))
    sums.buffer[3 + blocks :] = jnp.zeros_like(sums.buffer[3 + blocks :])
    sums.flush(move)
    move.finish()


def up_whole(layer, sec, branch, second, wd, wd_other, slope, low, wu, wu_other, hat, scale, small, shards):
    blocks, rows, width = slope.shape
    wide = (rows, width)
    part = sds((shards, width // shards, blocks * width // 2), BF16)
    square = ((blocks, width, width), BF16)
    return call(
        functools.partial(up_whole_kernel, layer),
        sec,
        [
            (branch, NEAR),
            (second, NEAR),
            (wd, RAW),
            (wd_other, RAW),
            (slope, FAR),
            (low, FAR),
            (wu, RAW),
            (wu_other, RAW),
            (hat, FAR),
            (scale, FAR),
            (small, FAR),
        ],
        [(sds(wide, F32), NEAR), (sds(wide, BF16), NEAR), (sds((8, width), F32), NEAR), (part, NEAR), (part, NEAR)],
        [square, square, (wide, BF16)],
        "up_grad",
        6 * rows * width * width * blocks,
        30 << 20,
    )


def attend_whole_kernel(
    layer, shards, sec, attend, ctx, first, x, q, k, v, probs, wo_a, wo_b, w_a, w_b, down, up,
    gx, gx_low, send, keep, turned, wo, w, gc, grads, sems,
):
    move = Mover(sems)
    mine = sec[0] == layer
    rows_all, width = x.buffer.shape
    seqs = probs.buffer.shape[0]
    wide = width // 2
    tall = width // shards
    pairs = wide // 128
    waits = attend.fetch(move) + [move.choose(mine, wo_a.ref, wo_b.ref, wo)]
    near = probs.fetch(move) + v.fetch(move) + k.fetch(move) + q.fetch(move)
    later = x.fetch(move) + ctx.fetch(move) + down.fetch(move) + up.fetch(move)
    last = [
        move.choose(
            mine,
            w_a.ref.at[:, pl.ds(i * width + half * wide, wide)],
            w_b.ref.at[:, pl.ds(i * width + half * wide, wide)],
            w.at[:, pl.ds((3 * half + i) * wide, wide)],
        )
        for i in range(3)
        for half in range(2)
    ] + first.fetch(move)
    ready(waits)
    attend, q, k, v, probs = (item.buffer for item in (attend, q, k, v, probs))
    gc[...] = dot_t(attend[...], wo[...]).astype(BF16)
    ready(near)
    halves = lane_halves()
    lower = lax.broadcasted_iota(jnp.int32, (128, 128), 1) < 64

    def attention(half):
        @pl.loop(0, pairs)
        def _(index):
            lanes = pl.ds(pl.multiple_of(half * wide + index * 128, 128), 128)

            def put(part, rows, value):
                there = pl.ds(pl.multiple_of((3 * half + part) * wide + index * 128, 128), 128)
                grads[rows, there] = value.astype(BF16)

            for seq in range(seqs):
                rows = slice(seq * 128, seq * 128 + 128)
                grad = gc[rows, lanes]
                p = probs[seq, half * pairs + index]
                full = dot(p.astype(BF16), grad)
                put(2, rows, jnp.where(lower, full[:128], full[128:]))
                gp = dot_t(two_heads(v[rows, lanes], halves), grad)
                parts = []
                for side in (slice(0, 128), slice(128, 256)):
                    g, pp = gp[side], p[side]
                    parts.append(pp * (g - jnp.sum(g * pp, axis=0, keepdims=True)))
                gs = jnp.concatenate(parts, axis=0).astype(BF16)
                put(0, rows, t_dot(gs, two_heads(k[rows, lanes] * SCALE, halves)))
                full = dot(gs, q[rows, lanes] * SCALE)
                put(1, rows, jnp.where(lower, full[:128], full[128:]))

    def products(half, out):
        three = pl.ds(pl.multiple_of(half * 3 * wide, 128), 3 * wide)
        lanes = pl.ds(pl.multiple_of(half * wide, wide), wide)
        block = dot(turned[...], grads[:, three]).astype(BF16)
        block_out = dot(ctx.buffer[...], attend[:, lanes]).astype(BF16)
        for shard in range(shards):
            out.buffer[shard, :tall, : 3 * wide] = block[shard * tall : shard * tall + tall]
            out.buffer[shard, :tall, 3 * wide :] = block_out[shard * tall : shard * tall + tall]

    attention(1 - sec[0])
    ready(later)
    turned[...] = x.buffer[...].T
    products(1 - sec[0], send)
    attention(sec[0])
    products(sec[0], keep)
    little = jnp.concatenate([down.buffer[...], up.buffer[...]], axis=0).astype(BF16)
    for half, out in ((1 - sec[0], send), (sec[0], keep)):
        pad = []
        for part in (0, 2):
            lanes = pl.ds(pl.multiple_of((3 * half + part) * wide, wide), wide)
            pad.append(column_sum(grads[:, lanes].astype(F32)).astype(BF16))
        pad = jnp.concatenate([jnp.concatenate(pad, axis=1), jnp.zeros((15, width), BF16)], axis=0)
        for shard in range(shards):
            out.buffer[shard, tall:, 0:width] = little
            out.buffer[shard, tall:, width:] = pad
    ready(last)
    total = first.buffer[...] + dot_t(grads[...], w[...])
    gx.buffer[...] = total
    gx.flush(move)
    gx_low.buffer[...] = total.astype(BF16)
    gx_low.flush(move)
    move.finish()


def attend_whole(layer, sec, attend, ctx, first, x, q, k, v, probs, wo, wo_other, w, w_other, down, up, shards, low_kind):
    rows, width = x.shape
    wide = (rows, width)
    part = sds((shards, width // shards + 16, 2 * width), BF16)
    return call(
        functools.partial(attend_whole_kernel, layer, shards),
        sec,
        [(attend, NEAR), (ctx, FAR), (first, NEAR)]
        + [(item, FAR) for item in (x, q, k, v, probs)]
        + [(wo, RAW), (wo_other, RAW), (w, RAW), (w_other, RAW), (down, NEAR), (up, NEAR)],
        [(sds(wide, F32), FAR), (sds(wide, BF16), low_kind), (part, NEAR), (part, NEAR)],
        [((width, rows), BF16), ((width, width), BF16), ((width, 3 * width), BF16), (wide, BF16), ((rows, 3 * width), BF16)],
        "attend_grad",
        2 * rows * width * width * 10,
        30 << 20,
    )


def layer_forward(layer, sec, x, front, big, other, small, far=None):
    w_qkv, w_out, w_up, w_down = big
    o_qkv, o_out, o_up, o_down = other
    x_kind = FAR if layer == 0 else NEAR
    q, k, v, probs, (ctx_near, ctx) = front
    (hat_near, hat_one), scale_one, low, act, slope = up_forward(
        layer, sec, x, x_kind, ctx_near, w_out, o_out, w_up, o_up, small
    )
    act_near, act = act if layer == 0 else (act, act)
    kinds = (BOTH, FAR) if layer == 0 else (FAR, NEAR)
    y, hat_two, scale_two = down_forward(layer, sec, act_near, w_down, o_down, hat_near, small, *kinds)
    x = x if far is None else far
    return y, (x, q, k, v, probs, ctx, hat_one, scale_one, low, act, slope, hat_two, scale_two)


class Backward:
    def __init__(self, line, layer, sec, cache, big, other, small, shards):
        self.line, self.layer, self.sec, self.small, self.shards = line, layer, sec, small, shards
        self.cache, self.weights, self.made = cache, tuple(zip(big, other)), {}

    def down(self, gy):
        act, _, hat_two, scale_two = self.cache[-4:]
        kinds = (NEAR, FAR) if self.layer == 0 else (FAR, NEAR)
        second, branch, sums, send, keep = down_grad(
            self.line.sec, gy, kinds[0], hat_two, scale_two, self.small, act, kinds[1]
        )
        self.made.update(second=second, branch=branch, down_sums=sums)
        self.line.add(send, keep)

    def up_inputs(self):
        (w_up, o_up), (w_down, o_down) = self.weights[2:]
        low, _, slope = self.cache[-5:-2]
        return w_down, o_down, slope, low, w_up, o_up, self.shards

    def up_first(self):
        made = self.made
        made["part"], made["up_sums"], send = up_grad(
            self.layer, False, self.line.sec, made["branch"], made["second"], *self.up_inputs()
        )
        self.up_chunk = self.line.add(send, None)

    def up_last(self):
        made = self.made
        hat_one, scale_one = self.cache[-7:-5]
        more = (hat_one, scale_one, self.small, made["up_sums"])
        made["first"], made["attend"], made["up_sums"], self.up_chunk.keep = up_grad(
            self.layer, True, self.line.sec, made["branch"], made["part"], *self.up_inputs(), more
        )

    def up(self):
        made = self.made
        hat_one, scale_one = self.cache[-7:-5]
        ins = self.up_inputs()
        made["first"], made["attend"], made["up_sums"], send, keep = up_whole(
            self.layer, self.line.sec, made["branch"], made["second"], *ins[:-1], hat_one, scale_one, self.small, ins[-1]
        )
        self.line.add(send, keep)

    def attention(self):
        made = self.made
        made["gx"], made["gx_low"], send, keep = attend_whole(
            self.layer, self.line.sec, made["attend"], self.cache[5], made["first"], self.cache[0], *self.heads()
        )
        self.line.add(send, keep)

    def heads(self):
        q, k, v, probs = self.cache[1:5]
        (w_qkv, o_qkv), (w_out, o_out) = self.weights[:2]
        low_kind = FAR if self.layer == 0 else BOTH
        sums = (self.made["down_sums"], self.made["up_sums"])
        return (q, k, v, probs, w_out, o_out, w_qkv, o_qkv) + sums + (self.shards, low_kind)

    def attend_first(self):
        made = self.made
        made["part"], made["turned"], send = attend_grad(
            self.layer, False, self.line.sec, made["attend"], self.cache[5], made["first"], self.cache[0], *self.heads()
        )
        self.attend_chunk = self.line.add(send, None)

    def attend_last(self):
        made = self.made
        made["gx"], made["gx_low"], self.attend_chunk.keep = attend_grad(
            self.layer, True, self.line.sec, made["attend"], self.cache[5], made["part"], made["turned"], *self.heads()
        )


def exchange(array, axis, bit):
    length = lax.axis_size(axis)
    return lax.ppermute(array, axis, [(i, i ^ bit) for i in range(length)])


def pick(array, index, axis):
    return lax.dynamic_index_in_dim(array, index, axis, keepdims=False)


def split_at(rows):
    return (rows // 2 + 15) // 16 * 16


class Sums:
    def __init__(self, columns):
        self.columns, self.ins, self.outs, self.code = columns, [], [], []
        self.rows, self.far, self.later = {}, set(), []

    def use(self, array):
        for index, known in enumerate(self.ins):
            if known is array:
                return index
        self.ins.append(array)
        return len(self.ins) - 1

    def result(self, shape):
        self.outs.append(sds(tuple(shape) + (self.columns,), BF16))
        return len(self.outs) - 1

    def region(self, way, rows):
        first = self.rows.get(way, 0)
        self.rows[way] = first + rows
        return first

    def run(self, ids):
        ways = sorted(self.rows)
        shapes = self.outs + [sds((self.rows[way], self.columns), BF16) for way in ways]
        n_in, n_out = len(self.ins), len(self.outs)

        far = sorted(self.far)
        space = lambda index: pltpu.HBM if index in self.far else pltpu.VMEM

        def kernel(ids_ref, *refs):
            first = n_in + len(shapes)
            sends = dict(zip(ways, refs[n_in + n_out : first]))
            ins, move = list(refs[:n_in]), Mover(refs[-1])
            waits = []
            for index, buffer in zip(far, refs[first:-1]):
                move.load(ins[index], buffer)
                waits.append(move.last)
                ins[index] = buffer
            for code in self.code:
                code(ids_ref, ins, refs[n_in : n_in + n_out], sends)
            ready(waits)
            for code in self.later:
                code(ids_ref, ins, refs[n_in : n_in + n_out], sends)

        vmem = pl.BlockSpec(memory_space=pltpu.VMEM)
        results = pl.pallas_call(
            kernel,
            in_specs=[pl.BlockSpec(memory_space=pltpu.SMEM)]
            + [pl.BlockSpec(memory_space=space(index)) for index in range(n_in)],
            out_specs=[vmem] * len(shapes),
            out_shape=shapes,
            scratch_shapes=[pltpu.VMEM(self.ins[index].shape, BF16) for index in far]
            + [pltpu.SemaphoreType.DMA((8,))],
            compiler_params=pltpu.CompilerParams(vmem_limit_bytes=SPARE),
            name="join_sums",
        )(
            ids,
            *(pltpu.with_memory_space_constraint(array, space(index)) for index, array in enumerate(self.ins)),
        )
        return results[:n_out], dict(zip(ways, results[n_out:]))


def at_rows(first, index, count):
    return pl.ds(pl.multiple_of(first + index * count, 16), count)


def sum_section(sums, chunk):
    kept, got = sums.use(chunk.keep), sums.use(chunk.got["section"])
    if chunk.far:
        sums.far |= {kept, got}
    _, rows, _ = chunk.keep.shape
    cut = chunk.cut
    rest = rows - cut
    top, bottom = sums.result((2, cut)), sums.result((2, rest))
    chunk.first = {"x": sums.region("x", 2 * cut), "y": sums.region("y", 2 * rest)}
    to_x, to_y = chunk.first["x"], chunk.first["y"]

    def code(ids, ins, outs, sends):
        low, high = ids[1], ids[2]
        for i in range(2):
            add = lambda shard, lines: ins[kept][shard, lines] + ins[got][shard, lines]
            sends["x"][to_x + i * cut : to_x + i * cut + cut] = add(2 * i + 1 - low, slice(0, cut))
            outs[top][i] = add(2 * i + low, slice(0, cut))
            sends["y"][to_y + i * rest : to_y + i * rest + rest] = add(2 * (1 - high) + i, slice(cut, rows))
            outs[bottom][i] = add(2 * high + i, slice(cut, rows))

    (sums.later if chunk.far else sums.code).append(code)
    return [top, bottom]


def sum_first(sums, chunk):
    top, bottom = (sums.use(item) for item in chunk.kept)
    got_x, got_y = sums.use(chunk.got["x"]), sums.use(chunk.got["y"])
    at_x, at_y = chunk.first["x"], chunk.first["y"]
    cut, rest = chunk.kept[0].shape[1], chunk.kept[1].shape[1]
    new_top, new_bottom = sums.result((cut,)), sums.result((rest,))
    chunk.first = {"y": sums.region("y", cut), "x": sums.region("x", rest)}
    to_x, to_y = chunk.first["x"], chunk.first["y"]

    def code(ids, ins, outs, sends):
        low, high = ids[1], ids[2]
        upper = lambda i: ins[top][i] + ins[got_x][at_rows(at_x, i, cut)]
        lower = lambda i: ins[bottom][i] + ins[got_y][at_rows(at_y, i, rest)]
        sends["y"][to_y : to_y + cut] = upper(1 - high)
        outs[new_top][...] = upper(high)
        sends["x"][to_x : to_x + rest] = lower(1 - low)
        outs[new_bottom][...] = lower(low)

    sums.code.append(code)
    return [new_top, new_bottom]


def sum_second(sums, chunk):
    top, bottom = (sums.use(item) for item in chunk.kept)
    got_x, got_y = sums.use(chunk.got["x"]), sums.use(chunk.got["y"])
    at_x, at_y = chunk.first["x"], chunk.first["y"]
    cut, rest = chunk.kept[0].shape[0], chunk.kept[1].shape[0]
    part = sums.result((cut + rest,))
    onward = chunk.line.short
    if onward:
        sums.rows["ends"] = max(sums.rows.get("ends", 0), cut + rest)

    def code(ids, ins, outs, sends):
        outs[part][:cut] = ins[top][...] + ins[got_y][at_y : at_y + cut]
        outs[part][cut:] = ins[bottom][...] + ins[got_x][at_x : at_x + rest]
        if onward:

            @pl.when(ids[3] == 1)
            def _():
                sends["ends"][: cut + rest] = outs[part][...]

    sums.code.append(code)
    return [part]


def sum_ends(sums, chunk):
    part, got = sums.use(chunk.kept[0]), sums.use(chunk.got["ends"])
    rows = chunk.kept[0].shape[0]
    chunk.first = {"middle": sums.region("middle", rows)}
    to = chunk.first["middle"]

    def code(ids, ins, outs, sends):
        sends["middle"][to : to + rows] = ins[part][...] + ins[got][:rows]

    sums.code.append(code)
    return []


def sum_middle(sums, chunk):
    sent, got = sums.use(chunk.sent["middle"]), sums.use(chunk.got["middle"])
    at, rows = chunk.first["middle"], chunk.rows
    whole = sums.result((rows,))
    sums.rows["ends"] = max(sums.rows.get("ends", 0), rows)

    def code(ids, ins, outs, sends):
        outs[whole][...] = ins[sent][at : at + rows] + ins[got][at : at + rows]

        @pl.when(ids[3] == 0)
        def _():
            sends["ends"][:rows] = outs[whole][...]

    sums.code.append(code)
    return [whole]


def sum_last(sums, chunk):
    whole, got = sums.use(chunk.kept[0]), sums.use(chunk.got["ends"])
    rows = chunk.rows
    results = [sums.result((rows,))]
    if chunk.partner is not None:
        other = sums.use(chunk.partner.done[0])
        results.append(sums.result((rows,)))

    def code(ids, ins, outs, sends):
        def put(value, outer):
            if chunk.partner is None:
                outs[results[0]][...] = value(slice(None))
                return
            for first, (to_value, to_other) in ((0, results), (1, results[::-1])):

                @pl.when((ids[0] == first) & (ids[3] == outer))
                def _():
                    outs[to_value][...] = value(slice(None))
                    outs[to_other][...] = ins[other][...]

        if chunk.partner is None:
            pl.when(ids[3] == 1)(lambda: put(lambda _: ins[got][:rows], 1))
            pl.when(ids[3] == 0)(lambda: put(lambda _: ins[whole][...], 0))
        else:
            put(lambda _: ins[got][:rows], 1)
            put(lambda _: ins[whole][...], 0)

    sums.code.append(code)
    return results


class Chunk:
    def __init__(self, line, send, keep, partner):
        self.line, self.send, self.keep, self.partner = line, send, keep, partner
        self.at, self.kept, self.got, self.sent, self.done = 0, [], {}, {}, None
        self.rows, self.far = send.shape[1], len(line.chunks) == 0
        self.cut = split_at(self.rows)


class Line:
    def __init__(self, sec):
        self.sec = sec
        self.square = lax.axis_size("inner") == 4
        self.short = lax.axis_size("outer") == 4
        spot, place = lax.axis_index("inner"), lax.axis_index("outer")
        outside = (place == 0) | (place == lax.axis_size("outer") - 1)
        self.ids = jnp.stack([lax.axis_index("section"), spot % 2, spot // 2, outside, spot]).astype(jnp.int32)
        self.chunks, self.made = [], {}
        self.sums = (sum_section, sum_first, sum_second, sum_ends, sum_middle, sum_last)

    def add(self, send, keep):
        count = len(self.chunks)
        chunk = Chunk(self, send, keep, self.chunks[count - 3] if count >= 3 else None)
        self.chunks.append(chunk)
        return chunk

    def move(self, way, array):
        if way == "section":
            return exchange(array, "section", 1)
        if way in ("x", "y"):
            return exchange(array, "inner", 1 if way == "x" else 2)
        return lax.ppermute(array, "outer", [(0, 1), (1, 0), (2, 3), (3, 2)] if way == "ends" else [(1, 2), (2, 1)])

    def advance(self, owner, *works):
        moving = [chunk for chunk in self.chunks if chunk.done is None and chunk.at > 0]
        sends = {}
        if moving and self.square:
            sums = Sums(moving[0].send.shape[-1])
            places = [self.sums[chunk.at - 1](sums, chunk) for chunk in moving]
            outs, sends = sums.run(self.ids)
            for chunk, place in zip(moving, places):
                chunk.kept, chunk.sent = [outs[index] for index in place], sends
        for chunk in moving:
            chunk.at += 1
            if not self.square:
                half = chunk.keep.astype(F32) + chunk.got["section"].astype(F32)
                half = lax.psum_scatter(half.astype(BF16), "inner", scatter_dimension=0, tiled=False)
                chunk.done = [lax.psum(half, "outer")]
            elif chunk.at == 4 and not self.short:
                chunk.done = [lax.psum(chunk.kept[0], "outer")]
            elif chunk.at == 7:
                chunk.done = chunk.kept
        new = [chunk for chunk in self.chunks if chunk.at == 0]
        gots = {way: self.move(way, array) for way, array in sends.items()}
        arrived = [self.move("section", chunk.send) for chunk in new]
        for work in works:
            work()
        fresh = [chunk for chunk in self.chunks if chunk not in new and chunk.at == 0]
        late = [chunk for chunk in self.chunks if chunk.keep is not None and chunk.at == 0]
        owner.made, parts, keeps, gots, arrived = lax.optimization_barrier(
            (owner.made, [chunk.send for chunk in fresh], [chunk.keep for chunk in late], gots, arrived)
        )
        for chunk, part in zip(fresh, parts):
            chunk.send = part
        for chunk, part in zip(late, keeps):
            chunk.keep = part
        for chunk in moving:
            chunk.got = gots
        for chunk, part in zip(new, arrived):
            chunk.at, chunk.got = 1, {"section": part}

    def finish(self):
        while any(chunk.done is None for chunk in self.chunks):
            self.advance(self)
        pairs = []
        for chunk in self.chunks[3:]:
            if len(chunk.done) == 1:
                two, one = chunk.partner.done[0], chunk.done[0]
                mine, send = (jnp.where(self.ids[0] == 0, *item) for item in ((one, two), (two, one)))
            else:
                mine, send = chunk.done
            pairs.append((mine, exchange(send, "section", 1)))
        return pairs


def assemble_kernel(sec, y_one, y_two, y_got, one, two_low, got, y_out, g_out, y, low, wide, sems):
    move = Mover(sems)
    first = sec[0] == 0
    loads = [
        move.choose(first, y_one.ref, y_got.ref, y.at[0]),
        move.choose(first, y_got.ref, y_two.ref, y.at[1]),
        move.choose(first, one.ref, got.ref, wide.at[0]),
    ]
    move.load(two_low.ref, low)
    loads.append(move.last)
    pl.when(first)(lambda: move.choose(first, got.ref, got.ref, wide.at[1]).wait())
    ready(loads)
    move.used += 1

    @pl.when(jnp.logical_not(first))
    def _():
        wide[1] = low[...].astype(F32)

    move.store(y, y_out.ref)
    move.store(wide, g_out.ref)
    move.finish()


def assemble(sec, y_one, y_two, y_got, one, two_low, got):
    flat = one.shape
    return call(
        assemble_kernel,
        sec,
        [(item, RAW) for item in (y_one, y_two, y_got, one, two_low, got)],
        [(sds((2,) + flat, BF16), RAW), (sds((2,) + flat, F32), RAW)],
        [((2,) + flat, BF16), (flat, BF16), ((2,) + flat, F32)],
        "assemble",
        1000,
        10 << 20,
    )


class Rest:
    def __init__(self, sec):
        self.sec, self.made = sec, {}

    def send(self, one, two_low):
        low = two_low.astype(F32)
        self.made["got"] = exchange(jnp.where(self.sec[0] == 0, low, one), "section", 1)

    def assemble(self, y_one, y_two, one, two_low):
        self.made["outs"] = assemble(self.sec, y_one, y_two, self.made["y"], one, two_low, self.made["got"])


def last_kernel(ids, down_mine, down_got, up_mine, up_got, mine, got, w_down, qkv, out, b_qv, b_out, gain, offset, b_up, b_down, w_up, sems):
    move = Mover(sems)
    up_wide = w_up.buffer.shape[1] // 2
    for half, side in ((ids[0], up_mine), (1 - ids[0], up_got)):
        w_up.buffer[:, pl.ds(pl.multiple_of(half * up_wide, up_wide), up_wide)] = side.buffer[...].astype(F32)
    w_up.flush(move)
    hidden, width = w_down.buffer.shape
    for half, side in ((ids[0], down_mine), (1 - ids[0], down_got)):
        rows = jnp.concatenate([side.buffer[:, :hidden], side.buffer[:, hidden:]], axis=0)
        w_down.buffer[:, pl.ds(pl.multiple_of(half * (width // 2), width // 2), width // 2)] = rows.T.astype(F32)
    w_down.flush(move)
    mine, got = mine.buffer, got.buffer
    tall, wide = qkv.buffer.shape[0], out.buffer.shape[1] // 2
    for half, side in ((ids[0], mine), (1 - ids[0], got)):
        for part in range(4):
            block = side[:tall, part * wide : part * wide + wide].astype(F32)
            target, first = (qkv, 2 * part * wide) if part < 3 else (out, 0)
            lanes = pl.ds(pl.multiple_of(first + half * wide, wide), wide)
            target.buffer[:, lanes] = block
    qkv.flush(move)
    out.flush(move)
    rows = mine[tall:, : 2 * wide].astype(F32)
    own, other = (side[tall : tall + 1, 2 * wide :].astype(F32) for side in (mine, got))

    def write(first_half, place):
        left, right = (own, other) if first_half else (other, own)
        span = slice(place * tall, place * tall + tall)
        for row in range(2):
            bias = jnp.concatenate([side[:, row * wide : row * wide + wide] for side in (left, right)], axis=1)
            b_qv.buffer[row : row + 1, :] = bias[:, span]
        b_out.buffer[...] = rows[10:11, span]
        gain.buffer[0:1, :] = rows[8:9, span]
        gain.buffer[1:2, :] = rows[0:1, span]
        offset.buffer[0:1, :] = rows[9:10, span]
        offset.buffer[1:2, :] = rows[1:2, span]
        b_up.buffer[...] = rows[11 + place : 12 + place]
        b_down.buffer[...] = rows[2:3, span]

    for first_half in (True, False):
        for place in range(2 * wide // tall):
            here = (ids[0] == (0 if first_half else 1)) & (ids[4] == place)
            pl.when(here)(functools.partial(write, first_half, place))
    for item in (b_qv, b_out, gain, offset, b_up, b_down):
        item.flush(move)
    move.finish()


def last(ids, down, up, attend, width, shards):
    tall = width // shards
    shapes = [(down[0].shape[1] // 2, width), (tall, 3 * width), (tall, width), (2, tall), (1, tall), (2, tall), (2, tall), (1, width), (1, tall)]
    shapes.append((tall, 2 * up[0].shape[1]))
    return call(
        last_kernel,
        ids,
        [(item, NEAR) for item in (*down, *up, *attend)],
        [(sds(shape, F32), FAR) for shape in shapes],
        [],
        "last",
        1000,
        5 << 20,
    )


def local(
    hidden_in, caption_len, region_len, cotangent, w_qkv, b_qv, w_out, b_out, ln_gain, ln_bias, w_up, b_up, w_down, b_down
):
    section = lax.axis_index("section")
    shards = lax.axis_size("inner")
    sec = section.astype(jnp.int32)[None]
    seqs_local, length, width = hidden_in.shape
    seqs = seqs_local // 2
    rows = seqs * length
    positions = jnp.arange(length, dtype=jnp.int32)[None, :]
    mine = lambda array: lax.dynamic_slice_in_dim(array, section * seqs, seqs, 0)
    caption, region = mine(caption_len)[:, None], mine(region_len)[:, None]
    valid = (positions < caption) | (positions >= CAP) & (positions < CAP + region)
    mask = jnp.concatenate([valid, valid], axis=1).astype(F32).T
    x = mine(hidden_in).reshape(rows, width)
    gy = jnp.where(valid[:, :, None], mine(cotangent), jnp.zeros((), BF16)).reshape(rows, width)

    blocks = w_up.shape[2] // width
    little = jnp.concatenate(
        [b_qv[0], b_out, ln_gain[0], ln_bias[0], b_down, b_up.reshape(blocks, width), jnp.zeros((8 - blocks, width), F32)]
    )
    little_other = exchange(little, "section", 1)
    big = (w_qkv[0], w_out[0], w_up[0], w_down[0])
    o_qkv = exchange(big[0], "section", 1)

    smalls = [jnp.where(section == layer, little, little_other) for layer in (0, 1)]
    o_qkv, smalls, mask, x, late_out, late_up = lax.optimization_barrier(
        (o_qkv, smalls, mask, x, big[1], big[2])
    )
    o_out, o_up = exchange(late_out, "section", 1), exchange(late_up, "section", 1)
    front = attend_forward(0, sec, x, FAR, big[0], o_qkv, smalls[0], mask)
    front, o_out, o_up, late_down = lax.optimization_barrier((front, o_out, o_up, big[3]))
    other = (o_qkv, o_out, o_up, exchange(late_down, "section", 1))
    y_one, cache_one = layer_forward(0, sec, x, front, big, other, smalls[0])
    y_near, y_one = y_one
    made = second_layer(sec, y_near, mask, big, other, smalls[1], gy)
    q, k, v, probs, ctx, hat_one, scale_one, low, slope, y_two = made[:10]
    cache_two = (y_one, q, k, v, probs, ctx, hat_one, scale_one, low, None, slope, None, None)
    line = Line(sec)
    two = Backward(line, 1, sec, cache_two, big, other, smalls[1], shards)
    one = Backward(line, 0, sec, cache_one, big, other, smalls[0], shards)
    two.made.update(second=made[10], branch=made[11], down_sums=made[12])
    line.add(made[13], made[14])
    exchanged_y = exchange(jnp.where(section == 0, y_two, y_one), "section", 1)
    line.advance(two, two.up_first)
    line.advance(two, two.up_last)
    line.advance(two, two.attention)
    gx_two_near, gx_two_low = two.made["gx_low"]
    line.advance(one, lambda: one.down(gx_two_near))
    line.advance(one, one.up)
    line.advance(one, one.attention)
    gx_one = one.made["gx"]

    rest = Rest(sec)
    rest.made["y"] = exchanged_y
    for _ in range(3):
        line.advance(line)
    line.advance(rest, lambda: rest.send(gx_one, gx_two_low))
    line.advance(rest, lambda: rest.assemble(y_one, y_two, gx_one, gx_two_low))
    activations, input_grads = rest.made["outs"]
    activations = activations.reshape(seqs_local, length, width)
    input_grads = input_grads.reshape(seqs_local, length, width)
    down, up, attend = line.finish()
    g_w_down, g_w_qkv, g_w_out, g_b_qv, g_b_out, g_gain, g_offset, g_b_up, g_b_down, g_w_up = last(
        line.ids, down, up, attend, width, shards
    )
    return (
        activations[None],
        input_grads[None],
        g_w_qkv[None],
        g_b_qv[None],
        g_w_out[None],
        g_b_out,
        g_gain[None],
        g_offset[None],
        g_w_up[None],
        g_b_up,
        g_w_down[None],
        g_b_down,
    )


def solution(mesh):
    rows = ("inner", "outer")
    return jax.shard_map(
        local,
        mesh=mesh,
        in_specs=(
            P(rows, None, None),
            P(rows),
            P(rows),
            P(rows, None, None),
            P("section", None, None),
            P("section", None, None),
            P("section", None, None),
            P("section", None),
            P("section", None, None),
            P("section", None, None),
            P("section", None, None),
            P("section", None),
            P("section", None, None),
            P("section", None),
        ),
        out_specs=(
            P("section", rows, None, None),
            P("section", rows, None, None),
            P("section", "inner", None),
            P("section", None, "inner"),
            P("section", "inner", None),
            P("section", "inner"),
            P("section", None, "inner"),
            P("section", None, "inner"),
            P("section", "inner", None),
            P("section", "inner"),
            P("section", "inner", None),
            P("section", "inner"),
        ),
        check_vma=False,
    )
```

```python
import functools
import math

import jax
import jax.numpy as jnp
from jax import lax
from jax.experimental import pallas as pl
from jax.experimental.pallas import tpu as pltpu
from jax.sharding import PartitionSpec as P

HEADS = 12
CAP = 28
EPS = 1e-12
SCALE = 0.125
SPARE = 8 * 1024 * 1024
F32 = jnp.float32
BF16 = jnp.bfloat16
B_Q, B_V, B_OUT, GAIN_ONE, GAIN_TWO, OFFSET_ONE, OFFSET_TWO, B_DOWN, B_UP = range(9)


def dot(left, right):
    return jnp.dot(left, right, preferred_element_type=F32)


def dot_t(left, right):
    return lax.dot_general(left, right, (((1,), (1,)), ((), ())), preferred_element_type=F32)


def t_dot(left, right):
    return lax.dot_general(left, right, (((0,), (0,)), ((), ())), preferred_element_type=F32)


def column_sum(values):
    return jnp.sum(values, axis=0, keepdims=True)


def standardize(summed):
    centre = jnp.mean(summed, axis=-1, keepdims=True)
    shifted = summed - centre
    spread = jnp.mean(shifted * shifted, axis=-1, keepdims=True)
    scale = lax.rsqrt(spread + EPS)
    return shifted * scale, scale


def norm_back(grad, hat, scale, gain):
    scaled = grad * gain
    return scale * (
        scaled
        - jnp.mean(scaled, axis=-1, keepdims=True)
        - hat * jnp.mean(scaled * hat, axis=-1, keepdims=True)
    )


def gauss_share(value):
    bell = jnp.exp2(value * value * -0.7213475204444817)
    part = 1.0 / (1.0 + 0.2316418882 * jnp.abs(value))
    tail = 0.5307027145
    for item in (-0.7265760135, 0.7107068705, -0.142248368, 0.127414796):
        tail = tail * part + item
    tail = tail * part * bell
    return jnp.where(value < 0.0, tail, 1.0 - tail), bell


def lane_halves():
    lane = lax.broadcasted_iota(jnp.int32, (1, 128), 1)
    lower = jnp.where(lane < 64, 1.0, 0.0)
    return lower.astype(BF16), (1.0 - lower).astype(BF16)


def two_heads(block, halves):
    return jnp.concatenate([block * halves[0], block * halves[1]], axis=0)


def sds(shape, dtype):
    return jax.ShapeDtypeStruct(shape, dtype)


class Mover:
    def __init__(self, sems):
        self.sems, self.used, self.outs = sems, 0, []

    def copy(self, source, target):
        self.used += 1
        return pltpu.make_async_copy(source, target, self.sems.at[self.used - 1])

    def load(self, source, target):
        self.last = self.copy(source, target)
        self.last.start()

    def choose(self, first, one, two, target):
        copy = self.copy(one, target)
        other = pltpu.make_async_copy(two, target, self.sems.at[self.used - 1])
        pl.when(first)(copy.start)
        pl.when(jnp.logical_not(first))(other.start)
        return copy

    def store(self, source, target):
        copy = self.copy(source, target)
        copy.start()
        self.outs.append(copy)

    def finish(self):
        for copy in self.outs:
            copy.wait()


class Operand:
    def __init__(self, ref, buffer, far):
        self.ref, self.buffer, self.far = ref, buffer, far

    def fetch(self, move, *index):
        if self.far:
            move.load(*(ref.at[index] if index else ref for ref in (self.ref, self.buffer)))
            return [move.last]
        return []

    def flush(self, move, *index):
        if self.far:
            move.store(*(ref.at[index] if index else ref for ref in (self.buffer, self.ref)))


NEAR, FAR, RAW, BOTH, FREE = "near", "far", "raw", "both", "free"


def run(*parts):
    for part in parts:
        next(part)
    for part in parts:
        for _ in part:
            pass


def ready(waits):
    for item in waits:
        item.wait()


def call(kernel, ids, ins, outs, scratch, name, flops, nbytes):
    space = lambda kind: {NEAR: pltpu.VMEM, FREE: pl.ANY}.get(kind, pltpu.HBM)
    spread = [(shape, part) for shape, kind in outs for part in ((NEAR, RAW) if kind == BOTH else (kind,))]
    kinds = [kind for _, kind in ins] + [kind for _, kind in spread]
    shapes = [array for array, _ in ins] + [shape for shape, _ in spread]
    buffers = [pltpu.VMEM(shape.shape, shape.dtype) for shape, kind in zip(shapes, kinds) if kind == FAR]

    def body(ids_ref, *refs):
        count = len(kinds)
        spare = list(refs[count : count + len(buffers)])
        left = list(refs[:count])
        operands = []
        for _, kind in list(ins) + list(outs):
            ref = left.pop(0)
            if kind == BOTH:
                operands.append(Operand(left.pop(0), ref, True))
            else:
                operands.append(Operand(ref, spare.pop(0) if kind == FAR else ref, kind == FAR))
        kernel(ids_ref, *operands, *refs[count + len(buffers) :])

    size = lambda shape, dtype: math.prod(shape) * jnp.dtype(dtype).itemsize
    limit = SPARE + sum(size(*item) for item in scratch)
    limit += sum(size(shape.shape, shape.dtype) for shape, kind in zip(shapes, kinds) if kind == FAR)
    results = pl.pallas_call(
        body,
        in_specs=[pl.BlockSpec(memory_space=pltpu.SMEM)]
        + [pl.BlockSpec(memory_space=space(kind)) for _, kind in ins],
        out_specs=[pl.BlockSpec(memory_space=space(kind)) for _, kind in spread],
        out_shape=[space(kind)(shape.shape, shape.dtype) for shape, kind in spread],
        scratch_shapes=buffers + [pltpu.VMEM(*item) for item in scratch] + [pltpu.SemaphoreType.DMA((64,))],
        compiler_params=pltpu.CompilerParams(vmem_limit_bytes=limit),
        cost_estimate=pl.CostEstimate(flops=flops, bytes_accessed=nbytes, transcendentals=0),
        name=name,
    )(ids, *(pltpu.with_memory_space_constraint(array, space(kind)) for array, kind in ins))
    results = list(results)
    return [(results.pop(0), results.pop(0)) if kind == BOTH else results.pop(0) for _, kind in outs]


def attend_phase(q, k, v, probs, ctx, mask, pairs):
    seqs = mask.shape[1]
    halves = lane_halves()
    feature = lax.broadcasted_iota(jnp.int32, (128, 128), 0)
    first_half = jnp.where(feature < 64, 1.0, 0.0).astype(BF16)
    second_half = jnp.where(feature < 64, 0.0, 1.0).astype(BF16)

    for seq in range(seqs):
        rows = slice(seq * 128, seq * 128 + 128)
        seen = jnp.broadcast_to(mask[:, seq : seq + 1], (256, 128)) > 0.5
        for pair in range(*pairs):
            lanes = slice(pair * 128, pair * 128 + 128)
            scores = dot_t(two_heads(k[rows, lanes], halves), q[rows, lanes] * SCALE)
            scores = jnp.where(seen, scores, -1e30)
            parts = []
            for part in (scores[:128], scores[128:]):
                e = jnp.exp(part - jnp.max(part, axis=0, keepdims=True))
                parts.append(e * (1.0 / jnp.sum(e, axis=0, keepdims=True)))
            parts = jnp.concatenate(parts, axis=0)
            probs[seq, pair] = parts
            turned = v[rows, lanes].T
            turned = jnp.concatenate([turned * first_half, turned * second_half], axis=1)
            ctx[lanes, rows] = dot(turned, parts.astype(BF16)).astype(BF16)


def attend_steps(move, layer, sec, x, w_a, w_b, small, mask, q, k, v, probs, ctx, w):
    mine = sec[0] == layer
    rows, width = x.buffer.shape
    waits = x.fetch(move) + small.fetch(move) + mask.fetch(move)
    parts = [
        move.choose(mine, w_a.ref.at[:, pl.ds(i * width, width)], w_b.ref.at[:, pl.ds(i * width, width)], w.at[i])
        for i in (1, 0, 2)
    ]
    yield
    ready(waits)
    x, small = x.buffer, small.buffer
    parts[0].wait()
    k.buffer[...] = dot(x[...], w[1]).astype(BF16)
    k.flush(move)
    parts[1].wait()
    q.buffer[...] = (dot(x[...], w[0]) + small[B_Q : B_Q + 1]).astype(BF16)
    q.flush(move)
    parts[2].wait()
    v.buffer[...] = (dot(x[...], w[2]) + small[B_V : B_V + 1]).astype(BF16)
    v.flush(move)
    half = width // 128 // 2
    for i in range(2):
        attend_phase(
            q.buffer, k.buffer, v.buffer, probs.buffer, ctx.buffer, mask.buffer, (i * half, i * half + half)
        )
        probs.flush(move, slice(None), pl.ds(i * half, half))
    ctx.flush(move)


def attend_kernel(layer, sec, *refs):
    move = Mover(refs[-1])
    run(attend_steps(move, layer, sec, *refs[:-1]))
    move.finish()


def attend_forward(layer, sec, x, x_kind, w_own, w_other, small, mask):
    rows, width = x.shape
    seqs = mask.shape[1]
    pairs = width // 128
    wide = sds((rows, width), BF16)
    return call(
        functools.partial(attend_kernel, layer),
        sec,
        [(x, x_kind), (w_own, RAW), (w_other, RAW), (small, FAR), (mask, FAR)],
        [(wide, FAR)] * 3 + [(sds((seqs, pairs, 256, 128), F32), FAR), (sds((width, rows), BF16), BOTH)],
        [((3, width, width), BF16)],
        "attend_forward",
        2 * rows * width * width * 4,
        12 << 20,
    )


def up_kernel(layer, sec, x, ctx, wo_a, wo_b, wu_a, wu_b, small, hat, scale, turned, act, slope, wo, wu, low, sems):
    move = Mover(sems)
    mine = sec[0] == layer
    blocks, _, wide = wu.shape
    waits = ctx.fetch(move) + [move.choose(mine, wo_a.ref, wo_b.ref, wo)] + small.fetch(move) + x.fetch(move)
    span = lambda i: pl.ds(i * wide, wide)
    parts = [move.choose(mine, wu_a.ref.at[:, span(i)], wu_b.ref.at[:, span(i)], wu.at[i]) for i in range(blocks)]
    ready(waits)
    small = small.buffer
    summed = x.buffer[...].astype(F32) + t_dot(ctx.buffer[...], wo[...]) + small[B_OUT : B_OUT + 1]
    unit, root = standardize(summed)
    hat.buffer[...] = unit
    hat.flush(move)
    scale.buffer[...] = jnp.broadcast_to(root, scale.buffer.shape)
    scale.flush(move)
    low[...] = (unit * small[GAIN_ONE : GAIN_ONE + 1] + small[OFFSET_ONE : OFFSET_ONE + 1]).astype(BF16)
    turned.buffer[...] = low[...].T
    turned.flush(move)
    for i in range(blocks):
        parts[i].wait()
        pre = dot(low[...], wu[i]) + small[B_UP + i : B_UP + i + 1]
        share, bell = gauss_share(pre)
        act.buffer[i] = (pre * share).astype(BF16)
        slope.buffer[i] = share + pre * 0.3989422804014327 * bell
        act.flush(move, i)
        slope.flush(move, i)
    move.finish()


def up_forward(layer, sec, x, x_kind, ctx, wo, wo_other, wu, wu_other, small):
    rows, width = x.shape
    blocks = wu.shape[1] // width
    wide = (rows, width)
    other_kind = FREE if layer == 0 else RAW
    return call(
        functools.partial(up_kernel, layer),
        sec,
        [(x, x_kind), (ctx, NEAR), (wo, RAW), (wo_other, other_kind), (wu, RAW), (wu_other, other_kind), (small, FAR)],
        [
            (sds(wide, F32), BOTH),
            (sds((rows, 128), F32), FAR),
            (sds((width, rows), BF16), FAR),
            (sds((blocks,) + wide, BF16), BOTH if layer == 0 else NEAR),
            (sds((blocks,) + wide, F32), FAR),
        ],
        [((width, width), BF16), ((blocks, width, width), BF16), (wide, BF16)],
        "up_forward",
        2 * rows * width * width * (blocks + 1),
        20 << 20,
    )


def down_kernel(layer, sec, act, wd_a, wd_b, hat, small, y, two, scale, wd, total, sems):
    move = Mover(sems)
    mine = sec[0] == layer
    blocks, wide, _ = wd.shape
    parts = []
    for i in range(blocks):
        span = pl.ds(i * wide, wide)
        parts.append(act.fetch(move, i) + [move.choose(mine, wd_a.ref.at[span], wd_b.ref.at[span], wd.at[i])])
        if i == 0:
            waits = small.fetch(move) + hat.fetch(move)
    for i in range(blocks):
        ready(parts[i])
        product = dot(act.buffer[i], wd[i])
        total[...] = product if i == 0 else total[...] + product
    ready(waits)
    small = small.buffer
    normed = hat.buffer[...] * small[GAIN_ONE : GAIN_ONE + 1] + small[OFFSET_ONE : OFFSET_ONE + 1]
    unit, root = standardize(total[...] + normed + small[B_DOWN : B_DOWN + 1])
    y.buffer[...] = (unit * small[GAIN_TWO : GAIN_TWO + 1] + small[OFFSET_TWO : OFFSET_TWO + 1]).astype(BF16)
    y.flush(move)
    two.buffer[...] = unit
    two.flush(move)
    scale.buffer[...] = jnp.broadcast_to(root, scale.buffer.shape)
    scale.flush(move)
    move.finish()


def down_forward(layer, sec, act, wd, wd_other, hat, small, y_kind, two_kind):
    blocks, rows, width = act.shape
    wide = (rows, width)
    return call(
        functools.partial(down_kernel, layer),
        sec,
        [(act, NEAR), (wd, RAW), (wd_other, FREE if layer == 0 else RAW), (hat, NEAR), (small, FAR)],
        [(sds(wide, BF16), y_kind), (sds(wide, F32), two_kind), (sds((rows, 128), F32), two_kind)],
        [((blocks, width, width), BF16), (wide, F32)],
        "down_forward",
        2 * rows * width * width * blocks,
        12 << 20,
    )


def up_down_steps(
    move, layer, sec, x, ctx, wo_a, wo_b, wu_a, wu_b, wd_a, wd_b, small,
    hat, scale, turned, act, slope, y, two, scale_two, wo, wu, wd, low, total,
):
    mine = sec[0] == layer
    blocks, _, wide = wu.shape
    waits = ctx.fetch(move) + [move.choose(mine, wo_a.ref, wo_b.ref, wo)] + small.fetch(move) + x.fetch(move)
    ups, downs = [], []
    for i in range(blocks):
        span = pl.ds(i * wide, wide)
        ups.append(move.choose(mine, wu_a.ref.at[:, span], wu_b.ref.at[:, span], wu.at[i]))
        downs.append(move.choose(mine, wd_a.ref.at[span], wd_b.ref.at[span], wd.at[i]))
    yield
    ready(waits)
    small = small.buffer
    summed = x.buffer[...].astype(F32) + t_dot(ctx.buffer[...], wo[...]) + small[B_OUT : B_OUT + 1]
    unit, root = standardize(summed)
    hat.buffer[...] = unit
    hat.flush(move)
    scale.buffer[...] = jnp.broadcast_to(root, scale.buffer.shape)
    scale.flush(move)
    normed = unit * small[GAIN_ONE : GAIN_ONE + 1] + small[OFFSET_ONE : OFFSET_ONE + 1]
    total[...] = normed + small[B_DOWN : B_DOWN + 1]
    low[...] = normed.astype(BF16)
    turned.buffer[...] = low[...].T
    turned.flush(move)
    for i in range(blocks):
        ups[i].wait()
        pre = dot(low[...], wu[i]) + small[B_UP + i : B_UP + i + 1]
        share, bell = gauss_share(pre)
        act.buffer[i] = (pre * share).astype(BF16)
        slope.buffer[i] = share + pre * 0.3989422804014327 * bell
        slope.flush(move, i)
        downs[i].wait()
        total[...] += dot(act.buffer[i], wd[i])
    unit, root = standardize(total[...])
    y.buffer[...] = (unit * small[GAIN_TWO : GAIN_TWO + 1] + small[OFFSET_TWO : OFFSET_TWO + 1]).astype(BF16)
    y.flush(move)
    two.buffer[...] = unit
    scale_two.buffer[...] = jnp.broadcast_to(root, scale_two.buffer.shape)


def down_grad_steps(move, sec, gy, hat, scale, small, act, second, branch, sums, send, keep, turned):
    blocks = act.buffer.shape[0]
    low_rows, wide = send.buffer.shape[1], act.buffer.shape[2]
    tall = 2 * low_rows
    waits = gy.fetch(move) + small.fetch(move) + scale.fetch(move) + hat.fetch(move)
    parts = [act.fetch(move, i) for i in range(blocks)]
    yield
    ready(waits)
    grad = gy.buffer[...].astype(F32)
    sums.buffer[0:1] = column_sum(grad * hat.buffer[...])
    sums.buffer[1:2] = column_sum(grad)
    unit = norm_back(grad, hat.buffer[...], scale.buffer[:, 0:1], small.buffer[GAIN_TWO : GAIN_TWO + 1])
    second.buffer[...] = unit
    second.flush(move)
    low = unit.astype(BF16)
    branch.buffer[...] = low
    branch.flush(move)
    sums.buffer[2:3] = column_sum(low.astype(F32))
    sums.buffer[3:] = jnp.zeros_like(sums.buffer[3:])
    sums.flush(move)
    turned[...] = branch.buffer[...].T
    for half, out in ((1 - sec[0], send), (sec[0], keep)):
        left = pl.ds(pl.multiple_of(half * tall, tall), tall)
        for i in range(blocks):
            if out is send:
                ready(parts[i])
            block = dot(turned[left, :], act.buffer[i]).astype(BF16)
            out.buffer[i, :, :wide] = block[:low_rows]
            out.buffer[i, :, wide:] = block[low_rows:]
            out.flush(move, i)


def down_grad_kernel(sec, *refs):
    move = Mover(refs[-1])
    run(down_grad_steps(move, sec, *refs[:-1]))
    move.finish()


def down_grad(sec, gy, gy_kind, hat, scale, small, act, kind):
    rows, width = gy.shape
    blocks = act.shape[0]
    wide = (rows, width)
    part = sds((blocks, width // 4, 2 * width), BF16)
    return call(
        down_grad_kernel,
        sec,
        [(gy, gy_kind), (hat, kind), (scale, kind), (small, FAR), (act, kind)],
        [(sds(wide, F32), NEAR), (sds(wide, BF16), NEAR), (sds((8, width), F32), NEAR), (part, NEAR), (part, FAR if kind == NEAR else NEAR)],
        [((width, rows), BF16)],
        "down_grad",
        2 * rows * width * width * blocks,
        14 << 20,
    )


def up_grad_kernel(layer, last, sec, *refs):
    refs = list(refs)
    take = lambda count: [refs.pop(0) for _ in range(count)]
    branch, base, wd_a, wd_b, slope_h, low, wu_a, wu_b = take(8)
    if last:
        hat, scale, small, sums_in = take(4)
        first, attend, sums, out = take(4)
    else:
        first, sums, out = take(3)
    wd, wu, slope, pre, sems = refs
    move = Mover(sems)
    mine = sec[0] == layer
    half, wide, _ = wd.shape
    side = sec[0] if last else 1 - sec[0]
    at = [side * half + i for i in range(half)]
    span = [pl.ds(pl.multiple_of(place * wide, wide), wide) for place in at]
    parts = []
    early = branch.fetch(move)
    for i in range(half):
        move.load(slope_h.ref.at[at[i]], slope.at[i])
        parts.append(
            [
                move.last,
                move.choose(mine, wd_a.ref.at[span[i]], wd_b.ref.at[span[i]], wd.at[i]),
                move.choose(mine, wu_a.ref.at[:, span[i]], wu_b.ref.at[:, span[i]], wu.at[i]),
            ]
        )
        if i == 0:
            early += low.fetch(move)
    late = base.fetch(move)
    if last:
        late += hat.fetch(move) + scale.fetch(move) + small.fetch(move)
        sums.buffer[...] = sums_in.buffer[...]
    else:
        sums.buffer[...] = jnp.zeros_like(sums.buffer)
    ready(early)
    total = first.buffer
    shards, tall, _ = out.buffer.shape
    for i in range(half):
        ready(parts[i])
        pre[...] = (dot_t(branch.buffer[...], wd[i]) * slope[i]).astype(BF16)
        sums.buffer[pl.ds(3 + at[i], 1)] = column_sum(pre[...].astype(F32))
        block = dot(low.buffer[...], pre[...]).astype(BF16)
        for shard in range(shards):
            out.buffer[shard, :, i * wide : i * wide + wide] = block[shard * tall : shard * tall + tall]
        if i == 0:
            ready(late)
            total[...] = base.buffer[...] + dot_t(pre[...], wu[i])
        else:
            total[...] += dot_t(pre[...], wu[i])
    if last:
        grad = total[...]
        sums.buffer[0:1] = column_sum(grad * hat.buffer[...])
        sums.buffer[1:2] = column_sum(grad)
        unit = norm_back(grad, hat.buffer[...], scale.buffer[:, 0:1], small.buffer[GAIN_ONE : GAIN_ONE + 1])
        attend.buffer[...] = unit.astype(BF16)
        total[...] = unit
        sums.buffer[2:3] = column_sum(attend.buffer[...].astype(F32))
    move.finish()


def up_grad(layer, last, sec, branch, base, wd, wd_other, slope, low, wu, wu_other, shards, more=()):
    blocks, rows, width = slope.shape
    half = blocks // 2
    wide = (rows, width)
    part = sds((shards, width // shards, half * width), BF16)
    square = ((half, width, width), BF16)
    near = lambda *shapes: [(shape, NEAR) for shape in shapes]
    ins = [
        (branch, NEAR),
        (base, NEAR),
        (wd, RAW),
        (wd_other, RAW),
        (slope, RAW),
        (low, FAR),
        (wu, RAW),
        (wu_other, RAW),
    ]
    if last:
        hat, scale, small, sums = more
        ins += [(hat, FAR), (scale, FAR), (small, FAR), (sums, NEAR)]
        outs = near(sds(wide, F32), sds(wide, BF16), sds((8, width), F32), part)
    else:
        outs = near(sds(wide, F32), sds((8, width), F32), part)
    return call(
        functools.partial(up_grad_kernel, layer, last),
        sec,
        ins,
        outs,
        [square, square, ((half,) + wide, F32), (wide, BF16)],
        "up_grad_last" if last else "up_grad_first",
        3 * rows * width * width * blocks,
        15 << 20,
    )


def attend_grad_kernel(layer, last, sec, *refs):
    refs = list(refs)
    take = lambda count: [refs.pop(0) for _ in range(count)]
    attend, ctx, base, x, q_h, k_h, v_h, p_h, wo_a, wo_b, w_a, w_b, down, up = take(14)
    if last:
        gx, gx_low, out = take(3)
    else:
        total, turned, out = take(3)
    q, k, v, probs, wo, w, gc, grads, sems = refs
    move = Mover(sems)
    mine = sec[0] == layer
    rows_all, wide = q.shape
    width = 2 * wide
    seqs = probs.shape[0]
    shards = out.buffer.shape[0]
    tall = width // shards
    pairs = wide // 128
    side = sec[0] if last else 1 - sec[0]
    lanes_half = pl.ds(pl.multiple_of(side * wide, wide), wide)
    waits = attend.fetch(move) + [move.choose(mine, wo_a.ref.at[lanes_half], wo_b.ref.at[lanes_half], wo)]
    near = []
    for source, target in (
        (p_h.ref.at[:, pl.ds(side * pairs, pairs)], probs),
        (v_h.ref.at[:, lanes_half], v),
        (k_h.ref.at[:, lanes_half], k),
        (q_h.ref.at[:, lanes_half], q),
    ):
        move.load(source, target)
        near.append(move.last)
    later = x.fetch(move) + ctx.fetch(move) + down.fetch(move) + up.fetch(move)
    finals = base.fetch(move)
    for i in range(3):
        there = pl.ds(pl.multiple_of(i * width + side * wide, wide), wide)
        finals.append(move.choose(mine, w_a.ref.at[:, there], w_b.ref.at[:, there], w.at[:, pl.ds(i * wide, wide)]))
    ready(waits)
    gc[...] = dot_t(attend.buffer[...], wo[...]).astype(BF16)
    ready(near)
    halves = lane_halves()
    lower = lax.broadcasted_iota(jnp.int32, (128, 128), 1) < 64

    for pair in range(pairs):
        lanes = slice(pair * 128, pair * 128 + 128)
        for seq in range(seqs):
            rows = slice(seq * 128, seq * 128 + 128)

            def put(part, value):
                grads[rows, part * wide + pair * 128 : part * wide + pair * 128 + 128] = value.astype(BF16)

            grad = gc[rows, lanes]
            p = probs[seq, pair]
            full = dot(p.astype(BF16), grad)
            put(2, jnp.where(lower, full[:128], full[128:]))
            gp = dot_t(two_heads(v[rows, lanes], halves), grad)
            parts = []
            for part in (slice(0, 128), slice(128, 256)):
                g, pp = gp[part], p[part]
                parts.append(pp * (g - jnp.sum(g * pp, axis=0, keepdims=True)))
            gs = jnp.concatenate(parts, axis=0).astype(BF16)
            put(0, t_dot(gs, two_heads(k[rows, lanes] * SCALE, halves)))
            full = dot(gs, q[rows, lanes] * SCALE)
            put(1, jnp.where(lower, full[:128], full[128:]))
    ready(later)
    if last:
        turned = x
    else:
        turned.buffer[...] = x.buffer[...].T
    left = dot(turned.buffer[...], grads[...]).astype(BF16)
    right = dot(ctx.buffer[...], attend.buffer[:, lanes_half]).astype(BF16)
    little = jnp.concatenate([down.buffer[...], up.buffer[...]], axis=0).astype(BF16)
    zeros = jnp.zeros_like(little)
    b_q = column_sum(grads[:, 0:wide].astype(F32)).astype(BF16)
    b_v = column_sum(grads[:, 2 * wide :].astype(F32)).astype(BF16)
    pad = jnp.concatenate([b_q, b_v], axis=1)
    pad = jnp.concatenate([pad, jnp.zeros((15, width), BF16)], axis=0)
    for shard in range(shards):
        out.buffer[shard, :tall, 0 : 3 * wide] = left[shard * tall : shard * tall + tall]
        out.buffer[shard, :tall, 3 * wide :] = right[shard * tall : shard * tall + tall]
        out.buffer[shard, tall:, 0:width] = little
        out.buffer[shard, tall:, width:] = pad
    ready(finals)
    sum_all = base.buffer[...] + dot_t(grads[...], w[...])
    if last:
        gx.buffer[...] = sum_all
        gx.flush(move)
        gx_low.buffer[...] = sum_all.astype(BF16)
        gx_low.flush(move)
    else:
        total.buffer[...] = sum_all
    move.finish()


def attend_grad(layer, last, sec, attend, ctx, base, x, q, k, v, probs, wo, wo_other, w, w_other, down, up, shards, low_kind):
    rows, width = attend.shape
    seqs = probs.shape[0]
    wide = width // 2
    flat = (rows, width)
    part = (sds((shards, width // shards + 16, 2 * width), BF16), NEAR)
    if last:
        outs = [(sds(flat, F32), FAR), (sds(flat, BF16), low_kind), part]
    else:
        outs = [(sds(flat, F32), NEAR), (sds((width, rows), BF16), NEAR), part]
    half = ((rows, wide), BF16)
    return call(
        functools.partial(attend_grad_kernel, layer, last),
        sec,
        [(attend, NEAR), (ctx, FAR), (base, NEAR), (x, NEAR if last else FAR)]
        + [(item, RAW) for item in (q, k, v, probs, wo, wo_other, w, w_other)]
        + [(down, NEAR), (up, NEAR)],
        outs,
        [
            half,
            half,
            half,
            ((seqs, wide // 128) + probs.shape[2:], F32),
            ((wide, width), BF16),
            ((width, 3 * wide), BF16),
            half,
            ((rows, 3 * wide), BF16),
        ],
        "attend_grad_last" if last else "attend_grad_first",
        rows * width * width * 10,
        15 << 20,
    )


def second_kernel(sec, *refs):
    refs = list(refs)
    take = lambda count: [refs.pop(0) for _ in range(count)]
    inside = lambda item: Operand(None, item, False)
    x, w_a, w_b, small, mask = take(5)
    weights, (gy,) = take(6), take(1)
    q, k, v, probs, ctx, hat, scale, turned, slope, y = take(10)
    second, branch, sums, send, keep = take(5)
    w, wo, wu, wd, low, total, act, two, scale_two, branch_turned, sems = refs
    move = Mover(sems)
    near = inside(small.buffer)
    act, two, scale_two = inside(act), inside(two), inside(scale_two)
    run(
        attend_steps(move, 1, sec, x, w_a, w_b, small, mask, q, k, v, probs, ctx, w),
        up_down_steps(
            move, 1, sec, x, inside(ctx.buffer), *weights, near,
            hat, scale, turned, act, slope, y, two, scale_two, wo, wu, wd, low, total,
        ),
        down_grad_steps(move, sec, gy, two, scale_two, near, act, second, branch, sums, send, keep, branch_turned),
    )
    move.finish()


def second_layer(sec, x, mask, big, other, small, gy):
    rows, width = x.shape
    seqs = mask.shape[1]
    pairs = width // 128
    (w, w_other), (wo, wo_other), (wu, wu_other), (wd, wd_other) = zip(big, other)
    blocks = wu.shape[1] // width
    wide = (rows, width)
    part = sds((blocks, width // 4, 2 * width), BF16)
    square = lambda count: ((count, width, width), BF16)
    return call(
        second_kernel,
        sec,
        [(x, NEAR), (w, RAW), (w_other, RAW), (small, FAR), (mask, FAR)]
        + [(item, RAW) for item in (wo, wo_other, wu, wu_other, wd, wd_other)]
        + [(gy, FAR)],
        [(sds(wide, BF16), FAR)] * 3
        + [
            (sds((seqs, pairs, 256, 128), F32), FAR),
            (sds((width, rows), BF16), FAR),
            (sds(wide, F32), FAR),
            (sds((rows, 128), F32), FAR),
            (sds((width, rows), BF16), FAR),
            (sds((blocks,) + wide, F32), FAR),
            (sds(wide, BF16), FAR),
            (sds(wide, F32), NEAR),
            (sds(wide, BF16), NEAR),
            (sds((8, width), F32), NEAR),
            (part, NEAR),
            (part, FAR),
        ],
        [
            square(3),
            ((width, width), BF16),
            square(blocks),
            square(blocks),
            (wide, BF16),
            (wide, F32),
            ((blocks,) + wide, BF16),
            (wide, F32),
            ((rows, 128), F32),
            ((width, rows), BF16),
        ],
        "second_layer",
        2 * rows * width * width * (3 * blocks + 5),
        50 << 20,
    )


def up_whole_kernel(
    layer, sec, branch, second, wd_a, wd_b, slope, low, wu_a, wu_b, hat, scale, small,
    first, attend, sums, send, keep, wd, wu, pre, sems,
):
    move = Mover(sems)
    mine = sec[0] == layer
    blocks, wide, _ = wd.shape
    half = blocks // 2
    at = [lax.rem(i + half * (1 - sec[0]), blocks) for i in range(blocks)]
    span = [pl.ds(pl.multiple_of(place * wide, wide), wide) for place in at]
    parts = []
    early = branch.fetch(move)
    for i in range(blocks):
        parts.append(
            [move.choose(mine, wd_a.ref.at[span[i]], wd_b.ref.at[span[i]], wd.at[i])]
            + slope.fetch(move, at[i])
            + [
                move.choose(
                    mine,
                    wu_a.ref.at[:, span[i]],
                    wu_b.ref.at[:, span[i]],
                    wu.at[i // half, :, pl.ds(i % half * wide, wide)],
                )
            ]
        )
        if i == 0:
            early += low.fetch(move)
    late = second.fetch(move) + hat.fetch(move) + scale.fetch(move) + small.fetch(move)
    ready(early)
    branch, low, total = branch.buffer, low.buffer, first.buffer
    for side, out in enumerate((send, keep)):
        for i in range(half):
            block = side * half + i
            ready(parts[block])
            lanes = slice(i * wide, i * wide + wide)
            pre[:, lanes] = (dot_t(branch[...], wd[block]) * slope.buffer[at[block]]).astype(BF16)
            sums.buffer[pl.ds(3 + at[block], 1)] = column_sum(pre[:, lanes].astype(F32))
        product = dot(low[...], pre[...]).astype(BF16)
        shards, tall, _ = out.buffer.shape
        for shard in range(shards):
            out.buffer[shard] = product[shard * tall : shard * tall + tall]
        if side == 0:
            ready(late)
            total[...] = second.buffer[...] + dot_t(pre[...], wu[side])
        else:
            total[...] += dot_t(pre[...], wu[side])
    grad = total[...]
    sums.buffer[0:1] = column_sum(grad * hat.buffer[...])
    sums.buffer[1:2] = column_sum(grad)
    unit = norm_back(grad, hat.buffer[...], scale.buffer[:, 0:1], small.buffer[GAIN_ONE : GAIN_ONE + 1])
    attend.buffer[...] = unit.astype(BF16)
    attend.flush(move)
    total[...] = unit
    first.flush(move)
    sums.buffer[2:3] = column_sum(attend.buffer[...].astype(F32))
    sums.buffer[3 + blocks :] = jnp.zeros_like(sums.buffer[3 + blocks :])
    sums.flush(move)
    move.finish()


def up_whole(layer, sec, branch, second, wd, wd_other, slope, low, wu, wu_other, hat, scale, small, shards):
    blocks, rows, width = slope.shape
    wide = (rows, width)
    part = sds((shards, width // shards, blocks * width // 2), BF16)
    square = ((blocks, width, width), BF16)
    return call(
        functools.partial(up_whole_kernel, layer),
        sec,
        [
            (branch, NEAR),
            (second, NEAR),
            (wd, RAW),
            (wd_other, RAW),
            (slope, FAR),
            (low, FAR),
            (wu, RAW),
            (wu_other, RAW),
            (hat, FAR),
            (scale, FAR),
            (small, FAR),
        ],
        [(sds(wide, F32), NEAR), (sds(wide, BF16), NEAR), (sds((8, width), F32), NEAR), (part, NEAR), (part, NEAR)],
        [square, ((2, width, blocks // 2 * width), BF16), ((rows, blocks // 2 * width), BF16)],
        "up_grad",
        6 * rows * width * width * blocks,
        30 << 20,
    )


def attend_whole_kernel(
    layer, shards, sec, attend, ctx, first, x, q, k, v, probs, wo_a, wo_b, w_a, w_b, down, up,
    gx, gx_low, send, keep, turned, wo, w, gc, grads, sems,
):
    move = Mover(sems)
    mine = sec[0] == layer
    rows_all, width = x.buffer.shape
    seqs = probs.buffer.shape[0]
    wide = width // 2
    tall = width // shards
    pairs = wide // 128
    waits = attend.fetch(move) + [move.choose(mine, wo_a.ref, wo_b.ref, wo)]
    near = probs.fetch(move) + v.fetch(move) + k.fetch(move) + q.fetch(move)
    later = x.fetch(move) + ctx.fetch(move) + down.fetch(move) + up.fetch(move)
    last = [
        move.choose(
            mine,
            w_a.ref.at[:, pl.ds(i * width + half * wide, wide)],
            w_b.ref.at[:, pl.ds(i * width + half * wide, wide)],
            w.at[:, pl.ds((3 * half + i) * wide, wide)],
        )
        for i in range(3)
        for half in range(2)
    ] + first.fetch(move)
    ready(waits)
    attend, q, k, v, probs = (item.buffer for item in (attend, q, k, v, probs))
    gc[...] = dot_t(attend[...], wo[...]).astype(BF16)
    ready(near)
    halves = lane_halves()
    lower = lax.broadcasted_iota(jnp.int32, (128, 128), 1) < 64

    def attention(half):
        for index in range(pairs):
            lanes = pl.ds(pl.multiple_of(half * wide + index * 128, 128), 128)

            def put(part, rows, value, index=index):
                there = pl.ds(pl.multiple_of((3 * half + part) * wide + index * 128, 128), 128)
                grads[rows, there] = value.astype(BF16)

            for seq in range(seqs):
                rows = slice(seq * 128, seq * 128 + 128)
                grad = gc[rows, lanes]
                p = probs[seq, half * pairs + index]
                full = dot(p.astype(BF16), grad)
                put(2, rows, jnp.where(lower, full[:128], full[128:]))
                gp = dot_t(two_heads(v[rows, lanes], halves), grad)
                parts = []
                for side in (slice(0, 128), slice(128, 256)):
                    g, pp = gp[side], p[side]
                    parts.append(pp * (g - jnp.sum(g * pp, axis=0, keepdims=True)))
                gs = jnp.concatenate(parts, axis=0).astype(BF16)
                put(0, rows, t_dot(gs, two_heads(k[rows, lanes] * SCALE, halves)))
                full = dot(gs, q[rows, lanes] * SCALE)
                put(1, rows, jnp.where(lower, full[:128], full[128:]))

    def products(half, out):
        three = pl.ds(pl.multiple_of(half * 3 * wide, 128), 3 * wide)
        lanes = pl.ds(pl.multiple_of(half * wide, wide), wide)
        block = dot(turned[...], grads[:, three]).astype(BF16)
        block_out = dot(ctx.buffer[...], attend[:, lanes]).astype(BF16)
        for shard in range(shards):
            out.buffer[shard, :tall, : 3 * wide] = block[shard * tall : shard * tall + tall]
            out.buffer[shard, :tall, 3 * wide :] = block_out[shard * tall : shard * tall + tall]

    attention(1 - sec[0])
    ready(later)
    turned[...] = x.buffer[...].T
    products(1 - sec[0], send)
    attention(sec[0])
    products(sec[0], keep)
    little = jnp.concatenate([down.buffer[...], up.buffer[...]], axis=0).astype(BF16)
    for half, out in ((1 - sec[0], send), (sec[0], keep)):
        pad = []
        for part in (0, 2):
            lanes = pl.ds(pl.multiple_of((3 * half + part) * wide, wide), wide)
            pad.append(column_sum(grads[:, lanes].astype(F32)).astype(BF16))
        pad = jnp.concatenate([jnp.concatenate(pad, axis=1), jnp.zeros((15, width), BF16)], axis=0)
        for shard in range(shards):
            out.buffer[shard, tall:, 0:width] = little
            out.buffer[shard, tall:, width:] = pad
    ready(last)
    total = first.buffer[...] + dot_t(grads[...], w[...])
    gx.buffer[...] = total
    gx.flush(move)
    gx_low.buffer[...] = total.astype(BF16)
    gx_low.flush(move)
    move.finish()


def attend_whole(layer, sec, attend, ctx, first, x, q, k, v, probs, wo, wo_other, w, w_other, down, up, shards, low_kind):
    rows, width = x.shape
    wide = (rows, width)
    part = sds((shards, width // shards + 16, 2 * width), BF16)
    return call(
        functools.partial(attend_whole_kernel, layer, shards),
        sec,
        [(attend, NEAR), (ctx, FAR), (first, NEAR)]
        + [(item, FAR) for item in (x, q, k, v, probs)]
        + [(wo, RAW), (wo_other, RAW), (w, RAW), (w_other, RAW), (down, NEAR), (up, NEAR)],
        [(sds(wide, F32), FAR), (sds(wide, BF16), low_kind), (part, NEAR), (part, NEAR)],
        [((width, rows), BF16), ((width, width), BF16), ((width, 3 * width), BF16), (wide, BF16), ((rows, 3 * width), BF16)],
        "attend_grad",
        2 * rows * width * width * 10,
        30 << 20,
    )


def layer_forward(layer, sec, x, front, big, other, small, far=None):
    w_qkv, w_out, w_up, w_down = big
    o_qkv, o_out, o_up, o_down = other
    x_kind = FAR if layer == 0 else NEAR
    q, k, v, probs, (ctx_near, ctx) = front
    (hat_near, hat_one), scale_one, low, act, slope = up_forward(
        layer, sec, x, x_kind, ctx_near, w_out, o_out, w_up, o_up, small
    )
    act_near, act = act if layer == 0 else (act, act)
    kinds = (BOTH, FAR) if layer == 0 else (FAR, NEAR)
    y, hat_two, scale_two = down_forward(layer, sec, act_near, w_down, o_down, hat_near, small, *kinds)
    x = x if far is None else far
    return y, (x, q, k, v, probs, ctx, hat_one, scale_one, low, act, slope, hat_two, scale_two)


class Backward:
    def __init__(self, line, layer, sec, cache, big, other, small, shards):
        self.line, self.layer, self.sec, self.small, self.shards = line, layer, sec, small, shards
        self.cache, self.weights, self.made = cache, tuple(zip(big, other)), {}

    def down(self, gy):
        act, _, hat_two, scale_two = self.cache[-4:]
        kinds = (NEAR, FAR) if self.layer == 0 else (FAR, NEAR)
        second, branch, sums, send, keep = down_grad(
            self.line.sec, gy, kinds[0], hat_two, scale_two, self.small, act, kinds[1]
        )
        self.made.update(second=second, branch=branch, down_sums=sums)
        self.line.add(send, keep)

    def up_inputs(self):
        (w_up, o_up), (w_down, o_down) = self.weights[2:]
        low, _, slope = self.cache[-5:-2]
        return w_down, o_down, slope, low, w_up, o_up, self.shards

    def up_first(self):
        made = self.made
        made["part"], made["up_sums"], send = up_grad(
            self.layer, False, self.line.sec, made["branch"], made["second"], *self.up_inputs()
        )
        self.up_chunk = self.line.add(send, None)

    def up_last(self):
        made = self.made
        hat_one, scale_one = self.cache[-7:-5]
        more = (hat_one, scale_one, self.small, made["up_sums"])
        made["first"], made["attend"], made["up_sums"], self.up_chunk.keep = up_grad(
            self.layer, True, self.line.sec, made["branch"], made["part"], *self.up_inputs(), more
        )

    def up(self):
        made = self.made
        hat_one, scale_one = self.cache[-7:-5]
        ins = self.up_inputs()
        made["first"], made["attend"], made["up_sums"], send, keep = up_whole(
            self.layer, self.line.sec, made["branch"], made["second"], *ins[:-1], hat_one, scale_one, self.small, ins[-1]
        )
        self.line.add(send, keep)

    def attention(self):
        made = self.made
        made["gx"], made["gx_low"], send, keep = attend_whole(
            self.layer, self.line.sec, made["attend"], self.cache[5], made["first"], self.cache[0], *self.heads()
        )
        self.line.add(send, keep)

    def heads(self):
        q, k, v, probs = self.cache[1:5]
        (w_qkv, o_qkv), (w_out, o_out) = self.weights[:2]
        low_kind = FAR if self.layer == 0 else BOTH
        sums = (self.made["down_sums"], self.made["up_sums"])
        return (q, k, v, probs, w_out, o_out, w_qkv, o_qkv) + sums + (self.shards, low_kind)

    def attend_first(self):
        made = self.made
        made["part"], made["turned"], send = attend_grad(
            self.layer, False, self.line.sec, made["attend"], self.cache[5], made["first"], self.cache[0], *self.heads()
        )
        self.attend_chunk = self.line.add(send, None)

    def attend_last(self):
        made = self.made
        made["gx"], made["gx_low"], self.attend_chunk.keep = attend_grad(
            self.layer, True, self.line.sec, made["attend"], self.cache[5], made["part"], made["turned"], *self.heads()
        )


def exchange(array, axis, bit):
    length = lax.axis_size(axis)
    return lax.ppermute(array, axis, [(i, i ^ bit) for i in range(length)])


def pick(array, index, axis):
    return lax.dynamic_index_in_dim(array, index, axis, keepdims=False)


def split_at(rows):
    return (rows // 2 + 15) // 16 * 16


class Sums:
    def __init__(self, columns):
        self.columns, self.ins, self.outs, self.code = columns, [], [], []
        self.rows, self.far, self.later = {}, set(), []

    def use(self, array):
        for index, known in enumerate(self.ins):
            if known is array:
                return index
        self.ins.append(array)
        return len(self.ins) - 1

    def result(self, shape):
        self.outs.append(sds(tuple(shape) + (self.columns,), BF16))
        return len(self.outs) - 1

    def region(self, way, rows):
        first = self.rows.get(way, 0)
        self.rows[way] = first + rows
        return first

    def run(self, ids):
        ways = sorted(self.rows)
        shapes = self.outs + [sds((self.rows[way], self.columns), BF16) for way in ways]
        n_in, n_out = len(self.ins), len(self.outs)

        far = sorted(self.far)
        space = lambda index: pltpu.HBM if index in self.far else pltpu.VMEM

        def kernel(ids_ref, *refs):
            first = n_in + len(shapes)
            sends = dict(zip(ways, refs[n_in + n_out : first]))
            ins, move = list(refs[:n_in]), Mover(refs[-1])
            waits = []
            for index, buffer in zip(far, refs[first:-1]):
                move.load(ins[index], buffer)
                waits.append(move.last)
                ins[index] = buffer
            for code in self.code:
                code(ids_ref, ins, refs[n_in : n_in + n_out], sends)
            ready(waits)
            for code in self.later:
                code(ids_ref, ins, refs[n_in : n_in + n_out], sends)

        vmem = pl.BlockSpec(memory_space=pltpu.VMEM)
        results = pl.pallas_call(
            kernel,
            in_specs=[pl.BlockSpec(memory_space=pltpu.SMEM)]
            + [pl.BlockSpec(memory_space=space(index)) for index in range(n_in)],
            out_specs=[vmem] * len(shapes),
            out_shape=shapes,
            scratch_shapes=[pltpu.VMEM(self.ins[index].shape, BF16) for index in far]
            + [pltpu.SemaphoreType.DMA((8,))],
            compiler_params=pltpu.CompilerParams(vmem_limit_bytes=SPARE),
            name="join_sums",
        )(
            ids,
            *(pltpu.with_memory_space_constraint(array, space(index)) for index, array in enumerate(self.ins)),
        )
        return results[:n_out], dict(zip(ways, results[n_out:]))


def at_rows(first, index, count):
    return pl.ds(pl.multiple_of(first + index * count, 16), count)


def sum_section(sums, chunk):
    kept, got = sums.use(chunk.keep), sums.use(chunk.got["section"])
    if chunk.far:
        sums.far |= {kept, got}
    _, rows, _ = chunk.keep.shape
    cut = chunk.cut
    rest = rows - cut
    top, bottom = sums.result((2, cut)), sums.result((2, rest))
    chunk.first = {"x": sums.region("x", 2 * cut), "y": sums.region("y", 2 * rest)}
    to_x, to_y = chunk.first["x"], chunk.first["y"]

    def code(ids, ins, outs, sends):
        low, high = ids[1], ids[2]
        for i in range(2):
            add = lambda shard, lines: ins[kept][shard, lines] + ins[got][shard, lines]
            sends["x"][to_x + i * cut : to_x + i * cut + cut] = add(2 * i + 1 - low, slice(0, cut))
            outs[top][i] = add(2 * i + low, slice(0, cut))
            sends["y"][to_y + i * rest : to_y + i * rest + rest] = add(2 * (1 - high) + i, slice(cut, rows))
            outs[bottom][i] = add(2 * high + i, slice(cut, rows))

    (sums.later if chunk.far else sums.code).append(code)
    return [top, bottom]


def sum_first(sums, chunk):
    top, bottom = (sums.use(item) for item in chunk.kept)
    got_x, got_y = sums.use(chunk.got["x"]), sums.use(chunk.got["y"])
    at_x, at_y = chunk.first["x"], chunk.first["y"]
    cut, rest = chunk.kept[0].shape[1], chunk.kept[1].shape[1]
    new_top, new_bottom = sums.result((cut,)), sums.result((rest,))
    chunk.first = {"y": sums.region("y", cut), "x": sums.region("x", rest)}
    to_x, to_y = chunk.first["x"], chunk.first["y"]

    def code(ids, ins, outs, sends):
        low, high = ids[1], ids[2]
        upper = lambda i: ins[top][i] + ins[got_x][at_rows(at_x, i, cut)]
        lower = lambda i: ins[bottom][i] + ins[got_y][at_rows(at_y, i, rest)]
        sends["y"][to_y : to_y + cut] = upper(1 - high)
        outs[new_top][...] = upper(high)
        sends["x"][to_x : to_x + rest] = lower(1 - low)
        outs[new_bottom][...] = lower(low)

    sums.code.append(code)
    return [new_top, new_bottom]


def sum_second(sums, chunk):
    top, bottom = (sums.use(item) for item in chunk.kept)
    got_x, got_y = sums.use(chunk.got["x"]), sums.use(chunk.got["y"])
    at_x, at_y = chunk.first["x"], chunk.first["y"]
    cut, rest = chunk.kept[0].shape[0], chunk.kept[1].shape[0]
    part = sums.result((cut + rest,))
    onward = chunk.line.short
    if onward:
        sums.rows["ends"] = max(sums.rows.get("ends", 0), cut + rest)

    def code(ids, ins, outs, sends):
        outs[part][:cut] = ins[top][...] + ins[got_y][at_y : at_y + cut]
        outs[part][cut:] = ins[bottom][...] + ins[got_x][at_x : at_x + rest]
        if onward:

            @pl.when(ids[3] == 1)
            def _():
                sends["ends"][: cut + rest] = outs[part][...]

    sums.code.append(code)
    return [part]


def sum_ends(sums, chunk):
    part, got = sums.use(chunk.kept[0]), sums.use(chunk.got["ends"])
    rows = chunk.kept[0].shape[0]
    chunk.first = {"middle": sums.region("middle", rows)}
    to = chunk.first["middle"]

    def code(ids, ins, outs, sends):
        sends["middle"][to : to + rows] = ins[part][...] + ins[got][:rows]

    sums.code.append(code)
    return []


def sum_middle(sums, chunk):
    sent, got = sums.use(chunk.sent["middle"]), sums.use(chunk.got["middle"])
    at, rows = chunk.first["middle"], chunk.rows
    whole = sums.result((rows,))
    sums.rows["ends"] = max(sums.rows.get("ends", 0), rows)

    def code(ids, ins, outs, sends):
        outs[whole][...] = ins[sent][at : at + rows] + ins[got][at : at + rows]

        @pl.when(ids[3] == 0)
        def _():
            sends["ends"][:rows] = outs[whole][...]

    sums.code.append(code)
    return [whole]


def sum_last(sums, chunk):
    whole, got = sums.use(chunk.kept[0]), sums.use(chunk.got["ends"])
    rows = chunk.rows
    results = [sums.result((rows,))]
    if chunk.partner is not None:
        other = sums.use(chunk.partner.done[0])
        results.append(sums.result((rows,)))

    def code(ids, ins, outs, sends):
        def put(value, outer):
            if chunk.partner is None:
                outs[results[0]][...] = value(slice(None))
                return
            for first, (to_value, to_other) in ((0, results), (1, results[::-1])):

                @pl.when((ids[0] == first) & (ids[3] == outer))
                def _():
                    outs[to_value][...] = value(slice(None))
                    outs[to_other][...] = ins[other][...]

        if chunk.partner is None:
            pl.when(ids[3] == 1)(lambda: put(lambda _: ins[got][:rows], 1))
            pl.when(ids[3] == 0)(lambda: put(lambda _: ins[whole][...], 0))
        else:
            put(lambda _: ins[got][:rows], 1)
            put(lambda _: ins[whole][...], 0)

    sums.code.append(code)
    return results


class Chunk:
    def __init__(self, line, send, keep, partner):
        self.line, self.send, self.keep, self.partner = line, send, keep, partner
        self.at, self.kept, self.got, self.sent, self.done = 0, [], {}, {}, None
        self.rows, self.far = send.shape[1], len(line.chunks) == 0
        self.cut = split_at(self.rows)


class Line:
    def __init__(self, sec):
        self.sec = sec
        self.square = lax.axis_size("inner") == 4
        self.short = lax.axis_size("outer") == 4
        spot, place = lax.axis_index("inner"), lax.axis_index("outer")
        outside = (place == 0) | (place == lax.axis_size("outer") - 1)
        self.ids = jnp.stack([lax.axis_index("section"), spot % 2, spot // 2, outside, spot]).astype(jnp.int32)
        self.chunks, self.made = [], {}
        self.sums = (sum_section, sum_first, sum_second, sum_ends, sum_middle, sum_last)

    def add(self, send, keep):
        count = len(self.chunks)
        chunk = Chunk(self, send, keep, self.chunks[count - 3] if count >= 3 else None)
        self.chunks.append(chunk)
        return chunk

    def move(self, way, array):
        if way == "section":
            return exchange(array, "section", 1)
        if way in ("x", "y"):
            return exchange(array, "inner", 1 if way == "x" else 2)
        return lax.ppermute(array, "outer", [(0, 1), (1, 0), (2, 3), (3, 2)] if way == "ends" else [(1, 2), (2, 1)])

    def advance(self, owner, *works):
        moving = [chunk for chunk in self.chunks if chunk.done is None and chunk.at > 0]
        sends = {}
        if moving and self.square:
            sums = Sums(moving[0].send.shape[-1])
            places = [self.sums[chunk.at - 1](sums, chunk) for chunk in moving]
            outs, sends = sums.run(self.ids)
            for chunk, place in zip(moving, places):
                chunk.kept, chunk.sent = [outs[index] for index in place], sends
        for chunk in moving:
            chunk.at += 1
            if not self.square:
                half = chunk.keep.astype(F32) + chunk.got["section"].astype(F32)
                half = lax.psum_scatter(half.astype(BF16), "inner", scatter_dimension=0, tiled=False)
                chunk.done = [lax.psum(half, "outer")]
            elif chunk.at == 4 and not self.short:
                chunk.done = [lax.psum(chunk.kept[0], "outer")]
            elif chunk.at == 7:
                chunk.done = chunk.kept
        new = [chunk for chunk in self.chunks if chunk.at == 0]
        gots = {way: self.move(way, array) for way, array in sends.items()}
        arrived = [self.move("section", chunk.send) for chunk in new]
        for work in works:
            work()
        fresh = [chunk for chunk in self.chunks if chunk not in new and chunk.at == 0]
        late = [chunk for chunk in self.chunks if chunk.keep is not None and chunk.at == 0]
        owner.made, parts, keeps, gots, arrived = lax.optimization_barrier(
            (owner.made, [chunk.send for chunk in fresh], [chunk.keep for chunk in late], gots, arrived)
        )
        for chunk, part in zip(fresh, parts):
            chunk.send = part
        for chunk, part in zip(late, keeps):
            chunk.keep = part
        for chunk in moving:
            chunk.got = gots
        for chunk, part in zip(new, arrived):
            chunk.at, chunk.got = 1, {"section": part}

    def finish(self):
        while any(chunk.done is None for chunk in self.chunks):
            self.advance(self)
        pairs = []
        for chunk in self.chunks[3:]:
            if len(chunk.done) == 1:
                two, one = chunk.partner.done[0], chunk.done[0]
                mine, send = (jnp.where(self.ids[0] == 0, *item) for item in ((one, two), (two, one)))
            else:
                mine, send = chunk.done
            pairs.append((mine, exchange(send, "section", 1)))
        return pairs


def assemble_kernel(sec, y_one, y_two, y_got, one, two_low, got, y_out, g_out, y, low, wide, sems):
    move = Mover(sems)
    first = sec[0] == 0
    loads = [
        move.choose(first, y_one.ref, y_got.ref, y.at[0]),
        move.choose(first, y_got.ref, y_two.ref, y.at[1]),
        move.choose(first, one.ref, got.ref, wide.at[0]),
    ]
    move.load(two_low.ref, low)
    loads.append(move.last)
    pl.when(first)(lambda: move.choose(first, got.ref, got.ref, wide.at[1]).wait())
    ready(loads)
    move.used += 1

    @pl.when(jnp.logical_not(first))
    def _():
        wide[1] = low[...].astype(F32)

    move.store(y, y_out.ref)
    move.store(wide, g_out.ref)
    move.finish()


def assemble(sec, y_one, y_two, y_got, one, two_low, got):
    flat = one.shape
    return call(
        assemble_kernel,
        sec,
        [(item, RAW) for item in (y_one, y_two, y_got, one, two_low, got)],
        [(sds((2,) + flat, BF16), RAW), (sds((2,) + flat, F32), RAW)],
        [((2,) + flat, BF16), (flat, BF16), ((2,) + flat, F32)],
        "assemble",
        1000,
        10 << 20,
    )


class Rest:
    def __init__(self, sec):
        self.sec, self.made = sec, {}

    def send(self, one, two_low):
        low = two_low.astype(F32)
        self.made["got"] = exchange(jnp.where(self.sec[0] == 0, low, one), "section", 1)

    def assemble(self, y_one, y_two, one, two_low):
        self.made["outs"] = assemble(self.sec, y_one, y_two, self.made["y"], one, two_low, self.made["got"])


def last_kernel(ids, down_mine, down_got, up_mine, up_got, mine, got, w_down, qkv, out, b_qv, b_out, gain, offset, b_up, b_down, w_up, sems):
    move = Mover(sems)
    up_wide = w_up.buffer.shape[1] // 2
    for half, side in ((ids[0], up_mine), (1 - ids[0], up_got)):
        w_up.buffer[:, pl.ds(pl.multiple_of(half * up_wide, up_wide), up_wide)] = side.buffer[...].astype(F32)
    w_up.flush(move)
    hidden, width = w_down.buffer.shape
    for half, side in ((ids[0], down_mine), (1 - ids[0], down_got)):
        rows = jnp.concatenate([side.buffer[:, :hidden], side.buffer[:, hidden:]], axis=0)
        w_down.buffer[:, pl.ds(pl.multiple_of(half * (width // 2), width // 2), width // 2)] = rows.T.astype(F32)
    w_down.flush(move)
    mine, got = mine.buffer, got.buffer
    tall, wide = qkv.buffer.shape[0], out.buffer.shape[1] // 2
    for half, side in ((ids[0], mine), (1 - ids[0], got)):
        for part in range(4):
            block = side[:tall, part * wide : part * wide + wide].astype(F32)
            target, first = (qkv, 2 * part * wide) if part < 3 else (out, 0)
            lanes = pl.ds(pl.multiple_of(first + half * wide, wide), wide)
            target.buffer[:, lanes] = block
    qkv.flush(move)
    out.flush(move)
    rows = mine[tall:, : 2 * wide].astype(F32)
    own, other = (side[tall : tall + 1, 2 * wide :].astype(F32) for side in (mine, got))

    def write(first_half, place):
        left, right = (own, other) if first_half else (other, own)
        span = slice(place * tall, place * tall + tall)
        for row in range(2):
            bias = jnp.concatenate([side[:, row * wide : row * wide + wide] for side in (left, right)], axis=1)
            b_qv.buffer[row : row + 1, :] = bias[:, span]
        b_out.buffer[...] = rows[10:11, span]
        gain.buffer[0:1, :] = rows[8:9, span]
        gain.buffer[1:2, :] = rows[0:1, span]
        offset.buffer[0:1, :] = rows[9:10, span]
        offset.buffer[1:2, :] = rows[1:2, span]
        b_up.buffer[...] = rows[11 + place : 12 + place]
        b_down.buffer[...] = rows[2:3, span]

    for first_half in (True, False):
        for place in range(2 * wide // tall):
            here = (ids[0] == (0 if first_half else 1)) & (ids[4] == place)
            pl.when(here)(functools.partial(write, first_half, place))
    for item in (b_qv, b_out, gain, offset, b_up, b_down):
        item.flush(move)
    move.finish()


def last(ids, down, up, attend, width, shards):
    tall = width // shards
    shapes = [(down[0].shape[1] // 2, width), (tall, 3 * width), (tall, width), (2, tall), (1, tall), (2, tall), (2, tall), (1, width), (1, tall)]
    shapes.append((tall, 2 * up[0].shape[1]))
    return call(
        last_kernel,
        ids,
        [(item, NEAR) for item in (*down, *up, *attend)],
        [(sds(shape, F32), FAR) for shape in shapes],
        [],
        "last",
        1000,
        5 << 20,
    )


def local(
    hidden_in, caption_len, region_len, cotangent, w_qkv, b_qv, w_out, b_out, ln_gain, ln_bias, w_up, b_up, w_down, b_down
):
    section = lax.axis_index("section")
    shards = lax.axis_size("inner")
    sec = section.astype(jnp.int32)[None]
    seqs_local, length, width = hidden_in.shape
    seqs = seqs_local // 2
    rows = seqs * length
    positions = jnp.arange(length, dtype=jnp.int32)[None, :]
    mine = lambda array: lax.dynamic_slice_in_dim(array, section * seqs, seqs, 0)
    caption, region = mine(caption_len)[:, None], mine(region_len)[:, None]
    valid = (positions < caption) | (positions >= CAP) & (positions < CAP + region)
    mask = jnp.concatenate([valid, valid], axis=1).astype(F32).T
    x = mine(hidden_in).reshape(rows, width)
    gy = jnp.where(valid[:, :, None], mine(cotangent), jnp.zeros((), BF16)).reshape(rows, width)

    blocks = w_up.shape[2] // width
    little = jnp.concatenate(
        [b_qv[0], b_out, ln_gain[0], ln_bias[0], b_down, b_up.reshape(blocks, width), jnp.zeros((8 - blocks, width), F32)]
    )
    little_other = exchange(little, "section", 1)
    big = (w_qkv[0], w_out[0], w_up[0], w_down[0])
    o_qkv = exchange(big[0], "section", 1)

    smalls = [jnp.where(section == layer, little, little_other) for layer in (0, 1)]
    o_qkv, smalls, mask, x, late_out, late_up = lax.optimization_barrier(
        (o_qkv, smalls, mask, x, big[1], big[2])
    )
    o_out, o_up = exchange(late_out, "section", 1), exchange(late_up, "section", 1)
    front = attend_forward(0, sec, x, FAR, big[0], o_qkv, smalls[0], mask)
    front, o_out, o_up, late_down = lax.optimization_barrier((front, o_out, o_up, big[3]))
    other = (o_qkv, o_out, o_up, exchange(late_down, "section", 1))
    y_one, cache_one = layer_forward(0, sec, x, front, big, other, smalls[0])
    y_near, y_one = y_one
    made = second_layer(sec, y_near, mask, big, other, smalls[1], gy)
    q, k, v, probs, ctx, hat_one, scale_one, low, slope, y_two = made[:10]
    cache_two = (y_one, q, k, v, probs, ctx, hat_one, scale_one, low, None, slope, None, None)
    line = Line(sec)
    two = Backward(line, 1, sec, cache_two, big, other, smalls[1], shards)
    one = Backward(line, 0, sec, cache_one, big, other, smalls[0], shards)
    two.made.update(second=made[10], branch=made[11], down_sums=made[12])
    line.add(made[13], made[14])
    exchanged_y = exchange(jnp.where(section == 0, y_two, y_one), "section", 1)
    line.advance(two, two.up_first)
    line.advance(two, two.up_last)
    line.advance(two, two.attention)
    gx_two_near, gx_two_low = two.made["gx_low"]
    line.advance(one, lambda: one.down(gx_two_near))
    line.advance(one, one.up)
    line.advance(one, one.attention)
    gx_one = one.made["gx"]

    rest = Rest(sec)
    rest.made["y"] = exchanged_y
    for _ in range(3):
        line.advance(line)
    line.advance(rest, lambda: rest.send(gx_one, gx_two_low))
    line.advance(rest, lambda: rest.assemble(y_one, y_two, gx_one, gx_two_low))
    activations, input_grads = rest.made["outs"]
    activations = activations.reshape(seqs_local, length, width)
    input_grads = input_grads.reshape(seqs_local, length, width)
    down, up, attend = line.finish()
    g_w_down, g_w_qkv, g_w_out, g_b_qv, g_b_out, g_gain, g_offset, g_b_up, g_b_down, g_w_up = last(
        line.ids, down, up, attend, width, shards
    )
    return (
        activations[None],
        input_grads[None],
        g_w_qkv[None],
        g_b_qv[None],
        g_w_out[None],
        g_b_out,
        g_gain[None],
        g_offset[None],
        g_w_up[None],
        g_b_up,
        g_w_down[None],
        g_b_down,
    )


def solution(mesh):
    rows = ("inner", "outer")
    return jax.shard_map(
        local,
        mesh=mesh,
        in_specs=(
            P(rows, None, None),
            P(rows),
            P(rows),
            P(rows, None, None),
            P("section", None, None),
            P("section", None, None),
            P("section", None, None),
            P("section", None),
            P("section", None, None),
            P("section", None, None),
            P("section", None, None),
            P("section", None),
            P("section", None, None),
            P("section", None),
        ),
        out_specs=(
            P("section", rows, None, None),
            P("section", rows, None, None),
            P("section", "inner", None),
            P("section", None, "inner"),
            P("section", "inner", None),
            P("section", "inner"),
            P("section", None, "inner"),
            P("section", None, "inner"),
            P("section", "inner", None),
            P("section", "inner"),
            P("section", "inner", None),
            P("section", "inner"),
        ),
        check_vma=False,
    )
```

```python
import functools
import math

import jax
import jax.numpy as jnp
from jax import lax
from jax.experimental import pallas as pl
from jax.experimental.pallas import tpu as pltpu
from jax.sharding import PartitionSpec as P

HEADS = 12
CAP = 28
EPS = 1e-12
SCALE = 0.125
SPARE = 8 * 1024 * 1024
F32 = jnp.float32
BF16 = jnp.bfloat16
B_Q, B_V, B_OUT, GAIN_ONE, GAIN_TWO, OFFSET_ONE, OFFSET_TWO, B_DOWN, B_UP = range(9)


def dot(left, right):
    return jnp.dot(left, right, preferred_element_type=F32)


def dot_t(left, right):
    return lax.dot_general(left, right, (((1,), (1,)), ((), ())), preferred_element_type=F32)


def t_dot(left, right):
    return lax.dot_general(left, right, (((0,), (0,)), ((), ())), preferred_element_type=F32)


def column_sum(values):
    return jnp.sum(values, axis=0, keepdims=True)


def standardize(summed):
    centre = jnp.mean(summed, axis=-1, keepdims=True)
    shifted = summed - centre
    spread = jnp.mean(shifted * shifted, axis=-1, keepdims=True)
    scale = lax.rsqrt(spread + EPS)
    return shifted * scale, scale


def norm_back(grad, hat, scale, gain):
    scaled = grad * gain
    return scale * (
        scaled
        - jnp.mean(scaled, axis=-1, keepdims=True)
        - hat * jnp.mean(scaled * hat, axis=-1, keepdims=True)
    )


def gauss_share(value):
    bell = jnp.exp2(value * value * -0.7213475204444817)
    part = 1.0 / (1.0 + 0.2316418882 * jnp.abs(value))
    tail = 0.5307027145
    for item in (-0.7265760135, 0.7107068705, -0.142248368, 0.127414796):
        tail = tail * part + item
    tail = tail * part * bell
    return jnp.where(value < 0.0, tail, 1.0 - tail), bell


def lane_halves():
    lane = lax.broadcasted_iota(jnp.int32, (1, 128), 1)
    lower = jnp.where(lane < 64, 1.0, 0.0)
    return lower.astype(BF16), (1.0 - lower).astype(BF16)


def two_heads(block, halves):
    return jnp.concatenate([block * halves[0], block * halves[1]], axis=0)


def sds(shape, dtype):
    return jax.ShapeDtypeStruct(shape, dtype)


class Mover:
    def __init__(self, sems):
        self.sems, self.used, self.outs = sems, 0, []

    def copy(self, source, target):
        self.used += 1
        return pltpu.make_async_copy(source, target, self.sems.at[self.used - 1])

    def load(self, source, target):
        self.last = self.copy(source, target)
        self.last.start()

    def choose(self, first, one, two, target):
        copy = self.copy(one, target)
        other = pltpu.make_async_copy(two, target, self.sems.at[self.used - 1])
        pl.when(first)(copy.start)
        pl.when(jnp.logical_not(first))(other.start)
        return copy

    def store(self, source, target):
        copy = self.copy(source, target)
        copy.start()
        self.outs.append(copy)

    def finish(self):
        for copy in self.outs:
            copy.wait()


class Operand:
    def __init__(self, ref, buffer, far):
        self.ref, self.buffer, self.far = ref, buffer, far

    def fetch(self, move, *index):
        if self.far:
            move.load(*(ref.at[index] if index else ref for ref in (self.ref, self.buffer)))
            return [move.last]
        return []

    def flush(self, move, *index):
        if self.far:
            move.store(*(ref.at[index] if index else ref for ref in (self.buffer, self.ref)))


NEAR, FAR, RAW, BOTH, FREE = "near", "far", "raw", "both", "free"


def run(*parts):
    for part in parts:
        next(part)
    for part in parts:
        for _ in part:
            pass


def ready(waits):
    for item in waits:
        item.wait()


def call(kernel, ids, ins, outs, scratch, name, flops, nbytes):
    space = lambda kind: {NEAR: pltpu.VMEM, FREE: pl.ANY}.get(kind, pltpu.HBM)
    spread = [(shape, part) for shape, kind in outs for part in ((NEAR, RAW) if kind == BOTH else (kind,))]
    kinds = [kind for _, kind in ins] + [kind for _, kind in spread]
    shapes = [array for array, _ in ins] + [shape for shape, _ in spread]
    buffers = [pltpu.VMEM(shape.shape, shape.dtype) for shape, kind in zip(shapes, kinds) if kind == FAR]

    def body(ids_ref, *refs):
        count = len(kinds)
        spare = list(refs[count : count + len(buffers)])
        left = list(refs[:count])
        operands = []
        for _, kind in list(ins) + list(outs):
            ref = left.pop(0)
            if kind == BOTH:
                operands.append(Operand(left.pop(0), ref, True))
            else:
                operands.append(Operand(ref, spare.pop(0) if kind == FAR else ref, kind == FAR))
        kernel(ids_ref, *operands, *refs[count + len(buffers) :])

    size = lambda shape, dtype: math.prod(shape) * jnp.dtype(dtype).itemsize
    limit = SPARE + sum(size(*item) for item in scratch)
    limit += sum(size(shape.shape, shape.dtype) for shape, kind in zip(shapes, kinds) if kind == FAR)
    results = pl.pallas_call(
        body,
        in_specs=[pl.BlockSpec(memory_space=pltpu.SMEM)]
        + [pl.BlockSpec(memory_space=space(kind)) for _, kind in ins],
        out_specs=[pl.BlockSpec(memory_space=space(kind)) for _, kind in spread],
        out_shape=[space(kind)(shape.shape, shape.dtype) for shape, kind in spread],
        scratch_shapes=buffers + [pltpu.VMEM(*item) for item in scratch] + [pltpu.SemaphoreType.DMA((64,))],
        compiler_params=pltpu.CompilerParams(vmem_limit_bytes=limit),
        cost_estimate=pl.CostEstimate(flops=flops, bytes_accessed=nbytes, transcendentals=0),
        name=name,
    )(ids, *(pltpu.with_memory_space_constraint(array, space(kind)) for array, kind in ins))
    results = list(results)
    return [(results.pop(0), results.pop(0)) if kind == BOTH else results.pop(0) for _, kind in outs]


def attend_phase(q, k, v, probs, ctx, mask, pairs):
    seqs = mask.shape[1]
    halves = lane_halves()
    feature = lax.broadcasted_iota(jnp.int32, (128, 128), 0)
    first_half = jnp.where(feature < 64, 1.0, 0.0).astype(BF16)
    second_half = jnp.where(feature < 64, 0.0, 1.0).astype(BF16)

    for seq in range(seqs):
        rows = slice(seq * 128, seq * 128 + 128)
        seen = jnp.broadcast_to(mask[:, seq : seq + 1], (256, 128)) > 0.5
        for pair in range(*pairs):
            lanes = slice(pair * 128, pair * 128 + 128)
            scores = dot_t(two_heads(k[rows, lanes], halves), q[rows, lanes] * SCALE)
            scores = jnp.where(seen, scores, -1e30)
            parts = []
            for part in (scores[:128], scores[128:]):
                e = jnp.exp(part - jnp.max(part, axis=0, keepdims=True))
                parts.append(e * (1.0 / jnp.sum(e, axis=0, keepdims=True)))
            parts = jnp.concatenate(parts, axis=0)
            probs[seq, pair] = parts
            turned = v[rows, lanes].T
            turned = jnp.concatenate([turned * first_half, turned * second_half], axis=1)
            ctx[lanes, rows] = dot(turned, parts.astype(BF16)).astype(BF16)


def attend_steps(move, layer, sec, x, w_a, w_b, small, mask, q, k, v, probs, ctx, w):
    mine = sec[0] == layer
    rows, width = x.buffer.shape
    waits = x.fetch(move) + small.fetch(move) + mask.fetch(move)
    parts = [
        move.choose(mine, w_a.ref.at[:, pl.ds(i * width, width)], w_b.ref.at[:, pl.ds(i * width, width)], w.at[i])
        for i in (1, 0, 2)
    ]
    yield
    ready(waits)
    x, small = x.buffer, small.buffer
    parts[0].wait()
    k.buffer[...] = dot(x[...], w[1]).astype(BF16)
    k.flush(move)
    parts[1].wait()
    q.buffer[...] = (dot(x[...], w[0]) + small[B_Q : B_Q + 1]).astype(BF16)
    q.flush(move)
    parts[2].wait()
    v.buffer[...] = (dot(x[...], w[2]) + small[B_V : B_V + 1]).astype(BF16)
    v.flush(move)
    half = width // 128 // 2
    for i in range(2):
        attend_phase(
            q.buffer, k.buffer, v.buffer, probs.buffer, ctx.buffer, mask.buffer, (i * half, i * half + half)
        )
        probs.flush(move, slice(None), pl.ds(i * half, half))
    ctx.flush(move)


def attend_kernel(layer, sec, *refs):
    move = Mover(refs[-1])
    run(attend_steps(move, layer, sec, *refs[:-1]))
    move.finish()


def attend_forward(layer, sec, x, x_kind, w_own, w_other, small, mask):
    rows, width = x.shape
    seqs = mask.shape[1]
    pairs = width // 128
    wide = sds((rows, width), BF16)
    return call(
        functools.partial(attend_kernel, layer),
        sec,
        [(x, x_kind), (w_own, RAW), (w_other, RAW), (small, FAR), (mask, FAR)],
        [(wide, FAR)] * 3 + [(sds((seqs, pairs, 256, 128), F32), FAR), (sds((width, rows), BF16), BOTH)],
        [((3, width, width), BF16)],
        "attend_forward",
        2 * rows * width * width * 4,
        12 << 20,
    )


def up_kernel(layer, sec, x, ctx, wo_a, wo_b, wu_a, wu_b, small, hat, scale, turned, act, slope, wo, wu, low, sems):
    move = Mover(sems)
    mine = sec[0] == layer
    blocks, _, wide = wu.shape
    waits = ctx.fetch(move) + [move.choose(mine, wo_a.ref, wo_b.ref, wo)] + small.fetch(move) + x.fetch(move)
    span = lambda i: pl.ds(i * wide, wide)
    parts = [move.choose(mine, wu_a.ref.at[:, span(i)], wu_b.ref.at[:, span(i)], wu.at[i]) for i in range(blocks)]
    ready(waits)
    small = small.buffer
    summed = x.buffer[...].astype(F32) + t_dot(ctx.buffer[...], wo[...]) + small[B_OUT : B_OUT + 1]
    unit, root = standardize(summed)
    hat.buffer[...] = unit
    hat.flush(move)
    scale.buffer[...] = jnp.broadcast_to(root, scale.buffer.shape)
    scale.flush(move)
    low[...] = (unit * small[GAIN_ONE : GAIN_ONE + 1] + small[OFFSET_ONE : OFFSET_ONE + 1]).astype(BF16)
    turned.buffer[...] = low[...].T
    turned.flush(move)
    for i in range(blocks):
        parts[i].wait()
        pre = dot(low[...], wu[i]) + small[B_UP + i : B_UP + i + 1]
        share, bell = gauss_share(pre)
        act.buffer[i] = (pre * share).astype(BF16)
        slope.buffer[i] = share + pre * 0.3989422804014327 * bell
        act.flush(move, i)
        slope.flush(move, i)
    move.finish()


def up_forward(layer, sec, x, x_kind, ctx, wo, wo_other, wu, wu_other, small):
    rows, width = x.shape
    blocks = wu.shape[1] // width
    wide = (rows, width)
    other_kind = FREE if layer == 0 else RAW
    return call(
        functools.partial(up_kernel, layer),
        sec,
        [(x, x_kind), (ctx, NEAR), (wo, RAW), (wo_other, other_kind), (wu, RAW), (wu_other, other_kind), (small, FAR)],
        [
            (sds(wide, F32), BOTH),
            (sds((rows, 128), F32), FAR),
            (sds((width, rows), BF16), FAR),
            (sds((blocks,) + wide, BF16), BOTH if layer == 0 else NEAR),
            (sds((blocks,) + wide, F32), FAR),
        ],
        [((width, width), BF16), ((blocks, width, width), BF16), (wide, BF16)],
        "up_forward",
        2 * rows * width * width * (blocks + 1),
        20 << 20,
    )


def down_kernel(layer, sec, act, wd_a, wd_b, hat, small, y, two, scale, wd, total, sems):
    move = Mover(sems)
    mine = sec[0] == layer
    blocks, wide, _ = wd.shape
    parts = []
    for i in range(blocks):
        span = pl.ds(i * wide, wide)
        parts.append(act.fetch(move, i) + [move.choose(mine, wd_a.ref.at[span], wd_b.ref.at[span], wd.at[i])])
        if i == 0:
            waits = small.fetch(move) + hat.fetch(move)
    for i in range(blocks):
        ready(parts[i])
        product = dot(act.buffer[i], wd[i])
        total[...] = product if i == 0 else total[...] + product
    ready(waits)
    small = small.buffer
    normed = hat.buffer[...] * small[GAIN_ONE : GAIN_ONE + 1] + small[OFFSET_ONE : OFFSET_ONE + 1]
    unit, root = standardize(total[...] + normed + small[B_DOWN : B_DOWN + 1])
    y.buffer[...] = (unit * small[GAIN_TWO : GAIN_TWO + 1] + small[OFFSET_TWO : OFFSET_TWO + 1]).astype(BF16)
    y.flush(move)
    two.buffer[...] = unit
    two.flush(move)
    scale.buffer[...] = jnp.broadcast_to(root, scale.buffer.shape)
    scale.flush(move)
    move.finish()


def down_forward(layer, sec, act, wd, wd_other, hat, small, y_kind, two_kind):
    blocks, rows, width = act.shape
    wide = (rows, width)
    return call(
        functools.partial(down_kernel, layer),
        sec,
        [(act, NEAR), (wd, RAW), (wd_other, FREE if layer == 0 else RAW), (hat, NEAR), (small, FAR)],
        [(sds(wide, BF16), y_kind), (sds(wide, F32), two_kind), (sds((rows, 128), F32), two_kind)],
        [((blocks, width, width), BF16), (wide, F32)],
        "down_forward",
        2 * rows * width * width * blocks,
        12 << 20,
    )


def up_down_steps(
    move, layer, sec, x, ctx, wo_a, wo_b, wu_a, wu_b, wd_a, wd_b, small,
    hat, scale, turned, act, slope, y, two, scale_two, wo, wu, wd, low, total,
):
    mine = sec[0] == layer
    blocks, _, wide = wu.shape
    waits = ctx.fetch(move) + [move.choose(mine, wo_a.ref, wo_b.ref, wo)] + small.fetch(move) + x.fetch(move)
    ups, downs = [], []
    for i in range(blocks):
        span = pl.ds(i * wide, wide)
        ups.append(move.choose(mine, wu_a.ref.at[:, span], wu_b.ref.at[:, span], wu.at[i]))
        downs.append(move.choose(mine, wd_a.ref.at[span], wd_b.ref.at[span], wd.at[i]))
    yield
    ready(waits)
    small = small.buffer
    summed = x.buffer[...].astype(F32) + t_dot(ctx.buffer[...], wo[...]) + small[B_OUT : B_OUT + 1]
    unit, root = standardize(summed)
    hat.buffer[...] = unit
    hat.flush(move)
    scale.buffer[...] = jnp.broadcast_to(root, scale.buffer.shape)
    scale.flush(move)
    normed = unit * small[GAIN_ONE : GAIN_ONE + 1] + small[OFFSET_ONE : OFFSET_ONE + 1]
    total[...] = normed + small[B_DOWN : B_DOWN + 1]
    low[...] = normed.astype(BF16)
    turned.buffer[...] = low[...].T
    turned.flush(move)
    for i in range(blocks):
        ups[i].wait()
        pre = dot(low[...], wu[i]) + small[B_UP + i : B_UP + i + 1]
        share, bell = gauss_share(pre)
        act.buffer[i] = (pre * share).astype(BF16)
        slope.buffer[i] = share + pre * 0.3989422804014327 * bell
        slope.flush(move, i)
        downs[i].wait()
        total[...] += dot(act.buffer[i], wd[i])
    unit, root = standardize(total[...])
    y.buffer[...] = (unit * small[GAIN_TWO : GAIN_TWO + 1] + small[OFFSET_TWO : OFFSET_TWO + 1]).astype(BF16)
    y.flush(move)
    two.buffer[...] = unit
    scale_two.buffer[...] = jnp.broadcast_to(root, scale_two.buffer.shape)


def down_grad_steps(move, sec, gy, hat, scale, small, act, second, branch, sums, send, keep, turned):
    blocks = act.buffer.shape[0]
    low_rows, wide = send.buffer.shape[1], act.buffer.shape[2]
    tall = 2 * low_rows
    waits = gy.fetch(move) + small.fetch(move) + scale.fetch(move) + hat.fetch(move)
    parts = [act.fetch(move, i) for i in range(blocks)]
    yield
    ready(waits)
    grad = gy.buffer[...].astype(F32)
    sums.buffer[0:1] = column_sum(grad * hat.buffer[...])
    sums.buffer[1:2] = column_sum(grad)
    unit = norm_back(grad, hat.buffer[...], scale.buffer[:, 0:1], small.buffer[GAIN_TWO : GAIN_TWO + 1])
    second.buffer[...] = unit
    second.flush(move)
    low = unit.astype(BF16)
    branch.buffer[...] = low
    branch.flush(move)
    sums.buffer[2:3] = column_sum(low.astype(F32))
    sums.buffer[3:] = jnp.zeros_like(sums.buffer[3:])
    sums.flush(move)
    turned[...] = branch.buffer[...].T
    for half, out in ((1 - sec[0], send), (sec[0], keep)):
        left = pl.ds(pl.multiple_of(half * tall, tall), tall)
        for i in range(blocks):
            if out is send:
                ready(parts[i])
            block = dot(turned[left, :], act.buffer[i]).astype(BF16)
            out.buffer[i, :, :wide] = block[:low_rows]
            out.buffer[i, :, wide:] = block[low_rows:]
            out.flush(move, i)


def down_grad_kernel(sec, *refs):
    move = Mover(refs[-1])
    run(down_grad_steps(move, sec, *refs[:-1]))
    move.finish()


def down_grad(sec, gy, gy_kind, hat, scale, small, act, kind):
    rows, width = gy.shape
    blocks = act.shape[0]
    wide = (rows, width)
    part = sds((blocks, width // 4, 2 * width), BF16)
    return call(
        down_grad_kernel,
        sec,
        [(gy, gy_kind), (hat, kind), (scale, kind), (small, FAR), (act, kind)],
        [(sds(wide, F32), NEAR), (sds(wide, BF16), NEAR), (sds((8, width), F32), NEAR), (part, NEAR), (part, FAR if kind == NEAR else NEAR)],
        [((width, rows), BF16)],
        "down_grad",
        2 * rows * width * width * blocks,
        14 << 20,
    )


def up_grad_kernel(layer, last, sec, *refs):
    refs = list(refs)
    take = lambda count: [refs.pop(0) for _ in range(count)]
    branch, base, wd_a, wd_b, slope_h, low, wu_a, wu_b = take(8)
    if last:
        hat, scale, small, sums_in = take(4)
        first, attend, sums, out = take(4)
    else:
        first, sums, out = take(3)
    wd, wu, slope, pre, sems = refs
    move = Mover(sems)
    mine = sec[0] == layer
    half, wide, _ = wd.shape
    side = sec[0] if last else 1 - sec[0]
    at = [side * half + i for i in range(half)]
    span = [pl.ds(pl.multiple_of(place * wide, wide), wide) for place in at]
    parts = []
    early = branch.fetch(move)
    for i in range(half):
        move.load(slope_h.ref.at[at[i]], slope.at[i])
        parts.append(
            [
                move.last,
                move.choose(mine, wd_a.ref.at[span[i]], wd_b.ref.at[span[i]], wd.at[i]),
                move.choose(mine, wu_a.ref.at[:, span[i]], wu_b.ref.at[:, span[i]], wu.at[i]),
            ]
        )
        if i == 0:
            early += low.fetch(move)
    late = base.fetch(move)
    if last:
        late += hat.fetch(move) + scale.fetch(move) + small.fetch(move)
        sums.buffer[...] = sums_in.buffer[...]
    else:
        sums.buffer[...] = jnp.zeros_like(sums.buffer)
    ready(early)
    total = first.buffer
    shards, tall, _ = out.buffer.shape
    for i in range(half):
        ready(parts[i])
        pre[...] = (dot_t(branch.buffer[...], wd[i]) * slope[i]).astype(BF16)
        sums.buffer[pl.ds(3 + at[i], 1)] = column_sum(pre[...].astype(F32))
        block = dot(low.buffer[...], pre[...]).astype(BF16)
        for shard in range(shards):
            out.buffer[shard, :, i * wide : i * wide + wide] = block[shard * tall : shard * tall + tall]
        if i == 0:
            ready(late)
            total[...] = base.buffer[...] + dot_t(pre[...], wu[i])
        else:
            total[...] += dot_t(pre[...], wu[i])
    if last:
        grad = total[...]
        sums.buffer[0:1] = column_sum(grad * hat.buffer[...])
        sums.buffer[1:2] = column_sum(grad)
        unit = norm_back(grad, hat.buffer[...], scale.buffer[:, 0:1], small.buffer[GAIN_ONE : GAIN_ONE + 1])
        attend.buffer[...] = unit.astype(BF16)
        total[...] = unit
        sums.buffer[2:3] = column_sum(attend.buffer[...].astype(F32))
    move.finish()


def up_grad(layer, last, sec, branch, base, wd, wd_other, slope, low, wu, wu_other, shards, more=()):
    blocks, rows, width = slope.shape
    half = blocks // 2
    wide = (rows, width)
    part = sds((shards, width // shards, half * width), BF16)
    square = ((half, width, width), BF16)
    near = lambda *shapes: [(shape, NEAR) for shape in shapes]
    ins = [
        (branch, NEAR),
        (base, NEAR),
        (wd, RAW),
        (wd_other, RAW),
        (slope, RAW),
        (low, FAR),
        (wu, RAW),
        (wu_other, RAW),
    ]
    if last:
        hat, scale, small, sums = more
        ins += [(hat, FAR), (scale, FAR), (small, FAR), (sums, NEAR)]
        outs = near(sds(wide, F32), sds(wide, BF16), sds((8, width), F32), part)
    else:
        outs = near(sds(wide, F32), sds((8, width), F32), part)
    return call(
        functools.partial(up_grad_kernel, layer, last),
        sec,
        ins,
        outs,
        [square, square, ((half,) + wide, F32), (wide, BF16)],
        "up_grad_last" if last else "up_grad_first",
        3 * rows * width * width * blocks,
        15 << 20,
    )


def attend_grad_kernel(layer, last, sec, *refs):
    refs = list(refs)
    take = lambda count: [refs.pop(0) for _ in range(count)]
    attend, ctx, base, x, q_h, k_h, v_h, p_h, wo_a, wo_b, w_a, w_b, down, up = take(14)
    if last:
        gx, gx_low, out = take(3)
    else:
        total, turned, out = take(3)
    q, k, v, probs, wo, w, gc, grads, sems = refs
    move = Mover(sems)
    mine = sec[0] == layer
    rows_all, wide = q.shape
    width = 2 * wide
    seqs = probs.shape[0]
    shards = out.buffer.shape[0]
    tall = width // shards
    pairs = wide // 128
    side = sec[0] if last else 1 - sec[0]
    lanes_half = pl.ds(pl.multiple_of(side * wide, wide), wide)
    waits = attend.fetch(move) + [move.choose(mine, wo_a.ref.at[lanes_half], wo_b.ref.at[lanes_half], wo)]
    near = []
    for source, target in (
        (p_h.ref.at[:, pl.ds(side * pairs, pairs)], probs),
        (v_h.ref.at[:, lanes_half], v),
        (k_h.ref.at[:, lanes_half], k),
        (q_h.ref.at[:, lanes_half], q),
    ):
        move.load(source, target)
        near.append(move.last)
    later = x.fetch(move) + ctx.fetch(move) + down.fetch(move) + up.fetch(move)
    finals = base.fetch(move)
    for i in range(3):
        there = pl.ds(pl.multiple_of(i * width + side * wide, wide), wide)
        finals.append(move.choose(mine, w_a.ref.at[:, there], w_b.ref.at[:, there], w.at[:, pl.ds(i * wide, wide)]))
    ready(waits)
    gc[...] = dot_t(attend.buffer[...], wo[...]).astype(BF16)
    ready(near)
    halves = lane_halves()
    lower = lax.broadcasted_iota(jnp.int32, (128, 128), 1) < 64

    for pair in range(pairs):
        lanes = slice(pair * 128, pair * 128 + 128)
        for seq in range(seqs):
            rows = slice(seq * 128, seq * 128 + 128)

            def put(part, value):
                grads[rows, part * wide + pair * 128 : part * wide + pair * 128 + 128] = value.astype(BF16)

            grad = gc[rows, lanes]
            p = probs[seq, pair]
            full = dot(p.astype(BF16), grad)
            put(2, jnp.where(lower, full[:128], full[128:]))
            gp = dot_t(two_heads(v[rows, lanes], halves), grad)
            parts = []
            for part in (slice(0, 128), slice(128, 256)):
                g, pp = gp[part], p[part]
                parts.append(pp * (g - jnp.sum(g * pp, axis=0, keepdims=True)))
            gs = jnp.concatenate(parts, axis=0).astype(BF16)
            put(0, t_dot(gs, two_heads(k[rows, lanes] * SCALE, halves)))
            full = dot(gs, q[rows, lanes] * SCALE)
            put(1, jnp.where(lower, full[:128], full[128:]))
    ready(later)
    if last:
        turned = x
    else:
        turned.buffer[...] = x.buffer[...].T
    left = dot(turned.buffer[...], grads[...]).astype(BF16)
    right = dot(ctx.buffer[...], attend.buffer[:, lanes_half]).astype(BF16)
    little = jnp.concatenate([down.buffer[...], up.buffer[...]], axis=0).astype(BF16)
    zeros = jnp.zeros_like(little)
    b_q = column_sum(grads[:, 0:wide].astype(F32)).astype(BF16)
    b_v = column_sum(grads[:, 2 * wide :].astype(F32)).astype(BF16)
    pad = jnp.concatenate([b_q, b_v], axis=1)
    pad = jnp.concatenate([pad, jnp.zeros((15, width), BF16)], axis=0)
    for shard in range(shards):
        out.buffer[shard, :tall, 0 : 3 * wide] = left[shard * tall : shard * tall + tall]
        out.buffer[shard, :tall, 3 * wide :] = right[shard * tall : shard * tall + tall]
        out.buffer[shard, tall:, 0:width] = little
        out.buffer[shard, tall:, width:] = pad
    ready(finals)
    sum_all = base.buffer[...] + dot_t(grads[...], w[...])
    if last:
        gx.buffer[...] = sum_all
        gx.flush(move)
        gx_low.buffer[...] = sum_all.astype(BF16)
        gx_low.flush(move)
    else:
        total.buffer[...] = sum_all
    move.finish()


def attend_grad(layer, last, sec, attend, ctx, base, x, q, k, v, probs, wo, wo_other, w, w_other, down, up, shards, low_kind):
    rows, width = attend.shape
    seqs = probs.shape[0]
    wide = width // 2
    flat = (rows, width)
    part = (sds((shards, width // shards + 16, 2 * width), BF16), NEAR)
    if last:
        outs = [(sds(flat, F32), FAR), (sds(flat, BF16), low_kind), part]
    else:
        outs = [(sds(flat, F32), NEAR), (sds((width, rows), BF16), NEAR), part]
    half = ((rows, wide), BF16)
    return call(
        functools.partial(attend_grad_kernel, layer, last),
        sec,
        [(attend, NEAR), (ctx, FAR), (base, NEAR), (x, NEAR if last else FAR)]
        + [(item, RAW) for item in (q, k, v, probs, wo, wo_other, w, w_other)]
        + [(down, NEAR), (up, NEAR)],
        outs,
        [
            half,
            half,
            half,
            ((seqs, wide // 128) + probs.shape[2:], F32),
            ((wide, width), BF16),
            ((width, 3 * wide), BF16),
            half,
            ((rows, 3 * wide), BF16),
        ],
        "attend_grad_last" if last else "attend_grad_first",
        rows * width * width * 10,
        15 << 20,
    )


def second_kernel(sec, *refs):
    refs = list(refs)
    take = lambda count: [refs.pop(0) for _ in range(count)]
    inside = lambda item: Operand(None, item, False)
    x, w_a, w_b, small, mask = take(5)
    weights, (gy,) = take(6), take(1)
    q, k, v, probs, ctx, hat, scale, turned, slope, y = take(10)
    second, branch, sums, send, keep = take(5)
    w, wo, wu, wd, low, total, act, two, scale_two, branch_turned, sems = refs
    move = Mover(sems)
    near = inside(small.buffer)
    act, two, scale_two = inside(act), inside(two), inside(scale_two)
    run(
        attend_steps(move, 1, sec, x, w_a, w_b, small, mask, q, k, v, probs, ctx, w),
        up_down_steps(
            move, 1, sec, x, inside(ctx.buffer), *weights, near,
            hat, scale, turned, act, slope, y, two, scale_two, wo, wu, wd, low, total,
        ),
        down_grad_steps(move, sec, gy, two, scale_two, near, act, second, branch, sums, send, keep, branch_turned),
    )
    move.finish()


def second_layer(sec, x, mask, big, other, small, gy):
    rows, width = x.shape
    seqs = mask.shape[1]
    pairs = width // 128
    (w, w_other), (wo, wo_other), (wu, wu_other), (wd, wd_other) = zip(big, other)
    blocks = wu.shape[1] // width
    wide = (rows, width)
    part = sds((blocks, width // 4, 2 * width), BF16)
    square = lambda count: ((count, width, width), BF16)
    return call(
        second_kernel,
        sec,
        [(x, NEAR), (w, RAW), (w_other, RAW), (small, FAR), (mask, FAR)]
        + [(item, RAW) for item in (wo, wo_other, wu, wu_other, wd, wd_other)]
        + [(gy, FAR)],
        [(sds(wide, BF16), FAR)] * 3
        + [
            (sds((seqs, pairs, 256, 128), F32), FAR),
            (sds((width, rows), BF16), FAR),
            (sds(wide, F32), FAR),
            (sds((rows, 128), F32), FAR),
            (sds((width, rows), BF16), FAR),
            (sds((blocks,) + wide, F32), FAR),
            (sds(wide, BF16), FAR),
            (sds(wide, F32), NEAR),
            (sds(wide, BF16), NEAR),
            (sds((8, width), F32), NEAR),
            (part, NEAR),
            (part, FAR),
        ],
        [
            square(3),
            ((width, width), BF16),
            square(blocks),
            square(blocks),
            (wide, BF16),
            (wide, F32),
            ((blocks,) + wide, BF16),
            (wide, F32),
            ((rows, 128), F32),
            ((width, rows), BF16),
        ],
        "second_layer",
        2 * rows * width * width * (3 * blocks + 5),
        50 << 20,
    )


def up_whole_kernel(
    layer, sec, branch, second, wd_a, wd_b, slope, low, wu_a, wu_b, hat, scale, small,
    first, attend, sums, send, keep, wd, wu, pre, sems,
):
    move = Mover(sems)
    mine = sec[0] == layer
    blocks, wide, _ = wd.shape
    half = blocks // 2
    at = [lax.rem(i + half * (1 - sec[0]), blocks) for i in range(blocks)]
    span = [pl.ds(pl.multiple_of(place * wide, wide), wide) for place in at]
    parts = []
    early = branch.fetch(move)
    for i in range(blocks):
        parts.append(
            [move.choose(mine, wd_a.ref.at[span[i]], wd_b.ref.at[span[i]], wd.at[i])]
            + slope.fetch(move, at[i])
            + [
                move.choose(
                    mine,
                    wu_a.ref.at[:, span[i]],
                    wu_b.ref.at[:, span[i]],
                    wu.at[i // half, :, pl.ds(i % half * wide, wide)],
                )
            ]
        )
        if i == 0:
            early += low.fetch(move)
    late = second.fetch(move) + hat.fetch(move) + scale.fetch(move) + small.fetch(move)
    ready(early)
    branch, low, total = branch.buffer, low.buffer, first.buffer
    for side, out in enumerate((send, keep)):
        for i in range(half):
            block = side * half + i
            ready(parts[block])
            lanes = slice(i * wide, i * wide + wide)
            pre[:, lanes] = (dot_t(branch[...], wd[block]) * slope.buffer[at[block]]).astype(BF16)
            sums.buffer[pl.ds(3 + at[block], 1)] = column_sum(pre[:, lanes].astype(F32))
        product = dot(low[...], pre[...]).astype(BF16)
        shards, tall, _ = out.buffer.shape
        for shard in range(shards):
            out.buffer[shard] = product[shard * tall : shard * tall + tall]
        if side == 0:
            ready(late)
            total[...] = second.buffer[...] + dot_t(pre[...], wu[side])
        else:
            total[...] += dot_t(pre[...], wu[side])
    grad = total[...]
    sums.buffer[0:1] = column_sum(grad * hat.buffer[...])
    sums.buffer[1:2] = column_sum(grad)
    unit = norm_back(grad, hat.buffer[...], scale.buffer[:, 0:1], small.buffer[GAIN_ONE : GAIN_ONE + 1])
    attend.buffer[...] = unit.astype(BF16)
    attend.flush(move)
    total[...] = unit
    first.flush(move)
    sums.buffer[2:3] = column_sum(attend.buffer[...].astype(F32))
    sums.buffer[3 + blocks :] = jnp.zeros_like(sums.buffer[3 + blocks :])
    sums.flush(move)
    move.finish()


def up_whole(layer, sec, branch, second, wd, wd_other, slope, low, wu, wu_other, hat, scale, small, shards):
    blocks, rows, width = slope.shape
    wide = (rows, width)
    part = sds((shards, width // shards, blocks * width // 2), BF16)
    square = ((blocks, width, width), BF16)
    return call(
        functools.partial(up_whole_kernel, layer),
        sec,
        [
            (branch, NEAR),
            (second, NEAR),
            (wd, RAW),
            (wd_other, RAW),
            (slope, FAR),
            (low, FAR),
            (wu, RAW),
            (wu_other, RAW),
            (hat, FAR),
            (scale, FAR),
            (small, FAR),
        ],
        [(sds(wide, F32), NEAR), (sds(wide, BF16), NEAR), (sds((8, width), F32), NEAR), (part, NEAR), (part, NEAR)],
        [square, ((2, width, blocks // 2 * width), BF16), ((rows, blocks // 2 * width), BF16)],
        "up_grad",
        6 * rows * width * width * blocks,
        30 << 20,
    )


def attend_whole_kernel(
    layer, shards, sec, attend, ctx, first, x, q, k, v, probs, wo_a, wo_b, w_a, w_b, down, up,
    gx, gx_low, send, keep, turned, wo, w, gc, grads, sems,
):
    move = Mover(sems)
    mine = sec[0] == layer
    rows_all, width = x.buffer.shape
    seqs = probs.buffer.shape[0]
    wide = width // 2
    tall = width // shards
    pairs = wide // 128
    waits = attend.fetch(move) + [move.choose(mine, wo_a.ref, wo_b.ref, wo)]
    near = probs.fetch(move) + v.fetch(move) + k.fetch(move) + q.fetch(move)
    later = x.fetch(move) + ctx.fetch(move) + down.fetch(move) + up.fetch(move)
    last = [
        move.choose(
            mine,
            w_a.ref.at[:, pl.ds(i * width + half * wide, wide)],
            w_b.ref.at[:, pl.ds(i * width + half * wide, wide)],
            w.at[:, pl.ds((3 * half + i) * wide, wide)],
        )
        for i in range(3)
        for half in range(2)
    ] + first.fetch(move)
    ready(waits)
    attend, q, k, v, probs = (item.buffer for item in (attend, q, k, v, probs))
    gc[...] = dot_t(attend[...], wo[...]).astype(BF16)
    ready(near)
    halves = lane_halves()
    lower = lax.broadcasted_iota(jnp.int32, (128, 128), 1) < 64

    def attention(half):
        for index in range(pairs):
            lanes = pl.ds(pl.multiple_of(half * wide + index * 128, 128), 128)

            def put(part, rows, value, index=index):
                there = pl.ds(pl.multiple_of((3 * half + part) * wide + index * 128, 128), 128)
                grads[rows, there] = value.astype(BF16)

            for seq in range(seqs):
                rows = slice(seq * 128, seq * 128 + 128)
                grad = gc[rows, lanes]
                p = probs[seq, half * pairs + index]
                full = dot(p.astype(BF16), grad)
                put(2, rows, jnp.where(lower, full[:128], full[128:]))
                gp = dot_t(two_heads(v[rows, lanes], halves), grad)
                parts = []
                for side in (slice(0, 128), slice(128, 256)):
                    g, pp = gp[side], p[side]
                    parts.append(pp * (g - jnp.sum(g * pp, axis=0, keepdims=True)))
                gs = jnp.concatenate(parts, axis=0).astype(BF16)
                put(0, rows, t_dot(gs, two_heads(k[rows, lanes] * SCALE, halves)))
                full = dot(gs, q[rows, lanes] * SCALE)
                put(1, rows, jnp.where(lower, full[:128], full[128:]))

    def products(half, out):
        three = pl.ds(pl.multiple_of(half * 3 * wide, 128), 3 * wide)
        lanes = pl.ds(pl.multiple_of(half * wide, wide), wide)
        block = dot(turned[...], grads[:, three]).astype(BF16)
        block_out = dot(ctx.buffer[...], attend[:, lanes]).astype(BF16)
        for shard in range(shards):
            out.buffer[shard, :tall, : 3 * wide] = block[shard * tall : shard * tall + tall]
            out.buffer[shard, :tall, 3 * wide :] = block_out[shard * tall : shard * tall + tall]

    attention(1 - sec[0])
    ready(later)
    turned[...] = x.buffer[...].T
    products(1 - sec[0], send)
    attention(sec[0])
    products(sec[0], keep)
    little = jnp.concatenate([down.buffer[...], up.buffer[...]], axis=0).astype(BF16)
    for half, out in ((1 - sec[0], send), (sec[0], keep)):
        pad = []
        for part in (0, 2):
            lanes = pl.ds(pl.multiple_of((3 * half + part) * wide, wide), wide)
            pad.append(column_sum(grads[:, lanes].astype(F32)).astype(BF16))
        pad = jnp.concatenate([jnp.concatenate(pad, axis=1), jnp.zeros((15, width), BF16)], axis=0)
        for shard in range(shards):
            out.buffer[shard, tall:, 0:width] = little
            out.buffer[shard, tall:, width:] = pad
    ready(last)
    total = first.buffer[...] + dot_t(grads[...], w[...])
    gx.buffer[...] = total
    gx.flush(move)
    gx_low.buffer[...] = total.astype(BF16)
    gx_low.flush(move)
    move.finish()


def attend_whole(layer, sec, attend, ctx, first, x, q, k, v, probs, wo, wo_other, w, w_other, down, up, shards, low_kind):
    rows, width = x.shape
    wide = (rows, width)
    part = sds((shards, width // shards + 16, 2 * width), BF16)
    return call(
        functools.partial(attend_whole_kernel, layer, shards),
        sec,
        [(attend, NEAR), (ctx, FAR), (first, NEAR)]
        + [(item, FAR) for item in (x, q, k, v, probs)]
        + [(wo, RAW), (wo_other, RAW), (w, RAW), (w_other, RAW), (down, NEAR), (up, NEAR)],
        [(sds(wide, F32), FAR), (sds(wide, BF16), low_kind), (part, NEAR), (part, NEAR)],
        [((width, rows), BF16), ((width, width), BF16), ((width, 3 * width), BF16), (wide, BF16), ((rows, 3 * width), BF16)],
        "attend_grad",
        2 * rows * width * width * 10,
        30 << 20,
    )


def layer_forward(layer, sec, x, front, big, other, small, far=None):
    w_qkv, w_out, w_up, w_down = big
    o_qkv, o_out, o_up, o_down = other
    x_kind = FAR if layer == 0 else NEAR
    q, k, v, probs, (ctx_near, ctx) = front
    (hat_near, hat_one), scale_one, low, act, slope = up_forward(
        layer, sec, x, x_kind, ctx_near, w_out, o_out, w_up, o_up, small
    )
    act_near, act = act if layer == 0 else (act, act)
    kinds = (BOTH, FAR) if layer == 0 else (FAR, NEAR)
    y, hat_two, scale_two = down_forward(layer, sec, act_near, w_down, o_down, hat_near, small, *kinds)
    x = x if far is None else far
    return y, (x, q, k, v, probs, ctx, hat_one, scale_one, low, act, slope, hat_two, scale_two)


class Backward:
    def __init__(self, line, layer, sec, cache, big, other, small, shards):
        self.line, self.layer, self.sec, self.small, self.shards = line, layer, sec, small, shards
        self.cache, self.weights, self.made = cache, tuple(zip(big, other)), {}

    def down(self, gy):
        act, _, hat_two, scale_two = self.cache[-4:]
        kinds = (NEAR, FAR) if self.layer == 0 else (FAR, NEAR)
        second, branch, sums, send, keep = down_grad(
            self.line.sec, gy, kinds[0], hat_two, scale_two, self.small, act, kinds[1]
        )
        self.made.update(second=second, branch=branch, down_sums=sums)
        self.line.add(send, keep)

    def up_inputs(self):
        (w_up, o_up), (w_down, o_down) = self.weights[2:]
        low, _, slope = self.cache[-5:-2]
        return w_down, o_down, slope, low, w_up, o_up, self.shards

    def up_first(self):
        made = self.made
        made["part"], made["up_sums"], send = up_grad(
            self.layer, False, self.line.sec, made["branch"], made["second"], *self.up_inputs()
        )
        self.up_chunk = self.line.add(send, None)

    def up_last(self):
        made = self.made
        hat_one, scale_one = self.cache[-7:-5]
        more = (hat_one, scale_one, self.small, made["up_sums"])
        made["first"], made["attend"], made["up_sums"], self.up_chunk.keep = up_grad(
            self.layer, True, self.line.sec, made["branch"], made["part"], *self.up_inputs(), more
        )

    def up(self):
        made = self.made
        hat_one, scale_one = self.cache[-7:-5]
        ins = self.up_inputs()
        made["first"], made["attend"], made["up_sums"], send, keep = up_whole(
            self.layer, self.line.sec, made["branch"], made["second"], *ins[:-1], hat_one, scale_one, self.small, ins[-1]
        )
        self.line.add(send, keep)

    def attention(self):
        made = self.made
        made["gx"], made["gx_low"], send, keep = attend_whole(
            self.layer, self.line.sec, made["attend"], self.cache[5], made["first"], self.cache[0], *self.heads()
        )
        self.line.add(send, keep)

    def heads(self):
        q, k, v, probs = self.cache[1:5]
        (w_qkv, o_qkv), (w_out, o_out) = self.weights[:2]
        low_kind = FAR if self.layer == 0 else BOTH
        sums = (self.made["down_sums"], self.made["up_sums"])
        return (q, k, v, probs, w_out, o_out, w_qkv, o_qkv) + sums + (self.shards, low_kind)

    def attend_first(self):
        made = self.made
        made["part"], made["turned"], send = attend_grad(
            self.layer, False, self.line.sec, made["attend"], self.cache[5], made["first"], self.cache[0], *self.heads()
        )
        self.attend_chunk = self.line.add(send, None)

    def attend_last(self):
        made = self.made
        made["gx"], made["gx_low"], self.attend_chunk.keep = attend_grad(
            self.layer, True, self.line.sec, made["attend"], self.cache[5], made["part"], made["turned"], *self.heads()
        )


def exchange(array, axis, bit):
    length = lax.axis_size(axis)
    return lax.ppermute(array, axis, [(i, i ^ bit) for i in range(length)])


def pick(array, index, axis):
    return lax.dynamic_index_in_dim(array, index, axis, keepdims=False)


def split_at(rows):
    return (rows // 2 + 15) // 16 * 16


class Sums:
    def __init__(self, columns):
        self.columns, self.ins, self.outs, self.code = columns, [], [], []
        self.rows, self.far, self.later = {}, set(), []

    def use(self, array):
        for index, known in enumerate(self.ins):
            if known is array:
                return index
        self.ins.append(array)
        return len(self.ins) - 1

    def result(self, shape):
        self.outs.append(sds(tuple(shape) + (self.columns,), BF16))
        return len(self.outs) - 1

    def region(self, way, rows):
        first = self.rows.get(way, 0)
        self.rows[way] = first + rows
        return first

    def run(self, ids):
        ways = sorted(self.rows)
        shapes = self.outs + [sds((self.rows[way], self.columns), BF16) for way in ways]
        n_in, n_out = len(self.ins), len(self.outs)

        far = sorted(self.far)
        space = lambda index: pltpu.HBM if index in self.far else pltpu.VMEM

        def kernel(ids_ref, *refs):
            first = n_in + len(shapes)
            sends = dict(zip(ways, refs[n_in + n_out : first]))
            ins, move = list(refs[:n_in]), Mover(refs[-1])
            waits = []
            for index, buffer in zip(far, refs[first:-1]):
                move.load(ins[index], buffer)
                waits.append(move.last)
                ins[index] = buffer
            for code in self.code:
                code(ids_ref, ins, refs[n_in : n_in + n_out], sends)
            ready(waits)
            for code in self.later:
                code(ids_ref, ins, refs[n_in : n_in + n_out], sends)

        vmem = pl.BlockSpec(memory_space=pltpu.VMEM)
        results = pl.pallas_call(
            kernel,
            in_specs=[pl.BlockSpec(memory_space=pltpu.SMEM)]
            + [pl.BlockSpec(memory_space=space(index)) for index in range(n_in)],
            out_specs=[vmem] * len(shapes),
            out_shape=shapes,
            scratch_shapes=[pltpu.VMEM(self.ins[index].shape, BF16) for index in far]
            + [pltpu.SemaphoreType.DMA((8,))],
            compiler_params=pltpu.CompilerParams(vmem_limit_bytes=SPARE),
            name="join_sums",
        )(
            ids,
            *(pltpu.with_memory_space_constraint(array, space(index)) for index, array in enumerate(self.ins)),
        )
        return results[:n_out], dict(zip(ways, results[n_out:]))


def at_rows(first, index, count):
    return pl.ds(pl.multiple_of(first + index * count, 16), count)


def sum_section(sums, chunk):
    kept, got = sums.use(chunk.keep), sums.use(chunk.got["section"])
    if chunk.far:
        sums.far |= {kept, got}
    _, rows, _ = chunk.keep.shape
    cut = chunk.cut
    rest = rows - cut
    top, bottom = sums.result((2, cut)), sums.result((2, rest))
    chunk.first = {"x": sums.region("x", 2 * cut), "y": sums.region("y", 2 * rest)}
    to_x, to_y = chunk.first["x"], chunk.first["y"]

    def code(ids, ins, outs, sends):
        low, high = ids[1], ids[2]
        for i in range(2):
            add = lambda shard, lines: ins[kept][shard, lines] + ins[got][shard, lines]
            sends["x"][to_x + i * cut : to_x + i * cut + cut] = add(2 * i + 1 - low, slice(0, cut))
            outs[top][i] = add(2 * i + low, slice(0, cut))
            sends["y"][to_y + i * rest : to_y + i * rest + rest] = add(2 * (1 - high) + i, slice(cut, rows))
            outs[bottom][i] = add(2 * high + i, slice(cut, rows))

    (sums.later if chunk.far else sums.code).append(code)
    return [top, bottom]


def sum_first(sums, chunk):
    top, bottom = (sums.use(item) for item in chunk.kept)
    got_x, got_y = sums.use(chunk.got["x"]), sums.use(chunk.got["y"])
    at_x, at_y = chunk.first["x"], chunk.first["y"]
    cut, rest = chunk.kept[0].shape[1], chunk.kept[1].shape[1]
    new_top, new_bottom = sums.result((cut,)), sums.result((rest,))
    chunk.first = {"y": sums.region("y", cut), "x": sums.region("x", rest)}
    to_x, to_y = chunk.first["x"], chunk.first["y"]

    def code(ids, ins, outs, sends):
        low, high = ids[1], ids[2]
        upper = lambda i: ins[top][i] + ins[got_x][at_rows(at_x, i, cut)]
        lower = lambda i: ins[bottom][i] + ins[got_y][at_rows(at_y, i, rest)]
        sends["y"][to_y : to_y + cut] = upper(1 - high)
        outs[new_top][...] = upper(high)
        sends["x"][to_x : to_x + rest] = lower(1 - low)
        outs[new_bottom][...] = lower(low)

    sums.code.append(code)
    return [new_top, new_bottom]


def sum_second(sums, chunk):
    top, bottom = (sums.use(item) for item in chunk.kept)
    got_x, got_y = sums.use(chunk.got["x"]), sums.use(chunk.got["y"])
    at_x, at_y = chunk.first["x"], chunk.first["y"]
    cut, rest = chunk.kept[0].shape[0], chunk.kept[1].shape[0]
    part = sums.result((cut + rest,))
    onward = chunk.line.short
    if onward:
        sums.rows["ends"] = max(sums.rows.get("ends", 0), cut + rest)

    def code(ids, ins, outs, sends):
        outs[part][:cut] = ins[top][...] + ins[got_y][at_y : at_y + cut]
        outs[part][cut:] = ins[bottom][...] + ins[got_x][at_x : at_x + rest]
        if onward:

            @pl.when(ids[3] == 1)
            def _():
                sends["ends"][: cut + rest] = outs[part][...]

    sums.code.append(code)
    return [part]


def sum_ends(sums, chunk):
    part, got = sums.use(chunk.kept[0]), sums.use(chunk.got["ends"])
    rows = chunk.kept[0].shape[0]
    chunk.first = {"middle": sums.region("middle", rows)}
    to = chunk.first["middle"]

    def code(ids, ins, outs, sends):
        sends["middle"][to : to + rows] = ins[part][...] + ins[got][:rows]

    sums.code.append(code)
    return []


def sum_middle(sums, chunk):
    sent, got = sums.use(chunk.sent["middle"]), sums.use(chunk.got["middle"])
    at, rows = chunk.first["middle"], chunk.rows
    whole = sums.result((rows,))
    sums.rows["ends"] = max(sums.rows.get("ends", 0), rows)

    def code(ids, ins, outs, sends):
        outs[whole][...] = ins[sent][at : at + rows] + ins[got][at : at + rows]

        @pl.when(ids[3] == 0)
        def _():
            sends["ends"][:rows] = outs[whole][...]

    sums.code.append(code)
    return [whole]


def sum_last(sums, chunk):
    whole, got = sums.use(chunk.kept[0]), sums.use(chunk.got["ends"])
    rows = chunk.rows
    results = [sums.result((rows,))]
    if chunk.partner is not None:
        other = sums.use(chunk.partner.done[0])
        results.append(sums.result((rows,)))

    def code(ids, ins, outs, sends):
        def put(value, outer):
            if chunk.partner is None:
                outs[results[0]][...] = value(slice(None))
                return
            for first, (to_value, to_other) in ((0, results), (1, results[::-1])):

                @pl.when((ids[0] == first) & (ids[3] == outer))
                def _():
                    outs[to_value][...] = value(slice(None))
                    outs[to_other][...] = ins[other][...]

        if chunk.partner is None:
            pl.when(ids[3] == 1)(lambda: put(lambda _: ins[got][:rows], 1))
            pl.when(ids[3] == 0)(lambda: put(lambda _: ins[whole][...], 0))
        else:
            put(lambda _: ins[got][:rows], 1)
            put(lambda _: ins[whole][...], 0)

    sums.code.append(code)
    return results


class Chunk:
    def __init__(self, line, send, keep, partner):
        self.line, self.send, self.keep, self.partner = line, send, keep, partner
        self.at, self.kept, self.got, self.sent, self.done = 0, [], {}, {}, None
        self.rows, self.far = send.shape[1], len(line.chunks) == 0
        self.cut = split_at(self.rows)


class Line:
    def __init__(self, sec):
        self.sec = sec
        self.square = lax.axis_size("inner") == 4
        self.short = lax.axis_size("outer") == 4
        spot, place = lax.axis_index("inner"), lax.axis_index("outer")
        outside = (place == 0) | (place == lax.axis_size("outer") - 1)
        self.ids = jnp.stack([lax.axis_index("section"), spot % 2, spot // 2, outside, spot]).astype(jnp.int32)
        self.chunks, self.made = [], {}
        self.sums = (sum_section, sum_first, sum_second, sum_ends, sum_middle, sum_last)

    def add(self, send, keep):
        count = len(self.chunks)
        chunk = Chunk(self, send, keep, self.chunks[count - 3] if count >= 3 else None)
        self.chunks.append(chunk)
        return chunk

    def move(self, way, array):
        if way == "section":
            return exchange(array, "section", 1)
        if way in ("x", "y"):
            return exchange(array, "inner", 1 if way == "x" else 2)
        return lax.ppermute(array, "outer", [(0, 1), (1, 0), (2, 3), (3, 2)] if way == "ends" else [(1, 2), (2, 1)])

    def advance(self, owner, *works):
        moving = [chunk for chunk in self.chunks if chunk.done is None and chunk.at > 0]
        sends = {}
        if moving and self.square:
            sums = Sums(moving[0].send.shape[-1])
            places = [self.sums[chunk.at - 1](sums, chunk) for chunk in moving]
            outs, sends = sums.run(self.ids)
            for chunk, place in zip(moving, places):
                chunk.kept, chunk.sent = [outs[index] for index in place], sends
        for chunk in moving:
            chunk.at += 1
            if not self.square:
                half = chunk.keep.astype(F32) + chunk.got["section"].astype(F32)
                half = lax.psum_scatter(half.astype(BF16), "inner", scatter_dimension=0, tiled=False)
                chunk.done = [lax.psum(half, "outer")]
            elif chunk.at == 4 and not self.short:
                chunk.done = [lax.psum(chunk.kept[0], "outer")]
            elif chunk.at == 7:
                chunk.done = chunk.kept
        new = [chunk for chunk in self.chunks if chunk.at == 0]
        gots = {way: self.move(way, array) for way, array in sends.items()}
        arrived = [self.move("section", chunk.send) for chunk in new]
        for work in works:
            work()
        fresh = [chunk for chunk in self.chunks if chunk not in new and chunk.at == 0]
        late = [chunk for chunk in self.chunks if chunk.keep is not None and chunk.at == 0]
        owner.made, parts, keeps, gots, arrived = lax.optimization_barrier(
            (owner.made, [chunk.send for chunk in fresh], [chunk.keep for chunk in late], gots, arrived)
        )
        for chunk, part in zip(fresh, parts):
            chunk.send = part
        for chunk, part in zip(late, keeps):
            chunk.keep = part
        for chunk in moving:
            chunk.got = gots
        for chunk, part in zip(new, arrived):
            chunk.at, chunk.got = 1, {"section": part}

    def finish(self):
        while any(chunk.done is None for chunk in self.chunks):
            self.advance(self)
        pairs = []
        for chunk in self.chunks[3:]:
            if len(chunk.done) == 1:
                two, one = chunk.partner.done[0], chunk.done[0]
                mine, send = (jnp.where(self.ids[0] == 0, *item) for item in ((one, two), (two, one)))
            else:
                mine, send = chunk.done
            pairs.append((mine, exchange(send, "section", 1)))
        return pairs


def assemble_kernel(sec, y_one, y_two, y_got, one, two_low, got, y_out, g_out, y, low, wide, sems):
    move = Mover(sems)
    first = sec[0] == 0
    loads = [
        move.choose(first, y_one.ref, y_got.ref, y.at[0]),
        move.choose(first, y_got.ref, y_two.ref, y.at[1]),
        move.choose(first, one.ref, got.ref, wide.at[0]),
    ]
    move.load(two_low.ref, low)
    loads.append(move.last)
    pl.when(first)(lambda: move.choose(first, got.ref, got.ref, wide.at[1]).wait())
    ready(loads)
    move.used += 1

    @pl.when(jnp.logical_not(first))
    def _():
        wide[1] = low[...].astype(F32)

    move.store(y, y_out.ref)
    move.store(wide, g_out.ref)
    move.finish()


def assemble(sec, y_one, y_two, y_got, one, two_low, got):
    flat = one.shape
    return call(
        assemble_kernel,
        sec,
        [(item, RAW) for item in (y_one, y_two, y_got, one, two_low, got)],
        [(sds((2,) + flat, BF16), RAW), (sds((2,) + flat, F32), RAW)],
        [((2,) + flat, BF16), (flat, BF16), ((2,) + flat, F32)],
        "assemble",
        1000,
        10 << 20,
    )


class Rest:
    def __init__(self, sec):
        self.sec, self.made = sec, {}

    def send(self, one, two_low):
        low = two_low.astype(F32)
        self.made["got"] = exchange(jnp.where(self.sec[0] == 0, low, one), "section", 1)

    def assemble(self, y_one, y_two, one, two_low):
        self.made["outs"] = assemble(self.sec, y_one, y_two, self.made["y"], one, two_low, self.made["got"])


def last_kernel(ids, down_mine, down_got, up_mine, up_got, mine, got, w_down, qkv, out, b_qv, b_out, gain, offset, b_up, b_down, w_up, sems):
    move = Mover(sems)
    up_wide = w_up.buffer.shape[1] // 2
    for half, side in ((ids[0], up_mine), (1 - ids[0], up_got)):
        w_up.buffer[:, pl.ds(pl.multiple_of(half * up_wide, up_wide), up_wide)] = side.buffer[...].astype(F32)
    w_up.flush(move)
    hidden, width = w_down.buffer.shape
    for half, side in ((ids[0], down_mine), (1 - ids[0], down_got)):
        rows = jnp.concatenate([side.buffer[:, :hidden], side.buffer[:, hidden:]], axis=0)
        w_down.buffer[:, pl.ds(pl.multiple_of(half * (width // 2), width // 2), width // 2)] = rows.T.astype(F32)
    w_down.flush(move)
    mine, got = mine.buffer, got.buffer
    tall, wide = qkv.buffer.shape[0], out.buffer.shape[1] // 2
    for half, side in ((ids[0], mine), (1 - ids[0], got)):
        for part in range(4):
            block = side[:tall, part * wide : part * wide + wide].astype(F32)
            target, first = (qkv, 2 * part * wide) if part < 3 else (out, 0)
            lanes = pl.ds(pl.multiple_of(first + half * wide, wide), wide)
            target.buffer[:, lanes] = block
    qkv.flush(move)
    out.flush(move)
    rows = mine[tall:, : 2 * wide].astype(F32)
    own, other = (side[tall : tall + 1, 2 * wide :].astype(F32) for side in (mine, got))

    def write(first_half, place):
        left, right = (own, other) if first_half else (other, own)
        span = slice(place * tall, place * tall + tall)
        for row in range(2):
            bias = jnp.concatenate([side[:, row * wide : row * wide + wide] for side in (left, right)], axis=1)
            b_qv.buffer[row : row + 1, :] = bias[:, span]
        b_out.buffer[...] = rows[10:11, span]
        gain.buffer[0:1, :] = rows[8:9, span]
        gain.buffer[1:2, :] = rows[0:1, span]
        offset.buffer[0:1, :] = rows[9:10, span]
        offset.buffer[1:2, :] = rows[1:2, span]
        b_up.buffer[...] = rows[11 + place : 12 + place]
        b_down.buffer[...] = rows[2:3, span]

    for first_half in (True, False):
        for place in range(2 * wide // tall):
            here = (ids[0] == (0 if first_half else 1)) & (ids[4] == place)
            pl.when(here)(functools.partial(write, first_half, place))
    for item in (b_qv, b_out, gain, offset, b_up, b_down):
        item.flush(move)
    move.finish()


def last(ids, down, up, attend, width, shards):
    tall = width // shards
    shapes = [(down[0].shape[1] // 2, width), (tall, 3 * width), (tall, width), (2, tall), (1, tall), (2, tall), (2, tall), (1, width), (1, tall)]
    shapes.append((tall, 2 * up[0].shape[1]))
    return call(
        last_kernel,
        ids,
        [(item, NEAR) for item in (*down, *up, *attend)],
        [(sds(shape, F32), FAR) for shape in shapes],
        [],
        "last",
        1000,
        5 << 20,
    )


def local(
    hidden_in, caption_len, region_len, cotangent, w_qkv, b_qv, w_out, b_out, ln_gain, ln_bias, w_up, b_up, w_down, b_down
):
    section = lax.axis_index("section")
    shards = lax.axis_size("inner")
    sec = section.astype(jnp.int32)[None]
    seqs_local, length, width = hidden_in.shape
    seqs = seqs_local // 2
    rows = seqs * length
    positions = jnp.arange(length, dtype=jnp.int32)[None, :]
    mine = lambda array: lax.dynamic_slice_in_dim(array, section * seqs, seqs, 0)
    caption, region = mine(caption_len)[:, None], mine(region_len)[:, None]
    valid = (positions < caption) | (positions >= CAP) & (positions < CAP + region)
    mask = jnp.concatenate([valid, valid], axis=1).astype(F32).T
    x = mine(hidden_in).reshape(rows, width)
    gy = jnp.where(valid[:, :, None], mine(cotangent), jnp.zeros((), BF16)).reshape(rows, width)

    blocks = w_up.shape[2] // width
    little = jnp.concatenate(
        [b_qv[0], b_out, ln_gain[0], ln_bias[0], b_down, b_up.reshape(blocks, width), jnp.zeros((8 - blocks, width), F32)]
    )
    little_other = exchange(little, "section", 1)
    big = (w_qkv[0], w_out[0], w_up[0], w_down[0])
    o_qkv = exchange(big[0], "section", 1)

    smalls = [jnp.where(section == layer, little, little_other) for layer in (0, 1)]
    o_qkv, smalls, mask, x, late_out, late_up = lax.optimization_barrier(
        (o_qkv, smalls, mask, x, big[1], big[2])
    )
    o_out, o_up = exchange(late_out, "section", 1), exchange(late_up, "section", 1)
    front = attend_forward(0, sec, x, FAR, big[0], o_qkv, smalls[0], mask)
    front, o_out, o_up, late_down = lax.optimization_barrier((front, o_out, o_up, big[3]))
    other = (o_qkv, o_out, o_up, exchange(late_down, "section", 1))
    y_one, cache_one = layer_forward(0, sec, x, front, big, other, smalls[0])
    y_near, y_one = y_one
    made = second_layer(sec, y_near, mask, big, other, smalls[1], gy)
    q, k, v, probs, ctx, hat_one, scale_one, low, slope, y_two = made[:10]
    cache_two = (y_one, q, k, v, probs, ctx, hat_one, scale_one, low, None, slope, None, None)
    line = Line(sec)
    two = Backward(line, 1, sec, cache_two, big, other, smalls[1], shards)
    one = Backward(line, 0, sec, cache_one, big, other, smalls[0], shards)
    two.made.update(second=made[10], branch=made[11], down_sums=made[12])
    line.add(made[13], made[14])
    exchanged_y = exchange(jnp.where(section == 0, y_two, y_one), "section", 1)
    line.advance(two, two.up)
    line.advance(two, two.attention)
    gx_two_near, gx_two_low = two.made["gx_low"]
    line.advance(one, lambda: one.down(gx_two_near))
    line.advance(one, one.up)
    line.advance(one, one.attention)
    gx_one = one.made["gx"]

    rest = Rest(sec)
    rest.made["y"] = exchanged_y
    for _ in range(3):
        line.advance(line)
    line.advance(rest, lambda: rest.send(gx_one, gx_two_low))
    line.advance(rest, lambda: rest.assemble(y_one, y_two, gx_one, gx_two_low))
    activations, input_grads = rest.made["outs"]
    activations = activations.reshape(seqs_local, length, width)
    input_grads = input_grads.reshape(seqs_local, length, width)
    down, up, attend = line.finish()
    g_w_down, g_w_qkv, g_w_out, g_b_qv, g_b_out, g_gain, g_offset, g_b_up, g_b_down, g_w_up = last(
        line.ids, down, up, attend, width, shards
    )
    return (
        activations[None],
        input_grads[None],
        g_w_qkv[None],
        g_b_qv[None],
        g_w_out[None],
        g_b_out,
        g_gain[None],
        g_offset[None],
        g_w_up[None],
        g_b_up,
        g_w_down[None],
        g_b_down,
    )


def solution(mesh):
    rows = ("inner", "outer")
    return jax.shard_map(
        local,
        mesh=mesh,
        in_specs=(
            P(rows, None, None),
            P(rows),
            P(rows),
            P(rows, None, None),
            P("section", None, None),
            P("section", None, None),
            P("section", None, None),
            P("section", None),
            P("section", None, None),
            P("section", None, None),
            P("section", None, None),
            P("section", None),
            P("section", None, None),
            P("section", None),
        ),
        out_specs=(
            P("section", rows, None, None),
            P("section", rows, None, None),
            P("section", "inner", None),
            P("section", None, "inner"),
            P("section", "inner", None),
            P("section", "inner"),
            P("section", None, "inner"),
            P("section", None, "inner"),
            P("section", "inner", None),
            P("section", "inner"),
            P("section", "inner", None),
            P("section", "inner"),
        ),
        check_vma=False,
    )
```

```python
import functools
import math

import jax
import jax.numpy as jnp
from jax import lax
from jax.experimental import pallas as pl
from jax.experimental.pallas import tpu as pltpu
from jax.sharding import PartitionSpec as P

HEADS = 12
CAP = 28
EPS = 1e-12
SCALE = 0.125
SPARE = 8 * 1024 * 1024
F32 = jnp.float32
BF16 = jnp.bfloat16
B_Q, B_V, B_OUT, GAIN_ONE, GAIN_TWO, OFFSET_ONE, OFFSET_TWO, B_DOWN, B_UP = range(9)


def dot(left, right):
    return jnp.dot(left, right, preferred_element_type=F32)


def dot_t(left, right):
    return lax.dot_general(left, right, (((1,), (1,)), ((), ())), preferred_element_type=F32)


def t_dot(left, right):
    return lax.dot_general(left, right, (((0,), (0,)), ((), ())), preferred_element_type=F32)


def column_sum(values):
    return jnp.sum(values, axis=0, keepdims=True)


def standardize(summed):
    centre = jnp.mean(summed, axis=-1, keepdims=True)
    shifted = summed - centre
    spread = jnp.mean(shifted * shifted, axis=-1, keepdims=True)
    scale = lax.rsqrt(spread + EPS)
    return shifted * scale, scale


def norm_back(grad, hat, scale, gain):
    scaled = grad * gain
    return scale * (
        scaled
        - jnp.mean(scaled, axis=-1, keepdims=True)
        - hat * jnp.mean(scaled * hat, axis=-1, keepdims=True)
    )


def gauss_share(value):
    bell = jnp.exp2(value * value * -0.7213475204444817)
    part = 1.0 / (1.0 + 0.2316418882 * jnp.abs(value))
    tail = 0.5307027145
    for item in (-0.7265760135, 0.7107068705, -0.142248368, 0.127414796):
        tail = tail * part + item
    tail = tail * part * bell
    return jnp.where(value < 0.0, tail, 1.0 - tail), bell


def lane_halves():
    lane = lax.broadcasted_iota(jnp.int32, (1, 128), 1)
    lower = jnp.where(lane < 64, 1.0, 0.0)
    return lower.astype(BF16), (1.0 - lower).astype(BF16)


def two_heads(block, halves):
    return jnp.concatenate([block * halves[0], block * halves[1]], axis=0)


def sds(shape, dtype):
    return jax.ShapeDtypeStruct(shape, dtype)


class Mover:
    def __init__(self, sems):
        self.sems, self.used, self.outs = sems, 0, []

    def copy(self, source, target):
        self.used += 1
        return pltpu.make_async_copy(source, target, self.sems.at[self.used - 1])

    def load(self, source, target):
        self.last = self.copy(source, target)
        self.last.start()

    def choose(self, first, one, two, target):
        copy = self.copy(one, target)
        other = pltpu.make_async_copy(two, target, self.sems.at[self.used - 1])
        pl.when(first)(copy.start)
        pl.when(jnp.logical_not(first))(other.start)
        return copy

    def store(self, source, target):
        copy = self.copy(source, target)
        copy.start()
        self.outs.append(copy)

    def finish(self):
        for copy in self.outs:
            copy.wait()


class Operand:
    def __init__(self, ref, buffer, far):
        self.ref, self.buffer, self.far = ref, buffer, far

    def fetch(self, move, *index):
        if self.far:
            move.load(*(ref.at[index] if index else ref for ref in (self.ref, self.buffer)))
            return [move.last]
        return []

    def flush(self, move, *index):
        if self.far:
            move.store(*(ref.at[index] if index else ref for ref in (self.buffer, self.ref)))


NEAR, FAR, RAW, BOTH, FREE = "near", "far", "raw", "both", "free"


def run(*parts):
    for part in parts:
        next(part)
    for part in parts:
        for _ in part:
            pass


def ready(waits):
    for item in waits:
        item.wait()


def call(kernel, ids, ins, outs, scratch, name, flops, nbytes):
    space = lambda kind: {NEAR: pltpu.VMEM, FREE: pl.ANY}.get(kind, pltpu.HBM)
    spread = [(shape, part) for shape, kind in outs for part in ((NEAR, RAW) if kind == BOTH else (kind,))]
    kinds = [kind for _, kind in ins] + [kind for _, kind in spread]
    shapes = [array for array, _ in ins] + [shape for shape, _ in spread]
    buffers = [pltpu.VMEM(shape.shape, shape.dtype) for shape, kind in zip(shapes, kinds) if kind == FAR]

    def body(ids_ref, *refs):
        count = len(kinds)
        spare = list(refs[count : count + len(buffers)])
        left = list(refs[:count])
        operands = []
        for _, kind in list(ins) + list(outs):
            ref = left.pop(0)
            if kind == BOTH:
                operands.append(Operand(left.pop(0), ref, True))
            else:
                operands.append(Operand(ref, spare.pop(0) if kind == FAR else ref, kind == FAR))
        kernel(ids_ref, *operands, *refs[count + len(buffers) :])

    size = lambda shape, dtype: math.prod(shape) * jnp.dtype(dtype).itemsize
    limit = SPARE + sum(size(*item) for item in scratch)
    limit += sum(size(shape.shape, shape.dtype) for shape, kind in zip(shapes, kinds) if kind == FAR)
    results = pl.pallas_call(
        body,
        in_specs=[pl.BlockSpec(memory_space=pltpu.SMEM)]
        + [pl.BlockSpec(memory_space=space(kind)) for _, kind in ins],
        out_specs=[pl.BlockSpec(memory_space=space(kind)) for _, kind in spread],
        out_shape=[space(kind)(shape.shape, shape.dtype) for shape, kind in spread],
        scratch_shapes=buffers + [pltpu.VMEM(*item) for item in scratch] + [pltpu.SemaphoreType.DMA((64,))],
        compiler_params=pltpu.CompilerParams(vmem_limit_bytes=limit),
        cost_estimate=pl.CostEstimate(flops=flops, bytes_accessed=nbytes, transcendentals=0),
        name=name,
    )(ids, *(pltpu.with_memory_space_constraint(array, space(kind)) for array, kind in ins))
    results = list(results)
    return [(results.pop(0), results.pop(0)) if kind == BOTH else results.pop(0) for _, kind in outs]


def attend_phase(q, k, v, probs, ctx, mask, pairs):
    seqs = mask.shape[1]
    halves = lane_halves()
    feature = lax.broadcasted_iota(jnp.int32, (128, 128), 0)
    first_half = jnp.where(feature < 64, 1.0, 0.0).astype(BF16)
    second_half = jnp.where(feature < 64, 0.0, 1.0).astype(BF16)

    for seq in range(seqs):
        rows = slice(seq * 128, seq * 128 + 128)
        seen = jnp.broadcast_to(mask[:, seq : seq + 1], (256, 128)) > 0.5
        for pair in range(*pairs):
            lanes = slice(pair * 128, pair * 128 + 128)
            scores = dot_t(two_heads(k[rows, lanes], halves), q[rows, lanes] * SCALE)
            scores = jnp.where(seen, scores, -1e30)
            parts = []
            for part in (scores[:128], scores[128:]):
                e = jnp.exp(part - jnp.max(part, axis=0, keepdims=True))
                parts.append(e * (1.0 / jnp.sum(e, axis=0, keepdims=True)))
            parts = jnp.concatenate(parts, axis=0)
            probs[seq, pair] = parts
            turned = v[rows, lanes].T
            turned = jnp.concatenate([turned * first_half, turned * second_half], axis=1)
            ctx[lanes, rows] = dot(turned, parts.astype(BF16)).astype(BF16)


def attend_steps(move, layer, sec, x, w_a, w_b, small, mask, q, k, v, probs, ctx, w):
    mine = sec[0] == layer
    rows, width = x.buffer.shape
    waits = x.fetch(move) + small.fetch(move) + mask.fetch(move)
    parts = [
        move.choose(mine, w_a.ref.at[:, pl.ds(i * width, width)], w_b.ref.at[:, pl.ds(i * width, width)], w.at[i])
        for i in (1, 0, 2)
    ]
    yield
    ready(waits)
    x, small = x.buffer, small.buffer
    parts[0].wait()
    k.buffer[...] = dot(x[...], w[1]).astype(BF16)
    k.flush(move)
    parts[1].wait()
    q.buffer[...] = (dot(x[...], w[0]) + small[B_Q : B_Q + 1]).astype(BF16)
    q.flush(move)
    parts[2].wait()
    v.buffer[...] = (dot(x[...], w[2]) + small[B_V : B_V + 1]).astype(BF16)
    v.flush(move)
    half = width // 128 // 2
    for i in range(2):
        attend_phase(
            q.buffer, k.buffer, v.buffer, probs.buffer, ctx.buffer, mask.buffer, (i * half, i * half + half)
        )
        probs.flush(move, slice(None), pl.ds(i * half, half))
    ctx.flush(move)


def attend_kernel(layer, sec, *refs):
    move = Mover(refs[-1])
    run(attend_steps(move, layer, sec, *refs[:-1]))
    move.finish()


def attend_forward(layer, sec, x, x_kind, w_own, w_other, small, mask):
    rows, width = x.shape
    seqs = mask.shape[1]
    pairs = width // 128
    wide = sds((rows, width), BF16)
    return call(
        functools.partial(attend_kernel, layer),
        sec,
        [(x, x_kind), (w_own, RAW), (w_other, RAW), (small, FAR), (mask, FAR)],
        [(wide, FAR)] * 3 + [(sds((seqs, pairs, 256, 128), F32), FAR), (sds((width, rows), BF16), BOTH)],
        [((3, width, width), BF16)],
        "attend_forward",
        2 * rows * width * width * 4,
        12 << 20,
    )


def up_kernel(layer, sec, x, ctx, wo_a, wo_b, wu_a, wu_b, small, hat, scale, turned, act, slope, wo, wu, low, sems):
    move = Mover(sems)
    mine = sec[0] == layer
    blocks, _, wide = wu.shape
    waits = ctx.fetch(move) + [move.choose(mine, wo_a.ref, wo_b.ref, wo)] + small.fetch(move) + x.fetch(move)
    span = lambda i: pl.ds(i * wide, wide)
    parts = [move.choose(mine, wu_a.ref.at[:, span(i)], wu_b.ref.at[:, span(i)], wu.at[i]) for i in range(blocks)]
    ready(waits)
    small = small.buffer
    summed = x.buffer[...].astype(F32) + t_dot(ctx.buffer[...], wo[...]) + small[B_OUT : B_OUT + 1]
    unit, root = standardize(summed)
    hat.buffer[...] = unit
    hat.flush(move)
    scale.buffer[...] = jnp.broadcast_to(root, scale.buffer.shape)
    scale.flush(move)
    low[...] = (unit * small[GAIN_ONE : GAIN_ONE + 1] + small[OFFSET_ONE : OFFSET_ONE + 1]).astype(BF16)
    turned.buffer[...] = low[...].T
    turned.flush(move)
    for i in range(blocks):
        parts[i].wait()
        pre = dot(low[...], wu[i]) + small[B_UP + i : B_UP + i + 1]
        share, bell = gauss_share(pre)
        act.buffer[i] = (pre * share).astype(BF16)
        slope.buffer[i] = share + pre * 0.3989422804014327 * bell
        act.flush(move, i)
        slope.flush(move, i)
    move.finish()


def up_forward(layer, sec, x, x_kind, ctx, wo, wo_other, wu, wu_other, small):
    rows, width = x.shape
    blocks = wu.shape[1] // width
    wide = (rows, width)
    other_kind = FREE if layer == 0 else RAW
    return call(
        functools.partial(up_kernel, layer),
        sec,
        [(x, x_kind), (ctx, NEAR), (wo, RAW), (wo_other, other_kind), (wu, RAW), (wu_other, other_kind), (small, FAR)],
        [
            (sds(wide, F32), BOTH),
            (sds((rows, 128), F32), FAR),
            (sds((width, rows), BF16), FAR),
            (sds((blocks,) + wide, BF16), BOTH if layer == 0 else NEAR),
            (sds((blocks,) + wide, F32), FAR),
        ],
        [((width, width), BF16), ((blocks, width, width), BF16), (wide, BF16)],
        "up_forward",
        2 * rows * width * width * (blocks + 1),
        20 << 20,
    )


def down_kernel(layer, sec, act, wd_a, wd_b, hat, small, y, two, scale, wd, total, sems):
    move = Mover(sems)
    mine = sec[0] == layer
    blocks, wide, _ = wd.shape
    parts = []
    for i in range(blocks):
        span = pl.ds(i * wide, wide)
        parts.append(act.fetch(move, i) + [move.choose(mine, wd_a.ref.at[span], wd_b.ref.at[span], wd.at[i])])
        if i == 0:
            waits = small.fetch(move) + hat.fetch(move)
    for i in range(blocks):
        ready(parts[i])
        product = dot(act.buffer[i], wd[i])
        total[...] = product if i == 0 else total[...] + product
    ready(waits)
    small = small.buffer
    normed = hat.buffer[...] * small[GAIN_ONE : GAIN_ONE + 1] + small[OFFSET_ONE : OFFSET_ONE + 1]
    unit, root = standardize(total[...] + normed + small[B_DOWN : B_DOWN + 1])
    y.buffer[...] = (unit * small[GAIN_TWO : GAIN_TWO + 1] + small[OFFSET_TWO : OFFSET_TWO + 1]).astype(BF16)
    y.flush(move)
    two.buffer[...] = unit
    two.flush(move)
    scale.buffer[...] = jnp.broadcast_to(root, scale.buffer.shape)
    scale.flush(move)
    move.finish()


def down_forward(layer, sec, act, wd, wd_other, hat, small, y_kind, two_kind):
    blocks, rows, width = act.shape
    wide = (rows, width)
    return call(
        functools.partial(down_kernel, layer),
        sec,
        [(act, NEAR), (wd, RAW), (wd_other, FREE if layer == 0 else RAW), (hat, NEAR), (small, FAR)],
        [(sds(wide, BF16), y_kind), (sds(wide, F32), two_kind), (sds((rows, 128), F32), two_kind)],
        [((blocks, width, width), BF16), (wide, F32)],
        "down_forward",
        2 * rows * width * width * blocks,
        12 << 20,
    )


def up_down_steps(
    move, layer, sec, x, ctx, wo_a, wo_b, wu_a, wu_b, wd_a, wd_b, small,
    hat, scale, turned, act, slope, y, two, scale_two, wo, wu, wd, low, total,
):
    mine = sec[0] == layer
    blocks, _, wide = wu.shape
    waits = ctx.fetch(move) + [move.choose(mine, wo_a.ref, wo_b.ref, wo)] + small.fetch(move) + x.fetch(move)
    ups, downs = [], []
    for i in range(blocks):
        span = pl.ds(i * wide, wide)
        ups.append(move.choose(mine, wu_a.ref.at[:, span], wu_b.ref.at[:, span], wu.at[i]))
        downs.append(move.choose(mine, wd_a.ref.at[span], wd_b.ref.at[span], wd.at[i]))
    yield
    ready(waits)
    small = small.buffer
    summed = x.buffer[...].astype(F32) + t_dot(ctx.buffer[...], wo[...]) + small[B_OUT : B_OUT + 1]
    unit, root = standardize(summed)
    hat.buffer[...] = unit
    hat.flush(move)
    scale.buffer[...] = jnp.broadcast_to(root, scale.buffer.shape)
    scale.flush(move)
    normed = unit * small[GAIN_ONE : GAIN_ONE + 1] + small[OFFSET_ONE : OFFSET_ONE + 1]
    total[...] = normed + small[B_DOWN : B_DOWN + 1]
    low[...] = normed.astype(BF16)
    turned.buffer[...] = low[...].T
    turned.flush(move)
    for i in range(blocks):
        ups[i].wait()
        pre = dot(low[...], wu[i]) + small[B_UP + i : B_UP + i + 1]
        share, bell = gauss_share(pre)
        act.buffer[i] = (pre * share).astype(BF16)
        slope.buffer[i] = share + pre * 0.3989422804014327 * bell
        slope.flush(move, i)
        downs[i].wait()
        total[...] += dot(act.buffer[i], wd[i])
    unit, root = standardize(total[...])
    y.buffer[...] = (unit * small[GAIN_TWO : GAIN_TWO + 1] + small[OFFSET_TWO : OFFSET_TWO + 1]).astype(BF16)
    y.flush(move)
    two.buffer[...] = unit
    scale_two.buffer[...] = jnp.broadcast_to(root, scale_two.buffer.shape)


def down_grad_steps(move, sec, gy, hat, scale, small, act, second, branch, sums, send, keep, turned):
    blocks = act.buffer.shape[0]
    low_rows, wide = send.buffer.shape[1], act.buffer.shape[2]
    tall = 2 * low_rows
    waits = gy.fetch(move) + small.fetch(move) + scale.fetch(move) + hat.fetch(move)
    parts = [act.fetch(move, i) for i in range(blocks)]
    yield
    ready(waits)
    grad = gy.buffer[...].astype(F32)
    sums.buffer[0:1] = column_sum(grad * hat.buffer[...])
    sums.buffer[1:2] = column_sum(grad)
    unit = norm_back(grad, hat.buffer[...], scale.buffer[:, 0:1], small.buffer[GAIN_TWO : GAIN_TWO + 1])
    second.buffer[...] = unit
    second.flush(move)
    low = unit.astype(BF16)
    branch.buffer[...] = low
    branch.flush(move)
    sums.buffer[2:3] = column_sum(low.astype(F32))
    sums.buffer[3:] = jnp.zeros_like(sums.buffer[3:])
    sums.flush(move)
    turned[...] = branch.buffer[...].T
    for half, out in ((1 - sec[0], send), (sec[0], keep)):
        left = pl.ds(pl.multiple_of(half * tall, tall), tall)
        for i in range(blocks):
            if out is send:
                ready(parts[i])
            block = dot(turned[left, :], act.buffer[i]).astype(BF16)
            out.buffer[i, :, :wide] = block[:low_rows]
            out.buffer[i, :, wide:] = block[low_rows:]
            out.flush(move, i)


def down_grad_kernel(sec, *refs):
    move = Mover(refs[-1])
    run(down_grad_steps(move, sec, *refs[:-1]))
    move.finish()


def down_grad(sec, gy, gy_kind, hat, scale, small, act, kind):
    rows, width = gy.shape
    blocks = act.shape[0]
    wide = (rows, width)
    part = sds((blocks, width // 4, 2 * width), BF16)
    return call(
        down_grad_kernel,
        sec,
        [(gy, gy_kind), (hat, kind), (scale, kind), (small, FAR), (act, kind)],
        [(sds(wide, F32), NEAR), (sds(wide, BF16), NEAR), (sds((8, width), F32), NEAR), (part, NEAR), (part, FAR if kind == NEAR else NEAR)],
        [((width, rows), BF16)],
        "down_grad",
        2 * rows * width * width * blocks,
        14 << 20,
    )


def up_grad_kernel(layer, last, sec, *refs):
    refs = list(refs)
    take = lambda count: [refs.pop(0) for _ in range(count)]
    branch, base, wd_a, wd_b, slope_h, low, wu_a, wu_b = take(8)
    if last:
        hat, scale, small, sums_in = take(4)
        first, attend, sums, out = take(4)
    else:
        first, sums, out = take(3)
    wd, wu, slope, pre, sems = refs
    move = Mover(sems)
    mine = sec[0] == layer
    half, wide, _ = wd.shape
    side = sec[0] if last else 1 - sec[0]
    at = [side * half + i for i in range(half)]
    span = [pl.ds(pl.multiple_of(place * wide, wide), wide) for place in at]
    parts = []
    early = branch.fetch(move)
    for i in range(half):
        move.load(slope_h.ref.at[at[i]], slope.at[i])
        parts.append(
            [
                move.last,
                move.choose(mine, wd_a.ref.at[span[i]], wd_b.ref.at[span[i]], wd.at[i]),
                move.choose(mine, wu_a.ref.at[:, span[i]], wu_b.ref.at[:, span[i]], wu.at[i]),
            ]
        )
        if i == 0:
            early += low.fetch(move)
    late = base.fetch(move)
    if last:
        late += hat.fetch(move) + scale.fetch(move) + small.fetch(move)
        sums.buffer[...] = sums_in.buffer[...]
    else:
        sums.buffer[...] = jnp.zeros_like(sums.buffer)
    ready(early)
    total = first.buffer
    shards, tall, _ = out.buffer.shape
    for i in range(half):
        ready(parts[i])
        pre[...] = (dot_t(branch.buffer[...], wd[i]) * slope[i]).astype(BF16)
        sums.buffer[pl.ds(3 + at[i], 1)] = column_sum(pre[...].astype(F32))
        block = dot(low.buffer[...], pre[...]).astype(BF16)
        for shard in range(shards):
            out.buffer[shard, :, i * wide : i * wide + wide] = block[shard * tall : shard * tall + tall]
        if i == 0:
            ready(late)
            total[...] = base.buffer[...] + dot_t(pre[...], wu[i])
        else:
            total[...] += dot_t(pre[...], wu[i])
    if last:
        grad = total[...]
        sums.buffer[0:1] = column_sum(grad * hat.buffer[...])
        sums.buffer[1:2] = column_sum(grad)
        unit = norm_back(grad, hat.buffer[...], scale.buffer[:, 0:1], small.buffer[GAIN_ONE : GAIN_ONE + 1])
        attend.buffer[...] = unit.astype(BF16)
        total[...] = unit
        sums.buffer[2:3] = column_sum(attend.buffer[...].astype(F32))
    move.finish()


def up_grad(layer, last, sec, branch, base, wd, wd_other, slope, low, wu, wu_other, shards, more=()):
    blocks, rows, width = slope.shape
    half = blocks // 2
    wide = (rows, width)
    part = sds((shards, width // shards, half * width), BF16)
    square = ((half, width, width), BF16)
    near = lambda *shapes: [(shape, NEAR) for shape in shapes]
    ins = [
        (branch, NEAR),
        (base, NEAR),
        (wd, RAW),
        (wd_other, RAW),
        (slope, RAW),
        (low, FAR),
        (wu, RAW),
        (wu_other, RAW),
    ]
    if last:
        hat, scale, small, sums = more
        ins += [(hat, FAR), (scale, FAR), (small, FAR), (sums, NEAR)]
        outs = near(sds(wide, F32), sds(wide, BF16), sds((8, width), F32), part)
    else:
        outs = near(sds(wide, F32), sds((8, width), F32), part)
    return call(
        functools.partial(up_grad_kernel, layer, last),
        sec,
        ins,
        outs,
        [square, square, ((half,) + wide, F32), (wide, BF16)],
        "up_grad_last" if last else "up_grad_first",
        3 * rows * width * width * blocks,
        15 << 20,
    )


def attend_grad_kernel(layer, last, sec, *refs):
    refs = list(refs)
    take = lambda count: [refs.pop(0) for _ in range(count)]
    attend, ctx, base, x, q_h, k_h, v_h, p_h, wo_a, wo_b, w_a, w_b, down, up = take(14)
    if last:
        gx, gx_low, out = take(3)
    else:
        total, turned, out = take(3)
    q, k, v, probs, wo, w, gc, grads, sems = refs
    move = Mover(sems)
    mine = sec[0] == layer
    rows_all, wide = q.shape
    width = 2 * wide
    seqs = probs.shape[0]
    shards = out.buffer.shape[0]
    tall = width // shards
    pairs = wide // 128
    side = sec[0] if last else 1 - sec[0]
    lanes_half = pl.ds(pl.multiple_of(side * wide, wide), wide)
    waits = attend.fetch(move) + [move.choose(mine, wo_a.ref.at[lanes_half], wo_b.ref.at[lanes_half], wo)]
    near = []
    for source, target in (
        (p_h.ref.at[:, pl.ds(side * pairs, pairs)], probs),
        (v_h.ref.at[:, lanes_half], v),
        (k_h.ref.at[:, lanes_half], k),
        (q_h.ref.at[:, lanes_half], q),
    ):
        move.load(source, target)
        near.append(move.last)
    later = x.fetch(move) + ctx.fetch(move) + down.fetch(move) + up.fetch(move)
    finals = base.fetch(move)
    for i in range(3):
        there = pl.ds(pl.multiple_of(i * width + side * wide, wide), wide)
        finals.append(move.choose(mine, w_a.ref.at[:, there], w_b.ref.at[:, there], w.at[:, pl.ds(i * wide, wide)]))
    ready(waits)
    gc[...] = dot_t(attend.buffer[...], wo[...]).astype(BF16)
    ready(near)
    halves = lane_halves()
    lower = lax.broadcasted_iota(jnp.int32, (128, 128), 1) < 64

    for pair in range(pairs):
        lanes = slice(pair * 128, pair * 128 + 128)
        for seq in range(seqs):
            rows = slice(seq * 128, seq * 128 + 128)

            def put(part, value):
                grads[rows, part * wide + pair * 128 : part * wide + pair * 128 + 128] = value.astype(BF16)

            grad = gc[rows, lanes]
            p = probs[seq, pair]
            full = dot(p.astype(BF16), grad)
            put(2, jnp.where(lower, full[:128], full[128:]))
            gp = dot_t(two_heads(v[rows, lanes], halves), grad)
            parts = []
            for part in (slice(0, 128), slice(128, 256)):
                g, pp = gp[part], p[part]
                parts.append(pp * (g - jnp.sum(g * pp, axis=0, keepdims=True)))
            gs = jnp.concatenate(parts, axis=0).astype(BF16)
            put(0, t_dot(gs, two_heads(k[rows, lanes] * SCALE, halves)))
            full = dot(gs, q[rows, lanes] * SCALE)
            put(1, jnp.where(lower, full[:128], full[128:]))
    ready(later)
    if last:
        turned = x
    else:
        turned.buffer[...] = x.buffer[...].T
    left = dot(turned.buffer[...], grads[...]).astype(BF16)
    right = dot(ctx.buffer[...], attend.buffer[:, lanes_half]).astype(BF16)
    little = jnp.concatenate([down.buffer[...], up.buffer[...]], axis=0).astype(BF16)
    zeros = jnp.zeros_like(little)
    b_q = column_sum(grads[:, 0:wide].astype(F32)).astype(BF16)
    b_v = column_sum(grads[:, 2 * wide :].astype(F32)).astype(BF16)
    pad = jnp.concatenate([b_q, b_v], axis=1)
    pad = jnp.concatenate([pad, jnp.zeros((15, width), BF16)], axis=0)
    for shard in range(shards):
        out.buffer[shard, :tall, 0 : 3 * wide] = left[shard * tall : shard * tall + tall]
        out.buffer[shard, :tall, 3 * wide :] = right[shard * tall : shard * tall + tall]
        out.buffer[shard, tall:, 0:width] = little
        out.buffer[shard, tall:, width:] = pad
    ready(finals)
    sum_all = base.buffer[...] + dot_t(grads[...], w[...])
    if last:
        gx.buffer[...] = sum_all
        gx.flush(move)
        gx_low.buffer[...] = sum_all.astype(BF16)
        gx_low.flush(move)
    else:
        total.buffer[...] = sum_all
    move.finish()


def attend_grad(layer, last, sec, attend, ctx, base, x, q, k, v, probs, wo, wo_other, w, w_other, down, up, shards, low_kind):
    rows, width = attend.shape
    seqs = probs.shape[0]
    wide = width // 2
    flat = (rows, width)
    part = (sds((shards, width // shards + 16, 2 * width), BF16), NEAR)
    if last:
        outs = [(sds(flat, F32), FAR), (sds(flat, BF16), low_kind), part]
    else:
        outs = [(sds(flat, F32), NEAR), (sds((width, rows), BF16), NEAR), part]
    half = ((rows, wide), BF16)
    return call(
        functools.partial(attend_grad_kernel, layer, last),
        sec,
        [(attend, NEAR), (ctx, FAR), (base, NEAR), (x, NEAR if last else FAR)]
        + [(item, RAW) for item in (q, k, v, probs, wo, wo_other, w, w_other)]
        + [(down, NEAR), (up, NEAR)],
        outs,
        [
            half,
            half,
            half,
            ((seqs, wide // 128) + probs.shape[2:], F32),
            ((wide, width), BF16),
            ((width, 3 * wide), BF16),
            half,
            ((rows, 3 * wide), BF16),
        ],
        "attend_grad_last" if last else "attend_grad_first",
        rows * width * width * 10,
        15 << 20,
    )


def second_kernel(sec, *refs):
    refs = list(refs)
    take = lambda count: [refs.pop(0) for _ in range(count)]
    inside = lambda item: Operand(None, item, False)
    x, w_a, w_b, small, mask = take(5)
    weights, (gy,) = take(6), take(1)
    q, k, v, probs, ctx, hat, scale, turned, slope, y = take(10)
    second, branch, sums, send, keep = take(5)
    w, wo, wu, wd, low, total, act, two, scale_two, branch_turned, sems = refs
    move = Mover(sems)
    near = inside(small.buffer)
    act, two, scale_two = inside(act), inside(two), inside(scale_two)
    run(
        attend_steps(move, 1, sec, x, w_a, w_b, small, mask, q, k, v, probs, ctx, w),
        up_down_steps(
            move, 1, sec, x, inside(ctx.buffer), *weights, near,
            hat, scale, turned, act, slope, y, two, scale_two, wo, wu, wd, low, total,
        ),
        down_grad_steps(move, sec, gy, two, scale_two, near, act, second, branch, sums, send, keep, branch_turned),
    )
    move.finish()


def second_layer(sec, x, mask, big, other, small, gy):
    rows, width = x.shape
    seqs = mask.shape[1]
    pairs = width // 128
    (w, w_other), (wo, wo_other), (wu, wu_other), (wd, wd_other) = zip(big, other)
    blocks = wu.shape[1] // width
    wide = (rows, width)
    part = sds((blocks, width // 4, 2 * width), BF16)
    square = lambda count: ((count, width, width), BF16)
    return call(
        second_kernel,
        sec,
        [(x, NEAR), (w, RAW), (w_other, RAW), (small, FAR), (mask, FAR)]
        + [(item, RAW) for item in (wo, wo_other, wu, wu_other, wd, wd_other)]
        + [(gy, FAR)],
        [(sds(wide, BF16), FAR)] * 3
        + [
            (sds((seqs, pairs, 256, 128), F32), FAR),
            (sds((width, rows), BF16), FAR),
            (sds(wide, F32), FAR),
            (sds((rows, 128), F32), FAR),
            (sds((width, rows), BF16), FAR),
            (sds((blocks,) + wide, F32), FAR),
            (sds(wide, BF16), FAR),
            (sds(wide, F32), NEAR),
            (sds(wide, BF16), NEAR),
            (sds((8, width), F32), NEAR),
            (part, NEAR),
            (part, FAR),
        ],
        [
            square(3),
            ((width, width), BF16),
            square(blocks),
            square(blocks),
            (wide, BF16),
            (wide, F32),
            ((blocks,) + wide, BF16),
            (wide, F32),
            ((rows, 128), F32),
            ((width, rows), BF16),
        ],
        "second_layer",
        2 * rows * width * width * (3 * blocks + 5),
        50 << 20,
    )


def up_whole_kernel(
    layer, sec, branch, second, wd_a, wd_b, slope, low, wu_a, wu_b, hat, scale, small,
    first, attend, sums, send, keep, wd, wu, pre, sems,
):
    move = Mover(sems)
    mine = sec[0] == layer
    blocks, wide, _ = wd.shape
    half = blocks // 2
    at = [lax.rem(i + half * (1 - sec[0]), blocks) for i in range(blocks)]
    span = [pl.ds(pl.multiple_of(place * wide, wide), wide) for place in at]
    parts = []
    early = branch.fetch(move)
    for i in range(blocks):
        parts.append(
            [move.choose(mine, wd_a.ref.at[span[i]], wd_b.ref.at[span[i]], wd.at[i])]
            + slope.fetch(move, at[i])
            + [
                move.choose(
                    mine,
                    wu_a.ref.at[:, span[i]],
                    wu_b.ref.at[:, span[i]],
                    wu.at[i // half, :, pl.ds(i % half * wide, wide)],
                )
            ]
        )
        if i == 0:
            early += low.fetch(move)
    late = second.fetch(move) + hat.fetch(move) + scale.fetch(move) + small.fetch(move)
    ready(early)
    branch, low, total = branch.buffer, low.buffer, first.buffer
    for side, out in enumerate((send, keep)):
        for i in range(half):
            block = side * half + i
            ready(parts[block])
            lanes = slice(i * wide, i * wide + wide)
            pre[:, lanes] = (dot_t(branch[...], wd[block]) * slope.buffer[at[block]]).astype(BF16)
            sums.buffer[pl.ds(3 + at[block], 1)] = column_sum(pre[:, lanes].astype(F32))
        product = dot(low[...], pre[...]).astype(BF16)
        shards, tall, _ = out.buffer.shape
        for shard in range(shards):
            out.buffer[shard] = product[shard * tall : shard * tall + tall]
        if side == 0:
            ready(late)
            total[...] = second.buffer[...] + dot_t(pre[...], wu[side])
        else:
            total[...] += dot_t(pre[...], wu[side])
    grad = total[...]
    sums.buffer[0:1] = column_sum(grad * hat.buffer[...])
    sums.buffer[1:2] = column_sum(grad)
    unit = norm_back(grad, hat.buffer[...], scale.buffer[:, 0:1], small.buffer[GAIN_ONE : GAIN_ONE + 1])
    attend.buffer[...] = unit.astype(BF16)
    attend.flush(move)
    total[...] = unit
    first.flush(move)
    sums.buffer[2:3] = column_sum(attend.buffer[...].astype(F32))
    sums.buffer[3 + blocks :] = jnp.zeros_like(sums.buffer[3 + blocks :])
    sums.flush(move)
    move.finish()


def up_whole(layer, sec, branch, second, wd, wd_other, slope, low, wu, wu_other, hat, scale, small, shards):
    blocks, rows, width = slope.shape
    wide = (rows, width)
    part = sds((shards, width // shards, blocks * width // 2), BF16)
    square = ((blocks, width, width), BF16)
    return call(
        functools.partial(up_whole_kernel, layer),
        sec,
        [
            (branch, NEAR),
            (second, NEAR),
            (wd, RAW),
            (wd_other, RAW),
            (slope, FAR),
            (low, FAR),
            (wu, RAW),
            (wu_other, RAW),
            (hat, FAR),
            (scale, FAR),
            (small, FAR),
        ],
        [(sds(wide, F32), NEAR), (sds(wide, BF16), NEAR), (sds((8, width), F32), NEAR), (part, NEAR), (part, NEAR)],
        [square, ((2, width, blocks // 2 * width), BF16), ((rows, blocks // 2 * width), BF16)],
        "up_grad",
        6 * rows * width * width * blocks,
        30 << 20,
    )


def attend_whole_kernel(
    layer, shards, sec, attend, ctx, first, x, q, k, v, probs, wo_a, wo_b, w_a, w_b, down, up,
    gx, gx_low, send, keep, turned, wo, w, gc, grads, sems,
):
    move = Mover(sems)
    mine = sec[0] == layer
    rows_all, width = x.buffer.shape
    seqs = probs.buffer.shape[0]
    wide = width // 2
    tall = width // shards
    pairs = wide // 128
    waits = attend.fetch(move) + [move.choose(mine, wo_a.ref, wo_b.ref, wo)]
    near = probs.fetch(move) + v.fetch(move) + k.fetch(move) + q.fetch(move)
    later = x.fetch(move) + ctx.fetch(move) + down.fetch(move) + up.fetch(move)
    last = [
        move.choose(
            mine,
            w_a.ref.at[:, pl.ds(i * width + half * wide, wide)],
            w_b.ref.at[:, pl.ds(i * width + half * wide, wide)],
            w.at[:, pl.ds((3 * half + i) * wide, wide)],
        )
        for i in range(3)
        for half in range(2)
    ] + first.fetch(move)
    ready(waits)
    attend, q, k, v, probs = (item.buffer for item in (attend, q, k, v, probs))
    gc[...] = dot_t(attend[...], wo[...]).astype(BF16)
    ready(near)
    halves = lane_halves()
    lower = lax.broadcasted_iota(jnp.int32, (128, 128), 1) < 64

    def attention(half):
        for index in range(pairs):
            lanes = pl.ds(pl.multiple_of(half * wide + index * 128, 128), 128)

            def put(part, rows, value, index=index):
                there = pl.ds(pl.multiple_of((3 * half + part) * wide + index * 128, 128), 128)
                grads[rows, there] = value.astype(BF16)

            for seq in range(seqs):
                rows = slice(seq * 128, seq * 128 + 128)
                grad = gc[rows, lanes]
                p = probs[seq, half * pairs + index]
                full = dot(p.astype(BF16), grad)
                put(2, rows, jnp.where(lower, full[:128], full[128:]))
                gp = dot_t(two_heads(v[rows, lanes], halves), grad)
                parts = []
                for side in (slice(0, 128), slice(128, 256)):
                    g, pp = gp[side], p[side]
                    parts.append(pp * (g - jnp.sum(g * pp, axis=0, keepdims=True)))
                gs = jnp.concatenate(parts, axis=0).astype(BF16)
                put(0, rows, t_dot(gs, two_heads(k[rows, lanes] * SCALE, halves)))
                full = dot(gs, q[rows, lanes] * SCALE)
                put(1, rows, jnp.where(lower, full[:128], full[128:]))

    def products(half, out):
        three = pl.ds(pl.multiple_of(half * 3 * wide, 128), 3 * wide)
        lanes = pl.ds(pl.multiple_of(half * wide, wide), wide)
        block = dot(turned[...], grads[:, three]).astype(BF16)
        block_out = dot(ctx.buffer[...], attend[:, lanes]).astype(BF16)
        for shard in range(shards):
            out.buffer[shard, :tall, : 3 * wide] = block[shard * tall : shard * tall + tall]
            out.buffer[shard, :tall, 3 * wide :] = block_out[shard * tall : shard * tall + tall]

    attention(1 - sec[0])
    ready(later)
    turned[...] = x.buffer[...].T
    products(1 - sec[0], send)
    attention(sec[0])
    products(sec[0], keep)
    little = jnp.concatenate([down.buffer[...], up.buffer[...]], axis=0).astype(BF16)
    for half, out in ((1 - sec[0], send), (sec[0], keep)):
        pad = []
        for part in (0, 2):
            lanes = pl.ds(pl.multiple_of((3 * half + part) * wide, wide), wide)
            pad.append(column_sum(grads[:, lanes].astype(F32)).astype(BF16))
        pad = jnp.concatenate([jnp.concatenate(pad, axis=1), jnp.zeros((15, width), BF16)], axis=0)
        for shard in range(shards):
            out.buffer[shard, tall:, 0:width] = little
            out.buffer[shard, tall:, width:] = pad
    ready(last)
    total = first.buffer[...] + dot_t(grads[...], w[...])
    gx.buffer[...] = total
    gx.flush(move)
    gx_low.buffer[...] = total.astype(BF16)
    gx_low.flush(move)
    move.finish()


def attend_whole(layer, sec, attend, ctx, first, x, q, k, v, probs, wo, wo_other, w, w_other, down, up, shards, low_kind):
    rows, width = x.shape
    wide = (rows, width)
    part = sds((shards, width // shards + 16, 2 * width), BF16)
    return call(
        functools.partial(attend_whole_kernel, layer, shards),
        sec,
        [(attend, NEAR), (ctx, FAR), (first, NEAR)]
        + [(item, FAR) for item in (x, q, k, v, probs)]
        + [(wo, RAW), (wo_other, RAW), (w, RAW), (w_other, RAW), (down, NEAR), (up, NEAR)],
        [(sds(wide, F32), FAR), (sds(wide, BF16), low_kind), (part, NEAR), (part, NEAR)],
        [((width, rows), BF16), ((width, width), BF16), ((width, 3 * width), BF16), (wide, BF16), ((rows, 3 * width), BF16)],
        "attend_grad",
        2 * rows * width * width * 10,
        30 << 20,
    )


def layer_forward(layer, sec, x, front, big, other, small, far=None):
    w_qkv, w_out, w_up, w_down = big
    o_qkv, o_out, o_up, o_down = other
    x_kind = FAR if layer == 0 else NEAR
    q, k, v, probs, (ctx_near, ctx) = front
    (hat_near, hat_one), scale_one, low, act, slope = up_forward(
        layer, sec, x, x_kind, ctx_near, w_out, o_out, w_up, o_up, small
    )
    act_near, act = act if layer == 0 else (act, act)
    kinds = (BOTH, FAR) if layer == 0 else (FAR, NEAR)
    y, hat_two, scale_two = down_forward(layer, sec, act_near, w_down, o_down, hat_near, small, *kinds)
    x = x if far is None else far
    return y, (x, q, k, v, probs, ctx, hat_one, scale_one, low, act, slope, hat_two, scale_two)


class Backward:
    def __init__(self, line, layer, sec, cache, big, other, small, shards):
        self.line, self.layer, self.sec, self.small, self.shards = line, layer, sec, small, shards
        self.cache, self.weights, self.made = cache, tuple(zip(big, other)), {}

    def down(self, gy):
        act, _, hat_two, scale_two = self.cache[-4:]
        kinds = (NEAR, FAR) if self.layer == 0 else (FAR, NEAR)
        second, branch, sums, send, keep = down_grad(
            self.line.sec, gy, kinds[0], hat_two, scale_two, self.small, act, kinds[1]
        )
        self.made.update(second=second, branch=branch, down_sums=sums)
        self.line.add(send, keep)

    def up_inputs(self):
        (w_up, o_up), (w_down, o_down) = self.weights[2:]
        low, _, slope = self.cache[-5:-2]
        return w_down, o_down, slope, low, w_up, o_up, self.shards

    def up_first(self):
        made = self.made
        made["part"], made["up_sums"], send = up_grad(
            self.layer, False, self.line.sec, made["branch"], made["second"], *self.up_inputs()
        )
        self.up_chunk = self.line.add(send, None)

    def up_last(self):
        made = self.made
        hat_one, scale_one = self.cache[-7:-5]
        more = (hat_one, scale_one, self.small, made["up_sums"])
        made["first"], made["attend"], made["up_sums"], self.up_chunk.keep = up_grad(
            self.layer, True, self.line.sec, made["branch"], made["part"], *self.up_inputs(), more
        )

    def up(self):
        made = self.made
        hat_one, scale_one = self.cache[-7:-5]
        ins = self.up_inputs()
        made["first"], made["attend"], made["up_sums"], send, keep = up_whole(
            self.layer, self.line.sec, made["branch"], made["second"], *ins[:-1], hat_one, scale_one, self.small, ins[-1]
        )
        self.line.add(send, keep)

    def attention(self):
        made = self.made
        made["gx"], made["gx_low"], send, keep = attend_whole(
            self.layer, self.line.sec, made["attend"], self.cache[5], made["first"], self.cache[0], *self.heads()
        )
        self.line.add(send, keep)

    def heads(self):
        q, k, v, probs = self.cache[1:5]
        (w_qkv, o_qkv), (w_out, o_out) = self.weights[:2]
        low_kind = FAR if self.layer == 0 else BOTH
        sums = (self.made["down_sums"], self.made["up_sums"])
        return (q, k, v, probs, w_out, o_out, w_qkv, o_qkv) + sums + (self.shards, low_kind)

    def attend_first(self):
        made = self.made
        made["part"], made["turned"], send = attend_grad(
            self.layer, False, self.line.sec, made["attend"], self.cache[5], made["first"], self.cache[0], *self.heads()
        )
        self.attend_chunk = self.line.add(send, None)

    def attend_last(self):
        made = self.made
        made["gx"], made["gx_low"], self.attend_chunk.keep = attend_grad(
            self.layer, True, self.line.sec, made["attend"], self.cache[5], made["part"], made["turned"], *self.heads()
        )


def exchange(array, axis, bit):
    length = lax.axis_size(axis)
    return lax.ppermute(array, axis, [(i, i ^ bit) for i in range(length)])


def pick(array, index, axis):
    return lax.dynamic_index_in_dim(array, index, axis, keepdims=False)


def split_at(rows):
    return (rows // 2 + 15) // 16 * 16


class Sums:
    def __init__(self, columns):
        self.columns, self.ins, self.outs, self.code = columns, [], [], []
        self.rows, self.far, self.later = {}, set(), []

    def use(self, array):
        for index, known in enumerate(self.ins):
            if known is array:
                return index
        self.ins.append(array)
        return len(self.ins) - 1

    def result(self, shape):
        self.outs.append(sds(tuple(shape) + (self.columns,), BF16))
        return len(self.outs) - 1

    def region(self, way, rows):
        first = self.rows.get(way, 0)
        self.rows[way] = first + rows
        return first

    def run(self, ids):
        ways = sorted(self.rows)
        shapes = self.outs + [sds((self.rows[way], self.columns), BF16) for way in ways]
        n_in, n_out = len(self.ins), len(self.outs)

        far = sorted(self.far)
        space = lambda index: pltpu.HBM if index in self.far else pltpu.VMEM

        def kernel(ids_ref, *refs):
            first = n_in + len(shapes)
            sends = dict(zip(ways, refs[n_in + n_out : first]))
            ins, move = list(refs[:n_in]), Mover(refs[-1])
            waits = {}
            for shard in range(self.ins[far[0]].shape[0] if far else 0):
                for index, buffer in zip(far, refs[first:-1]):
                    move.load(refs[index].at[shard], buffer.at[shard])
                    waits.setdefault(shard, []).append(move.last)
                    ins[index] = buffer
            for code in self.code:
                code(ids_ref, ins, refs[n_in : n_in + n_out], sends)
            for shard, items in waits.items():
                ready(items)
                for code in self.later:
                    code(ids_ref, ins, refs[n_in : n_in + n_out], sends, shard)

        vmem = pl.BlockSpec(memory_space=pltpu.VMEM)
        results = pl.pallas_call(
            kernel,
            in_specs=[pl.BlockSpec(memory_space=pltpu.SMEM)]
            + [pl.BlockSpec(memory_space=space(index)) for index in range(n_in)],
            out_specs=[vmem] * len(shapes),
            out_shape=shapes,
            scratch_shapes=[pltpu.VMEM(self.ins[index].shape, BF16) for index in far]
            + [pltpu.SemaphoreType.DMA((8,))],
            compiler_params=pltpu.CompilerParams(vmem_limit_bytes=SPARE),
            name="join_sums",
        )(
            ids,
            *(pltpu.with_memory_space_constraint(array, space(index)) for index, array in enumerate(self.ins)),
        )
        return results[:n_out], dict(zip(ways, results[n_out:]))


def at_rows(first, index, count):
    return pl.ds(pl.multiple_of(first + index * count, 16), count)


def sum_section(sums, chunk):
    kept, got = sums.use(chunk.keep), sums.use(chunk.got["section"])
    if chunk.far:
        sums.far |= {kept, got}
    _, rows, _ = chunk.keep.shape
    cut = chunk.cut
    rest = rows - cut
    top, bottom = sums.result((2, cut)), sums.result((2, rest))
    chunk.first = {"x": sums.region("x", 2 * cut), "y": sums.region("y", 2 * rest)}
    to_x, to_y = chunk.first["x"], chunk.first["y"]

    def code_shard(ids, ins, outs, sends, shard):
        upper = ins[kept][shard, :cut] + ins[got][shard, :cut]
        lower = ins[kept][shard, cut:] + ins[got][shard, cut:]
        row, column = shard // 2, shard % 2

        @pl.when(ids[1] == column)
        def _():
            outs[top][row] = upper

        @pl.when(ids[1] != column)
        def _():
            sends["x"][to_x + row * cut : to_x + row * cut + cut] = upper

        @pl.when(ids[2] == row)
        def _():
            outs[bottom][column] = lower

        @pl.when(ids[2] != row)
        def _():
            sends["y"][to_y + column * rest : to_y + column * rest + rest] = lower

    def code(ids, ins, outs, sends):
        low, high = ids[1], ids[2]
        for i in range(2):
            add = lambda shard, lines: ins[kept][shard, lines] + ins[got][shard, lines]
            sends["x"][to_x + i * cut : to_x + i * cut + cut] = add(2 * i + 1 - low, slice(0, cut))
            outs[top][i] = add(2 * i + low, slice(0, cut))
            sends["y"][to_y + i * rest : to_y + i * rest + rest] = add(2 * (1 - high) + i, slice(cut, rows))
            outs[bottom][i] = add(2 * high + i, slice(cut, rows))

    if chunk.far:
        sums.later.append(code_shard)
    else:
        sums.code.append(code)
    return [top, bottom]


def sum_first(sums, chunk):
    top, bottom = (sums.use(item) for item in chunk.kept)
    got_x, got_y = sums.use(chunk.got["x"]), sums.use(chunk.got["y"])
    at_x, at_y = chunk.first["x"], chunk.first["y"]
    cut, rest = chunk.kept[0].shape[1], chunk.kept[1].shape[1]
    new_top, new_bottom = sums.result((cut,)), sums.result((rest,))
    chunk.first = {"y": sums.region("y", cut), "x": sums.region("x", rest)}
    to_x, to_y = chunk.first["x"], chunk.first["y"]

    def code(ids, ins, outs, sends):
        low, high = ids[1], ids[2]
        upper = lambda i: ins[top][i] + ins[got_x][at_rows(at_x, i, cut)]
        lower = lambda i: ins[bottom][i] + ins[got_y][at_rows(at_y, i, rest)]
        sends["y"][to_y : to_y + cut] = upper(1 - high)
        outs[new_top][...] = upper(high)
        sends["x"][to_x : to_x + rest] = lower(1 - low)
        outs[new_bottom][...] = lower(low)

    sums.code.append(code)
    return [new_top, new_bottom]


def sum_second(sums, chunk):
    top, bottom = (sums.use(item) for item in chunk.kept)
    got_x, got_y = sums.use(chunk.got["x"]), sums.use(chunk.got["y"])
    at_x, at_y = chunk.first["x"], chunk.first["y"]
    cut, rest = chunk.kept[0].shape[0], chunk.kept[1].shape[0]
    part = sums.result((cut + rest,))
    onward = chunk.line.short
    if onward:
        sums.rows["ends"] = max(sums.rows.get("ends", 0), cut + rest)

    def code(ids, ins, outs, sends):
        outs[part][:cut] = ins[top][...] + ins[got_y][at_y : at_y + cut]
        outs[part][cut:] = ins[bottom][...] + ins[got_x][at_x : at_x + rest]
        if onward:

            @pl.when(ids[3] == 1)
            def _():
                sends["ends"][: cut + rest] = outs[part][...]

    sums.code.append(code)
    return [part]


def sum_ends(sums, chunk):
    part, got = sums.use(chunk.kept[0]), sums.use(chunk.got["ends"])
    rows = chunk.kept[0].shape[0]
    chunk.first = {"middle": sums.region("middle", rows)}
    to = chunk.first["middle"]

    def code(ids, ins, outs, sends):
        sends["middle"][to : to + rows] = ins[part][...] + ins[got][:rows]

    sums.code.append(code)
    return []


def sum_middle(sums, chunk):
    sent, got = sums.use(chunk.sent["middle"]), sums.use(chunk.got["middle"])
    at, rows = chunk.first["middle"], chunk.rows
    whole = sums.result((rows,))
    sums.rows["ends"] = max(sums.rows.get("ends", 0), rows)

    def code(ids, ins, outs, sends):
        outs[whole][...] = ins[sent][at : at + rows] + ins[got][at : at + rows]

        @pl.when(ids[3] == 0)
        def _():
            sends["ends"][:rows] = outs[whole][...]

    sums.code.append(code)
    return [whole]


def sum_last(sums, chunk):
    whole, got = sums.use(chunk.kept[0]), sums.use(chunk.got["ends"])
    rows = chunk.rows
    results = [sums.result((rows,))]
    if chunk.partner is not None:
        other = sums.use(chunk.partner.done[0])
        results.append(sums.result((rows,)))

    def code(ids, ins, outs, sends):
        def put(value, outer):
            if chunk.partner is None:
                outs[results[0]][...] = value(slice(None))
                return
            for first, (to_value, to_other) in ((0, results), (1, results[::-1])):

                @pl.when((ids[0] == first) & (ids[3] == outer))
                def _():
                    outs[to_value][...] = value(slice(None))
                    outs[to_other][...] = ins[other][...]

        if chunk.partner is None:
            pl.when(ids[3] == 1)(lambda: put(lambda _: ins[got][:rows], 1))
            pl.when(ids[3] == 0)(lambda: put(lambda _: ins[whole][...], 0))
        else:
            put(lambda _: ins[got][:rows], 1)
            put(lambda _: ins[whole][...], 0)

    sums.code.append(code)
    return results


class Chunk:
    def __init__(self, line, send, keep, partner):
        self.line, self.send, self.keep, self.partner = line, send, keep, partner
        self.at, self.kept, self.got, self.sent, self.done = 0, [], {}, {}, None
        self.rows, self.far = send.shape[1], len(line.chunks) == 0
        self.cut = split_at(self.rows)


class Line:
    def __init__(self, sec):
        self.sec = sec
        self.square = lax.axis_size("inner") == 4
        self.short = lax.axis_size("outer") == 4
        spot, place = lax.axis_index("inner"), lax.axis_index("outer")
        outside = (place == 0) | (place == lax.axis_size("outer") - 1)
        self.ids = jnp.stack([lax.axis_index("section"), spot % 2, spot // 2, outside, spot]).astype(jnp.int32)
        self.chunks, self.made = [], {}
        self.sums = (sum_section, sum_first, sum_second, sum_ends, sum_middle, sum_last)

    def add(self, send, keep):
        count = len(self.chunks)
        chunk = Chunk(self, send, keep, self.chunks[count - 3] if count >= 3 else None)
        self.chunks.append(chunk)
        return chunk

    def move(self, way, array):
        if way == "section":
            return exchange(array, "section", 1)
        if way in ("x", "y"):
            return exchange(array, "inner", 1 if way == "x" else 2)
        return lax.ppermute(array, "outer", [(0, 1), (1, 0), (2, 3), (3, 2)] if way == "ends" else [(1, 2), (2, 1)])

    def advance(self, owner, *works):
        moving = [chunk for chunk in self.chunks if chunk.done is None and chunk.at > 0]
        sends = {}
        if moving and self.square:
            sums = Sums(moving[0].send.shape[-1])
            places = [self.sums[chunk.at - 1](sums, chunk) for chunk in moving]
            outs, sends = sums.run(self.ids)
            for chunk, place in zip(moving, places):
                chunk.kept, chunk.sent = [outs[index] for index in place], sends
        for chunk in moving:
            chunk.at += 1
            if not self.square:
                half = chunk.keep.astype(F32) + chunk.got["section"].astype(F32)
                half = lax.psum_scatter(half.astype(BF16), "inner", scatter_dimension=0, tiled=False)
                chunk.done = [lax.psum(half, "outer")]
            elif chunk.at == 4 and not self.short:
                chunk.done = [lax.psum(chunk.kept[0], "outer")]
            elif chunk.at == 7:
                chunk.done = chunk.kept
        new = [chunk for chunk in self.chunks if chunk.at == 0]
        gots = {way: self.move(way, array) for way, array in sends.items()}
        arrived = [self.move("section", chunk.send) for chunk in new]
        for work in works:
            work()
        fresh = [chunk for chunk in self.chunks if chunk not in new and chunk.at == 0]
        late = [chunk for chunk in self.chunks if chunk.keep is not None and chunk.at == 0]
        owner.made, parts, keeps, gots, arrived = lax.optimization_barrier(
            (owner.made, [chunk.send for chunk in fresh], [chunk.keep for chunk in late], gots, arrived)
        )
        for chunk, part in zip(fresh, parts):
            chunk.send = part
        for chunk, part in zip(late, keeps):
            chunk.keep = part
        for chunk in moving:
            chunk.got = gots
        for chunk, part in zip(new, arrived):
            chunk.at, chunk.got = 1, {"section": part}

    def finish(self):
        while any(chunk.done is None for chunk in self.chunks):
            self.advance(self)
        pairs = []
        for chunk in self.chunks[3:]:
            if len(chunk.done) == 1:
                two, one = chunk.partner.done[0], chunk.done[0]
                mine, send = (jnp.where(self.ids[0] == 0, *item) for item in ((one, two), (two, one)))
            else:
                mine, send = chunk.done
            pairs.append((mine, exchange(send, "section", 1)))
        return pairs


def assemble_kernel(sec, y_one, y_two, y_got, one, two_low, got, y_out, g_out, y, low, wide, sems):
    move = Mover(sems)
    first = sec[0] == 0
    loads = [
        move.choose(first, y_one.ref, y_got.ref, y.at[0]),
        move.choose(first, y_got.ref, y_two.ref, y.at[1]),
        move.choose(first, one.ref, got.ref, wide.at[0]),
    ]
    move.load(two_low.ref, low)
    loads.append(move.last)
    pl.when(first)(lambda: move.choose(first, got.ref, got.ref, wide.at[1]).wait())
    ready(loads)
    move.used += 1

    @pl.when(jnp.logical_not(first))
    def _():
        wide[1] = low[...].astype(F32)

    move.store(y, y_out.ref)
    move.store(wide, g_out.ref)
    move.finish()


def assemble(sec, y_one, y_two, y_got, one, two_low, got):
    flat = one.shape
    return call(
        assemble_kernel,
        sec,
        [(item, RAW) for item in (y_one, y_two, y_got, one, two_low, got)],
        [(sds((2,) + flat, BF16), RAW), (sds((2,) + flat, F32), RAW)],
        [((2,) + flat, BF16), (flat, BF16), ((2,) + flat, F32)],
        "assemble",
        1000,
        10 << 20,
    )


class Rest:
    def __init__(self, sec):
        self.sec, self.made = sec, {}

    def send(self, one, two_low):
        low = two_low.astype(F32)
        self.made["got"] = exchange(jnp.where(self.sec[0] == 0, low, one), "section", 1)

    def assemble(self, y_one, y_two, one, two_low):
        self.made["outs"] = assemble(self.sec, y_one, y_two, self.made["y"], one, two_low, self.made["got"])


def last_kernel(ids, down_mine, down_got, up_mine, up_got, mine, got, w_down, qkv, out, b_qv, b_out, gain, offset, b_up, b_down, w_up, sems):
    move = Mover(sems)
    up_wide = w_up.buffer.shape[1] // 2
    for half, side in ((ids[0], up_mine), (1 - ids[0], up_got)):
        w_up.buffer[:, pl.ds(pl.multiple_of(half * up_wide, up_wide), up_wide)] = side.buffer[...].astype(F32)
    w_up.flush(move)
    hidden, width = w_down.buffer.shape
    for half, side in ((ids[0], down_mine), (1 - ids[0], down_got)):
        rows = jnp.concatenate([side.buffer[:, :hidden], side.buffer[:, hidden:]], axis=0)
        w_down.buffer[:, pl.ds(pl.multiple_of(half * (width // 2), width // 2), width // 2)] = rows.T.astype(F32)
    w_down.flush(move)
    mine, got = mine.buffer, got.buffer
    tall, wide = qkv.buffer.shape[0], out.buffer.shape[1] // 2
    for half, side in ((ids[0], mine), (1 - ids[0], got)):
        for part in range(4):
            block = side[:tall, part * wide : part * wide + wide].astype(F32)
            target, first = (qkv, 2 * part * wide) if part < 3 else (out, 0)
            lanes = pl.ds(pl.multiple_of(first + half * wide, wide), wide)
            target.buffer[:, lanes] = block
    qkv.flush(move)
    out.flush(move)
    rows = mine[tall:, : 2 * wide].astype(F32)
    own, other = (side[tall : tall + 1, 2 * wide :].astype(F32) for side in (mine, got))

    def write(first_half, place):
        left, right = (own, other) if first_half else (other, own)
        span = slice(place * tall, place * tall + tall)
        for row in range(2):
            bias = jnp.concatenate([side[:, row * wide : row * wide + wide] for side in (left, right)], axis=1)
            b_qv.buffer[row : row + 1, :] = bias[:, span]
        b_out.buffer[...] = rows[10:11, span]
        gain.buffer[0:1, :] = rows[8:9, span]
        gain.buffer[1:2, :] = rows[0:1, span]
        offset.buffer[0:1, :] = rows[9:10, span]
        offset.buffer[1:2, :] = rows[1:2, span]
        b_up.buffer[...] = rows[11 + place : 12 + place]
        b_down.buffer[...] = rows[2:3, span]

    for first_half in (True, False):
        for place in range(2 * wide // tall):
            here = (ids[0] == (0 if first_half else 1)) & (ids[4] == place)
            pl.when(here)(functools.partial(write, first_half, place))
    for item in (b_qv, b_out, gain, offset, b_up, b_down):
        item.flush(move)
    move.finish()


def last(ids, down, up, attend, width, shards):
    tall = width // shards
    shapes = [(down[0].shape[1] // 2, width), (tall, 3 * width), (tall, width), (2, tall), (1, tall), (2, tall), (2, tall), (1, width), (1, tall)]
    shapes.append((tall, 2 * up[0].shape[1]))
    return call(
        last_kernel,
        ids,
        [(item, NEAR) for item in (*down, *up, *attend)],
        [(sds(shape, F32), FAR) for shape in shapes],
        [],
        "last",
        1000,
        5 << 20,
    )


def local(
    hidden_in, caption_len, region_len, cotangent, w_qkv, b_qv, w_out, b_out, ln_gain, ln_bias, w_up, b_up, w_down, b_down
):
    section = lax.axis_index("section")
    shards = lax.axis_size("inner")
    sec = section.astype(jnp.int32)[None]
    seqs_local, length, width = hidden_in.shape
    seqs = seqs_local // 2
    rows = seqs * length
    positions = jnp.arange(length, dtype=jnp.int32)[None, :]
    mine = lambda array: lax.dynamic_slice_in_dim(array, section * seqs, seqs, 0)
    caption, region = mine(caption_len)[:, None], mine(region_len)[:, None]
    valid = (positions < caption) | (positions >= CAP) & (positions < CAP + region)
    mask = jnp.concatenate([valid, valid], axis=1).astype(F32).T
    x = mine(hidden_in).reshape(rows, width)
    gy = jnp.where(valid[:, :, None], mine(cotangent), jnp.zeros((), BF16)).reshape(rows, width)

    blocks = w_up.shape[2] // width
    little = jnp.concatenate(
        [b_qv[0], b_out, ln_gain[0], ln_bias[0], b_down, b_up.reshape(blocks, width), jnp.zeros((8 - blocks, width), F32)]
    )
    little_other = exchange(little, "section", 1)
    big = (w_qkv[0], w_out[0], w_up[0], w_down[0])
    o_qkv = exchange(big[0], "section", 1)

    smalls = [jnp.where(section == layer, little, little_other) for layer in (0, 1)]
    o_qkv, smalls, mask, x, late_out, late_up = lax.optimization_barrier(
        (o_qkv, smalls, mask, x, big[1], big[2])
    )
    o_out, o_up = exchange(late_out, "section", 1), exchange(late_up, "section", 1)
    front = attend_forward(0, sec, x, FAR, big[0], o_qkv, smalls[0], mask)
    front, o_out, o_up, late_down = lax.optimization_barrier((front, o_out, o_up, big[3]))
    other = (o_qkv, o_out, o_up, exchange(late_down, "section", 1))
    y_one, cache_one = layer_forward(0, sec, x, front, big, other, smalls[0])
    y_near, y_one = y_one
    made = second_layer(sec, y_near, mask, big, other, smalls[1], gy)
    q, k, v, probs, ctx, hat_one, scale_one, low, slope, y_two = made[:10]
    cache_two = (y_one, q, k, v, probs, ctx, hat_one, scale_one, low, None, slope, None, None)
    line = Line(sec)
    two = Backward(line, 1, sec, cache_two, big, other, smalls[1], shards)
    one = Backward(line, 0, sec, cache_one, big, other, smalls[0], shards)
    two.made.update(second=made[10], branch=made[11], down_sums=made[12])
    line.add(made[13], made[14])
    exchanged_y = exchange(jnp.where(section == 0, y_two, y_one), "section", 1)
    line.advance(two, two.up)
    line.advance(two, two.attention)
    gx_two_near, gx_two_low = two.made["gx_low"]
    line.advance(one, lambda: one.down(gx_two_near))
    line.advance(one, one.up)
    line.advance(one, one.attention)
    gx_one = one.made["gx"]

    rest = Rest(sec)
    rest.made["y"] = exchanged_y
    for _ in range(3):
        line.advance(line)
    line.advance(rest, lambda: rest.send(gx_one, gx_two_low))
    line.advance(rest, lambda: rest.assemble(y_one, y_two, gx_one, gx_two_low))
    activations, input_grads = rest.made["outs"]
    activations = activations.reshape(seqs_local, length, width)
    input_grads = input_grads.reshape(seqs_local, length, width)
    down, up, attend = line.finish()
    g_w_down, g_w_qkv, g_w_out, g_b_qv, g_b_out, g_gain, g_offset, g_b_up, g_b_down, g_w_up = last(
        line.ids, down, up, attend, width, shards
    )
    return (
        activations[None],
        input_grads[None],
        g_w_qkv[None],
        g_b_qv[None],
        g_w_out[None],
        g_b_out,
        g_gain[None],
        g_offset[None],
        g_w_up[None],
        g_b_up,
        g_w_down[None],
        g_b_down,
    )


def solution(mesh):
    rows = ("inner", "outer")
    return jax.shard_map(
        local,
        mesh=mesh,
        in_specs=(
            P(rows, None, None),
            P(rows),
            P(rows),
            P(rows, None, None),
            P("section", None, None),
            P("section", None, None),
            P("section", None, None),
            P("section", None),
            P("section", None, None),
            P("section", None, None),
            P("section", None, None),
            P("section", None),
            P("section", None, None),
            P("section", None),
        ),
        out_specs=(
            P("section", rows, None, None),
            P("section", rows, None, None),
            P("section", "inner", None),
            P("section", None, "inner"),
            P("section", "inner", None),
            P("section", "inner"),
            P("section", None, "inner"),
            P("section", None, "inner"),
            P("section", "inner", None),
            P("section", "inner"),
            P("section", "inner", None),
            P("section", "inner"),
        ),
        check_vma=False,
    )
```
